32 devices in a mesh: section: 4 (over y, x), rows: 8 (over z, core).
Axes of the slice: x: 2, y: 2, z: 4, core: 2. Of those that a mesh axis runs over, the one named last changes fastest.
Arguments:
- inputs: bfloat16 [4, 2, 512, 2000], P('section', None, 'rows'), may hold values from -6 to 6
- resets: int32 [4, 2, 512], P(None, None, 'rows'), may hold values from 0 to 1, as said below
- valid_mask: int32 [4, 2, 512], P(None, None, 'rows'), may hold values from 0 to 1, as said below
- weights: bfloat16 [4, 2000, 2000], P('section'), may hold values from -0.125 to 0.125
- recurrence: float32 [4, 2000], P('section'), may hold values from 0.7 to 0.99
- state_bias: float32 [4, 2000], P('section'), may hold values from -3 to 3
- norm_gain: float32 [4, 2000], P('section'), may hold values from 0.2 to 0.8
- norm_shift: float32 [4, 2000], P('section'), may hold values from -3 to 3
- cotangent: bfloat16 [4, 2, 512, 2000], P('section', None, 'rows'), may hold values from -6 to 6
Outputs:
- outputs: bfloat16 [4, 2, 512, 2000], P('section', None, 'rows')
- grad_inputs: bfloat16 [4, 2, 512, 2000], P('section', None, 'rows')
- grad_weights: float32 [4, 2000, 2000], P('section')
- grad_recurrence: float32 [4, 2000], P('section')
- grad_bias: float32 [4, 2000], P('section')
- grad_gain: float32 [4, 2000], P('section')
- grad_shift: float32 [4, 2000], P('section')
The draws below stay inside these ranges and needn't reach their ends.
Inputs may be any that keep to these rules, and one draw needn't show every extreme that they name: `resets`: 1 marks the first frame of a clip, where the state restarts from zero; frame 0 of every sequence is 1, and in every micro-batch one sequence has no other 1. `valid_mask`: 1 marks a valid frame; frame 0 of every sequence is valid.
All inputs are finite; a program needn't handle non-finite values.
Results may differ from the reference program's by a relative error of at most 0.011.
Values may be sent and summed in bfloat16 or wider, within the bound.
A program may use at most 320 MiB of HBM per device.

```python
import math
import jax
import jax.numpy as jnp
from jax import lax

H = 2000
F_DEV = 64
SEQS = 2
MB = 4
FRAMES = 512
LAYERS = 4


def draw_resets(key, part):
    key = jax.random.fold_in(key, 11)
    key_flags, key_spare = jax.random.split(key)
    shape_all = (MB, SEQS, FRAMES)
    flags = (jax.random.randint(key_flags, shape_all, 0, 2 * F_DEV) == 0).astype(jnp.int32)
    spared = jax.random.randint(key_spare, (MB, 1, 1), 0, SEQS)
    seq_index = lax.broadcasted_iota(jnp.int32, shape_all, 1)
    frame_index = lax.broadcasted_iota(jnp.int32, shape_all, 2)
    flags = jnp.where(seq_index == spared, 0, flags)
    return jnp.where(frame_index == 0, 1, flags).astype(jnp.int32)


def draw_valid_mask(key, part):
    key = jax.random.fold_in(key, 23)
    shape_all = (MB, SEQS, FRAMES)
    marks = (jax.random.randint(key, shape_all, 0, 16) != 0).astype(jnp.int32)
    frame_index = lax.broadcasted_iota(jnp.int32, shape_all, 2)
    return jnp.where(frame_index == 0, 1, marks).astype(jnp.int32)


def shard_levels(own_key, dims, cuts, least, largest):
    loudness, own = 1.0, jax.random.fold_in(own_key, 6)
    for axis_at, blocks in cuts:
        draws = jnp.exp(jax.random.uniform(jax.random.fold_in(own, axis_at), (blocks,), jnp.float32, least / len(cuts), largest / len(cuts)))
        loudness = loudness * jnp.repeat(draws, dims[axis_at] // blocks).reshape([-1 if axis == axis_at else 1 for axis in range(len(dims))])
    return loudness


def normal_values(stream_key, shape, width, reach, cuts=(), kind=jnp.bfloat16):
    array = jax.random.normal(stream_key, shape, jnp.float32) * width
    if len(cuts) > 0:
        array = shard_levels(stream_key, shape, cuts, -0.22, 0.18) * array
    return jnp.clip(array, min=-reach, max=reach).astype(kind)


def setup_inputs(seed: int = 0) -> dict:
    keys = jax.random.split(jax.random.key(seed), 10)
    return {
        "inputs": normal_values(keys[0], (MB, SEQS, FRAMES, H), 1.0, 6.0, ((0, 4), (2, 8))),
        "resets": draw_resets(jax.random.fold_in(keys[9], 71), 0),
        "valid_mask": draw_valid_mask(jax.random.fold_in(keys[9], 71), 0),
        "weights": normal_values(keys[3], (LAYERS, H, H), H ** -0.5, 0.125, ((0, 4),)),
        "recurrence": jnp.clip(jnp.exp(math.log(0.99) - 0.34662463 * jax.random.uniform(keys[4], (LAYERS, H), jnp.float32) ** shard_levels(keys[4], (LAYERS, H), ((0, 4),), -0.2, 0.2)), 0.7, 0.99),
        "state_bias": normal_values(keys[5], (LAYERS, H), 0.5, 3.0, ((0, 4),), jnp.float32),
        "norm_gain": jnp.clip(jnp.exp(math.log(0.8) - 1.3862944 * jax.random.uniform(keys[6], (LAYERS, H), jnp.float32) ** shard_levels(keys[6], (LAYERS, H), ((0, 4),), -0.2, 0.2)), 0.2, 0.8),
        "norm_shift": normal_values(keys[7], (LAYERS, H), 0.5, 3.0, ((0, 4),), jnp.float32),
        "cotangent": normal_values(keys[8], (MB, SEQS, FRAMES, H), 1.0, 6.0, ((0, 4), (2, 8))),
    }


norm_eps = 1e-05

@jax.custom_vjp
def low(v):
    return lax.optimization_barrier(v.astype(jnp.bfloat16)).astype(jnp.float32)

@jax.custom_vjp
def low_back(v):
    return v

def low_keep(v):
    return (low(v), None)

def low_pass(kept, grad):
    return (grad,)

def back_keep(v):
    return (v, None)

def back_low(kept, grad):
    return (low(grad),)
low.defvjp(low_keep, low_pass)
low_back.defvjp(back_keep, back_low)

def decay_combine(earlier, latter):
    return (earlier[0] * latter[0], latter[0] * earlier[1] + latter[1])

def block_forward(params, batch_input, batch_reset, batch_valid):
    weights, recurrence, state_bias, norm_gain, norm_shift = params
    valid_rows = batch_valid.astype(jnp.float32)[..., None]
    keep_state = (1 - batch_reset).astype(jnp.float32)[..., None]
    frame_count = jnp.sum(valid_rows)
    main_path = batch_input
    carry_path = batch_input
    for layer_index in range(LAYERS):
        projected = low_back(jnp.einsum('sfh,hk->sfk', main_path, weights[layer_index], precision=lax.Precision.HIGHEST))
        row_mean = lax.optimization_barrier(jnp.sum(projected * valid_rows, axis=(0, 1))) / frame_count
        centred = projected - row_mean
        spread = lax.optimization_barrier(jnp.sum(centred * centred * valid_rows, axis=(0, 1))) / frame_count
        normed = centred * lax.rsqrt(spread + norm_eps)
        drive_term = norm_gain[layer_index] * normed + norm_shift[layer_index]
        decay_rate = recurrence[layer_index] * keep_state
        unused_decay, states = lax.associative_scan(decay_combine, (decay_rate, drive_term), axis=1)
        hidden = valid_rows * jax.nn.silu(states + state_bias[layer_index])
        if layer_index % 2 == 0:
            carry_path = main_path
            main_path = low_back(low(hidden))
        elif layer_index == LAYERS - 1:
            main_path = low(carry_path + hidden)
        else:
            main_path = low_back(low(carry_path + hidden))
    return main_path

def add_pair(first_term, second_term):
    return first_term + second_term

def reference(inputs, resets, valid_mask, weights, recurrence, state_bias, norm_gain, norm_shift, cotangent):
    params = (weights.astype(jnp.float32), recurrence, state_bias, norm_gain, norm_shift)

    def one_batch(totals, batch_items):
        batch_input, batch_reset, batch_valid, batch_cot = batch_items

        def forward(weight_set, data):
            return block_forward(weight_set, data, batch_reset, batch_valid)
        result, pullback = jax.vjp(forward, params, batch_input.astype(jnp.float32))
        param_grads, input_grad = pullback(batch_cot.astype(jnp.float32))
        totals = jax.tree.map(add_pair, totals, param_grads)
        return (totals, (result.astype(jnp.bfloat16), input_grad.astype(jnp.bfloat16)))
    zero_grads = jax.tree.map(jnp.zeros_like, params)
    totals, (outputs, grad_inputs) = lax.scan(one_batch, zero_grads, (inputs, resets, valid_mask, cotangent))
    return (outputs, grad_inputs, totals[0], totals[1], totals[2], totals[3], totals[4])
```

```python
import functools

import jax
import jax.numpy as jnp
from jax import lax
from jax.experimental import pallas as pl
from jax.experimental.pallas import tpu as pltpu
from jax.sharding import PartitionSpec as P

MESH = pl.DeviceIdType.MESH
norm_eps = 1e-05
F32, BF16 = jnp.float32, jnp.bfloat16
SECTIONS = 4
GROUP = 8


class Sizes:
    def __init__(self, nz, seqs, frames, hidden):
        self.nz, self.seqs, self.frames = nz, seqs, frames
        self.pieces = GROUP // seqs
        self.steps = frames // self.pieces
        self.half = seqs * frames
        self.rows = 2 * self.half
        self.groups = self.rows // GROUP
        self.bw = -(-hidden // 1024) * 128
        self.padded = 8 * self.bw
        self.part = 4 * self.bw // nz
        self.items = 4 * SECTIONS


def wait_bytes(ref, sem):
    pltpu.make_async_copy(ref, ref, sem).wait()


def remote(src, dst, send, recv, device):
    return pltpu.make_async_remote_copy(
        src_ref=src, dst_ref=dst, send_sem=send, recv_sem=recv, device_id=device, device_id_type=MESH
    )


def kernel(
    sz, inp, cot, par_in, mask_in, w_in,
    outg, ging, gout, smallg,
    mainbuf, wbuf, ysend, yrecv, own, xbuf, states, carry_in, chunk_a, chunk_aex, chunk_s0,
    keepf, validf, maskbuf, par, pre_send, pre_recv, ex_send, ex_recv, e1_send, e1_recv, e2_send, e2_recv,
    scal, s1ex, dbuf, dabuf, cex, aexr, dpbuf, pkeep, sibsend, sibrecv, xsend, xrecv, gw, gsend, grecv, gpiece,
    small, outbuf,
    in_ss, in_fs, in_rs, cot_ss, cot_rs, par_ss, par_rs, mask_ss, mask_rs, w_ls, w_ss, w_rs, w_up, w_dn,
    pre_ss, pre_rs, mx_ss, mx_rs, ms_ss, ms_rs, mf_ss, mf_rs, y_ss, y_rs, ex_ss, ex_rs,
    o_ss, o_rs, e1_ss, e1_rs, e2_ss, e2_rs, dp_ss, dp_rs, sb_ss, sb_rs, xp_ss, xp_rs,
    gi_ss, gi_rs, gr_ss, gr_rs, gx_ss, gx_rs, gz_rs, gz_up, gz_dn, gz_sb, gs_rs, sm_ss, sm_rs,
):
    nz, bw, items, groups, steps = sz.nz, sz.bw, sz.items, sz.groups, sz.steps
    pieces, seqs = sz.pieces, sz.seqs
    s, r = lax.axis_index("section"), lax.axis_index("rows")
    y, x, z, c = s // 2, s % 2, r // 2, r % 2
    s_x, s_y, s_d = s + 1 - 2 * x, s + 2 - 4 * y, 3 - s
    r_c = r + 1 - 2 * c
    to_x, to_y, to_d, to_c = (s_x, r), (s_y, r), (s_d, r), (s, r_c)
    j_own, j_x, j_c, j_xc = 2 * x + c, 2 * (1 - x) + c, 2 * x + 1 - c, 2 * (1 - x) + 1 - c
    me = 2 * s + c
    part = sz.part
    sub = lax.broadcasted_iota(jnp.int32, (GROUP, bw), 0)
    place = sub % pieces

    def z_peer(distance):
        return (s, 2 * ((z + distance) % nz) + c)

    def z_slot(p):
        return (z - p + nz - 1) % nz

    def by_seq(rows):
        value = jnp.broadcast_to(rows[seqs - 1], (GROUP, bw))
        for q in range(seqs - 2, -1, -1):
            value = jnp.where(sub < (q + 1) * pieces, jnp.broadcast_to(rows[q], (GROUP, bw)), value)
        return value

    def last_of(value, q):
        return value[(q + 1) * pieces - 1 : (q + 1) * pieces]

    def first_of(value, q):
        return value[q * pieces : q * pieces + 1]

    def entering(a, b, reverse):
        out_a, out_b = [None, None], [None, None]
        t_a = t_b = None
        for h in (1, 0) if reverse else (0, 1):
            ia, ib = a[h], b[h]
            hop = 1
            while hop < pieces:
                if reverse:
                    ok, shift = place < pieces - hop, GROUP - hop
                else:
                    ok, shift = place >= hop, hop
                pa = jnp.where(ok, pltpu.roll(ia, shift, 0), 1.0)
                pb = jnp.where(ok, pltpu.roll(ib, shift, 0), 0.0)
                ib = ia * pb + ib
                ia = ia * pa
                hop *= 2
            if reverse:
                ok, shift, edge = place < pieces - 1, GROUP - 1, first_of
            else:
                ok, shift, edge = place >= 1, 1, last_of
            xa = jnp.where(ok, pltpu.roll(ia, shift, 0), 1.0)
            xb = jnp.where(ok, pltpu.roll(ib, shift, 0), 0.0)
            na = [edge(ia, q) for q in range(seqs)]
            nb = [edge(ib, q) for q in range(seqs)]
            if t_a is not None:
                ea, eb = by_seq(t_a), by_seq(t_b)
                xb = xa * eb + xb
                xa = xa * ea
                nb = [na[q] * t_b[q] + nb[q] for q in range(seqs)]
                na = [na[q] * t_a[q] for q in range(seqs)]
            t_a, t_b = na, nb
            out_a[h], out_b[h] = xa, xb
        return out_a, out_b, t_a, t_b

    def pack(rows):
        rows = rows + [jnp.zeros((1, bw), F32)] * (8 - len(rows))
        value = jnp.zeros((8, bw), F32)
        for q, row in enumerate(rows):
            value = jnp.where(sub == q, jnp.broadcast_to(row, (8, bw)), value)
        return value

    def total(value):
        return jnp.sum(value, axis=0, keepdims=True)

    def over_z(body, start):
        return lax.fori_loop(0, nz, body, start, unroll=nz <= 8)

    def send_z(src, dst_of, send_sem, recv_sem):
        def one(k, _):
            remote(src, dst_of(k - 1), send_sem, recv_sem, z_peer(k)).start()
            return 0

        lax.fori_loop(1, nz, one, 0, unroll=nz <= 8)

    def not_me(t, h):
        return jnp.logical_or(t != s, h != c)

    barrier = pltpu.get_barrier_semaphore()
    for t in (s, s_x, s_y, s_d):
        for q in (r, r_c):
            if not (t is s and q is r):
                pl.semaphore_signal(barrier, inc=1, device_id=(t, q), device_id_type=MESH)

    def greet(k, _):
        pl.semaphore_signal(barrier, inc=1, device_id=z_peer(k), device_id_type=MESH)
        return 0

    lax.fori_loop(1, nz, greet, 0)
    pl.semaphore_wait(barrier, 7 + nz - 1)

    pltpu.make_async_copy(par_in.at[me], par.at[s], par_rs.at[s]).start()
    for n, t in enumerate((s_x, s_y, s_d)):
        remote(par_in.at[2 * t + c], par.at[s], par_ss.at[n], par_rs.at[s], (t, r)).start()
    pltpu.make_async_copy(mask_in, maskbuf.at[c], mask_rs.at[c]).start()
    remote(mask_in, maskbuf.at[c], mask_ss.at[0], mask_rs.at[c], to_c).start()
    pltpu.make_async_copy(w_in.at[y, j_own], wbuf.at[s], w_ls).start()

    def w_cross():
        for n, t in enumerate((s_x, s_y, s_d)):
            src = w_in.at[t // 2, 2 * (t % 2) + c, pl.ds(z * part, part)]
            remote(src, wbuf.at[s, pl.ds(z * part, part)], w_ss.at[n], w_rs.at[s, z], (t, r)).start()

    @pl.when(s == 0)
    def _():
        w_cross()

    in_dst = mainbuf.at[s, :, c]
    pltpu.make_async_copy(inp.at[pl.ds(4 * y, 4)], in_dst, in_rs.at[s, c]).start()
    remote(inp.at[pl.ds(4 * y, 4)], in_dst, in_ss.at[0], in_rs.at[s, c], to_x).start()
    remote(inp.at[pl.ds(4 - 4 * y, 4)], in_dst, in_ss.at[1], in_rs.at[s, c], to_y).start()
    remote(inp.at[pl.ds(4 - 4 * y, 4)], in_dst, in_ss.at[2], in_rs.at[s, c], to_d).start()
    remote(inp.at[pl.ds(4 * y, 4)], in_dst, in_ss.at[3], in_rs.at[s, c], to_c).start()

    wait_bytes(maskbuf.at[0], mask_rs.at[0])
    wait_bytes(maskbuf.at[1], mask_rs.at[1])

    def masks_of(m, _):
        for h in range(2):
            lo, hi = h * steps, (h + 1) * steps
            keepf[m, lo:hi] = maskbuf[h, 0, m].astype(F32).reshape(steps, GROUP, bw)
            validf[m, lo:hi] = maskbuf[h, 1, m].astype(F32).reshape(steps, GROUP, bw)
        return 0

    lax.fori_loop(0, 4, masks_of, 0)
    for t in range(SECTIONS):
        wait_bytes(par.at[t], par_rs.at[t])

    def decays_of(i, _):
        l, m = i // 4, i % 4
        u = jnp.broadcast_to(par[l, 0:1], (GROUP, bw))
        a_h, v_h = [], []
        for h in range(2):
            a = jnp.ones((GROUP, bw), F32)
            v = jnp.zeros((GROUP, bw), F32)
            for t in range(steps):
                d = u * keepf[m, h * steps + t]
                a = d * a
                v = d * v + 1.0
            a_h.append(a)
            v_h.append(v)
        xa, xb, ta, tb = entering(a_h, v_h, False)
        for h in range(2):
            chunk_a[i, h] = a_h[h]
            chunk_aex[i, h] = xa[h]
            chunk_s0[i, h] = xb[h]
        valid_count = total(jnp.sum(validf[m], axis=0))
        value = pack(ta + tb + [valid_count])
        pre_send[i] = value
        pre_recv[nz - 1, i] = value
        return 0

    lax.fori_loop(0, items, decays_of, 0)
    send_z(pre_send, lambda k: pre_recv.at[k], pre_ss, pre_rs)

    for n, t in enumerate((s_x, s_y, s_d)):
        wait_bytes(mainbuf.at[t, :, c], in_rs.at[t, c])
        remote(mainbuf.at[t, :, c], mainbuf.at[t, :, c], in_fs.at[n], in_rs.at[t, c], to_c).start()
    wait_bytes(in_dst, in_rs.at[s, c])

    def w_hop(l, d, finish):
        def piece(p):
            return wbuf.at[l, pl.ds(p * part, part)]

        def move(p, up, down):
            @pl.when(jnp.logical_and(p >= 0, p < nz))
            def _():
                if not finish:
                    wait_bytes(piece(p), w_rs.at[l, p])
                if up:
                    @pl.when(z + 1 < nz)
                    def _():
                        copy = remote(piece(p), piece(p), w_up.at[l, p], w_rs.at[l, p], (s, r + 2))
                        copy.wait_send() if finish else copy.start()
                if down:
                    @pl.when(z >= 1)
                    def _():
                        copy = remote(piece(p), piece(p), w_dn.at[l, p], w_rs.at[l, p], (s, r - 2))
                        copy.wait_send() if finish else copy.start()

        @pl.when(jnp.logical_and(l != s, jnp.logical_and(l < SECTIONS, d < nz)))
        def _():
            @pl.when(d == 0)
            def _():
                move(z, True, True)

            @pl.when(d > 0)
            def _():
                move(z - d, True, False)
                move(z + d, False, True)

    def w_hops(l, first, count, finish=False):
        def one(d, _):
            w_hop(l, d, finish)
            return 0

        lax.fori_loop(first, first + count, one, 0)

    w_hops(0, 0, nz)
    wait_bytes(wbuf.at[s], w_ls)

    @pl.when(s != 0)
    def _():
        w_cross()

    for t in range(SECTIONS):
        for h in range(2):
            src = cot.at[2 * t + h]

            @pl.when(not_me(t, h))
            def _(src=src, t=t, h=h):
                remote(src, dbuf.at[s, c], cot_ss.at[t, h], cot_rs.at[s, c], (t, 2 * z + h)).start()

            @pl.when(jnp.logical_not(not_me(t, h)))
            def _(src=src):
                pltpu.make_async_copy(src, dbuf.at[s, c], cot_rs.at[s, c]).start()

    wait_bytes(pre_recv.at[pl.ds(0, nz - 1)], pre_rs)

    def arrived(i):
        block = mainbuf.at[i, j_x]
        wait_bytes(block, mx_rs.at[i])
        remote(block, block, mf_ss.at[i], mf_rs.at[i], to_c).start()

    def project(i):
        l, m = i // 4, i % 4

        @pl.when(l == 0)
        def _():
            wait_bytes(mainbuf.at[i, :, 1 - c], in_rs.at[m, 1 - c])

        @pl.when(l > 0)
        def _():
            wait_bytes(mainbuf.at[i, j_c], ms_rs.at[i])
            wait_bytes(mainbuf.at[i, j_xc], mf_rs.at[i])
            wait_bytes(ysend.at[m], y_ss.at[m])

        acc = jnp.zeros((sz.rows, 2 * bw), F32)
        for j in range(4):
            acc = acc + jnp.dot(
                mainbuf[i, j].reshape(sz.rows, bw), wbuf[l, j * bw : (j + 1) * bw], preferred_element_type=F32
            )
        ysend[m] = acc[:, bw:].astype(BF16)
        remote(ysend.at[m], yrecv.at[i % 8], y_ss.at[m], y_rs.at[i % 8], to_y).start()
        own[m] = acc[:, :bw].reshape(groups, GROUP, bw)

    def moments(i):
        l, m = i // 4, i % 4
        wait_bytes(yrecv.at[i % 8], y_rs.at[i % 8])
        pre = own[m] + yrecv[i % 8].astype(F32).reshape(groups, GROUP, bw)
        valid = validf[m]
        pre_sum = total(jnp.sum(pre * valid, axis=0))
        local_count = pre_send[i, 2 * seqs : 2 * seqs + 1]
        pivot = pre_sum / jnp.maximum(local_count, 1.0)
        shifted = pre - pivot
        xbuf[i] = shifted
        square = total(jnp.sum(shifted * shifted * valid, axis=0))
        u = jnp.broadcast_to(par[l, 0:1], (GROUP, bw))
        ends = []
        for h in range(2):
            v = jnp.zeros((GROUP, bw), F32)
            for t in range(steps):
                v = (u * keepf[m, h * steps + t]) * v + shifted[h * steps + t]
            ends.append(v)
        unused_a, xb, unused_t, tb = entering([chunk_a[i, 0], chunk_a[i, 1]], ends, False)
        for h in range(2):
            s1ex[m, h] = xb[h]
        value = pack([pre_sum, square] + tb)

        @pl.when(l > 0)
        def _():
            wait_bytes(ex_recv.at[i % 8, pl.ds(0, nz - 1)], ex_ss.at[m])

        ex_send[m] = value
        ex_recv[i % 8, nz - 1] = value
        send_z(ex_send.at[m], lambda k: ex_recv.at[i % 8, k], ex_ss.at[m], ex_rs.at[i % 8])

    def finish_layer(i):
        l, m = i // 4, i % 4
        wait_bytes(ex_recv.at[i % 8, pl.ds(0, nz - 1)], ex_rs.at[i % 8])
        u, bias = par[l, 0:1], par[l, 1:2]
        gain, shift = par[l, 2:3], par[l, 3:4]

        def add_sum(p, carry):
            slot = z_slot(p)
            return (
                carry[0] + ex_recv[i % 8, slot, 0:1],
                carry[1] + pre_recv[slot, i, 2 * seqs : 2 * seqs + 1],
            )

        zero = jnp.zeros((1, bw), F32)
        sum_all, count_all = over_z(add_sum, (zero, zero))
        mean = sum_all / count_all

        def pivot_of(slot):
            count = pre_recv[slot, i, 2 * seqs : 2 * seqs + 1]
            return ex_recv[i % 8, slot, 0:1] / jnp.maximum(count, 1.0), count

        def add_square(p, carry):
            slot = z_slot(p)
            pivot, count = pivot_of(slot)
            return carry + ex_recv[i % 8, slot, 1:2] + count * (pivot - mean) * (pivot - mean)

        var = over_z(add_square, zero) / count_all
        inv = lax.rsqrt(var + norm_eps)
        alpha = gain * inv

        def hop_in(p, carry):
            slot = z_slot(p)
            pivot, unused = pivot_of(slot)
            beta = shift + alpha * (pivot - mean)
            after = []
            for q in range(seqs):
                value = (
                    alpha * ex_recv[i % 8, slot, 2 + q : 3 + q]
                    + beta * pre_recv[slot, i, seqs + q : seqs + q + 1]
                    + pre_recv[slot, i, q : q + 1] * carry[q]
                )
                after.append(jnp.where(p < z, value, carry[q]))
            return tuple(after)

        enter = by_seq(list(over_z(hop_in, (zero,) * seqs)))
        pivot, unused = pivot_of(nz - 1)
        beta = shift + alpha * (pivot - mean)
        offset = (pivot - mean) * inv
        scal[i] = pack([alpha, 1.0 / count_all])
        wide = [jnp.broadcast_to(v, (GROUP, bw)) for v in (u, bias, alpha, beta, inv, offset)]
        u, bias, alpha, beta, inv, offset = wide
        side = mainbuf.at[jnp.maximum(i - 4, 0), j_own]
        odd = (l % 2).astype(F32)
        to_next = l < SECTIONS - 1
        target = jnp.minimum(i + 4, items - 1)
        for h in range(2):
            v = alpha * s1ex[m, h] + beta * chunk_s0[i, h] + chunk_aex[i, h] * enter
            carry_in[i, h] = v
            hidden = []
            for t in range(steps):
                g = h * steps + t
                shifted = xbuf[i, g]
                v = (u * keepf[m, g]) * v + (alpha * shifted + beta)
                states[i, g] = v
                xbuf[i, g] = shifted * inv + offset
                w = v + bias
                hidden.append(validf[m, g] * (w * jax.nn.sigmoid(w)))
            value = jnp.concatenate(hidden, axis=0) + odd * side[h].astype(F32)
            outbuf[m, h] = value.astype(BF16)

        @pl.when(to_next)
        def _():
            block = mainbuf.at[target, j_own]
            block[...] = outbuf[m]
            remote(block, block, mx_ss.at[target], mx_rs.at[target], to_x).start()
            remote(block, block, ms_ss.at[target], ms_rs.at[target], to_c).start()

        @pl.when(jnp.logical_not(to_next))
        def _():
            for h in range(2):
                @pl.when(not_me(m, h))
                def _(h=h):
                    remote(outbuf.at[m, h], outg.at[me], o_ss.at[m, h], o_rs.at[me], (m, 2 * z + h)).start()

                @pl.when(jnp.logical_not(not_me(m, h)))
                def _(h=h):
                    pltpu.make_async_copy(outbuf.at[m, h], outg.at[me], o_rs.at[me]).start()

    hop_count = -(-nz // 4)

    def forward_tick(k, _):
        @pl.when(k < items)
        def _():
            project(k)

        @pl.when(k >= 2)
        def _():
            finish_layer(k - 2)

        @pl.when(jnp.logical_and(k >= 1, k < items + 1))
        def _():
            moments(k - 1)

        @pl.when(jnp.logical_and(k + 1 >= 4, k + 1 < items))
        def _():
            arrived(k + 1)

        @pl.when(k < 12)
        def _():
            w_hops(k // 4 + 1, (k % 4) * hop_count, hop_count)

        return 0

    lax.fori_loop(0, items + 2, forward_tick, 0)

    def back_index(b):
        l, m = SECTIONS - 1 - b // 4, b % 4
        return l, m, l * 4 + m

    def act_back(b):
        l, m, i = back_index(b)

        @pl.when(b < 4)
        def _():
            for h in range(2):
                wait_bytes(dbuf.at[m, h], cot_rs.at[m, h])

        u = jnp.broadcast_to(par[l, 0:1], (GROUP, bw))
        bias = jnp.broadcast_to(par[l, 1:2], (GROUP, bw))
        ends = [None, None]
        sum_act = jnp.zeros((GROUP, bw), F32)
        for h in (1, 0):
            grad = dbuf[b, h].astype(F32).reshape(steps, GROUP, bw)
            v = jnp.zeros((GROUP, bw), F32)
            for t in range(steps - 1, -1, -1):
                g = h * steps + t
                w = states[i, g] + bias
                sg = jax.nn.sigmoid(w)
                da = grad[t] * validf[m, g] * (sg * (1.0 + w * (1.0 - sg)))
                dabuf[m, g] = da
                sum_act = sum_act + da
                v = (u * keepf[m, g]) * (da + v)
            ends[h] = v
        xa, xb, unused, tb = entering([chunk_a[i, 0], chunk_a[i, 1]], ends, True)
        for h in range(2):
            aexr[m, h] = xa[h]
            cex[m, h] = xb[h]
        value = pack(tb + [total(sum_act)])

        @pl.when(b >= 4)
        def _():
            wait_bytes(e1_recv.at[b % 8, pl.ds(0, nz - 1)], e1_ss.at[m])

        e1_send[m] = value
        e1_recv[b % 8, nz - 1] = value
        send_z(e1_send.at[m], lambda k: e1_recv.at[b % 8, k], e1_ss.at[m], e1_rs.at[b % 8])

    def state_back(b):
        l, m, i = back_index(b)
        wait_bytes(e1_recv.at[b % 8, pl.ds(0, nz - 1)], e1_rs.at[b % 8])
        zero = jnp.zeros((1, bw), F32)

        def hop_in(n, carry):
            p = nz - 1 - n
            slot = z_slot(p)
            after = []
            for q in range(seqs):
                value = e1_recv[b % 8, slot, q : q + 1] + pre_recv[slot, i, q : q + 1] * carry[q]
                after.append(jnp.where(p > z, value, carry[q]))
            return tuple(after) + (carry[seqs] + e1_recv[b % 8, slot, seqs : seqs + 1],)

        *enter, sum_act = over_z(hop_in, (zero,) * (seqs + 1))
        enter = by_seq(enter)
        u = jnp.broadcast_to(par[l, 0:1], (GROUP, bw))
        sum_shift = jnp.zeros((GROUP, bw), F32)
        sum_gain = jnp.zeros((GROUP, bw), F32)
        sum_rate = jnp.zeros((GROUP, bw), F32)
        for h in (1, 0):
            v = cex[m, h] + aexr[m, h] * enter
            for t in range(steps - 1, -1, -1):
                g = h * steps + t
                keep = keepf[m, g]
                ds = dabuf[m, g] + v
                dabuf[m, g] = ds
                sum_shift = sum_shift + ds
                sum_gain = sum_gain + ds * xbuf[i, g]
                before = carry_in[i, h] if t == 0 else states[i, g - 1]
                sum_rate = sum_rate + (ds * keep) * before
                v = (u * keep) * ds
        value = pack([total(sum_gain), total(sum_shift), total(sum_rate)])

        @pl.when(b >= 4)
        def _():
            wait_bytes(e2_recv.at[b % 8, pl.ds(0, nz - 1)], e2_ss.at[m])

        e2_send[m] = value
        e2_recv[b % 8, nz - 1] = value
        send_z(e2_send.at[m], lambda k: e2_recv.at[b % 8, k], e2_ss.at[m], e2_rs.at[b % 8])
        added = pack([zero, zero, zero, sum_act])

        @pl.when(m == 0)
        def _():
            small[l] = added

        @pl.when(m > 0)
        def _():
            small[l] = small[l] + added

    def norm_back(b):
        l, m, i = back_index(b)
        wait_bytes(e2_recv.at[b % 8, pl.ds(0, nz - 1)], e2_rs.at[b % 8])

        def add(p, carry):
            return carry + e2_recv[b % 8, z_slot(p)]

        sums = over_z(add, jnp.zeros((8, bw), F32))
        small[l] = small[l] + sums
        alpha = jnp.broadcast_to(scal[i, 0:1], (GROUP, bw))
        per_count = scal[i, 1:2]
        gain_part = jnp.broadcast_to(sums[0:1] * per_count, (GROUP, bw))
        shift_part = jnp.broadcast_to(sums[1:2] * per_count, (GROUP, bw))
        rows = []
        for g in range(groups):
            rows.append(alpha * (dabuf[m, g] - validf[m, g] * (shift_part + xbuf[i, g] * gain_part)))
        dpbuf[i, 0] = jnp.concatenate(rows, axis=0).astype(BF16)
        remote(dpbuf.at[i, 0], dpbuf.at[i, 1], dp_ss.at[i], dp_rs.at[i], to_y).start()

    nt = (((1,), (1,)), ((), ()))
    tn = (((0,), (0,)), ((), ()))

    def input_back(b):
        l, m, i = back_index(b)
        wait_bytes(dpbuf.at[i, 1], dp_rs.at[i])
        dp = jnp.concatenate([dpbuf[i, 0], dpbuf[i, 1]], axis=1)

        def toward(j):
            w = wbuf[l, pl.ds(pl.multiple_of(j * bw, bw), bw), :]
            return lax.dot_general(dp, w, nt, preferred_element_type=F32)

        @pl.when(b >= 4)
        def _():
            wait_bytes(sibsend.at[m], sb_ss.at[m])

        sibsend[m, 0] = toward(j_c).astype(BF16)
        sibsend[m, 1] = toward(j_xc).astype(BF16)
        remote(sibsend.at[m], sibrecv.at[b % 8], sb_ss.at[m], sb_rs.at[b % 8], to_c).start()
        pkeep[m, 0] = toward(j_own)
        pkeep[m, 1] = toward(j_x)

    def weight_back(b):
        l, m, i = back_index(b)
        dp = jnp.concatenate([dpbuf[i, 0], dpbuf[i, 1]], axis=1)
        for j in range(4):
            rows = pl.ds(j * bw, bw)
            new = lax.dot_general(mainbuf[i, j].reshape(sz.rows, bw), dp, tn, preferred_element_type=F32)

            @pl.when(m == 0)
            def _(new=new, rows=rows):
                gw[rows] = new

            @pl.when(jnp.logical_and(m > 0, m < 3))
            def _(new=new, rows=rows):
                gw[rows] = gw[rows] + new

            @pl.when(m == 3)
            def _(new=new, rows=rows):
                gsend[l, rows] = (gw[rows] + new).astype(BF16)

        @pl.when(m == 3)
        def _():
            def one(k, _):
                p = (z + k) % nz
                src = gsend.at[l, pl.ds(p * part, part)]
                remote(src, grecv.at[l, k - 1], gr_ss.at[l], gr_rs.at[l], z_peer(k)).start()
                return 0

            lax.fori_loop(1, nz, one, 0)

    def cross_back(b):
        m = b % 4
        wait_bytes(sibrecv.at[b % 8], sb_rs.at[b % 8])

        @pl.when(b >= 4)
        def _():
            wait_bytes(xsend.at[m], xp_ss.at[m])

        xsend[m] = (pkeep[m, 1] + sibrecv[b % 8, 1].astype(F32)).astype(BF16)
        remote(xsend.at[m], xrecv.at[b % 8], xp_ss.at[m], xp_rs.at[b % 8], to_x).start()
        pkeep[m, 0] = pkeep[m, 0] + sibrecv[b % 8, 0].astype(F32)

    def join_back(b):
        l, m, i = back_index(b)
        wait_bytes(xrecv.at[b % 8], xp_rs.at[b % 8])
        even = (1 - l % 2).astype(F32)
        side = dbuf[jnp.maximum(b - 4, 0)].astype(F32).reshape(sz.rows, bw)
        value = pkeep[m, 0] + xrecv[b % 8].astype(F32) + even * side
        dbuf[b + 4] = value.astype(BF16).reshape(2, sz.half, bw)

        @pl.when(l == 0)
        def _():
            for h in range(2):
                src = dbuf.at[b + 4, h]

                @pl.when(not_me(m, h))
                def _(src=src, h=h):
                    remote(src, ging.at[me], gi_ss.at[m, h], gi_rs.at[me], (m, 2 * z + h)).start()

                @pl.when(jnp.logical_not(not_me(m, h)))
                def _(src=src):
                    pltpu.make_async_copy(src, ging.at[me], gi_rs.at[me]).start()

    def gather_weights(l):
        wait_bytes(grecv.at[l], gr_rs.at[l])

        def add(k, carry):
            return carry + grecv[l, k].astype(F32)

        start = gsend[l, pl.ds(pl.multiple_of(z * part, part), part), :].astype(F32)
        gpiece[l] = lax.fori_loop(0, nz - 1, add, start).astype(BF16)

        @pl.when(l != s)
        def _():
            remote(gpiece.at[l], gout.at[c, z, s], gx_ss.at[l], gx_rs.at[s], (l, r)).start()

        @pl.when(l == s)
        def _():
            pltpu.make_async_copy(gpiece.at[l], gout.at[c, z, s], gx_rs.at[s]).start()

    def backward_tick(k, _):
        @pl.when(k >= 4)
        def _():
            join_back(k - 4)

        @pl.when(k < items)
        def _():
            act_back(k)

        @pl.when(jnp.logical_and(k >= 3, k < items + 3))
        def _():
            input_back(k - 3)

        @pl.when(jnp.logical_and(k >= 1, k < items + 1))
        def _():
            state_back(k - 1)

        @pl.when(jnp.logical_and(k >= 3, k < items + 3))
        def _():
            cross_back(k - 3)

        @pl.when(jnp.logical_and(k >= 2, k < items + 2))
        def _():
            norm_back(k - 2)

        @pl.when(jnp.logical_and(k >= 3, k < items + 3))
        def _():
            weight_back(k - 3)

        @pl.when(jnp.logical_and(k >= 10, k % 4 == 2))
        def _():
            gather_weights(SECTIONS - 1 - (k - 10) // 4)

        return 0

    lax.fori_loop(0, items + 4, backward_tick, 0)

    for t in range(SECTIONS):
        for h in range(2):
            @pl.when(not_me(t, h))
            def _(t=t, h=h):
                remote(small.at[t], smallg.at[me], sm_ss.at[t, h], sm_rs.at[me], (t, 2 * z + h)).start()

            @pl.when(jnp.logical_not(not_me(t, h)))
            def _(t=t):
                pltpu.make_async_copy(small.at[t], smallg.at[me], sm_rs.at[me]).start()

    gather_weights(0)
    for t in range(SECTIONS):
        wait_bytes(gout.at[c, z, t], gx_rs.at[t])

    def g_move(p, up, down, finish):
        @pl.when(jnp.logical_and(p >= 0, p < nz))
        def _():
            block = gout.at[c, p]
            if not finish:
                @pl.when(p != z)
                def _():
                    wait_bytes(block, gz_rs.at[p])
            if up:
                @pl.when(z + 1 < nz)
                def _():
                    copy = remote(block, block, gz_up.at[p], gz_rs.at[p], (s, r + 2))
                    copy.wait_send() if finish else copy.start()
            if down:
                @pl.when(z >= 1)
                def _():
                    copy = remote(block, block, gz_dn.at[p], gz_rs.at[p], (s, r - 2))
                    copy.wait_send() if finish else copy.start()
            copy = remote(block, block, gz_sb.at[p], gs_rs.at[p], to_c)
            copy.wait_send() if finish else copy.start()

    def g_hops(finish):
        g_move(z, True, True, finish)

        def one(d, _):
            g_move(z - d, True, False, finish)
            g_move(z + d, False, True, finish)
            return 0

        lax.fori_loop(1, nz, one, 0)

    g_hops(False)

    def drain_z(p, _):
        wait_bytes(gout.at[1 - c, p], gs_rs.at[p])
        return 0

    lax.fori_loop(0, nz, drain_z, 0)
    for e in range(8):
        wait_bytes(outg.at[e], o_rs.at[e])
        wait_bytes(ging.at[e], gi_rs.at[e])
        wait_bytes(smallg.at[e], sm_rs.at[e])
    g_hops(True)
    for l in range(SECTIONS):
        w_hops(l, 0, nz, True)
        wait_bytes(grecv.at[l], gr_ss.at[l])

        @pl.when(l != s)
        def _(l=l):
            wait_bytes(gpiece.at[l], gx_ss.at[l])

        wait_bytes(ysend.at[l], y_ss.at[l])
        wait_bytes(ex_recv.at[l, pl.ds(0, nz - 1)], ex_ss.at[l])
        wait_bytes(e1_recv.at[l, pl.ds(0, nz - 1)], e1_ss.at[l])
        wait_bytes(e2_recv.at[l, pl.ds(0, nz - 1)], e2_ss.at[l])
        wait_bytes(sibsend.at[l], sb_ss.at[l])
        wait_bytes(xsend.at[l], xp_ss.at[l])
        for h in range(2):
            @pl.when(not_me(l, h))
            def _(l=l, h=h):
                wait_bytes(dbuf.at[s, c], cot_ss.at[l, h])
                wait_bytes(outbuf.at[l, h], o_ss.at[l, h])
                wait_bytes(dbuf.at[items + l, h], gi_ss.at[l, h])
                wait_bytes(small.at[l], sm_ss.at[l, h])

    def drain(i, _):
        wait_bytes(dpbuf.at[i, 0], dp_ss.at[i])

        @pl.when(i >= 4)
        def _():
            wait_bytes(mainbuf.at[i, j_own], mx_ss.at[i])
            wait_bytes(mainbuf.at[i, j_own], ms_ss.at[i])
            wait_bytes(mainbuf.at[i, j_x], mf_ss.at[i])

        return 0

    lax.fori_loop(0, items, drain, 0)
    for n in range(4):
        wait_bytes(in_dst, in_ss.at[n])
    for n, t in enumerate((s_x, s_y, s_d)):
        wait_bytes(mainbuf.at[t, :, c], in_fs.at[n])
        wait_bytes(par.at[s], par_ss.at[n])
        wait_bytes(wbuf.at[s, pl.ds(z * part, part)], w_ss.at[n])
    wait_bytes(maskbuf.at[c], mask_ss.at[0])
    wait_bytes(pre_recv.at[pl.ds(0, nz - 1)], pre_ss)


def run_kernel(sz, inp, cot, par, masks, weights):
    nz, bw, items, groups = sz.nz, sz.bw, sz.items, sz.groups
    half, rows, part = sz.half, sz.rows, sz.part
    dma = pltpu.SemaphoreType.DMA
    vm = pltpu.VMEM
    step = (GROUP, bw)
    scratch = [
        vm((items, 4, 2, half, bw), BF16),
        vm((SECTIONS, 4 * bw, 2 * bw), BF16),
        vm((4, rows, bw), BF16),
        vm((8, rows, bw), BF16),
        vm((4, groups) + step, F32),
        vm((items, groups) + step, F32),
        vm((items, groups) + step, F32),
        vm((items, 2) + step, F32),
        vm((items, 2) + step, F32),
        vm((items, 2) + step, F32),
        vm((items, 2) + step, F32),
        vm((4, groups) + step, F32),
        vm((4, groups) + step, F32),
        vm((2, 2, 4, half, bw), BF16),
        vm((SECTIONS,) + step, F32),
        vm((items,) + step, F32),
        vm((nz, items) + step, F32),
        vm((4,) + step, F32),
        vm((8, nz) + step, F32),
        vm((4,) + step, F32),
        vm((8, nz) + step, F32),
        vm((4,) + step, F32),
        vm((8, nz) + step, F32),
        vm((items,) + step, F32),
        vm((4, 2) + step, F32),
        vm((items + 4, 2, half, bw), BF16),
        vm((4, groups) + step, F32),
        vm((4, 2) + step, F32),
        vm((4, 2) + step, F32),
        vm((items, 2, rows, bw), BF16),
        vm((4, 2, rows, bw), F32),
        vm((4, 2, rows, bw), BF16),
        vm((8, 2, rows, bw), BF16),
        vm((4, rows, bw), BF16),
        vm((8, rows, bw), BF16),
        vm((4 * bw, 2 * bw), F32),
        vm((SECTIONS, 4 * bw, 2 * bw), BF16),
        vm((SECTIONS, nz - 1, part, 2 * bw), BF16),
        vm((SECTIONS, part, 2 * bw), BF16),
        vm((SECTIONS,) + step, F32),
        vm((4, 2, half, bw), BF16),
    ]
    sems = [
        dma((4,)), dma((3,)), dma((4, 2)), dma((4, 2)), dma((4, 2)), dma((3,)), dma((4,)),
        dma((1,)), dma((2,)), dma, dma((3,)), dma((4, nz)), dma((4, nz)), dma((4, nz)),
        dma, dma, dma((items,)), dma((items,)), dma((items,)), dma((items,)), dma((items,)), dma((items,)),
        dma((4,)), dma((8,)), dma((4,)), dma((8,)),
        dma((4, 2)), dma((8,)), dma((4,)), dma((8,)), dma((4,)), dma((8,)),
        dma((items,)), dma((items,)), dma((4,)), dma((8,)), dma((4,)), dma((8,)),
        dma((4, 2)), dma((8,)), dma((4,)), dma((4,)), dma((4,)), dma((4,)),
        dma((nz,)), dma((nz,)), dma((nz,)), dma((nz,)), dma((nz,)), dma((4, 2)), dma((8,)),
    ]
    anywhere = pl.BlockSpec(memory_space=pl.ANY)
    return pl.pallas_call(
        functools.partial(kernel, sz),
        out_shape=(
            jax.ShapeDtypeStruct((8, half, bw), BF16),
            jax.ShapeDtypeStruct((8, half, bw), BF16),
            jax.ShapeDtypeStruct((2, nz, 4, part, 2 * bw), BF16),
            jax.ShapeDtypeStruct((8, 8, bw), F32),
        ),
        in_specs=[anywhere] * 5,
        out_specs=(anywhere,) * 4,
        scratch_shapes=scratch + sems,
        compiler_params=pltpu.CompilerParams(
            collective_id=0, has_side_effects=True, vmem_limit_bytes=63 * 2**20
        ),
    )(inp, cot, par, masks, weights)


def local(sz, inputs, resets, valid_mask, weights, recurrence, state_bias, norm_gain, norm_shift, cotangent):
    hidden = inputs.shape[-1]
    bw, padded, seqs, pieces, steps = sz.bw, sz.padded, sz.seqs, sz.pieces, sz.steps
    spare = padded - hidden

    def to_blocks(a):
        a = a[0].reshape(seqs, pieces, steps, hidden).transpose(2, 0, 1, 3).reshape(sz.half, hidden)
        a = jnp.pad(a, ((0, 0), (0, spare)))
        return a.reshape(sz.half, 8, bw).transpose(1, 0, 2)

    def from_blocks(a):
        a = a.transpose(1, 0, 2).reshape(sz.half, padded)[:, :hidden]
        return a.reshape(steps, seqs, pieces, hidden).transpose(1, 2, 0, 3).reshape(1, seqs, sz.frames, hidden)

    def to_steps(flags):
        flags = flags.reshape(4, seqs, pieces, steps).transpose(0, 3, 1, 2).reshape(4, sz.half, 1)
        return jnp.broadcast_to(flags.astype(BF16), (4, sz.half, bw))

    masks = jnp.stack([to_steps(1 - resets), to_steps(valid_mask)])
    par = jnp.concatenate([recurrence, state_bias, norm_gain, norm_shift], axis=0)
    par = jnp.pad(par, ((0, 4), (0, spare))).reshape(8, 8, bw).transpose(1, 0, 2)
    w = jnp.pad(weights[0], ((0, spare), (0, spare))).reshape(2, 4 * bw, 2, 4, bw)
    w = jnp.stack([w[0], w[1, :, ::-1]]).transpose(0, 3, 1, 2, 4).reshape(2, 4, 4 * bw, 2 * bw)
    outg, ging, gout, smallg = run_kernel(sz, to_blocks(inputs), to_blocks(cotangent), par, masks, w)
    g = gout.reshape(2, sz.nz, 2, 2, sz.part, 2, bw)
    g = jnp.stack([g[:, :, 0], g[:, :, 1, :, :, ::-1]])
    g = g.transpose(0, 2, 4, 5, 3, 1, 6).reshape(padded, padded)[:hidden, :hidden].astype(F32)
    small = smallg.transpose(1, 0, 2).reshape(8, padded)[:, :hidden]
    return (
        from_blocks(outg),
        from_blocks(ging),
        g[None],
        small[2:3],
        small[3:4],
        small[0:1],
        small[1:2],
    )


def solution(mesh):
    def step(inputs, *rest):
        sz = Sizes(mesh.shape["rows"] // 2, inputs.shape[1], inputs.shape[2], inputs.shape[3])
        return local(sz, inputs, *rest)

    frames = P("section", None, "rows", None)
    flags = P(None, None, "rows")
    vectors = P("section", None)
    matrix = P("section", None, None)
    return jax.shard_map(
        step,
        mesh=mesh,
        in_specs=(frames, flags, flags, matrix, vectors, vectors, vectors, vectors, frames),
        out_specs=(frames, frames, matrix, vectors, vectors, vectors, vectors),
        check_vma=False,
    )
```

```python
import functools

import jax
import jax.numpy as jnp
from jax import lax
from jax.experimental import pallas as pl
from jax.experimental.pallas import tpu as pltpu
from jax.sharding import PartitionSpec as P

MESH = pl.DeviceIdType.MESH
norm_eps = 1e-05
F32, BF16 = jnp.float32, jnp.bfloat16
SECTIONS = 4
GROUP = 8


class Sizes:
    def __init__(self, nz, seqs, frames, hidden):
        self.nz, self.seqs, self.frames = nz, seqs, frames
        self.pieces = GROUP // seqs
        self.steps = frames // self.pieces
        self.half = seqs * frames
        self.rows = 2 * self.half
        self.groups = self.rows // GROUP
        self.bw = -(-hidden // 1024) * 128
        self.padded = 8 * self.bw
        self.part = 4 * self.bw // nz
        self.items = 4 * SECTIONS
        self.hidden = hidden
        self.last = hidden - 7 * self.bw


def wait_bytes(ref, sem):
    pltpu.make_async_copy(ref, ref, sem).wait()


def local_copy(src, dst, sem):
    pltpu.make_async_copy(src, dst, sem).start()


def remote(src, dst, send, recv, device):
    return pltpu.make_async_remote_copy(
        src_ref=src, dst_ref=dst, send_sem=send, recv_sem=recv, device_id=device, device_id_type=MESH
    )


def kernel(
    sz, inp_raw, cot_raw, w_raw, resets, valid_mask, recurrence, state_bias, norm_gain, norm_shift,
    out, grad_inp, grad_rec, grad_bias, grad_gain, grad_shift, gout,
    mainbuf, wbuf, ysend, yrecv, own, xbuf, states, carry_in, chunk_a, chunk_aex, chunk_s0,
    keepf, validf, flagbuf, par, parblk, pre_send, pre_recv, ex_send, ex_recv, e1_send, e1_recv,
    scal, slopes, s1ex, dbuf, cex, aexr, dpbuf, pkeep, sibsend, sibrecv, xsend, xrecv, gw, gsend, grecv,
    gpiece, small, small_recv, outbuf, raw, blocks, wst, wx, outg, ging, smallg, blank,
    raw_ls, wst_ls, in_ss, in_fs, in_rs, cot_ss, cot_rs, par_ss, par_rs, flag_ss, flag_rs, w_ss, w_rs, w_fs,
    pre_ss, pre_rs, mx_ss, mx_rs, ms_ss, ms_rs, mf_ss, mf_rs, y_ss, y_rs, ex_ss, ex_rs,
    o_ss, o_rs, e1_ss, e1_rs, dp_ss, dp_rs, sb_ss, sb_rs, xp_ss, xp_rs,
    gi_ss, gi_rs, gr_ss, gr_rs, gx_ss, gx_rs, gz_rs, gz_up, gz_dn, gz_sb, gs_rs, st_ss, st_rs, sm_ss, sm_rs,
):
    nz, bw, items, groups, steps = sz.nz, sz.bw, sz.items, sz.groups, sz.steps
    pieces, seqs = sz.pieces, sz.seqs
    s, r = lax.axis_index("section"), lax.axis_index("rows")
    y, x, z, c = s // 2, s % 2, r // 2, r % 2
    s_x, s_y, s_d = s + 1 - 2 * x, s + 2 - 4 * y, 3 - s
    r_c = r + 1 - 2 * c
    to_x, to_y, to_d, to_c = (s_x, r), (s_y, r), (s_d, r), (s, r_c)
    j_own, j_x, j_c, j_xc = 2 * x + c, 2 * (1 - x) + c, 2 * x + 1 - c, 2 * (1 - x) + 1 - c
    me = 2 * s + c
    part, half, last = sz.part, sz.half, sz.last
    mine = SECTIONS - 1 - s
    pair_half = z % 2
    to_pair = (s, r + 2 - 4 * pair_half)
    sub = lax.broadcasted_iota(jnp.int32, (GROUP, bw), 0)
    place = sub % pieces

    def z_peer(distance):
        return (s, 2 * ((z + distance) % nz) + c)

    def z_slot(p):
        return (z - p + nz - 1) % nz

    def by_seq(rows):
        value = jnp.broadcast_to(rows[seqs - 1], (GROUP, bw))
        for q in range(seqs - 2, -1, -1):
            value = jnp.where(sub < (q + 1) * pieces, jnp.broadcast_to(rows[q], (GROUP, bw)), value)
        return value

    def last_of(value, q):
        return value[(q + 1) * pieces - 1 : (q + 1) * pieces]

    def first_of(value, q):
        return value[q * pieces : q * pieces + 1]

    def entering(a, b, reverse):
        out_a, out_b = [None, None], [None, None]
        t_a = t_b = None
        for h in (1, 0) if reverse else (0, 1):
            ia, ib = a[h], b[h]
            hop = 1
            while hop < pieces:
                if reverse:
                    ok, shift = place < pieces - hop, GROUP - hop
                else:
                    ok, shift = place >= hop, hop
                pa = jnp.where(ok, pltpu.roll(ia, shift, 0), 1.0)
                pb = jnp.where(ok, pltpu.roll(ib, shift, 0), 0.0)
                ib = ia * pb + ib
                ia = ia * pa
                hop *= 2
            if reverse:
                ok, shift, edge = place < pieces - 1, GROUP - 1, first_of
            else:
                ok, shift, edge = place >= 1, 1, last_of
            xa = jnp.where(ok, pltpu.roll(ia, shift, 0), 1.0)
            xb = jnp.where(ok, pltpu.roll(ib, shift, 0), 0.0)
            na = [edge(ia, q) for q in range(seqs)]
            nb = [edge(ib, q) for q in range(seqs)]
            if t_a is not None:
                ea, eb = by_seq(t_a), by_seq(t_b)
                xb = xa * eb + xb
                xa = xa * ea
                nb = [na[q] * t_b[q] + nb[q] for q in range(seqs)]
                na = [na[q] * t_a[q] for q in range(seqs)]
            t_a, t_b = na, nb
            out_a[h], out_b[h] = xa, xb
        return out_a, out_b, t_a, t_b

    def pack(rows):
        rows = rows + [jnp.zeros((1, bw), F32)] * (8 - len(rows))
        value = jnp.zeros((8, bw), F32)
        for q, row in enumerate(rows):
            value = jnp.where(sub == q, jnp.broadcast_to(row, (8, bw)), value)
        return value

    def total(value):
        return jnp.sum(value, axis=0, keepdims=True)

    def over_z(body, start):
        return lax.fori_loop(0, nz, body, start, unroll=nz <= 8)

    def send_z(src, dst_of, send_sem, recv_sem):
        def one(k, _):
            remote(src, dst_of(k - 1), send_sem, recv_sem, z_peer(k)).start()
            return 0

        lax.fori_loop(1, nz, one, 0, unroll=nz <= 8)

    def not_me(t, h):
        return jnp.logical_or(t != s, h != c)

    blank[...] = jnp.zeros((GROUP, bw), F32)

    def width(e):
        return bw if e < 7 else last

    barrier = pltpu.get_barrier_semaphore()
    for t in (s, s_x, s_y, s_d):
        for q in (r, r_c):
            if not (t is s and q is r):
                pl.semaphore_signal(barrier, inc=1, device_id=(t, q), device_id_type=MESH)

    def greet(k, _):
        pl.semaphore_signal(barrier, inc=1, device_id=z_peer(k), device_id_type=MESH)
        return 0

    lax.fori_loop(1, nz, greet, 0)

    local_copy(inp_raw.at[0], raw.at[0], raw_ls.at[0])
    local_copy(cot_raw.at[0], raw.at[1], raw_ls.at[1])
    w_rows = [(1 - y, 2 * pair_half), (1 - y, 2 * pair_half + 1), (y, 2 * pair_half), (y, 2 * pair_half + 1)]
    w_rows += [(y, 2 - 2 * pair_half), (y, 3 - 2 * pair_half)]

    def w_load(n, wait):
        yy, j = w_rows[n]
        k, slot = 4 * yy + j, n % 3

        def go(rows):
            copy = pltpu.make_async_copy(
                w_raw.at[0, pl.ds(pl.multiple_of(k * bw, bw), rows)], wst.at[slot, pl.ds(0, rows)], wst_ls.at[slot]
            )
            copy.wait() if wait else copy.start()

        @pl.when(k < 7)
        def _():
            go(bw)

        @pl.when(k == 7)
        def _():
            if not wait:
                wst[slot, last:] = jnp.zeros((bw - last, sz.hidden), BF16)
            go(last)

    def w_cut(n, column, toward, dst):
        slot = n % 3
        for e in range(8):
            @pl.when(column == e % 4)
            def _(e=e):
                place_of = jnp.where(toward == e // 4, 0, 1)
                if e == 7:
                    dst[place_of] = jnp.zeros((bw, bw), BF16)
                dst[place_of, :, : width(e)] = wst[slot, :, e * bw : e * bw + width(e)]

    for n in range(3):
        w_load(n, False)

    parblk[...] = jnp.zeros(parblk.shape, F32)
    for n, ref in enumerate((recurrence, state_bias, norm_gain, norm_shift)):
        for e in range(8):
            parblk[e, n : n + 1, : width(e)] = ref[0:1, e * bw : e * bw + width(e)]
    par[s] = parblk[me]
    flagbuf[c] = jnp.zeros(flagbuf.shape[1:], F32)
    for n, ref in enumerate((resets, valid_mask)):
        for m in range(4):
            row = seqs * (4 * n + m)
            flagbuf[c, row : row + seqs, : sz.frames] = ref[SECTIONS - 1 - m].astype(F32)

    for n in range(6):
        w_load(n, True)
        j = w_rows[n][1]
        rows = pl.ds(pl.multiple_of(j * bw, bw), bw)
        half_rows = pl.ds((n % 2) * bw, bw)
        if n < 2:
            w_cut(n, j_own, 1 - y, wx.at[1, :, half_rows])
            w_cut(n, j_x, 1 - y, wx.at[2, :, half_rows])
        elif n < 4:
            w_cut(n, j_x, y, wx.at[0, :, half_rows])
            w_cut(n, j_own, y, wbuf.at[s, :, rows])
        else:
            w_cut(n, j_own, y, wbuf.at[s, :, rows])
        if n + 3 < 6:
            w_load(n + 3, False)

    row = lax.broadcasted_iota(jnp.int32, (half, half), 0)
    col = lax.broadcasted_iota(jnp.int32, (half, half), 1)
    frame_of = (row % GROUP // pieces) * sz.frames + (row % pieces) * steps + row // GROUP
    permute = (col == frame_of).astype(BF16)
    row_of = row
    frame_at = (col % GROUP // pieces) * sz.frames + (col % pieces) * steps + col // GROUP

    def cut_frames(n):
        wait_bytes(raw.at[n], raw_ls.at[n])
        for e in range(8):
            value = raw[n, :, :, e * bw : e * bw + width(e)].reshape(half, width(e))
            if e == 7:
                blocks[n, e] = jnp.zeros((half, bw), BF16)
            blocks[n, e, :, : width(e)] = jnp.dot(permute, value, preferred_element_type=F32).astype(BF16)

    cut_frames(0)
    pl.semaphore_wait(barrier, 7 + nz - 1)

    for n, t in enumerate((s_x, s_y, s_d)):
        remote(parblk.at[2 * t + c], par.at[s], par_ss.at[n], par_rs.at[s], (t, r)).start()
    remote(flagbuf.at[c], flagbuf.at[c], flag_ss.at[0], flag_rs.at[c], to_c).start()

    def w_cross():
        for k in range(2):
            j = 2 * pair_half + k
            for n, t in enumerate((s_x, s_y, s_d)):
                src = wx.at[n, :, pl.ds(k * bw, bw)]
                dst = wbuf.at[s, :, pl.ds(pl.multiple_of(j * bw, bw), bw)]
                remote(src, dst, w_ss.at[n, k], w_rs.at[s, j], (t, r)).start()

    @pl.when(s == 0)
    def _():
        w_cross()

    in_dst = mainbuf.at[mine, :, c]
    near, far = blocks.at[0, pl.ds(4 * y, 4)], blocks.at[0, pl.ds(4 - 4 * y, 4)]
    remote(far, in_dst, in_ss.at[2], in_rs.at[mine, c], to_d).start()
    remote(near, in_dst, in_ss.at[0], in_rs.at[mine, c], to_x).start()
    remote(far, in_dst, in_ss.at[1], in_rs.at[mine, c], to_y).start()
    remote(near, in_dst, in_ss.at[3], in_rs.at[mine, c], to_c).start()
    local_copy(near, in_dst, in_rs.at[mine, c])

    @pl.when(s != 0)
    def _():
        w_cross()

    wait_bytes(flagbuf.at[1 - c], flag_rs.at[1 - c])
    row = lax.broadcasted_iota(jnp.int32, (half, sz.frames), 0)
    col = lax.broadcasted_iota(jnp.int32, (half, sz.frames), 1)
    at_frame = col == (row % pieces) * steps + row // GROUP
    of_seq = row % GROUP // pieces
    ones = jnp.ones((sz.frames, bw), BF16)

    def masks_of(m, _):
        for h in range(2):
            lo, hi = h * steps, (h + 1) * steps
            for n in range(2):
                flags = jnp.zeros((half, sz.frames), F32)
                for q in range(seqs):
                    line = flagbuf[h, pl.ds(seqs * (4 * n + m) + q, 1), : sz.frames]
                    flags = jnp.where(jnp.logical_and(at_frame, of_seq == q), line, flags)
                value = jnp.dot(flags.astype(BF16), ones, preferred_element_type=F32).reshape(steps, GROUP, bw)
                if n == 0:
                    keepf[m, lo:hi] = 1.0 - value
                else:
                    validf[m, lo:hi] = value
        return 0

    lax.fori_loop(0, 4, masks_of, 0)
    for t in (s_x, s_y, s_d):
        wait_bytes(par.at[t], par_rs.at[t])

    def decays_of(i, _):
        l, m = i // 4, i % 4
        u = jnp.broadcast_to(par[l, 0:1], (GROUP, bw))
        a_h, v_h = [], []
        for h in range(2):
            a = jnp.ones((GROUP, bw), F32)
            v = jnp.zeros((GROUP, bw), F32)
            for t in range(steps):
                d = u * keepf[m, h * steps + t]
                a = d * a
                v = d * v + 1.0
            a_h.append(a)
            v_h.append(v)
        xa, xb, ta, tb = entering(a_h, v_h, False)
        for h in range(2):
            chunk_a[i, h] = a_h[h]
            chunk_aex[i, h] = xa[h]
            chunk_s0[i, h] = xb[h]
        valid_count = total(jnp.sum(validf[m], axis=0))
        value = pack(ta + tb + [valid_count])
        pre_send[i] = value
        pre_recv[nz - 1, i] = value
        return 0

    lax.fori_loop(0, items, decays_of, 0)
    send_z(pre_send, lambda k: pre_recv.at[k], pre_ss, pre_rs)

    for n, t in enumerate((s_d, s_x, s_y)):
        slot = SECTIONS - 1 - t
        wait_bytes(mainbuf.at[slot, :, c], in_rs.at[slot, c])
        remote(mainbuf.at[slot, :, c], mainbuf.at[slot, :, c], in_fs.at[n], in_rs.at[slot, c], to_c).start()
    wait_bytes(in_dst, in_rs.at[mine, c])

    def w_rows_of(l, j):
        return wbuf.at[l, :, pl.ds(pl.multiple_of(j * bw, bw), bw)]

    def w_pass(l, k):
        j = 2 * pair_half + k

        @pl.when(l != s)
        def _():
            wait_bytes(w_rows_of(l, j), w_rs.at[l, j])
            remote(w_rows_of(l, j), w_rows_of(l, j), w_fs.at[l, k], w_rs.at[l, j], to_pair).start()

    def w_arrive(l):
        @pl.when(l != s)
        def _():
            for k in range(2):
                j = 2 - 2 * pair_half + k
                wait_bytes(w_rows_of(l, j), w_rs.at[l, j])

    w_pass(0, 0)
    w_pass(0, 1)
    cut_frames(1)
    for t in range(SECTIONS):
        for h in range(2):
            src = blocks.at[1, 2 * t + h]

            @pl.when(not_me(t, h))
            def _(src=src, t=t, h=h):
                remote(src, dbuf.at[mine, c], cot_ss.at[t, h], cot_rs.at[mine, c], (t, 2 * z + h)).start()

            @pl.when(jnp.logical_not(not_me(t, h)))
            def _(src=src):
                local_copy(src, dbuf.at[mine, c], cot_rs.at[mine, c])

    wait_bytes(pre_recv.at[pl.ds(0, nz - 1)], pre_rs)

    def arrived(i):
        block = mainbuf.at[i, j_x]
        wait_bytes(block, mx_rs.at[i])
        remote(block, block, mf_ss.at[i], mf_rs.at[i], to_c).start()

    def project(i):
        l, m = i // 4, i % 4

        @pl.when(m == 0)
        def _():
            w_arrive(l)

        @pl.when(l == 0)
        def _():
            wait_bytes(mainbuf.at[i, :, 1 - c], in_rs.at[m, 1 - c])

        @pl.when(l > 0)
        def _():
            wait_bytes(mainbuf.at[i, j_c], ms_rs.at[i])
            wait_bytes(mainbuf.at[i, j_xc], mf_rs.at[i])
            wait_bytes(ysend.at[m], y_ss.at[m])

        def to_half(n):
            acc = jnp.zeros((sz.rows, bw), F32)
            for j in range(4):
                acc = acc + jnp.dot(
                    mainbuf[i, j].reshape(sz.rows, bw), wbuf[l, n, j * bw : (j + 1) * bw], preferred_element_type=F32
                )
            return acc

        ysend[m] = to_half(1).astype(BF16)
        remote(ysend.at[m], yrecv.at[i % 8], y_ss.at[m], y_rs.at[i % 8], to_y).start()
        own[m] = to_half(0).reshape(groups, GROUP, bw)

    def moments(i):
        l, m = i // 4, i % 4
        wait_bytes(yrecv.at[i % 8], y_rs.at[i % 8])
        pre = own[m] + yrecv[i % 8].astype(F32).reshape(groups, GROUP, bw)
        valid = validf[m]
        pre_sum = total(jnp.sum(pre * valid, axis=0))
        local_count = pre_send[i, 2 * seqs : 2 * seqs + 1]
        pivot = pre_sum / jnp.maximum(local_count, 1.0)
        shifted = pre - pivot
        xbuf[i] = shifted
        square = total(jnp.sum(shifted * shifted * valid, axis=0))
        u = jnp.broadcast_to(par[l, 0:1], (GROUP, bw))
        ends = []
        for h in range(2):
            v = jnp.zeros((GROUP, bw), F32)
            for t in range(steps):
                v = (u * keepf[m, h * steps + t]) * v + shifted[h * steps + t]
            ends.append(v)
        unused_a, xb, unused_t, tb = entering([chunk_a[i, 0], chunk_a[i, 1]], ends, False)
        for h in range(2):
            s1ex[m, h] = xb[h]
        value = pack([pre_sum, square] + tb)

        @pl.when(l > 0)
        def _():
            wait_bytes(ex_recv.at[i % 8, pl.ds(0, nz - 1)], ex_ss.at[m])

        ex_send[m] = value
        ex_recv[i % 8, nz - 1] = value
        send_z(ex_send.at[m], lambda k: ex_recv.at[i % 8, k], ex_ss.at[m], ex_rs.at[i % 8])

    def finish_layer(i):
        l, m = i // 4, i % 4
        wait_bytes(ex_recv.at[i % 8, pl.ds(0, nz - 1)], ex_rs.at[i % 8])
        u, bias = par[l, 0:1], par[l, 1:2]
        gain, shift = par[l, 2:3], par[l, 3:4]

        def add_sum(p, carry):
            slot = z_slot(p)
            return (
                carry[0] + ex_recv[i % 8, slot, 0:1],
                carry[1] + pre_recv[slot, i, 2 * seqs : 2 * seqs + 1],
            )

        zero = jnp.zeros((1, bw), F32)
        sum_all, count_all = over_z(add_sum, (zero, zero))
        mean = sum_all / count_all

        def pivot_of(slot):
            count = pre_recv[slot, i, 2 * seqs : 2 * seqs + 1]
            return ex_recv[i % 8, slot, 0:1] / jnp.maximum(count, 1.0), count

        def add_square(p, carry):
            slot = z_slot(p)
            pivot, count = pivot_of(slot)
            return carry + ex_recv[i % 8, slot, 1:2] + count * (pivot - mean) * (pivot - mean)

        var = over_z(add_square, zero) / count_all
        inv = lax.rsqrt(var + norm_eps)
        alpha = gain * inv

        def hop_in(p, carry):
            slot = z_slot(p)
            pivot, unused = pivot_of(slot)
            beta = shift + alpha * (pivot - mean)
            after = []
            for q in range(seqs):
                value = (
                    alpha * ex_recv[i % 8, slot, 2 + q : 3 + q]
                    + beta * pre_recv[slot, i, seqs + q : seqs + q + 1]
                    + pre_recv[slot, i, q : q + 1] * carry[q]
                )
                after.append(jnp.where(p < z, value, carry[q]))
            return tuple(after)

        enter = by_seq(list(over_z(hop_in, (zero,) * seqs)))
        pivot, unused = pivot_of(nz - 1)
        beta = shift + alpha * (pivot - mean)
        offset = (pivot - mean) * inv
        scal[i] = pack([alpha, 1.0 / count_all])
        wide = [jnp.broadcast_to(v, (GROUP, bw)) for v in (u, bias, alpha, beta, inv, offset)]
        u, bias, alpha, beta, inv, offset = wide
        side = mainbuf.at[jnp.maximum(i - 4, 0), j_own]
        odd = (l % 2).astype(F32)
        to_next = l < SECTIONS - 1
        target = jnp.minimum(i + 4, items - 1)
        for h in range(2):
            v = alpha * s1ex[m, h] + beta * chunk_s0[i, h] + chunk_aex[i, h] * enter
            carry_in[i, h] = v
            hidden = []
            for t in range(steps):
                g = h * steps + t
                shifted = xbuf[i, g]
                v = (u * keepf[m, g]) * v + (alpha * shifted + beta)
                states[i, g] = v
                xbuf[i, g] = shifted * inv + offset
                w = v + bias
                hidden.append(validf[m, g] * (w * jax.nn.sigmoid(w)))
            value = jnp.concatenate(hidden, axis=0) + odd * side[h].astype(F32)
            outbuf[m, h] = value.astype(BF16)

        @pl.when(to_next)
        def _():
            block = mainbuf.at[target, j_own]
            block[...] = outbuf[m]
            remote(block, block, mx_ss.at[target], mx_rs.at[target], to_x).start()
            remote(block, block, ms_ss.at[target], ms_rs.at[target], to_c).start()

        @pl.when(jnp.logical_not(to_next))
        def _():
            for h in range(2):
                @pl.when(not_me(SECTIONS - 1 - m, h))
                def _(h=h):
                    remote(outbuf.at[m, h], outg.at[me], o_ss.at[m, h], o_rs.at[me], (SECTIONS - 1 - m, 2 * z + h)).start()

                @pl.when(jnp.logical_not(not_me(SECTIONS - 1 - m, h)))
                def _(h=h):
                    local_copy(outbuf.at[m, h], outg.at[me], o_rs.at[me])

    def carry_slopes(i):
        l, m = i // 4, i % 4
        u = jnp.broadcast_to(par[l, 0:1], (GROUP, bw))
        a_h = [chunk_a[i, 0], chunk_a[i, 1]]
        xa, unused_b, unused_a, unused_t = entering(a_h, [jnp.zeros((GROUP, bw), F32)] * 2, True)
        sum_one = jnp.zeros((GROUP, bw), F32)
        sum_normed = jnp.zeros((GROUP, bw), F32)
        for h in (1, 0):
            v = xa[h]
            for t in range(steps - 1, -1, -1):
                g = h * steps + t
                sum_one = sum_one + v
                sum_normed = sum_normed + v * xbuf[i, g]
                v = (u * keepf[m, g]) * v
        rows = []
        for value in (sum_one, sum_normed):
            for q in range(seqs):
                inside = jnp.logical_and(sub >= q * pieces, sub < (q + 1) * pieces)
                rows.append(total(jnp.where(inside, value, 0.0)))
        slopes[i] = pack(rows)

    def forward_tick(k, _):
        @pl.when(k < items)
        def _():
            project(k)

        @pl.when(k >= 2)
        def _():
            finish_layer(k - 2)
            carry_slopes(k - 2)

        @pl.when(jnp.logical_and(k >= 1, k < items + 1))
        def _():
            moments(k - 1)

        @pl.when(jnp.logical_and(k + 1 >= 4, k + 1 < items))
        def _():
            arrived(k + 1)

        @pl.when(k < 12)
        def _():
            for n in range(2):
                @pl.when(k % 4 == n)
                def _(n=n):
                    w_pass(k // 4 + 1, n)

        return 0

    lax.fori_loop(0, items + 2, forward_tick, 0)

    def back_index(b):
        l, m = SECTIONS - 1 - b // 4, b % 4
        return l, m, l * 4 + m

    def act_back(b):
        l, m, i = back_index(b)

        @pl.when(b < 4)
        def _():
            for h in range(2):
                wait_bytes(dbuf.at[m, h], cot_rs.at[m, h])

        u = jnp.broadcast_to(par[l, 0:1], (GROUP, bw))
        bias = jnp.broadcast_to(par[l, 1:2], (GROUP, bw))
        ends = [None, None]
        sum_act = jnp.zeros((GROUP, bw), F32)
        for h in (1, 0):
            grad = dbuf[b, h].astype(F32).reshape(steps, GROUP, bw)
            v = jnp.zeros((GROUP, bw), F32)
            for t in range(steps - 1, -1, -1):
                g = h * steps + t
                w = states[i, g] + bias
                sg = jax.nn.sigmoid(w)
                da = grad[t] * validf[m, g] * (sg * (1.0 + w * (1.0 - sg)))
                own[m, g] = da
                sum_act = sum_act + da
                v = (u * keepf[m, g]) * (da + v)
            ends[h] = v
        xa, xb, unused, tb = entering([chunk_a[i, 0], chunk_a[i, 1]], ends, True)
        for h in range(2):
            aexr[m, h] = xa[h]
            cex[m, h] = xb[h]
        sum_local = jnp.zeros((GROUP, bw), F32)
        sum_normed = jnp.zeros((GROUP, bw), F32)
        for h in (1, 0):
            v = xb[h]
            for t in range(steps - 1, -1, -1):
                g = h * steps + t
                ds = own[m, g] + v
                sum_local = sum_local + ds
                sum_normed = sum_normed + ds * xbuf[i, g]
                v = (u * keepf[m, g]) * ds
        value = pack(tb + [total(sum_local), total(sum_normed)] + [slopes[i, n : n + 1] for n in range(2 * seqs)])

        @pl.when(b >= 4)
        def _():
            wait_bytes(e1_recv.at[b % 8, pl.ds(0, nz - 1)], e1_ss.at[m])

        e1_send[m] = value
        e1_recv[b % 8, nz - 1] = value
        send_z(e1_send.at[m], lambda k: e1_recv.at[b % 8, k], e1_ss.at[m], e1_rs.at[b % 8])
        add_small(l, m, 3, sum_act)

    def add_small(l, m, n, value):
        added = jnp.where(sub == n, jnp.broadcast_to(total(value), (GROUP, bw)), 0.0)
        if n == 3:
            before = jnp.where(m == 0, 0.0, 1.0)
            small[l] = jnp.where(before > 0.0, small[l], 0.0) + added
        else:
            small[l] = small[l] + added

    def state_back(b):
        l, m, i = back_index(b)
        wait_bytes(e1_recv.at[b % 8, pl.ds(0, nz - 1)], e1_rs.at[b % 8])
        zero = blank[...]

        def line(value):
            return jnp.broadcast_to(value, (GROUP, bw))

        def hop_in(n, carry):
            p = nz - 1 - n
            slot = z_slot(p)
            sum_shift, sum_gain = carry[0], carry[1]
            flow, enter = carry[2 : 2 + seqs], carry[2 + seqs :]
            sum_shift = sum_shift + line(e1_recv[b % 8, slot, seqs : seqs + 1])
            sum_gain = sum_gain + line(e1_recv[b % 8, slot, seqs + 1 : seqs + 2])
            after, inside = [], []
            for q in range(seqs):
                one = seqs + 2 + q
                normed = one + seqs
                sum_shift = sum_shift + flow[q] * line(e1_recv[b % 8, slot, one : one + 1])
                sum_gain = sum_gain + flow[q] * line(e1_recv[b % 8, slot, normed : normed + 1])
                inside.append(jnp.where(p == z, flow[q], enter[q]))
                after.append(line(e1_recv[b % 8, slot, q : q + 1]) + line(pre_recv[slot, i, q : q + 1]) * flow[q])
            return (sum_shift, sum_gain, *after, *inside)

        sum_shift, sum_gain, *rest = over_z(hop_in, (zero,) * (2 + 2 * seqs))
        enter = by_seq(rest[seqs:])
        u = jnp.broadcast_to(par[l, 0:1], (GROUP, bw))
        alpha = jnp.broadcast_to(scal[i, 0:1], (GROUP, bw))
        per_count = scal[i, 1:2]
        gain_part, shift_part = sum_gain * per_count, sum_shift * per_count
        sum_rate = jnp.zeros((GROUP, bw), F32)
        rows = [None] * groups
        for h in (1, 0):
            v = cex[m, h] + aexr[m, h] * enter
            for t in range(steps - 1, -1, -1):
                g = h * steps + t
                keep = keepf[m, g]
                ds = own[m, g] + v
                before = carry_in[i, h] if t == 0 else states[i, g - 1]
                sum_rate = sum_rate + (ds * keep) * before
                v = (u * keep) * ds
                rows[g] = alpha * (ds - validf[m, g] * (shift_part + xbuf[i, g] * gain_part))
        @pl.when(b >= 8)
        def _():
            wait_bytes(dpbuf.at[b % 8, 0], dp_ss.at[b % 8])

        dpbuf[b % 8, 0] = jnp.concatenate(rows, axis=0).astype(BF16)
        remote(dpbuf.at[b % 8, 0], dpbuf.at[b % 8, 1], dp_ss.at[b % 8], dp_rs.at[b % 8], to_y).start()
        add_small(l, m, 2, sum_rate)
        small[l] = small[l] + pack([sum_gain[0:1], sum_shift[0:1]])

    nt = (((1,), (1,)), ((), ()))
    tn = (((0,), (0,)), ((), ()))

    def input_back(b):
        l, m, i = back_index(b)
        wait_bytes(dpbuf.at[b % 8, 1], dp_rs.at[b % 8])
        dp_own, dp_other = dpbuf[b % 8, 0], dpbuf[b % 8, 1]

        def toward(j):
            rows = pl.ds(pl.multiple_of(j * bw, bw), bw)
            first = lax.dot_general(dp_own, wbuf[l, 0, rows], nt, preferred_element_type=F32)
            return first + lax.dot_general(dp_other, wbuf[l, 1, rows], nt, preferred_element_type=F32)

        @pl.when(b >= 4)
        def _():
            wait_bytes(sibsend.at[m], sb_ss.at[m])

        sibsend[m, 0] = toward(j_c).astype(BF16)
        sibsend[m, 1] = toward(j_xc).astype(BF16)
        remote(sibsend.at[m], sibrecv.at[b % 8], sb_ss.at[m], sb_rs.at[b % 8], to_c).start()
        pkeep[m, 0] = toward(j_own)
        pkeep[m, 1] = toward(j_x)

    def weight_back(b):
        l, m, i = back_index(b)
        dp = jnp.concatenate([dpbuf[b % 8, 0], dpbuf[b % 8, 1]], axis=1)

        @pl.when(jnp.logical_and(m == 3, l < 2))
        def _():
            wait_bytes(grecv.at[l % 2], gr_ss.at[l % 2])

        for j in range(4):
            rows = pl.ds(j * bw, bw)
            new = lax.dot_general(mainbuf[i, j].reshape(sz.rows, bw), dp, tn, preferred_element_type=F32)

            @pl.when(m == 0)
            def _(new=new, rows=rows):
                gw[rows] = new

            @pl.when(jnp.logical_and(m > 0, m < 3))
            def _(new=new, rows=rows):
                gw[rows] = gw[rows] + new

            @pl.when(m == 3)
            def _(new=new, rows=rows):
                gsend[l % 2, rows] = (gw[rows] + new).astype(BF16)

        @pl.when(m == 3)
        def _():
            def one(k, _):
                p = (z + k) % nz
                src = gsend.at[l % 2, pl.ds(p * part, part)]
                remote(src, grecv.at[l % 2, k - 1], gr_ss.at[l % 2], gr_rs.at[l % 2], z_peer(k)).start()
                return 0

            lax.fori_loop(1, nz, one, 0)

    def cross_back(b):
        m = b % 4
        wait_bytes(sibrecv.at[b % 8], sb_rs.at[b % 8])

        @pl.when(b >= 4)
        def _():
            wait_bytes(xsend.at[m], xp_ss.at[m])

        xsend[m] = (pkeep[m, 1] + sibrecv[b % 8, 1].astype(F32)).astype(BF16)
        remote(xsend.at[m], xrecv.at[b % 8], xp_ss.at[m], xp_rs.at[b % 8], to_x).start()
        pkeep[m, 0] = pkeep[m, 0] + sibrecv[b % 8, 0].astype(F32)

    def join_back(b):
        l, m, i = back_index(b)
        wait_bytes(xrecv.at[b % 8], xp_rs.at[b % 8])
        even = (1 - l % 2).astype(F32)
        side = dbuf[jnp.maximum(b - 4, 0)].astype(F32).reshape(sz.rows, bw)
        value = pkeep[m, 0] + xrecv[b % 8].astype(F32) + even * side
        dbuf[b + 4] = value.astype(BF16).reshape(2, sz.half, bw)

        @pl.when(l == 0)
        def _():
            for h in range(2):
                src = dbuf.at[b + 4, h]

                @pl.when(not_me(SECTIONS - 1 - m, h))
                def _(src=src, h=h):
                    remote(src, ging.at[me], gi_ss.at[m, h], gi_rs.at[me], (SECTIONS - 1 - m, 2 * z + h)).start()

                @pl.when(jnp.logical_not(not_me(SECTIONS - 1 - m, h)))
                def _(src=src):
                    local_copy(src, ging.at[me], gi_rs.at[me])

    def gather_weights(l):
        wait_bytes(grecv.at[l % 2], gr_rs.at[l % 2])

        def add(k, carry):
            return carry + grecv[l % 2, k].astype(F32)

        start = gsend[l % 2, pl.ds(pl.multiple_of(z * part, part), part), :].astype(F32)
        gpiece[l] = lax.fori_loop(0, nz - 1, add, start).astype(BF16)

        @pl.when(l != s)
        def _():
            remote(gpiece.at[l], gout.at[c, z, s], gx_ss.at[l], gx_rs.at[s], (l, r)).start()

        @pl.when(l == s)
        def _():
            local_copy(gpiece.at[l], gout.at[c, z, s], gx_rs.at[s])

    def backward_tick(k, _):
        @pl.when(k >= 4)
        def _():
            join_back(k - 4)

        @pl.when(k < items)
        def _():
            act_back(k)

        @pl.when(jnp.logical_and(k >= 1, k < items + 1))
        def _():
            state_back(k - 1)

        @pl.when(jnp.logical_and(k >= 2, k < items + 2))
        def _():
            input_back(k - 2)
            weight_back(k - 2)
            cross_back(k - 2)

        @pl.when(jnp.logical_and(k >= 9, k % 4 == 1))
        def _():
            gather_weights(SECTIONS - 1 - (k - 9) // 4)

        return 0

    lax.fori_loop(0, items + 4, backward_tick, 0)

    send_z(small, lambda k: small_recv.at[k], st_ss, st_rs)
    wait_bytes(small_recv, st_rs)
    wait_bytes(small_recv, st_ss)

    def add_rest(k, _):
        for l in range(SECTIONS):
            small[l] = small[l] + jnp.where(sub >= 2, small_recv[k, l], 0.0)
        return 0

    lax.fori_loop(0, nz - 1, add_rest, 0)
    for t in range(SECTIONS):
        for h in range(2):
            @pl.when(not_me(t, h))
            def _(t=t, h=h):
                remote(small.at[t], smallg.at[me], sm_ss.at[t, h], sm_rs.at[me], (t, 2 * z + h)).start()

            @pl.when(jnp.logical_not(not_me(t, h)))
            def _(t=t):
                local_copy(small.at[t], smallg.at[me], sm_rs.at[me])

    gather_weights(0)
    for t in range(SECTIONS):
        wait_bytes(gout.at[c, z, t], gx_rs.at[t])

    def g_move(p, up, down, finish):
        @pl.when(jnp.logical_and(p >= 0, p < nz))
        def _():
            block = gout.at[c, p]
            if not finish:
                @pl.when(p != z)
                def _():
                    wait_bytes(block, gz_rs.at[p])
            if up:
                @pl.when(z + 1 < nz)
                def _():
                    copy = remote(block, block, gz_up.at[p], gz_rs.at[p], (s, r + 2))
                    copy.wait_send() if finish else copy.start()
            if down:
                @pl.when(z >= 1)
                def _():
                    copy = remote(block, block, gz_dn.at[p], gz_rs.at[p], (s, r - 2))
                    copy.wait_send() if finish else copy.start()
            copy = remote(block, block, gz_sb.at[p], gs_rs.at[p], to_c)
            copy.wait_send() if finish else copy.start()

    def g_hops(finish):
        g_move(z, True, True, finish)

        def one(d, _):
            g_move(z - d, True, False, finish)
            g_move(z + d, False, True, finish)
            return 0

        lax.fori_loop(1, nz, one, 0)

    g_hops(False)

    restore = (row_of == frame_at).astype(BF16)
    for e in range(8):
        wait_bytes(outg.at[e], o_rs.at[e])
        wait_bytes(ging.at[e], gi_rs.at[e])
        wait_bytes(smallg.at[e], sm_rs.at[e])
        for src, dst in ((outg, out), (ging, grad_inp)):
            value = jnp.dot(restore, src[e], preferred_element_type=F32).astype(BF16)
            value = value.reshape(seqs, sz.frames, bw)
            dst[0, :, :, e * bw : e * bw + width(e)] = value[:, :, : width(e)]
        for n, dst in enumerate((grad_gain, grad_shift, grad_rec, grad_bias)):
            dst[0:1, e * bw : e * bw + width(e)] = smallg[e, n : n + 1, : width(e)]

    def drain_z(p, _):
        wait_bytes(gout.at[1 - c, p], gs_rs.at[p])
        return 0

    lax.fori_loop(0, nz, drain_z, 0)
    g_hops(True)
    for l in range(2):
        wait_bytes(grecv.at[l], gr_ss.at[l])
    for l in range(SECTIONS):
        @pl.when(l != s)
        def _(l=l):
            wait_bytes(gpiece.at[l], gx_ss.at[l])
            for k in range(2):
                wait_bytes(w_rows_of(l, k), w_fs.at[l, k])

        wait_bytes(ysend.at[l], y_ss.at[l])
        wait_bytes(ex_recv.at[l, pl.ds(0, nz - 1)], ex_ss.at[l])
        wait_bytes(e1_recv.at[l, pl.ds(0, nz - 1)], e1_ss.at[l])
        wait_bytes(sibsend.at[l], sb_ss.at[l])
        wait_bytes(xsend.at[l], xp_ss.at[l])
        for h in range(2):
            @pl.when(not_me(l, h))
            def _(l=l, h=h):
                wait_bytes(dbuf.at[mine, c], cot_ss.at[l, h])
                wait_bytes(small.at[l], sm_ss.at[l, h])

            @pl.when(not_me(SECTIONS - 1 - l, h))
            def _(l=l, h=h):
                wait_bytes(outbuf.at[l, h], o_ss.at[l, h])
                wait_bytes(dbuf.at[items + l, h], gi_ss.at[l, h])

    def drain(i, _):
        @pl.when(i < 8)
        def _():
            wait_bytes(dpbuf.at[i, 0], dp_ss.at[i])

        @pl.when(i >= 4)
        def _():
            wait_bytes(mainbuf.at[i, j_own], mx_ss.at[i])
            wait_bytes(mainbuf.at[i, j_own], ms_ss.at[i])
            wait_bytes(mainbuf.at[i, j_x], mf_ss.at[i])

        return 0

    lax.fori_loop(0, items, drain, 0)
    for n in range(4):
        wait_bytes(in_dst, in_ss.at[n])
    for n in range(3):
        wait_bytes(in_dst, in_fs.at[n])
        wait_bytes(par.at[s], par_ss.at[n])
        for k in range(2):
            wait_bytes(wx.at[n, :, pl.ds(k * bw, bw)], w_ss.at[n, k])
    wait_bytes(flagbuf.at[c], flag_ss.at[0])
    wait_bytes(pre_recv.at[pl.ds(0, nz - 1)], pre_ss)


def run_kernel(sz, *args):
    nz, bw, items, groups = sz.nz, sz.bw, sz.items, sz.groups
    half, rows, part = sz.half, sz.rows, sz.part
    dma = pltpu.SemaphoreType.DMA
    vm = pltpu.VMEM
    step = (GROUP, bw)
    scratch = [
        vm((items, 4, 2, half, bw), BF16),
        vm((SECTIONS, 2, 4 * bw, bw), BF16),
        vm((4, rows, bw), BF16),
        vm((8, rows, bw), BF16),
        vm((4, groups) + step, F32),
        vm((items, groups) + step, F32),
        vm((items, groups) + step, F32),
        vm((items, 2) + step, F32),
        vm((items, 2) + step, F32),
        vm((items, 2) + step, F32),
        vm((items, 2) + step, F32),
        vm((4, groups) + step, F32),
        vm((4, groups) + step, F32),
        vm((2, 8 * sz.seqs, 128), F32),
        vm((SECTIONS,) + step, F32),
        vm((8,) + step, F32),
        vm((items,) + step, F32),
        vm((nz, items) + step, F32),
        vm((4,) + step, F32),
        vm((8, nz) + step, F32),
        vm((4,) + step, F32),
        vm((8, nz) + step, F32),
        vm((items,) + step, F32),
        vm((items,) + step, F32),
        vm((4, 2) + step, F32),
        vm((items + 4, 2, half, bw), BF16),
        vm((4, 2) + step, F32),
        vm((4, 2) + step, F32),
        vm((8, 2, rows, bw), BF16),
        vm((4, 2, rows, bw), F32),
        vm((4, 2, rows, bw), BF16),
        vm((8, 2, rows, bw), BF16),
        vm((4, rows, bw), BF16),
        vm((8, rows, bw), BF16),
        vm((4 * bw, 2 * bw), F32),
        vm((2, 4 * bw, 2 * bw), BF16),
        vm((2, nz - 1, part, 2 * bw), BF16),
        vm((SECTIONS, part, 2 * bw), BF16),
        vm((SECTIONS,) + step, F32),
        vm((nz - 1, SECTIONS) + step, F32),
        vm((4, 2, half, bw), BF16),
        vm((2, sz.seqs, sz.frames, sz.hidden), BF16),
        vm((2, 8, half, bw), BF16),
        vm((3, bw, sz.hidden), BF16),
        vm((3, 2, 2 * bw, bw), BF16),
        vm((8, half, bw), BF16),
        vm((8, half, bw), BF16),
        vm((8,) + step, F32),
        vm(step, F32),
    ]
    sems = [
        dma((2,)), dma((3,)), dma((4,)), dma((3,)), dma((4, 2)), dma((4, 2)), dma((4, 2)),
        dma((3,)), dma((4,)), dma((1,)), dma((2,)), dma((3, 2)), dma((4, 4)), dma((4, 2)),
        dma, dma, dma((items,)), dma((items,)), dma((items,)), dma((items,)), dma((items,)), dma((items,)),
        dma((4,)), dma((8,)), dma((4,)), dma((8,)),
        dma((4, 2)), dma((8,)), dma((4,)), dma((8,)),
        dma((8,)), dma((8,)), dma((4,)), dma((8,)), dma((4,)), dma((8,)),
        dma((4, 2)), dma((8,)), dma((2,)), dma((2,)), dma((4,)), dma((4,)),
        dma((nz,)), dma((nz,)), dma((nz,)), dma((nz,)), dma((nz,)), dma, dma, dma((4, 2)), dma((8,)),
    ]
    anywhere = pl.BlockSpec(memory_space=pl.ANY)
    inside = pl.BlockSpec(memory_space=pltpu.VMEM)
    frames = jax.ShapeDtypeStruct((1, sz.seqs, sz.frames, sz.hidden), BF16)
    vector = jax.ShapeDtypeStruct((1, sz.hidden), F32)
    return pl.pallas_call(
        functools.partial(kernel, sz),
        out_shape=(frames, frames) + (vector,) * 4 + (jax.ShapeDtypeStruct((2, nz, 4, part, 2 * bw), BF16),),
        in_specs=[anywhere] * 3 + [inside] * 6,
        out_specs=(inside,) * 6 + (anywhere,),
        scratch_shapes=scratch + sems,
        compiler_params=pltpu.CompilerParams(
            collective_id=0, has_side_effects=True, vmem_limit_bytes=63 * 2**20
        ),
    )(*args)


def place_weights(sz, pieces):
    bw, part, hidden = sz.bw, sz.part, sz.hidden
    count = bw // part

    def body(src, dst):
        upper = pl.program_id(0) // 4
        for yy in range(2):
            @pl.when(upper == yy)
            def _(yy=yy):
                for p in range(count):
                    for e in range(8):
                        n, x, c = (0 if e // 4 == yy else 1), e % 4 // 2, e % 2
                        wide = bw if e < 7 else sz.last
                        value = src[c, p, x, :, n * bw : n * bw + wide].astype(F32)
                        dst[p * part : (p + 1) * part, e * bw : e * bw + wide] = value

    return pl.pallas_call(
        body,
        grid=(8,),
        out_shape=jax.ShapeDtypeStruct((hidden, hidden), F32),
        in_specs=[pl.BlockSpec((2, count, 2, part, 2 * bw), lambda q: (0, q % 4, q // 4, 0, 0))],
        out_specs=pl.BlockSpec((bw, hidden), lambda q: (q, 0)),
        compiler_params=pltpu.CompilerParams(vmem_limit_bytes=32 * 2**20),
    )(pieces)


def local(sz, inputs, resets, valid_mask, weights, recurrence, state_bias, norm_gain, norm_shift, cotangent):
    outputs, grad_inputs, rec, bias, gain, shift, pieces = run_kernel(
        sz, inputs, cotangent, weights, resets, valid_mask, recurrence, state_bias, norm_gain, norm_shift
    )
    return outputs, grad_inputs, place_weights(sz, pieces)[None], rec, bias, gain, shift


def solution(mesh):
    def step(inputs, *rest):
        sz = Sizes(mesh.shape["rows"] // 2, inputs.shape[1], inputs.shape[2], inputs.shape[3])
        return local(sz, inputs, *rest)

    frames = P("section", None, "rows", None)
    flags = P(None, None, "rows")
    vectors = P("section", None)
    matrix = P("section", None, None)
    return jax.shard_map(
        step,
        mesh=mesh,
        in_specs=(frames, flags, flags, matrix, vectors, vectors, vectors, vectors, frames),
        out_specs=(frames, frames, matrix, vectors, vectors, vectors, vectors),
        check_vma=False,
    )
```

```python
import functools

import jax
import jax.numpy as jnp
from jax import lax
from jax.experimental import pallas as pl
from jax.experimental.pallas import tpu as pltpu
from jax.sharding import PartitionSpec as P

MESH = pl.DeviceIdType.MESH
norm_eps = 1e-05
F32, BF16 = jnp.float32, jnp.bfloat16
SECTIONS = 4
GROUP = 8


class Sizes:
    def __init__(self, nz, seqs, frames, hidden):
        self.nz, self.seqs, self.frames = nz, seqs, frames
        self.pieces = GROUP // seqs
        self.steps = frames // self.pieces
        self.half = seqs * frames
        self.rows = 2 * self.half
        self.groups = self.rows // GROUP
        self.bw = -(-hidden // 1024) * 128
        self.padded = 8 * self.bw
        self.part = 4 * self.bw // nz
        self.items = 4 * SECTIONS
        self.hidden = hidden
        self.last = hidden - 7 * self.bw


def wait_bytes(ref, sem):
    pltpu.make_async_copy(ref, ref, sem).wait()


def local_copy(src, dst, sem):
    pltpu.make_async_copy(src, dst, sem).start()


def remote(src, dst, send, recv, device):
    return pltpu.make_async_remote_copy(
        src_ref=src, dst_ref=dst, send_sem=send, recv_sem=recv, device_id=device, device_id_type=MESH
    )


def kernel(
    sz, inp_raw, cot_raw, w_raw, resets, valid_mask, recurrence, state_bias, norm_gain, norm_shift,
    out, grad_inp, grad_rec, grad_bias, grad_gain, grad_shift, gout,
    mainbuf, wbuf, ysend, yrecv, own, xbuf, states, carry_in, chunk_a, chunk_aex, chunk_s0,
    keepf, validf, flagbuf, par, parblk, pre_send, pre_recv, ex_send, ex_recv, e1_send, e1_recv,
    scal, slopes, s1ex, dbuf, cex, aexr, dpbuf, pkeep, sibsend, sibrecv, xrecv, gw, gall, gpart, gleave,
    small, small_recv, outbuf, raw, blocks, wst, wx, outg, ging, smallg, blank,
    raw_ls, wst_ls, in_ss, in_fs, in_rs, cot_ss, cot_rs, par_ss, par_rs, flag_ss, flag_rs, w_ss, w_rs, w_fs, w_ps,
    pre_ss, pre_rs, mx_ss, mx_rs, ms_ss, ms_rs, mf_ss, mf_rs, y_ss, y_rs, ex_ss, ex_rs,
    o_ss, o_rs, e1_ss, e1_rs, dp_ss, dp_rs, sb_ss, sb_rs, xp_ss, xp_rs,
    gi_ss, gi_rs, ga_ss, ga_rs, go_ss, gr_rs, gx_ss, gx_rs, gs_ss, gs_rs, st_ss, st_rs, sm_ss, sm_rs,
):
    nz, bw, items, groups, steps = sz.nz, sz.bw, sz.items, sz.groups, sz.steps
    pieces, seqs = sz.pieces, sz.seqs
    s, r = lax.axis_index("section"), lax.axis_index("rows")
    y, x, z, c = s // 2, s % 2, r // 2, r % 2
    s_x, s_y, s_d = s + 1 - 2 * x, s + 2 - 4 * y, 3 - s
    r_c = r + 1 - 2 * c
    to_x, to_y, to_d, to_c = (s_x, r), (s_y, r), (s_d, r), (s, r_c)
    j_own, j_x, j_c, j_xc = 2 * x + c, 2 * (1 - x) + c, 2 * x + 1 - c, 2 * (1 - x) + 1 - c
    me = 2 * s + c
    part, half, last = sz.part, sz.half, sz.last
    mine = SECTIONS - 1 - s
    pair_half = z % 2
    to_pair = (s, r + 2 - 4 * pair_half)
    sub = lax.broadcasted_iota(jnp.int32, (GROUP, bw), 0)
    place = sub % pieces

    def z_peer(distance):
        return (s, 2 * ((z + distance) % nz) + c)

    def z_slot(p):
        return (z - p + nz - 1) % nz

    def by_seq(rows):
        value = jnp.broadcast_to(rows[seqs - 1], (GROUP, bw))
        for q in range(seqs - 2, -1, -1):
            value = jnp.where(sub < (q + 1) * pieces, jnp.broadcast_to(rows[q], (GROUP, bw)), value)
        return value

    def last_of(value, q):
        return value[(q + 1) * pieces - 1 : (q + 1) * pieces]

    def first_of(value, q):
        return value[q * pieces : q * pieces + 1]

    def entering(a, b, reverse):
        out_a, out_b = [None, None], [None, None]
        t_a = t_b = None
        for h in (1, 0) if reverse else (0, 1):
            ia, ib = a[h], b[h]
            hop = 1
            while hop < pieces:
                if reverse:
                    ok, shift = place < pieces - hop, GROUP - hop
                else:
                    ok, shift = place >= hop, hop
                pa = jnp.where(ok, pltpu.roll(ia, shift, 0), 1.0)
                pb = jnp.where(ok, pltpu.roll(ib, shift, 0), 0.0)
                ib = ia * pb + ib
                ia = ia * pa
                hop *= 2
            if reverse:
                ok, shift, edge = place < pieces - 1, GROUP - 1, first_of
            else:
                ok, shift, edge = place >= 1, 1, last_of
            xa = jnp.where(ok, pltpu.roll(ia, shift, 0), 1.0)
            xb = jnp.where(ok, pltpu.roll(ib, shift, 0), 0.0)
            na = [edge(ia, q) for q in range(seqs)]
            nb = [edge(ib, q) for q in range(seqs)]
            if t_a is not None:
                ea, eb = by_seq(t_a), by_seq(t_b)
                xb = xa * eb + xb
                xa = xa * ea
                nb = [na[q] * t_b[q] + nb[q] for q in range(seqs)]
                na = [na[q] * t_a[q] for q in range(seqs)]
            t_a, t_b = na, nb
            out_a[h], out_b[h] = xa, xb
        return out_a, out_b, t_a, t_b

    def pack(rows):
        rows = rows + [jnp.zeros((1, bw), F32)] * (8 - len(rows))
        value = jnp.zeros((8, bw), F32)
        for q, row in enumerate(rows):
            value = jnp.where(sub == q, jnp.broadcast_to(row, (8, bw)), value)
        return value

    def total(value):
        return jnp.sum(value, axis=0, keepdims=True)

    def over_z(body, start):
        return lax.fori_loop(0, nz, body, start, unroll=nz <= 8)

    def send_z(src, dst_of, send_sem, recv_sem):
        def one(k, _):
            remote(src, dst_of(k - 1), send_sem, recv_sem, z_peer(k)).start()
            return 0

        lax.fori_loop(1, nz, one, 0, unroll=nz <= 8)

    def not_me(t, h):
        return jnp.logical_or(t != s, h != c)

    blank[...] = jnp.zeros((GROUP, bw), F32)

    def width(e):
        return bw if e < 7 else last

    barrier = pltpu.get_barrier_semaphore()
    for t in (s, s_x, s_y, s_d):
        for q in (r, r_c):
            if not (t is s and q is r):
                pl.semaphore_signal(barrier, inc=1, device_id=(t, q), device_id_type=MESH)

    def greet(k, _):
        pl.semaphore_signal(barrier, inc=1, device_id=z_peer(k), device_id_type=MESH)
        return 0

    lax.fori_loop(1, nz, greet, 0)

    local_copy(inp_raw.at[0], raw.at[0], raw_ls.at[0])
    local_copy(cot_raw.at[0], raw.at[1], raw_ls.at[1])
    w_rows = [(1 - y, 2 * pair_half), (1 - y, 2 * pair_half + 1), (y, 2 * pair_half), (y, 2 * pair_half + 1)]
    w_rows += [(y, 2 - 2 * pair_half), (y, 3 - 2 * pair_half)]

    def w_load(n, wait):
        yy, j = w_rows[n]
        k, slot = 4 * yy + j, n % 2

        def go(rows):
            copy = pltpu.make_async_copy(
                w_raw.at[0, pl.ds(pl.multiple_of(k * bw, bw), rows)], wst.at[slot, pl.ds(0, rows)], wst_ls.at[slot]
            )
            copy.wait() if wait else copy.start()

        @pl.when(k < 7)
        def _():
            go(bw)

        @pl.when(k == 7)
        def _():
            if not wait:
                wst[slot, last:] = jnp.zeros((bw - last, sz.hidden), BF16)
            go(last)

    def w_cut(n, column, toward, dst):
        slot = n % 2
        for e in range(8):
            @pl.when(column == e % 4)
            def _(e=e):
                place_of = jnp.where(toward == e // 4, 0, 1)
                if e == 7:
                    dst[place_of] = jnp.zeros((bw, bw), BF16)
                dst[place_of, :, : width(e)] = wst[slot, :, e * bw : e * bw + width(e)]

    for n in range(2):
        w_load(n, False)

    parblk[...] = jnp.zeros(parblk.shape, F32)
    for n, ref in enumerate((recurrence, state_bias, norm_gain, norm_shift)):
        for e in range(8):
            parblk[e, n : n + 1, : width(e)] = ref[0:1, e * bw : e * bw + width(e)]
    par[s] = parblk[me]
    flagbuf[c] = jnp.zeros(flagbuf.shape[1:], F32)
    for n, ref in enumerate((resets, valid_mask)):
        for m in range(4):
            row = seqs * (4 * n + m)
            flagbuf[c, row : row + seqs, : sz.frames] = ref[SECTIONS - 1 - m].astype(F32)

    def w_cross():
        for k in range(2):
            j = 2 * pair_half + k
            for n, t in enumerate((s_x, s_y, s_d)):
                src = wx.at[n, :, pl.ds(k * bw, bw)]
                dst = wbuf.at[s, :, pl.ds(pl.multiple_of(j * bw, bw), bw)]
                remote(src, dst, w_ss.at[n, k], w_rs.at[s, j], (t, r)).start()

    for n in range(6):
        if n == 4:
            pl.semaphore_wait(barrier, 7 + nz - 1)

            @pl.when(s == 0)
            def _():
                w_cross()

        w_load(n, True)
        j = w_rows[n][1]
        rows = pl.ds(pl.multiple_of(j * bw, bw), bw)
        half_rows = pl.ds((n % 2) * bw, bw)
        if n < 2:
            w_cut(n, j_own, 1 - y, wx.at[1, :, half_rows])
            w_cut(n, j_x, 1 - y, wx.at[2, :, half_rows])
        elif n < 4:
            w_cut(n, j_x, y, wx.at[0, :, half_rows])
            w_cut(n, j_own, y, wbuf.at[s, :, rows])
        else:
            w_cut(n, j_own, y, wbuf.at[s, :, rows])
        if n + 2 < 6:
            w_load(n + 2, False)

    row = lax.broadcasted_iota(jnp.int32, (half, half), 0)
    col = lax.broadcasted_iota(jnp.int32, (half, half), 1)
    frame_of = (row % GROUP // pieces) * sz.frames + (row % pieces) * steps + row // GROUP
    permute = (col == frame_of).astype(BF16)
    row_of = row
    frame_at = (col % GROUP // pieces) * sz.frames + (col % pieces) * steps + col // GROUP

    def cut_frames(n):
        wait_bytes(raw.at[n], raw_ls.at[n])
        for e in range(8):
            value = raw[n, :, :, e * bw : e * bw + width(e)].reshape(half, width(e))
            if e == 7:
                blocks[n, e] = jnp.zeros((half, bw), BF16)
            blocks[n, e, :, : width(e)] = jnp.dot(permute, value, preferred_element_type=F32).astype(BF16)

    cut_frames(0)

    for n, t in enumerate((s_x, s_y, s_d)):
        remote(parblk.at[2 * t + c], par.at[s], par_ss.at[n], par_rs.at[s], (t, r)).start()
    remote(flagbuf.at[c], flagbuf.at[c], flag_ss.at[0], flag_rs.at[c], to_c).start()

    in_dst = mainbuf.at[mine, :, c]
    near, far = blocks.at[0, pl.ds(4 * y, 4)], blocks.at[0, pl.ds(4 - 4 * y, 4)]
    remote(far, in_dst, in_ss.at[2], in_rs.at[mine, c], to_d).start()
    remote(near, in_dst, in_ss.at[0], in_rs.at[mine, c], to_x).start()
    remote(far, in_dst, in_ss.at[1], in_rs.at[mine, c], to_y).start()
    remote(near, in_dst, in_ss.at[3], in_rs.at[mine, c], to_c).start()
    local_copy(near, in_dst, in_rs.at[mine, c])

    @pl.when(s != 0)
    def _():
        w_cross()

    wait_bytes(flagbuf.at[1 - c], flag_rs.at[1 - c])
    row = lax.broadcasted_iota(jnp.int32, (half, sz.frames), 0)
    col = lax.broadcasted_iota(jnp.int32, (half, sz.frames), 1)
    at_frame = col == (row % pieces) * steps + row // GROUP
    of_seq = row % GROUP // pieces
    ones = jnp.ones((sz.frames, bw), BF16)

    def masks_of(m, _):
        for h in range(2):
            lo, hi = h * steps, (h + 1) * steps
            for n in range(2):
                flags = jnp.zeros((half, sz.frames), F32)
                for q in range(seqs):
                    line = flagbuf[h, pl.ds(seqs * (4 * n + m) + q, 1), : sz.frames]
                    flags = jnp.where(jnp.logical_and(at_frame, of_seq == q), line, flags)
                value = jnp.dot(flags.astype(BF16), ones, preferred_element_type=F32).reshape(steps, GROUP, bw)
                if n == 0:
                    keepf[m, lo:hi] = 1.0 - value
                else:
                    validf[m, lo:hi] = value
        return 0

    lax.fori_loop(0, 4, masks_of, 0)
    for t in (s_x, s_y, s_d):
        wait_bytes(par.at[t], par_rs.at[t])

    def decays_of(i, _):
        l, m = i // 4, i % 4
        u = jnp.broadcast_to(par[l, 0:1], (GROUP, bw))
        a_h, v_h = [], []
        for h in range(2):
            a = jnp.ones((GROUP, bw), F32)
            v = jnp.zeros((GROUP, bw), F32)
            for t in range(steps):
                d = u * keepf[m, h * steps + t]
                a = d * a
                v = d * v + 1.0
            a_h.append(a)
            v_h.append(v)
        xa, xb, ta, tb = entering(a_h, v_h, False)
        for h in range(2):
            chunk_a[i, h] = a_h[h]
            chunk_aex[i, h] = xa[h]
            chunk_s0[i, h] = xb[h]
        valid_count = total(jnp.sum(validf[m], axis=0))
        value = pack(ta + tb + [valid_count])
        pre_send[i] = value
        pre_recv[nz - 1, i] = value
        return 0

    lax.fori_loop(0, items, decays_of, 0)

    def send_decays(l):
        some = pl.ds(4 * l, 4)
        send_z(pre_send.at[some], lambda k: pre_recv.at[k, some], pre_ss.at[l], pre_rs.at[l])

    send_decays(0)

    def inputs_on(slot):
        block = mainbuf.at[slot, :, c]

        @pl.when(slot != mine)
        def _():
            wait_bytes(block, in_rs.at[slot, c])
            remote(block, block, in_fs.at[slot], in_rs.at[slot, c], to_c).start()

        @pl.when(slot == mine)
        def _():
            wait_bytes(block, in_rs.at[slot, c])

    for slot in range(3):
        inputs_on(slot)

    def w_rows_of(l, j):
        return wbuf.at[l, :, pl.ds(pl.multiple_of(j * bw, bw), bw)]

    def w_unit(l, j, n):
        return wbuf.at[l, n, pl.ds(pl.multiple_of(j * bw, bw), bw)]

    def w_pass(l, k, n):
        j = 2 * pair_half + k

        @pl.when(l != s)
        def _():
            if n == 0:
                wait_bytes(w_rows_of(l, j), w_rs.at[l, j])
            remote(w_unit(l, j, n), w_unit(l, j, n), w_fs.at[l, k, n], w_ps.at[l, k, n], to_pair).start()

    def w_arrive(l):
        @pl.when(l != s)
        def _():
            for k in range(2):
                for n in range(2):
                    wait_bytes(w_unit(l, 2 - 2 * pair_half + k, n), w_ps.at[l, k, n])

    for k in range(2):
        for n in range(2):
            w_pass(0, k, n)
    cut_frames(1)
    for t in range(SECTIONS):
        for h in range(2):
            src = blocks.at[1, 2 * t + h]

            @pl.when(not_me(t, h))
            def _(src=src, t=t, h=h):
                remote(src, dbuf.at[mine, c], cot_ss.at[t, h], cot_rs.at[mine, c], (t, 2 * z + h)).start()

            @pl.when(jnp.logical_not(not_me(t, h)))
            def _(src=src):
                local_copy(src, dbuf.at[mine, c], cot_rs.at[mine, c])

    def arrived(i):
        block = mainbuf.at[i, j_x]
        wait_bytes(block, mx_rs.at[i])
        remote(block, block, mf_ss.at[i], mf_rs.at[i], to_c).start()

    def project(i):
        l, m = i // 4, i % 4

        @pl.when(m == 0)
        def _():
            w_arrive(l)

        @pl.when(l == 0)
        def _():
            wait_bytes(mainbuf.at[i, :, 1 - c], in_rs.at[m, 1 - c])

        @pl.when(l > 0)
        def _():
            wait_bytes(mainbuf.at[i, j_c], ms_rs.at[i])
            wait_bytes(mainbuf.at[i, j_xc], mf_rs.at[i])
            wait_bytes(ysend.at[m], y_ss.at[m])

        def to_half(n):
            acc = jnp.zeros((sz.rows, bw), F32)
            for j in range(4):
                acc = acc + jnp.dot(
                    mainbuf[i, j].reshape(sz.rows, bw), wbuf[l, n, j * bw : (j + 1) * bw], preferred_element_type=F32
                )
            return acc

        ysend[m] = to_half(1).astype(BF16)
        remote(ysend.at[m], yrecv.at[i % 8], y_ss.at[m], y_rs.at[i % 8], to_y).start()
        own[m] = to_half(0).reshape(groups, GROUP, bw)

    def moments(i):
        l, m = i // 4, i % 4
        wait_bytes(yrecv.at[i % 8], y_rs.at[i % 8])
        pre = own[m] + yrecv[i % 8].astype(F32).reshape(groups, GROUP, bw)
        valid = validf[m]
        pre_sum = total(jnp.sum(pre * valid, axis=0))
        local_count = pre_send[i, 2 * seqs : 2 * seqs + 1]
        pivot = pre_sum / jnp.maximum(local_count, 1.0)
        shifted = pre - pivot
        xbuf[i] = shifted
        square = total(jnp.sum(shifted * shifted * valid, axis=0))
        u = jnp.broadcast_to(par[l, 0:1], (GROUP, bw))
        ends = []
        for h in range(2):
            v = jnp.zeros((GROUP, bw), F32)
            for t in range(steps):
                v = (u * keepf[m, h * steps + t]) * v + shifted[h * steps + t]
            ends.append(v)
        unused_a, xb, unused_t, tb = entering([chunk_a[i, 0], chunk_a[i, 1]], ends, False)
        for h in range(2):
            s1ex[m, h] = xb[h]
        value = pack([pre_sum, square] + tb)

        @pl.when(l > 0)
        def _():
            wait_bytes(ex_recv.at[i % 8, pl.ds(0, nz - 1)], ex_ss.at[m])

        ex_send[m] = value
        ex_recv[i % 8, nz - 1] = value
        send_z(ex_send.at[m], lambda k: ex_recv.at[i % 8, k], ex_ss.at[m], ex_rs.at[i % 8])

    def finish_layer(i):
        l, m = i // 4, i % 4

        @pl.when(m == 0)
        def _():
            wait_bytes(pre_recv.at[pl.ds(0, nz - 1), pl.ds(4 * l, 4)], pre_rs.at[l])

        wait_bytes(ex_recv.at[i % 8, pl.ds(0, nz - 1)], ex_rs.at[i % 8])
        u, bias = par[l, 0:1], par[l, 1:2]
        gain, shift = par[l, 2:3], par[l, 3:4]

        def add_sum(p, carry):
            slot = z_slot(p)
            return (
                carry[0] + ex_recv[i % 8, slot, 0:1],
                carry[1] + pre_recv[slot, i, 2 * seqs : 2 * seqs + 1],
            )

        zero = jnp.zeros((1, bw), F32)
        sum_all, count_all = over_z(add_sum, (zero, zero))
        mean = sum_all / count_all

        def pivot_of(slot):
            count = pre_recv[slot, i, 2 * seqs : 2 * seqs + 1]
            return ex_recv[i % 8, slot, 0:1] / jnp.maximum(count, 1.0), count

        def add_square(p, carry):
            slot = z_slot(p)
            pivot, count = pivot_of(slot)
            return carry + ex_recv[i % 8, slot, 1:2] + count * (pivot - mean) * (pivot - mean)

        var = over_z(add_square, zero) / count_all
        inv = lax.rsqrt(var + norm_eps)
        alpha = gain * inv

        def hop_in(p, carry):
            slot = z_slot(p)
            pivot, unused = pivot_of(slot)
            beta = shift + alpha * (pivot - mean)
            after = []
            for q in range(seqs):
                value = (
                    alpha * ex_recv[i % 8, slot, 2 + q : 3 + q]
                    + beta * pre_recv[slot, i, seqs + q : seqs + q + 1]
                    + pre_recv[slot, i, q : q + 1] * carry[q]
                )
                after.append(jnp.where(p < z, value, carry[q]))
            return tuple(after)

        enter = by_seq(list(over_z(hop_in, (zero,) * seqs)))
        pivot, unused = pivot_of(nz - 1)
        beta = shift + alpha * (pivot - mean)
        offset = (pivot - mean) * inv
        scal[i] = pack([alpha, 1.0 / count_all])
        wide = [jnp.broadcast_to(v, (GROUP, bw)) for v in (u, bias, alpha, beta, inv, offset)]
        u, bias, alpha, beta, inv, offset = wide
        side = mainbuf.at[jnp.maximum(i - 4, 0), j_own]
        odd = (l % 2).astype(F32)
        to_next = l < SECTIONS - 1
        target = jnp.minimum(i + 4, items - 1)
        for h in range(2):
            v = alpha * s1ex[m, h] + beta * chunk_s0[i, h] + chunk_aex[i, h] * enter
            carry_in[i, h] = v
            hidden = []
            for t in range(steps):
                g = h * steps + t
                shifted = xbuf[i, g]
                v = (u * keepf[m, g]) * v + (alpha * shifted + beta)
                states[i, g] = v
                xbuf[i, g] = shifted * inv + offset
                w = v + bias
                hidden.append(validf[m, g] * (w * jax.nn.sigmoid(w)))
            value = jnp.concatenate(hidden, axis=0) + odd * side[h].astype(F32)
            outbuf[m, h] = value.astype(BF16)

        @pl.when(to_next)
        def _():
            block = mainbuf.at[target, j_own]
            block[...] = outbuf[m]
            remote(block, block, mx_ss.at[target], mx_rs.at[target], to_x).start()
            remote(block, block, ms_ss.at[target], ms_rs.at[target], to_c).start()

        @pl.when(jnp.logical_not(to_next))
        def _():
            for h in range(2):
                @pl.when(not_me(SECTIONS - 1 - m, h))
                def _(h=h):
                    remote(outbuf.at[m, h], outg.at[me], o_ss.at[m, h], o_rs.at[me], (SECTIONS - 1 - m, 2 * z + h)).start()

                @pl.when(jnp.logical_not(not_me(SECTIONS - 1 - m, h)))
                def _(h=h):
                    local_copy(outbuf.at[m, h], outg.at[me], o_rs.at[me])

    def carry_slopes(i):
        l, m = i // 4, i % 4
        u = jnp.broadcast_to(par[l, 0:1], (GROUP, bw))
        a_h = [chunk_a[i, 0], chunk_a[i, 1]]
        xa, unused_b, unused_a, unused_t = entering(a_h, [jnp.zeros((GROUP, bw), F32)] * 2, True)
        sum_one = jnp.zeros((GROUP, bw), F32)
        sum_normed = jnp.zeros((GROUP, bw), F32)
        for h in (1, 0):
            v = xa[h]
            for t in range(steps - 1, -1, -1):
                g = h * steps + t
                sum_one = sum_one + v
                sum_normed = sum_normed + v * xbuf[i, g]
                v = (u * keepf[m, g]) * v
        rows = []
        for value in (sum_one, sum_normed):
            for q in range(seqs):
                inside = jnp.logical_and(sub >= q * pieces, sub < (q + 1) * pieces)
                rows.append(total(jnp.where(inside, value, 0.0)))
        slopes[i] = pack(rows)

    def forward_tick(k, _):
        @pl.when(k < items)
        def _():
            project(k)

        @pl.when(k == 1)
        def _():
            inputs_on(3)

        @pl.when(k >= 2)
        def _():
            finish_layer(k - 2)
            carry_slopes(k - 2)

        @pl.when(jnp.logical_and(k >= 1, k < items + 1))
        def _():
            moments(k - 1)

        @pl.when(jnp.logical_and(k + 1 >= 4, k + 1 < items))
        def _():
            arrived(k + 1)

        @pl.when(k < 12)
        def _():
            for n in range(4):
                @pl.when(k % 4 == n)
                def _(n=n):
                    w_pass(k // 4 + 1, n // 2, n % 2)

            @pl.when(k % 4 == 1)
            def _():
                send_decays(k // 4 + 1)

        return 0

    lax.fori_loop(0, items + 2, forward_tick, 0)

    for m in range(4):
        wait_bytes(ysend.at[m], y_ss.at[m])

    def back_index(b):
        l, m = SECTIONS - 1 - b // 4, b % 4
        return l, m, l * 4 + m

    def act_back(b):
        l, m, i = back_index(b)

        @pl.when(b < 4)
        def _():
            for h in range(2):
                wait_bytes(dbuf.at[m, h], cot_rs.at[m, h])

        u = jnp.broadcast_to(par[l, 0:1], (GROUP, bw))
        bias = jnp.broadcast_to(par[l, 1:2], (GROUP, bw))
        ends = [None, None]
        sum_act = jnp.zeros((GROUP, bw), F32)
        for h in (1, 0):
            grad = dbuf[b, h].astype(F32).reshape(steps, GROUP, bw)
            v = jnp.zeros((GROUP, bw), F32)
            for t in range(steps - 1, -1, -1):
                g = h * steps + t
                w = states[i, g] + bias
                sg = jax.nn.sigmoid(w)
                da = grad[t] * validf[m, g] * (sg * (1.0 + w * (1.0 - sg)))
                own[m, g] = da
                sum_act = sum_act + da
                v = (u * keepf[m, g]) * (da + v)
            ends[h] = v
        xa, xb, unused, tb = entering([chunk_a[i, 0], chunk_a[i, 1]], ends, True)
        for h in range(2):
            aexr[m, h] = xa[h]
            cex[m, h] = xb[h]
        sum_local = jnp.zeros((GROUP, bw), F32)
        sum_normed = jnp.zeros((GROUP, bw), F32)
        for h in (1, 0):
            v = xb[h]
            for t in range(steps - 1, -1, -1):
                g = h * steps + t
                ds = own[m, g] + v
                sum_local = sum_local + ds
                sum_normed = sum_normed + ds * xbuf[i, g]
                v = (u * keepf[m, g]) * ds
        value = pack(tb + [total(sum_local), total(sum_normed)] + [slopes[i, n : n + 1] for n in range(2 * seqs)])

        @pl.when(b >= 4)
        def _():
            wait_bytes(e1_recv.at[b % 8, pl.ds(0, nz - 1)], e1_ss.at[m])

        e1_send[m] = value
        e1_recv[b % 8, nz - 1] = value
        send_z(e1_send.at[m], lambda k: e1_recv.at[b % 8, k], e1_ss.at[m], e1_rs.at[b % 8])
        add_small(l, m, 3, sum_act)

    def add_small(l, m, n, value):
        added = jnp.where(sub == n, jnp.broadcast_to(total(value), (GROUP, bw)), 0.0)
        if n == 3:
            before = jnp.where(m == 0, 0.0, 1.0)
            small[l] = jnp.where(before > 0.0, small[l], 0.0) + added
        else:
            small[l] = small[l] + added

    def state_back(b):
        l, m, i = back_index(b)
        wait_bytes(e1_recv.at[b % 8, pl.ds(0, nz - 1)], e1_rs.at[b % 8])
        zero = blank[...]

        def line(value):
            return jnp.broadcast_to(value, (GROUP, bw))

        def hop_in(n, carry):
            p = nz - 1 - n
            slot = z_slot(p)
            sum_shift, sum_gain = carry[0], carry[1]
            flow, enter = carry[2 : 2 + seqs], carry[2 + seqs :]
            sum_shift = sum_shift + line(e1_recv[b % 8, slot, seqs : seqs + 1])
            sum_gain = sum_gain + line(e1_recv[b % 8, slot, seqs + 1 : seqs + 2])
            after, inside = [], []
            for q in range(seqs):
                one = seqs + 2 + q
                normed = one + seqs
                sum_shift = sum_shift + flow[q] * line(e1_recv[b % 8, slot, one : one + 1])
                sum_gain = sum_gain + flow[q] * line(e1_recv[b % 8, slot, normed : normed + 1])
                inside.append(jnp.where(p == z, flow[q], enter[q]))
                after.append(line(e1_recv[b % 8, slot, q : q + 1]) + line(pre_recv[slot, i, q : q + 1]) * flow[q])
            return (sum_shift, sum_gain, *after, *inside)

        sum_shift, sum_gain, *rest = over_z(hop_in, (zero,) * (2 + 2 * seqs))
        enter = by_seq(rest[seqs:])
        u = jnp.broadcast_to(par[l, 0:1], (GROUP, bw))
        alpha = jnp.broadcast_to(scal[i, 0:1], (GROUP, bw))
        per_count = scal[i, 1:2]
        gain_part, shift_part = sum_gain * per_count, sum_shift * per_count
        sum_rate = jnp.zeros((GROUP, bw), F32)
        rows = [None] * groups
        for h in (1, 0):
            v = cex[m, h] + aexr[m, h] * enter
            for t in range(steps - 1, -1, -1):
                g = h * steps + t
                keep = keepf[m, g]
                ds = own[m, g] + v
                before = carry_in[i, h] if t == 0 else states[i, g - 1]
                sum_rate = sum_rate + (ds * keep) * before
                v = (u * keep) * ds
                rows[g] = alpha * (ds - validf[m, g] * (shift_part + xbuf[i, g] * gain_part))
        @pl.when(b >= 8)
        def _():
            wait_bytes(dpbuf.at[b % 8, 0], dp_ss.at[b % 8])

        dpbuf[b % 8, 0] = jnp.concatenate(rows, axis=0).astype(BF16)
        remote(dpbuf.at[b % 8, 0], dpbuf.at[b % 8, 1], dp_ss.at[b % 8], dp_rs.at[b % 8], to_y).start()
        add_small(l, m, 2, sum_rate)
        small[l] = small[l] + pack([sum_gain[0:1], sum_shift[0:1]])

    nt = (((1,), (1,)), ((), ()))
    tn = (((0,), (0,)), ((), ()))

    def input_back(b):
        l, m, i = back_index(b)
        wait_bytes(dpbuf.at[b % 8, 1], dp_rs.at[b % 8])
        dp_own, dp_other = dpbuf[b % 8, 0], dpbuf[b % 8, 1]

        def toward(j):
            rows = pl.ds(pl.multiple_of(j * bw, bw), bw)
            first = lax.dot_general(dp_own, wbuf[l, 0, rows], nt, preferred_element_type=F32)
            return first + lax.dot_general(dp_other, wbuf[l, 1, rows], nt, preferred_element_type=F32)

        @pl.when(b >= 4)
        def _():
            wait_bytes(sibsend.at[m], sb_ss.at[m])

        sibsend[m, 0] = toward(j_c).astype(BF16)
        sibsend[m, 1] = toward(j_xc).astype(BF16)
        remote(sibsend.at[m], sibrecv.at[b % 8], sb_ss.at[m], sb_rs.at[b % 8], to_c).start()
        pkeep[m, 0] = toward(j_own)
        pkeep[m, 1] = toward(j_x)

    def weight_back(b):
        l, m, i = back_index(b)
        dp = jnp.concatenate([dpbuf[b % 8, 0], dpbuf[b % 8, 1]], axis=1)
        count = nz // 4
        for j in range(4):
            rows = pl.ds(j * bw, bw)
            new = lax.dot_general(mainbuf[i, j].reshape(sz.rows, bw), dp, tn, preferred_element_type=F32)

            @pl.when(m == 0)
            def _(new=new, rows=rows):
                gw[rows] = new

            @pl.when(jnp.logical_and(m > 0, m < 3))
            def _(new=new, rows=rows):
                gw[rows] = gw[rows] + new

            @pl.when(m == 3)
            def _(new=new, rows=rows, j=j):
                all_items = (gw[rows] + new).astype(BF16)
                for n in range(2):
                    value = all_items[:, n * bw : (n + 1) * bw].reshape(count, part, bw)
                    gall[l, j * count : (j + 1) * count, n] = value

    period = 2 * nz
    to_end, to_start = (s, r + 2), (s, r - 2)

    def g_from(p, n, up):
        return gpart.at[p + 1 if up else p, n], gr_rs.at[p + 1 if up else p, n]

    def g_ready(l, p, n, cross):
        unit = gall.at[l, p, n]
        if cross:
            to_section(l, unit, gout.at[c, s, p, n], gx_ss.at[l, p, n], gx_rs.at[s, p, n], gs_ss.at[s, p, n], gs_rs.at[s, p, n])

    def to_section(l, src, dst, cross_ss, cross_rs, other_ss, other_rs):
        @pl.when(l != s)
        def _():
            remote(src, dst, cross_ss, cross_rs, (l, r)).start()

        @pl.when(l == s)
        def _():
            local_copy(src, dst, cross_rs)
            remote(src, dst, other_ss, other_rs, to_c).start()

    def g_step(g, cross):
        for up in (True, False):
            place_z = z if up else nz - 1 - z
            ahead = nz - 1 - place_z
            t = g - 2 * place_z
            q = t // period
            k = t % period
            l = SECTIONS - 1 - q
            n = k % 2
            inside = jnp.logical_and(t >= 0, q < SECTIONS)

            @pl.when(jnp.logical_and(inside, k < 2 * ahead))
            def _(up=up, place_z=place_z, q=q, k=k, l=l, n=n):
                far = nz - 1 - k // 2
                p = far if up else nz - 1 - far
                unit = gall.at[l, p, n]

                buf, sem = g_from(p, n, up)
                way, slot = 0 if up else 1, k % 4
                leaving = gleave.at[way, slot]

                @pl.when(jnp.logical_or(q > 0, k >= 4))
                def _():
                    wait_bytes(leaving, ga_ss.at[way, slot])

                @pl.when(place_z > 0)
                def _():
                    wait_bytes(buf, sem)
                    leaving[...] = (unit[...].astype(F32) + buf[...].astype(F32)).astype(BF16)

                @pl.when(place_z == 0)
                def _():
                    leaving[...] = unit[...]

                remote(leaving, buf, ga_ss.at[way, slot], sem, to_end if up else to_start).start()

            @pl.when(jnp.logical_and(inside, k >= 2 * ahead))
            def _(up=up, place_z=place_z, ahead=ahead, k=k, l=l, n=n):
                back = (k - 2 * ahead) // 2
                p = z - back if up else z + back
                unit = gall.at[l, p, n]

                @pl.when(back == 0)
                def _():
                    if up:
                        whole = unit[...].astype(F32)
                        for way, there in ((True, z > 0), (False, z < nz - 1)):
                            buf, sem = g_from(p, n, way)

                            @pl.when(there)
                            def _(buf=buf, sem=sem):
                                wait_bytes(buf, sem)

                            whole = whole + jnp.where(there, buf[...].astype(F32), 0.0)
                        unit[...] = whole.astype(BF16)
                        g_ready(l, p, n, cross)

                @pl.when(back > 0)
                def _():
                    wait_bytes(unit, ga_rs.at[l, p, n])
                    g_ready(l, p, n, cross)

                @pl.when(ahead > 0)
                def _():
                    way = 0 if up else 1
                    remote(unit, unit, go_ss.at[l, p, n, way], ga_rs.at[l, p, n], to_end if up else to_start).start()

    def cross_back(b):
        m = b % 4
        wait_bytes(sibrecv.at[b % 8], sb_rs.at[b % 8])

        @pl.when(b >= 4)
        def _():
            wait_bytes(ysend.at[m], xp_ss.at[m])

        ysend[m] = (pkeep[m, 1] + sibrecv[b % 8, 1].astype(F32)).astype(BF16)
        remote(ysend.at[m], xrecv.at[b % 8], xp_ss.at[m], xp_rs.at[b % 8], to_x).start()
        pkeep[m, 0] = pkeep[m, 0] + sibrecv[b % 8, 0].astype(F32)

    def join_back(b):
        l, m, i = back_index(b)
        wait_bytes(xrecv.at[b % 8], xp_rs.at[b % 8])
        even = (1 - l % 2).astype(F32)
        side = dbuf[jnp.maximum(b - 4, 0)].astype(F32).reshape(sz.rows, bw)
        value = pkeep[m, 0] + xrecv[b % 8].astype(F32) + even * side
        dbuf[b + 4] = value.astype(BF16).reshape(2, sz.half, bw)

        @pl.when(l == 0)
        def _():
            for h in range(2):
                src = dbuf.at[b + 4, h]

                @pl.when(not_me(SECTIONS - 1 - m, h))
                def _(src=src, h=h):
                    remote(src, ging.at[me], gi_ss.at[m, h], gi_rs.at[me], (SECTIONS - 1 - m, 2 * z + h)).start()

                @pl.when(jnp.logical_not(not_me(SECTIONS - 1 - m, h)))
                def _(src=src):
                    local_copy(src, ging.at[me], gi_rs.at[me])

    first_step = 6

    def backward_tick(k, _):
        @pl.when(k >= 4)
        def _():
            join_back(k - 4)

        @pl.when(k < items)
        def _():
            act_back(k)

        @pl.when(k >= first_step)
        def _():
            g_step(k - first_step, False)

        @pl.when(jnp.logical_and(k >= 1, k < items + 1))
        def _():
            state_back(k - 1)

        @pl.when(jnp.logical_and(k >= 2, k < items + 2))
        def _():
            input_back(k - 2)
            weight_back(k - 2)
            cross_back(k - 2)

        return 0

    lax.fori_loop(0, items + 4, backward_tick, 0)

    send_z(small, lambda k: small_recv.at[k], st_ss, st_rs)
    wait_bytes(small_recv, st_rs)
    wait_bytes(small_recv, st_ss)

    def add_rest(k, _):
        for l in range(SECTIONS):
            small[l] = small[l] + jnp.where(sub >= 2, small_recv[k, l], 0.0)
        return 0

    lax.fori_loop(0, nz - 1, add_rest, 0)
    for t in range(SECTIONS):
        for h in range(2):
            @pl.when(not_me(t, h))
            def _(t=t, h=h):
                remote(small.at[t], smallg.at[me], sm_ss.at[t, h], sm_rs.at[me], (t, 2 * z + h)).start()

            @pl.when(jnp.logical_not(not_me(t, h)))
            def _(t=t):
                local_copy(small.at[t], smallg.at[me], sm_rs.at[me])

    steps_done = items + 4 - first_step
    steps_all = SECTIONS * period + 2 * (nz - 1)

    def whole_at(q, p, n):
        return q * period + 2 * (nz - 1) + 2 * jnp.abs(z - p) + n

    def cross_early(k, _):
        q, p, n = k // period, k % period // 2, k % 2
        l = SECTIONS - 1 - q

        @pl.when(whole_at(q, p, n) < steps_done)
        def _():
            g_ready(l, p, n, True)

        return 0

    lax.fori_loop(0, SECTIONS * period, cross_early, 0)

    def late_step(g, _):
        g_step(g, True)
        return 0

    lax.fori_loop(steps_done, steps_all, late_step, 0)

    def to_other_core(k, _):
        p, n = k // 2, k % 2
        for t in (s_x, s_y, s_d):
            unit = gout.at[c, t, p, n]
            wait_bytes(unit, gx_rs.at[t, p, n])
            remote(unit, unit, gs_ss.at[t, p, n], gs_rs.at[t, p, n], to_c).start()
        return 0

    lax.fori_loop(0, period, to_other_core, 0)

    restore = (row_of == frame_at).astype(BF16)
    for e in range(8):
        wait_bytes(outg.at[e], o_rs.at[e])
        wait_bytes(ging.at[e], gi_rs.at[e])
        wait_bytes(smallg.at[e], sm_rs.at[e])
        for src, dst in ((outg, out), (ging, grad_inp)):
            value = jnp.dot(restore, src[e], preferred_element_type=F32).astype(BF16)
            value = value.reshape(seqs, sz.frames, bw)
            dst[0, :, :, e * bw : e * bw + width(e)] = value[:, :, : width(e)]
        for n, dst in enumerate((grad_gain, grad_shift, grad_rec, grad_bias)):
            dst[0:1, e * bw : e * bw + width(e)] = smallg[e, n : n + 1, : width(e)]

    def drain_units(k, _):
        p, n = k // 2, k % 2
        unit = gall.at[0, p, n]
        for t in range(SECTIONS):
            wait_bytes(unit, gs_rs.at[t, p, n])
            wait_bytes(unit, gs_ss.at[t, p, n])

            @pl.when(t != s)
            def _(t=t):
                wait_bytes(unit, gx_ss.at[t, p, n])

            @pl.when(t == s)
            def _(t=t):
                wait_bytes(unit, gx_rs.at[t, p, n])

            @pl.when(jnp.logical_and(p <= z, z < nz - 1))
            def _(t=t):
                wait_bytes(unit, go_ss.at[t, p, n, 0])

            @pl.when(jnp.logical_and(p >= z, z > 0))
            def _(t=t):
                wait_bytes(unit, go_ss.at[t, p, n, 1])

        return 0

    lax.fori_loop(0, period, drain_units, 0)
    for way in range(2):
        ahead = nz - 1 - z if way == 0 else z
        for slot in range(4):
            @pl.when(slot < 2 * ahead)
            def _(way=way, slot=slot):
                wait_bytes(gleave.at[way, slot], ga_ss.at[way, slot])

    for l in range(SECTIONS):
        @pl.when(l != s)
        def _(l=l):
            for k in range(2):
                for n in range(2):
                    wait_bytes(w_unit(l, k, n), w_fs.at[l, k, n])

        wait_bytes(pre_recv.at[pl.ds(0, nz - 1), pl.ds(4 * l, 4)], pre_ss.at[l])
        wait_bytes(ex_recv.at[l, pl.ds(0, nz - 1)], ex_ss.at[l])
        wait_bytes(e1_recv.at[l, pl.ds(0, nz - 1)], e1_ss.at[l])
        wait_bytes(sibsend.at[l], sb_ss.at[l])
        wait_bytes(ysend.at[l], xp_ss.at[l])
        for h in range(2):
            @pl.when(not_me(l, h))
            def _(l=l, h=h):
                wait_bytes(dbuf.at[mine, c], cot_ss.at[l, h])
                wait_bytes(small.at[l], sm_ss.at[l, h])

            @pl.when(not_me(SECTIONS - 1 - l, h))
            def _(l=l, h=h):
                wait_bytes(outbuf.at[l, h], o_ss.at[l, h])
                wait_bytes(dbuf.at[items + l, h], gi_ss.at[l, h])

    def drain(i, _):
        @pl.when(i < 8)
        def _():
            wait_bytes(dpbuf.at[i, 0], dp_ss.at[i])

        @pl.when(i >= 4)
        def _():
            wait_bytes(mainbuf.at[i, j_own], mx_ss.at[i])
            wait_bytes(mainbuf.at[i, j_own], ms_ss.at[i])
            wait_bytes(mainbuf.at[i, j_x], mf_ss.at[i])

        return 0

    lax.fori_loop(0, items, drain, 0)
    for n in range(4):
        wait_bytes(in_dst, in_ss.at[n])
    for slot in range(4):
        @pl.when(slot != mine)
        def _(slot=slot):
            wait_bytes(in_dst, in_fs.at[slot])

    for n in range(3):
        wait_bytes(par.at[s], par_ss.at[n])
        for k in range(2):
            wait_bytes(wx.at[n, :, pl.ds(k * bw, bw)], w_ss.at[n, k])
    wait_bytes(flagbuf.at[c], flag_ss.at[0])


def run_kernel(sz, *args):
    nz, bw, items, groups = sz.nz, sz.bw, sz.items, sz.groups
    half, rows, part = sz.half, sz.rows, sz.part
    dma = pltpu.SemaphoreType.DMA
    vm = pltpu.VMEM
    step = (GROUP, bw)
    scratch = [
        vm((items, 4, 2, half, bw), BF16),
        vm((SECTIONS, 2, 4 * bw, bw), BF16),
        vm((4, rows, bw), BF16),
        vm((8, rows, bw), BF16),
        vm((4, groups) + step, F32),
        vm((items, groups) + step, F32),
        vm((items, groups) + step, F32),
        vm((items, 2) + step, F32),
        vm((items, 2) + step, F32),
        vm((items, 2) + step, F32),
        vm((items, 2) + step, F32),
        vm((4, groups) + step, F32),
        vm((4, groups) + step, F32),
        vm((2, 8 * sz.seqs, 128), F32),
        vm((SECTIONS,) + step, F32),
        vm((8,) + step, F32),
        vm((items,) + step, F32),
        vm((nz, items) + step, F32),
        vm((4,) + step, F32),
        vm((8, nz) + step, F32),
        vm((4,) + step, F32),
        vm((8, nz) + step, F32),
        vm((items,) + step, F32),
        vm((items,) + step, F32),
        vm((4, 2) + step, F32),
        vm((items + 4, 2, half, bw), BF16),
        vm((4, 2) + step, F32),
        vm((4, 2) + step, F32),
        vm((8, 2, rows, bw), BF16),
        vm((4, 2, rows, bw), F32),
        vm((4, 2, rows, bw), BF16),
        vm((8, 2, rows, bw), BF16),
        vm((8, rows, bw), BF16),
        vm((4 * bw, 2 * bw), F32),
        vm((SECTIONS, nz, 2, part, bw), BF16),
        vm((nz + 1, 2, part, bw), BF16),
        vm((2, 4, part, bw), BF16),
        vm((SECTIONS,) + step, F32),
        vm((nz - 1, SECTIONS) + step, F32),
        vm((4, 2, half, bw), BF16),
        vm((2, sz.seqs, sz.frames, sz.hidden), BF16),
        vm((2, 8, half, bw), BF16),
        vm((2, bw, sz.hidden), BF16),
        vm((3, 2, 2 * bw, bw), BF16),
        vm((8, half, bw), BF16),
        vm((8, half, bw), BF16),
        vm((8,) + step, F32),
        vm(step, F32),
    ]
    sems = [
        dma((2,)), dma((2,)), dma((4,)), dma((4,)), dma((4, 2)), dma((4, 2)), dma((4, 2)),
        dma((3,)), dma((4,)), dma((1,)), dma((2,)),
        dma((3, 2)), dma((4, 4)), dma((4, 2, 2)), dma((4, 2, 2)),
        dma((4,)), dma((4,)),
        dma((items,)), dma((items,)), dma((items,)), dma((items,)), dma((items,)), dma((items,)),
        dma((4,)), dma((8,)), dma((4,)), dma((8,)),
        dma((4, 2)), dma((8,)), dma((4,)), dma((8,)),
        dma((8,)), dma((8,)), dma((4,)), dma((8,)), dma((4,)), dma((8,)),
        dma((4, 2)), dma((8,)),
        dma((2, 4)), dma((4, nz, 2)), dma((4, nz, 2, 2)), dma((nz + 1, 2)),
        dma((4, nz, 2)), dma((4, nz, 2)), dma((4, nz, 2)), dma((4, nz, 2)),
        dma, dma, dma((4, 2)), dma((8,)),
    ]
    anywhere = pl.BlockSpec(memory_space=pl.ANY)
    inside = pl.BlockSpec(memory_space=pltpu.VMEM)
    frames = jax.ShapeDtypeStruct((1, sz.seqs, sz.frames, sz.hidden), BF16)
    vector = jax.ShapeDtypeStruct((1, sz.hidden), F32)
    return pl.pallas_call(
        functools.partial(kernel, sz),
        out_shape=(frames, frames) + (vector,) * 4 + (jax.ShapeDtypeStruct((2, SECTIONS, nz, 2, part, bw), BF16),),
        in_specs=[anywhere] * 3 + [inside] * 6,
        out_specs=(inside,) * 6 + (anywhere,),
        scratch_shapes=scratch + sems,
        compiler_params=pltpu.CompilerParams(
            collective_id=0, has_side_effects=True, vmem_limit_bytes=63 * 2**20
        ),
    )(*args)


def place_weights(sz, pieces):
    bw, part, hidden = sz.bw, sz.part, sz.hidden
    count = bw // part

    def body(src, dst):
        upper = pl.program_id(0) // 4
        for yy in range(2):
            @pl.when(upper == yy)
            def _(yy=yy):
                for p in range(count):
                    for e in range(8):
                        n, x, c = (0 if e // 4 == yy else 1), e % 4 // 2, e % 2
                        wide = bw if e < 7 else sz.last
                        value = src[c, x, p, n, :, :wide].astype(F32)
                        dst[p * part : (p + 1) * part, e * bw : e * bw + wide] = value

    return pl.pallas_call(
        body,
        grid=(8,),
        out_shape=jax.ShapeDtypeStruct((hidden, hidden), F32),
        in_specs=[pl.BlockSpec((2, 2, count, 2, part, bw), lambda q: (0, q // 4, q % 4, 0, 0, 0))],
        out_specs=pl.BlockSpec((bw, hidden), lambda q: (q, 0)),
        compiler_params=pltpu.CompilerParams(vmem_limit_bytes=32 * 2**20),
    )(pieces)


def local(sz, inputs, resets, valid_mask, weights, recurrence, state_bias, norm_gain, norm_shift, cotangent):
    outputs, grad_inputs, rec, bias, gain, shift, pieces = run_kernel(
        sz, inputs, cotangent, weights, resets, valid_mask, recurrence, state_bias, norm_gain, norm_shift
    )
    return outputs, grad_inputs, place_weights(sz, pieces)[None], rec, bias, gain, shift


def solution(mesh):
    def step(inputs, *rest):
        sz = Sizes(mesh.shape["rows"] // 2, inputs.shape[1], inputs.shape[2], inputs.shape[3])
        return local(sz, inputs, *rest)

    frames = P("section", None, "rows", None)
    flags = P(None, None, "rows")
    vectors = P("section", None)
    matrix = P("section", None, None)
    return jax.shard_map(
        step,
        mesh=mesh,
        in_specs=(frames, flags, flags, matrix, vectors, vectors, vectors, vectors, frames),
        out_specs=(frames, frames, matrix, vectors, vectors, vectors, vectors),
        check_vma=False,
    )
```

```python
import functools

import jax
import jax.numpy as jnp
from jax import lax
from jax.experimental import pallas as pl
from jax.experimental.pallas import tpu as pltpu
from jax.sharding import PartitionSpec as P

MESH = pl.DeviceIdType.MESH
norm_eps = 1e-05
F32, BF16 = jnp.float32, jnp.bfloat16
SECTIONS = 4
GROUP = 8


class Sizes:
    def __init__(self, nz, seqs, frames, hidden):
        self.nz, self.seqs, self.frames = nz, seqs, frames
        self.pieces = GROUP // seqs
        self.steps = frames // self.pieces
        self.half = seqs * frames
        self.rows = 2 * self.half
        self.groups = self.rows // GROUP
        self.bw = -(-hidden // 1024) * 128
        self.padded = 8 * self.bw
        self.part = 4 * self.bw // nz
        self.items = 4 * SECTIONS
        self.hidden = hidden
        self.last = hidden - 7 * self.bw


def wait_bytes(ref, sem):
    pltpu.make_async_copy(ref, ref, sem).wait()


def local_copy(src, dst, sem):
    pltpu.make_async_copy(src, dst, sem).start()


def remote(src, dst, send, recv, device):
    return pltpu.make_async_remote_copy(
        src_ref=src, dst_ref=dst, send_sem=send, recv_sem=recv, device_id=device, device_id_type=MESH
    )


def kernel(
    sz, inp_raw, cot_raw, w_raw, resets, valid_mask, recurrence, state_bias, norm_gain, norm_shift,
    out, grad_inp, grad_rec, grad_bias, grad_gain, grad_shift, gout,
    mainbuf, wbuf, ysend, yrecv, own, xbuf, states, carry_in, chunk_a, chunk_aex, chunk_s0,
    keepf, validf, flagbuf, par, parblk, pre_send, pre_recv, ex_send, ex_recv, e1_send, e1_recv,
    scal, slopes, s1ex, dbuf, cex, aexr, dpbuf, pkeep, sibsend, sibrecv, xrecv, gw, gall, gpart, gleave, grelay,
    small, small_recv, outbuf, raw, blocks, wst, wx, outg, ging, smallg, blank,
    raw_ls, wst_ls, in_ss, in_fs, in_rs, cot_ss, cot_rs, par_ss, par_rs, flag_ss, flag_rs, w_ss, w_rs, w_fs, w_ps,
    pre_ss, pre_rs, mx_ss, mx_rs, ms_ss, ms_rs, mf_ss, mf_rs, y_ss, y_rs, ex_ss, ex_rs,
    o_ss, o_rs, e1_ss, e1_rs, dp_ss, dp_rs, sb_ss, sb_rs, xp_ss, xp_rs,
    gi_ss, gi_rs, ga_ss, ga_rs, go_ss, gr_rs, gx_ss, gx_rs, gl_ss, gl_rs, gs_ss, gs_rs, st_ss, st_rs, sm_ss, sm_rs,
):
    nz, bw, items, groups, steps = sz.nz, sz.bw, sz.items, sz.groups, sz.steps
    pieces, seqs = sz.pieces, sz.seqs
    s, r = lax.axis_index("section"), lax.axis_index("rows")
    y, x, z, c = s // 2, s % 2, r // 2, r % 2
    s_x, s_y, s_d = s + 1 - 2 * x, s + 2 - 4 * y, 3 - s
    r_c = r + 1 - 2 * c
    to_x, to_y, to_d, to_c = (s_x, r), (s_y, r), (s_d, r), (s, r_c)
    j_own, j_x, j_c, j_xc = 2 * x + c, 2 * (1 - x) + c, 2 * x + 1 - c, 2 * (1 - x) + 1 - c
    me = 2 * s + c
    part, half, last = sz.part, sz.half, sz.last
    mine = SECTIONS - 1 - s
    pair_half = z % 2
    to_pair = (s, r + 2 - 4 * pair_half)
    sub = lax.broadcasted_iota(jnp.int32, (GROUP, bw), 0)
    place = sub % pieces

    def z_peer(distance):
        return (s, 2 * ((z + distance) % nz) + c)

    def z_slot(p):
        return (z - p + nz - 1) % nz

    def by_seq(rows):
        value = jnp.broadcast_to(rows[seqs - 1], (GROUP, bw))
        for q in range(seqs - 2, -1, -1):
            value = jnp.where(sub < (q + 1) * pieces, jnp.broadcast_to(rows[q], (GROUP, bw)), value)
        return value

    def last_of(value, q):
        return value[(q + 1) * pieces - 1 : (q + 1) * pieces]

    def first_of(value, q):
        return value[q * pieces : q * pieces + 1]

    def entering(a, b, reverse):
        out_a, out_b = [None, None], [None, None]
        t_a = t_b = None
        for h in (1, 0) if reverse else (0, 1):
            ia, ib = a[h], b[h]
            hop = 1
            while hop < pieces:
                if reverse:
                    ok, shift = place < pieces - hop, GROUP - hop
                else:
                    ok, shift = place >= hop, hop
                pa = jnp.where(ok, pltpu.roll(ia, shift, 0), 1.0)
                pb = jnp.where(ok, pltpu.roll(ib, shift, 0), 0.0)
                ib = ia * pb + ib
                ia = ia * pa
                hop *= 2
            if reverse:
                ok, shift, edge = place < pieces - 1, GROUP - 1, first_of
            else:
                ok, shift, edge = place >= 1, 1, last_of
            xa = jnp.where(ok, pltpu.roll(ia, shift, 0), 1.0)
            xb = jnp.where(ok, pltpu.roll(ib, shift, 0), 0.0)
            na = [edge(ia, q) for q in range(seqs)]
            nb = [edge(ib, q) for q in range(seqs)]
            if t_a is not None:
                ea, eb = by_seq(t_a), by_seq(t_b)
                xb = xa * eb + xb
                xa = xa * ea
                nb = [na[q] * t_b[q] + nb[q] for q in range(seqs)]
                na = [na[q] * t_a[q] for q in range(seqs)]
            t_a, t_b = na, nb
            out_a[h], out_b[h] = xa, xb
        return out_a, out_b, t_a, t_b

    def pack(rows):
        rows = rows + [jnp.zeros((1, bw), F32)] * (8 - len(rows))
        value = jnp.zeros((8, bw), F32)
        for q, row in enumerate(rows):
            value = jnp.where(sub == q, jnp.broadcast_to(row, (8, bw)), value)
        return value

    def total(value):
        return jnp.sum(value, axis=0, keepdims=True)

    def over_z(body, start):
        return lax.fori_loop(0, nz, body, start, unroll=nz <= 8)

    def send_z(src, dst_of, send_sem, recv_sem):
        def one(k, _):
            remote(src, dst_of(k - 1), send_sem, recv_sem, z_peer(k)).start()
            return 0

        lax.fori_loop(1, nz, one, 0, unroll=nz <= 8)

    def not_me(t, h):
        return jnp.logical_or(t != s, h != c)

    blank[...] = jnp.zeros((GROUP, bw), F32)

    def width(e):
        return bw if e < 7 else last

    barrier = pltpu.get_barrier_semaphore()
    for t in (s, s_x, s_y, s_d):
        for q in (r, r_c):
            if not (t is s and q is r):
                pl.semaphore_signal(barrier, inc=1, device_id=(t, q), device_id_type=MESH)

    def greet(k, _):
        pl.semaphore_signal(barrier, inc=1, device_id=z_peer(k), device_id_type=MESH)
        return 0

    lax.fori_loop(1, nz, greet, 0)

    local_copy(inp_raw.at[0], raw.at[0], raw_ls.at[0])
    local_copy(cot_raw.at[0], raw.at[1], raw_ls.at[1])
    w_rows = [(1 - y, 2 * pair_half), (1 - y, 2 * pair_half + 1), (y, 2 * pair_half), (y, 2 * pair_half + 1)]
    w_rows += [(y, 2 - 2 * pair_half), (y, 3 - 2 * pair_half)]

    def w_load(n, wait):
        yy, j = w_rows[n]
        k, slot = 4 * yy + j, n % 2

        def go(rows):
            copy = pltpu.make_async_copy(
                w_raw.at[0, pl.ds(pl.multiple_of(k * bw, bw), rows)], wst.at[slot, pl.ds(0, rows)], wst_ls.at[slot]
            )
            copy.wait() if wait else copy.start()

        @pl.when(k < 7)
        def _():
            go(bw)

        @pl.when(k == 7)
        def _():
            if not wait:
                wst[slot, last:] = jnp.zeros((bw - last, sz.hidden), BF16)
            go(last)

    def w_cut(n, column, toward, dst):
        slot = n % 2
        for e in range(8):
            @pl.when(column == e % 4)
            def _(e=e):
                place_of = jnp.where(toward == e // 4, 0, 1)
                if e == 7:
                    dst[place_of] = jnp.zeros((bw, bw), BF16)
                dst[place_of, :, : width(e)] = wst[slot, :, e * bw : e * bw + width(e)]

    for n in range(2):
        w_load(n, False)

    parblk[...] = jnp.zeros(parblk.shape, F32)
    for n, ref in enumerate((recurrence, state_bias, norm_gain, norm_shift)):
        for e in range(8):
            parblk[e, n : n + 1, : width(e)] = ref[0:1, e * bw : e * bw + width(e)]
    par[s] = parblk[me]
    flagbuf[c] = jnp.zeros(flagbuf.shape[1:], F32)
    for n, ref in enumerate((resets, valid_mask)):
        for m in range(4):
            row = seqs * (4 * n + m)
            flagbuf[c, row : row + seqs, : sz.frames] = ref[SECTIONS - 1 - m].astype(F32)

    def w_cross():
        for k in range(2):
            j = 2 * pair_half + k
            for n, t in enumerate((s_x, s_y, s_d)):
                src = wx.at[n, :, pl.ds(k * bw, bw)]
                dst = wbuf.at[s, :, pl.ds(pl.multiple_of(j * bw, bw), bw)]
                remote(src, dst, w_ss.at[n, k], w_rs.at[s, j], (t, r)).start()

    for n in range(6):
        if n == 4:
            pl.semaphore_wait(barrier, 7 + nz - 1)

            @pl.when(s == 0)
            def _():
                w_cross()

        w_load(n, True)
        j = w_rows[n][1]
        rows = pl.ds(pl.multiple_of(j * bw, bw), bw)
        half_rows = pl.ds((n % 2) * bw, bw)
        if n < 2:
            w_cut(n, j_own, 1 - y, wx.at[1, :, half_rows])
            w_cut(n, j_x, 1 - y, wx.at[2, :, half_rows])
        elif n < 4:
            w_cut(n, j_x, y, wx.at[0, :, half_rows])
            w_cut(n, j_own, y, wbuf.at[s, :, rows])
        else:
            w_cut(n, j_own, y, wbuf.at[s, :, rows])
        if n + 2 < 6:
            w_load(n + 2, False)

    row = lax.broadcasted_iota(jnp.int32, (half, half), 0)
    col = lax.broadcasted_iota(jnp.int32, (half, half), 1)
    frame_of = (row % GROUP // pieces) * sz.frames + (row % pieces) * steps + row // GROUP
    permute = (col == frame_of).astype(BF16)
    row_of = row
    frame_at = (col % GROUP // pieces) * sz.frames + (col % pieces) * steps + col // GROUP

    def cut_frames(n):
        wait_bytes(raw.at[n], raw_ls.at[n])
        for e in range(8):
            value = raw[n, :, :, e * bw : e * bw + width(e)].reshape(half, width(e))
            if e == 7:
                blocks[n, e] = jnp.zeros((half, bw), BF16)
            blocks[n, e, :, : width(e)] = jnp.dot(permute, value, preferred_element_type=F32).astype(BF16)

    cut_frames(0)

    for n, t in enumerate((s_x, s_y, s_d)):
        remote(parblk.at[2 * t + c], par.at[s], par_ss.at[n], par_rs.at[s], (t, r)).start()
    remote(flagbuf.at[c], flagbuf.at[c], flag_ss.at[0], flag_rs.at[c], to_c).start()

    in_dst = mainbuf.at[mine, :, c]
    near, far = blocks.at[0, pl.ds(4 * y, 4)], blocks.at[0, pl.ds(4 - 4 * y, 4)]
    remote(far, in_dst, in_ss.at[2], in_rs.at[mine, c], to_d).start()
    remote(near, in_dst, in_ss.at[0], in_rs.at[mine, c], to_x).start()
    remote(far, in_dst, in_ss.at[1], in_rs.at[mine, c], to_y).start()
    remote(near, in_dst, in_ss.at[3], in_rs.at[mine, c], to_c).start()
    local_copy(near, in_dst, in_rs.at[mine, c])

    @pl.when(s != 0)
    def _():
        w_cross()

    wait_bytes(flagbuf.at[1 - c], flag_rs.at[1 - c])
    row = lax.broadcasted_iota(jnp.int32, (half, sz.frames), 0)
    col = lax.broadcasted_iota(jnp.int32, (half, sz.frames), 1)
    at_frame = col == (row % pieces) * steps + row // GROUP
    of_seq = row % GROUP // pieces
    ones = jnp.ones((sz.frames, bw), BF16)

    def masks_of(m, _):
        for h in range(2):
            lo, hi = h * steps, (h + 1) * steps
            for n in range(2):
                flags = jnp.zeros((half, sz.frames), F32)
                for q in range(seqs):
                    line = flagbuf[h, pl.ds(seqs * (4 * n + m) + q, 1), : sz.frames]
                    flags = jnp.where(jnp.logical_and(at_frame, of_seq == q), line, flags)
                value = jnp.dot(flags.astype(BF16), ones, preferred_element_type=F32).reshape(steps, GROUP, bw)
                if n == 0:
                    keepf[m, lo:hi] = 1.0 - value
                else:
                    validf[m, lo:hi] = value
        return 0

    lax.fori_loop(0, 4, masks_of, 0)
    for t in (s_x, s_y, s_d):
        wait_bytes(par.at[t], par_rs.at[t])

    def decays_of(i, _):
        l, m = i // 4, i % 4
        u = jnp.broadcast_to(par[l, 0:1], (GROUP, bw))
        a_h, v_h = [], []
        for h in range(2):
            a = jnp.ones((GROUP, bw), F32)
            v = jnp.zeros((GROUP, bw), F32)
            for t in range(steps):
                d = u * keepf[m, h * steps + t]
                a = d * a
                v = d * v + 1.0
            a_h.append(a)
            v_h.append(v)
        xa, xb, ta, tb = entering(a_h, v_h, False)
        for h in range(2):
            chunk_a[i, h] = a_h[h]
            chunk_aex[i, h] = xa[h]
            chunk_s0[i, h] = xb[h]
        valid_count = total(jnp.sum(validf[m], axis=0))
        value = pack(ta + tb + [valid_count])
        pre_send[i] = value
        pre_recv[nz - 1, i] = value
        return 0

    lax.fori_loop(0, items, decays_of, 0)

    def send_decays(l):
        some = pl.ds(4 * l, 4)
        send_z(pre_send.at[some], lambda k: pre_recv.at[k, some], pre_ss.at[l], pre_rs.at[l])

    send_decays(0)

    def inputs_on(slot):
        block = mainbuf.at[slot, :, c]

        @pl.when(slot != mine)
        def _():
            wait_bytes(block, in_rs.at[slot, c])
            remote(block, block, in_fs.at[slot], in_rs.at[slot, c], to_c).start()

        @pl.when(slot == mine)
        def _():
            wait_bytes(block, in_rs.at[slot, c])

    for slot in range(3):
        inputs_on(slot)

    def w_rows_of(l, j):
        return wbuf.at[l, :, pl.ds(pl.multiple_of(j * bw, bw), bw)]

    def w_unit(l, j, n):
        return wbuf.at[l, n, pl.ds(pl.multiple_of(j * bw, bw), bw)]

    def w_pass(l, k, n):
        j = 2 * pair_half + k

        @pl.when(l != s)
        def _():
            if n == 0:
                wait_bytes(w_rows_of(l, j), w_rs.at[l, j])
            remote(w_unit(l, j, n), w_unit(l, j, n), w_fs.at[l, k, n], w_ps.at[l, k, n], to_pair).start()

    def w_arrive(l):
        @pl.when(l != s)
        def _():
            for k in range(2):
                for n in range(2):
                    wait_bytes(w_unit(l, 2 - 2 * pair_half + k, n), w_ps.at[l, k, n])

    for k in range(2):
        for n in range(2):
            w_pass(0, k, n)
    cut_frames(1)
    for t in range(SECTIONS):
        for h in range(2):
            src = blocks.at[1, 2 * t + h]

            @pl.when(not_me(t, h))
            def _(src=src, t=t, h=h):
                remote(src, dbuf.at[mine, c], cot_ss.at[t, h], cot_rs.at[mine, c], (t, 2 * z + h)).start()

            @pl.when(jnp.logical_not(not_me(t, h)))
            def _(src=src):
                local_copy(src, dbuf.at[mine, c], cot_rs.at[mine, c])

    def arrived(i):
        block = mainbuf.at[i, j_x]
        wait_bytes(block, mx_rs.at[i])
        remote(block, block, mf_ss.at[i], mf_rs.at[i], to_c).start()

    def project(i):
        l, m = i // 4, i % 4

        @pl.when(m == 0)
        def _():
            w_arrive(l)

        @pl.when(l == 0)
        def _():
            wait_bytes(mainbuf.at[i, :, 1 - c], in_rs.at[m, 1 - c])

        @pl.when(l > 0)
        def _():
            wait_bytes(mainbuf.at[i, j_c], ms_rs.at[i])
            wait_bytes(mainbuf.at[i, j_xc], mf_rs.at[i])
            wait_bytes(ysend.at[m], y_ss.at[m])

        def to_half(n):
            acc = jnp.zeros((sz.rows, bw), F32)
            for j in range(4):
                acc = acc + jnp.dot(
                    mainbuf[i, j].reshape(sz.rows, bw), wbuf[l, n, j * bw : (j + 1) * bw], preferred_element_type=F32
                )
            return acc

        ysend[m] = to_half(1).astype(BF16)
        remote(ysend.at[m], yrecv.at[i % 8], y_ss.at[m], y_rs.at[i % 8], to_y).start()
        own[m] = to_half(0).reshape(groups, GROUP, bw)

    def moments(i):
        l, m = i // 4, i % 4
        wait_bytes(yrecv.at[i % 8], y_rs.at[i % 8])
        pre = own[m] + yrecv[i % 8].astype(F32).reshape(groups, GROUP, bw)
        valid = validf[m]
        pre_sum = total(jnp.sum(pre * valid, axis=0))
        local_count = pre_send[i, 2 * seqs : 2 * seqs + 1]
        pivot = pre_sum / jnp.maximum(local_count, 1.0)
        shifted = pre - pivot
        xbuf[i] = shifted
        square = total(jnp.sum(shifted * shifted * valid, axis=0))
        u = jnp.broadcast_to(par[l, 0:1], (GROUP, bw))
        ends = []
        for h in range(2):
            v = jnp.zeros((GROUP, bw), F32)
            for t in range(steps):
                v = (u * keepf[m, h * steps + t]) * v + shifted[h * steps + t]
            ends.append(v)
        unused_a, xb, unused_t, tb = entering([chunk_a[i, 0], chunk_a[i, 1]], ends, False)
        for h in range(2):
            s1ex[m, h] = xb[h]
        value = pack([pre_sum, square] + tb)

        @pl.when(l > 0)
        def _():
            wait_bytes(ex_recv.at[i % 8, pl.ds(0, nz - 1)], ex_ss.at[m])

        ex_send[m] = value
        ex_recv[i % 8, nz - 1] = value
        send_z(ex_send.at[m], lambda k: ex_recv.at[i % 8, k], ex_ss.at[m], ex_rs.at[i % 8])

    def finish_layer(i):
        l, m = i // 4, i % 4

        @pl.when(m == 0)
        def _():
            wait_bytes(pre_recv.at[pl.ds(0, nz - 1), pl.ds(4 * l, 4)], pre_rs.at[l])

        wait_bytes(ex_recv.at[i % 8, pl.ds(0, nz - 1)], ex_rs.at[i % 8])
        u, bias = par[l, 0:1], par[l, 1:2]
        gain, shift = par[l, 2:3], par[l, 3:4]

        def add_sum(p, carry):
            slot = z_slot(p)
            return (
                carry[0] + ex_recv[i % 8, slot, 0:1],
                carry[1] + pre_recv[slot, i, 2 * seqs : 2 * seqs + 1],
            )

        zero = jnp.zeros((1, bw), F32)
        sum_all, count_all = over_z(add_sum, (zero, zero))
        mean = sum_all / count_all

        def pivot_of(slot):
            count = pre_recv[slot, i, 2 * seqs : 2 * seqs + 1]
            return ex_recv[i % 8, slot, 0:1] / jnp.maximum(count, 1.0), count

        def add_square(p, carry):
            slot = z_slot(p)
            pivot, count = pivot_of(slot)
            return carry + ex_recv[i % 8, slot, 1:2] + count * (pivot - mean) * (pivot - mean)

        var = over_z(add_square, zero) / count_all
        inv = lax.rsqrt(var + norm_eps)
        alpha = gain * inv

        def hop_in(p, carry):
            slot = z_slot(p)
            pivot, unused = pivot_of(slot)
            beta = shift + alpha * (pivot - mean)
            after = []
            for q in range(seqs):
                value = (
                    alpha * ex_recv[i % 8, slot, 2 + q : 3 + q]
                    + beta * pre_recv[slot, i, seqs + q : seqs + q + 1]
                    + pre_recv[slot, i, q : q + 1] * carry[q]
                )
                after.append(jnp.where(p < z, value, carry[q]))
            return tuple(after)

        enter = by_seq(list(over_z(hop_in, (zero,) * seqs)))
        pivot, unused = pivot_of(nz - 1)
        beta = shift + alpha * (pivot - mean)
        offset = (pivot - mean) * inv
        scal[i] = pack([alpha, 1.0 / count_all])
        wide = [jnp.broadcast_to(v, (GROUP, bw)) for v in (u, bias, alpha, beta, inv, offset)]
        u, bias, alpha, beta, inv, offset = wide
        side = mainbuf.at[jnp.maximum(i - 4, 0), j_own]
        odd = (l % 2).astype(F32)
        to_next = l < SECTIONS - 1
        target = jnp.minimum(i + 4, items - 1)
        for h in range(2):
            v = alpha * s1ex[m, h] + beta * chunk_s0[i, h] + chunk_aex[i, h] * enter
            carry_in[i, h] = v
            hidden = []
            for t in range(steps):
                g = h * steps + t
                shifted = xbuf[i, g]
                v = (u * keepf[m, g]) * v + (alpha * shifted + beta)
                states[i, g] = v
                xbuf[i, g] = shifted * inv + offset
                w = v + bias
                hidden.append(validf[m, g] * (w * jax.nn.sigmoid(w)))
            value = jnp.concatenate(hidden, axis=0) + odd * side[h].astype(F32)
            outbuf[m, h] = value.astype(BF16)

        @pl.when(to_next)
        def _():
            block = mainbuf.at[target, j_own]
            block[...] = outbuf[m]
            remote(block, block, mx_ss.at[target], mx_rs.at[target], to_x).start()
            remote(block, block, ms_ss.at[target], ms_rs.at[target], to_c).start()

        @pl.when(jnp.logical_not(to_next))
        def _():
            for h in range(2):
                @pl.when(not_me(SECTIONS - 1 - m, h))
                def _(h=h):
                    remote(outbuf.at[m, h], outg.at[me], o_ss.at[m, h], o_rs.at[me], (SECTIONS - 1 - m, 2 * z + h)).start()

                @pl.when(jnp.logical_not(not_me(SECTIONS - 1 - m, h)))
                def _(h=h):
                    local_copy(outbuf.at[m, h], outg.at[me], o_rs.at[me])

    def carry_slopes(i):
        l, m = i // 4, i % 4
        u = jnp.broadcast_to(par[l, 0:1], (GROUP, bw))
        a_h = [chunk_a[i, 0], chunk_a[i, 1]]
        xa, unused_b, unused_a, unused_t = entering(a_h, [jnp.zeros((GROUP, bw), F32)] * 2, True)
        sum_one = jnp.zeros((GROUP, bw), F32)
        sum_normed = jnp.zeros((GROUP, bw), F32)
        for h in (1, 0):
            v = xa[h]
            for t in range(steps - 1, -1, -1):
                g = h * steps + t
                sum_one = sum_one + v
                sum_normed = sum_normed + v * xbuf[i, g]
                v = (u * keepf[m, g]) * v
        rows = []
        for value in (sum_one, sum_normed):
            for q in range(seqs):
                inside = jnp.logical_and(sub >= q * pieces, sub < (q + 1) * pieces)
                rows.append(total(jnp.where(inside, value, 0.0)))
        slopes[i] = pack(rows)

    def back_index(b):
        l, m = SECTIONS - 1 - b // 4, b % 4
        return l, m, l * 4 + m

    def act_back(b):
        l, m, i = back_index(b)

        @pl.when(b < 4)
        def _():
            for h in range(2):
                wait_bytes(dbuf.at[m, h], cot_rs.at[m, h])

        u = jnp.broadcast_to(par[l, 0:1], (GROUP, bw))
        bias = jnp.broadcast_to(par[l, 1:2], (GROUP, bw))
        ends = [None, None]
        sum_act = jnp.zeros((GROUP, bw), F32)
        for h in (1, 0):
            grad = dbuf[b, h].astype(F32).reshape(steps, GROUP, bw)
            v = jnp.zeros((GROUP, bw), F32)
            for t in range(steps - 1, -1, -1):
                g = h * steps + t
                w = states[i, g] + bias
                sg = jax.nn.sigmoid(w)
                da = grad[t] * validf[m, g] * (sg * (1.0 + w * (1.0 - sg)))
                own[m, g] = da
                sum_act = sum_act + da
                v = (u * keepf[m, g]) * (da + v)
            ends[h] = v
        xa, xb, unused, tb = entering([chunk_a[i, 0], chunk_a[i, 1]], ends, True)
        for h in range(2):
            aexr[m, h] = xa[h]
            cex[m, h] = xb[h]
        sum_local = jnp.zeros((GROUP, bw), F32)
        sum_normed = jnp.zeros((GROUP, bw), F32)
        for h in (1, 0):
            v = xb[h]
            for t in range(steps - 1, -1, -1):
                g = h * steps + t
                ds = own[m, g] + v
                sum_local = sum_local + ds
                sum_normed = sum_normed + ds * xbuf[i, g]
                v = (u * keepf[m, g]) * ds
        value = pack(tb + [total(sum_local), total(sum_normed)] + [slopes[i, n : n + 1] for n in range(2 * seqs)])

        @pl.when(b >= 4)
        def _():
            wait_bytes(e1_recv.at[b % 8, pl.ds(0, nz - 1)], e1_ss.at[m])

        e1_send[m] = value
        e1_recv[b % 8, nz - 1] = value
        send_z(e1_send.at[m], lambda k: e1_recv.at[b % 8, k], e1_ss.at[m], e1_rs.at[b % 8])
        add_small(l, m, 3, sum_act)

    def add_small(l, m, n, value):
        added = jnp.where(sub == n, jnp.broadcast_to(total(value), (GROUP, bw)), 0.0)
        if n == 3:
            before = jnp.where(m == 0, 0.0, 1.0)
            small[l] = jnp.where(before > 0.0, small[l], 0.0) + added
        else:
            small[l] = small[l] + added

    def state_back(b):
        l, m, i = back_index(b)
        wait_bytes(e1_recv.at[b % 8, pl.ds(0, nz - 1)], e1_rs.at[b % 8])
        zero = blank[...]

        def line(value):
            return jnp.broadcast_to(value, (GROUP, bw))

        def hop_in(n, carry):
            p = nz - 1 - n
            slot = z_slot(p)
            sum_shift, sum_gain = carry[0], carry[1]
            flow, enter = carry[2 : 2 + seqs], carry[2 + seqs :]
            sum_shift = sum_shift + line(e1_recv[b % 8, slot, seqs : seqs + 1])
            sum_gain = sum_gain + line(e1_recv[b % 8, slot, seqs + 1 : seqs + 2])
            after, inside = [], []
            for q in range(seqs):
                one = seqs + 2 + q
                normed = one + seqs
                sum_shift = sum_shift + flow[q] * line(e1_recv[b % 8, slot, one : one + 1])
                sum_gain = sum_gain + flow[q] * line(e1_recv[b % 8, slot, normed : normed + 1])
                inside.append(jnp.where(p == z, flow[q], enter[q]))
                after.append(line(e1_recv[b % 8, slot, q : q + 1]) + line(pre_recv[slot, i, q : q + 1]) * flow[q])
            return (sum_shift, sum_gain, *after, *inside)

        sum_shift, sum_gain, *rest = over_z(hop_in, (zero,) * (2 + 2 * seqs))
        enter = by_seq(rest[seqs:])
        u = jnp.broadcast_to(par[l, 0:1], (GROUP, bw))
        alpha = jnp.broadcast_to(scal[i, 0:1], (GROUP, bw))
        per_count = scal[i, 1:2]
        gain_part, shift_part = sum_gain * per_count, sum_shift * per_count
        sum_rate = jnp.zeros((GROUP, bw), F32)
        rows = [None] * groups
        for h in (1, 0):
            v = cex[m, h] + aexr[m, h] * enter
            for t in range(steps - 1, -1, -1):
                g = h * steps + t
                keep = keepf[m, g]
                ds = own[m, g] + v
                before = carry_in[i, h] if t == 0 else states[i, g - 1]
                sum_rate = sum_rate + (ds * keep) * before
                v = (u * keep) * ds
                rows[g] = alpha * (ds - validf[m, g] * (shift_part + xbuf[i, g] * gain_part))
        @pl.when(b >= 8)
        def _():
            wait_bytes(dpbuf.at[b % 8, 0], dp_ss.at[b % 8])

        dpbuf[b % 8, 0] = jnp.concatenate(rows, axis=0).astype(BF16)
        remote(dpbuf.at[b % 8, 0], dpbuf.at[b % 8, 1], dp_ss.at[b % 8], dp_rs.at[b % 8], to_y).start()
        add_small(l, m, 2, sum_rate)
        small[l] = small[l] + pack([sum_gain[0:1], sum_shift[0:1]])

    nt = (((1,), (1,)), ((), ()))
    tn = (((0,), (0,)), ((), ()))

    def input_back(b):
        l, m, i = back_index(b)
        wait_bytes(dpbuf.at[b % 8, 1], dp_rs.at[b % 8])
        dp_own, dp_other = dpbuf[b % 8, 0], dpbuf[b % 8, 1]

        def toward(j):
            rows = pl.ds(pl.multiple_of(j * bw, bw), bw)
            first = lax.dot_general(dp_own, wbuf[l, 0, rows], nt, preferred_element_type=F32)
            return first + lax.dot_general(dp_other, wbuf[l, 1, rows], nt, preferred_element_type=F32)

        @pl.when(b >= 4)
        def _():
            wait_bytes(sibsend.at[m], sb_ss.at[m])

        sibsend[m, 0] = toward(j_c).astype(BF16)
        sibsend[m, 1] = toward(j_xc).astype(BF16)
        remote(sibsend.at[m], sibrecv.at[b % 8], sb_ss.at[m], sb_rs.at[b % 8], to_c).start()
        pkeep[m, 0] = toward(j_own)
        pkeep[m, 1] = toward(j_x)

    def weight_back(b):
        l, m, i = back_index(b)
        dp = jnp.concatenate([dpbuf[b % 8, 0], dpbuf[b % 8, 1]], axis=1)
        count = nz // 4
        for j in range(4):
            rows = pl.ds(j * bw, bw)
            new = lax.dot_general(mainbuf[i, j].reshape(sz.rows, bw), dp, tn, preferred_element_type=F32)

            @pl.when(m == 0)
            def _(new=new, rows=rows):
                gw[rows] = new

            @pl.when(jnp.logical_and(m > 0, m < 3))
            def _(new=new, rows=rows):
                gw[rows] = gw[rows] + new

            @pl.when(m == 3)
            def _(new=new, rows=rows, j=j):
                all_items = (gw[rows] + new).astype(BF16)
                for n in range(2):
                    value = all_items[:, n * bw : (n + 1) * bw].reshape(count, part, bw)
                    gall[l, j * count : (j + 1) * count, n] = value

    period = 2 * nz
    to_end, to_start = (s, r + 2), (s, r - 2)

    def g_from(p, n, up):
        return gpart.at[p + 1 if up else p, n], gr_rs.at[p + 1 if up else p, n]

    def g_ready(l, p, n, cross):
        if not cross:
            return
        unit, place_out = gall.at[l, p, n], gout.at[c, s, p, n]
        by_relay = jnp.logical_and(l == s_d, n == 1)

        @pl.when(jnp.logical_and(l != s, jnp.logical_not(by_relay)))
        def _():
            remote(unit, place_out, gx_ss.at[l, p, n], gx_rs.at[s, p, n], (l, r)).start()

        @pl.when(by_relay)
        def _():
            remote(unit, grelay.at[p], gx_ss.at[l, p, n], gl_rs.at[p], to_y).start()

        @pl.when(l == s)
        def _():
            local_copy(unit, place_out, gx_rs.at[s, p, n])
            remote(unit, place_out, gs_ss.at[s, p, n], gs_rs.at[s, p, n], to_c).start()

    def g_step(g, cross):
        for up in (True, False):
            place_z = z if up else nz - 1 - z
            ahead = nz - 1 - place_z
            t = g - 2 * place_z
            q = t // period
            k = t % period
            l = SECTIONS - 1 - q
            n = k % 2
            inside = jnp.logical_and(t >= 0, q < SECTIONS)

            @pl.when(jnp.logical_and(inside, k < 2 * ahead))
            def _(up=up, place_z=place_z, q=q, k=k, l=l, n=n):
                far = nz - 1 - k // 2
                p = far if up else nz - 1 - far
                unit = gall.at[l, p, n]

                buf, sem = g_from(p, n, up)
                way, slot = 0 if up else 1, k % 4
                leaving = gleave.at[way, slot]

                @pl.when(jnp.logical_or(q > 0, k >= 4))
                def _():
                    wait_bytes(leaving, ga_ss.at[way, slot])

                @pl.when(place_z > 0)
                def _():
                    wait_bytes(buf, sem)
                    leaving[...] = (unit[...].astype(F32) + buf[...].astype(F32)).astype(BF16)

                @pl.when(place_z == 0)
                def _():
                    leaving[...] = unit[...]

                remote(leaving, buf, ga_ss.at[way, slot], sem, to_end if up else to_start).start()

            @pl.when(jnp.logical_and(inside, k >= 2 * ahead))
            def _(up=up, place_z=place_z, ahead=ahead, k=k, l=l, n=n):
                back = (k - 2 * ahead) // 2
                p = z - back if up else z + back
                unit = gall.at[l, p, n]

                @pl.when(back == 0)
                def _():
                    if up:
                        whole = unit[...].astype(F32)
                        for way, there in ((True, z > 0), (False, z < nz - 1)):
                            buf, sem = g_from(p, n, way)

                            @pl.when(there)
                            def _(buf=buf, sem=sem):
                                wait_bytes(buf, sem)

                            whole = whole + jnp.where(there, buf[...].astype(F32), 0.0)
                        unit[...] = whole.astype(BF16)
                        g_ready(l, p, n, cross)

                @pl.when(back > 0)
                def _():
                    wait_bytes(unit, ga_rs.at[l, p, n])
                    g_ready(l, p, n, cross)

                @pl.when(ahead > 0)
                def _():
                    way = 0 if up else 1
                    remote(unit, unit, go_ss.at[l, p, n, way], ga_rs.at[l, p, n], to_end if up else to_start).start()

    def cross_back(b):
        m = b % 4
        wait_bytes(sibrecv.at[b % 8], sb_rs.at[b % 8])

        @pl.when(b < 4)
        def _():
            wait_bytes(ysend.at[m], y_ss.at[m])

        @pl.when(b >= 4)
        def _():
            wait_bytes(ysend.at[m], xp_ss.at[m])

        ysend[m] = (pkeep[m, 1] + sibrecv[b % 8, 1].astype(F32)).astype(BF16)
        remote(ysend.at[m], xrecv.at[b % 8], xp_ss.at[m], xp_rs.at[b % 8], to_x).start()
        pkeep[m, 0] = pkeep[m, 0] + sibrecv[b % 8, 0].astype(F32)

    def join_back(b):
        l, m, i = back_index(b)
        wait_bytes(xrecv.at[b % 8], xp_rs.at[b % 8])
        even = (1 - l % 2).astype(F32)
        side = dbuf[jnp.maximum(b - 4, 0)].astype(F32).reshape(sz.rows, bw)
        value = pkeep[m, 0] + xrecv[b % 8].astype(F32) + even * side
        dbuf[b + 4] = value.astype(BF16).reshape(2, sz.half, bw)

        @pl.when(l == 0)
        def _():
            for h in range(2):
                src = dbuf.at[b + 4, h]

                @pl.when(not_me(SECTIONS - 1 - m, h))
                def _(src=src, h=h):
                    remote(src, ging.at[me], gi_ss.at[m, h], gi_rs.at[me], (SECTIONS - 1 - m, 2 * z + h)).start()

                @pl.when(jnp.logical_not(not_me(SECTIONS - 1 - m, h)))
                def _(src=src):
                    local_copy(src, ging.at[me], gi_rs.at[me])

    first_step = 6

    def forward_tick(k):
        @pl.when(k < items)
        def _():
            project(k)

        @pl.when(k == 1)
        def _():
            inputs_on(3)

        @pl.when(jnp.logical_and(k >= 2, k < items + 2))
        def _():
            finish_layer(k - 2)
            carry_slopes(k - 2)

        @pl.when(jnp.logical_and(k >= 1, k < items + 1))
        def _():
            moments(k - 1)

        @pl.when(jnp.logical_and(k + 1 >= 4, k + 1 < items))
        def _():
            arrived(k + 1)

        @pl.when(k < 12)
        def _():
            for n in range(4):
                @pl.when(k % 4 == n)
                def _(n=n):
                    w_pass(k // 4 + 1, n // 2, n % 2)

            @pl.when(k % 4 == 1)
            def _():
                send_decays(k // 4 + 1)

    def backward_tick(k):
        @pl.when(k >= 4)
        def _():
            join_back(k - 4)

        @pl.when(jnp.logical_and(k >= 0, k < items))
        def _():
            act_back(k)

        @pl.when(k >= first_step)
        def _():
            g_step(k - first_step, False)

        @pl.when(jnp.logical_and(k >= 1, k < items + 1))
        def _():
            state_back(k - 1)

        @pl.when(jnp.logical_and(k >= 2, k < items + 2))
        def _():
            input_back(k - 2)
            weight_back(k - 2)
            cross_back(k - 2)

    start = items - 2

    def tick(k, _):
        forward_tick(k)
        backward_tick(k - start)
        return 0

    lax.fori_loop(0, start + items + 4, tick, 0)

    send_z(small, lambda k: small_recv.at[k], st_ss, st_rs)
    steps_done = items + 4 - first_step
    steps_all = SECTIONS * period + 2 * (nz - 1)

    def whole_at(q, p, n):
        return q * period + 2 * (nz - 1) + 2 * jnp.abs(z - p) + n

    def crosses_at(q, p, n):
        early = whole_at(q, p, n) < steps_done
        return jnp.where(early, steps_done + 2 * p + n, whole_at(q, p, n))

    def cross_early(g):
        p, n = (g - steps_done) // 2, (g - steps_done) % 2

        @pl.when(p < nz)
        def _():
            for q in range(SECTIONS):
                @pl.when(whole_at(q, p, n) < steps_done)
                def _(q=q):
                    g_ready(SECTIONS - 1 - q, p, n, True)

    def relay_lag(q):
        return jnp.where(q < 2, 12, 4)

    def g_relay(g):
        q = SECTIONS - 1 - s_x

        def one(p, _):
            @pl.when(crosses_at(q, p, 1) + relay_lag(q) == g)
            def _():
                wait_bytes(grelay.at[p], gl_rs.at[p])
                remote(grelay.at[p], gout.at[c, s_y, p, 1], gl_ss.at[p], gx_rs.at[s_y, p, 1], to_x).start()

            return 0

        lax.fori_loop(0, nz, one, 0)

    def g_to_other_core(g):
        q = SECTIONS - 1 - s
        lag = jnp.where(q < 2, 14, 6)

        def one(p, _):
            for n in range(2):
                sent = crosses_at(q, p, n) + lag

                def onward(t, n=n):
                    unit = gout.at[c, t, p, n]
                    wait_bytes(unit, gx_rs.at[t, p, n])
                    remote(unit, unit, gs_ss.at[t, p, n], gs_rs.at[t, p, n], to_c).start()

                @pl.when(sent == g)
                def _(n=n):
                    onward(s_x)
                    onward(s_y)
                    if n == 0:
                        onward(s_d)

                if n == 1:
                    @pl.when(sent + relay_lag(q) == g)
                    def _():
                        onward(s_d)
            return 0

        lax.fori_loop(0, nz, one, 0)

    def late_step(g, _):
        g_step(g, True)
        cross_early(g)
        g_relay(g)
        g_to_other_core(g)
        return 0

    def late_steps(first, last_step):
        lax.fori_loop(first, last_step, late_step, 0)

    late_steps(steps_done, steps_done + 3)
    wait_bytes(small_recv, st_rs)
    wait_bytes(small_recv, st_ss)

    def add_rest(k, _):
        for l in range(SECTIONS):
            small[l] = small[l] + jnp.where(sub >= 2, small_recv[k, l], 0.0)
        return 0

    lax.fori_loop(0, nz - 1, add_rest, 0)
    for t in range(SECTIONS):
        for h in range(2):
            @pl.when(not_me(t, h))
            def _(t=t, h=h):
                remote(small.at[t], smallg.at[me], sm_ss.at[t, h], sm_rs.at[me], (t, 2 * z + h)).start()

            @pl.when(jnp.logical_not(not_me(t, h)))
            def _(t=t):
                local_copy(small.at[t], smallg.at[me], sm_rs.at[me])

    late_steps(steps_done + 3, steps_done + 9)

    restore = (row_of == frame_at).astype(BF16)
    for e in range(8):
        wait_bytes(outg.at[e], o_rs.at[e])
        wait_bytes(ging.at[e], gi_rs.at[e])
        wait_bytes(smallg.at[e], sm_rs.at[e])
        for src, dst in ((outg, out), (ging, grad_inp)):
            value = jnp.dot(restore, src[e], preferred_element_type=F32).astype(BF16)
            value = value.reshape(seqs, sz.frames, bw)
            dst[0, :, :, e * bw : e * bw + width(e)] = value[:, :, : width(e)]
        for n, dst in enumerate((grad_gain, grad_shift, grad_rec, grad_bias)):
            dst[0:1, e * bw : e * bw + width(e)] = smallg[e, n : n + 1, : width(e)]

    late_steps(steps_done + 9, steps_all + 10)

    def drain_units(k, _):
        p, n = k // 2, k % 2
        unit = gall.at[0, p, n]
        for t in range(SECTIONS):
            wait_bytes(unit, gs_rs.at[t, p, n])
            wait_bytes(unit, gs_ss.at[t, p, n])

            @pl.when(t != s)
            def _(t=t):
                wait_bytes(unit, gx_ss.at[t, p, n])

            @pl.when(t == s)
            def _(t=t):
                wait_bytes(unit, gx_rs.at[t, p, n])

            @pl.when(jnp.logical_and(p <= z, z < nz - 1))
            def _(t=t):
                wait_bytes(unit, go_ss.at[t, p, n, 0])

            @pl.when(jnp.logical_and(p >= z, z > 0))
            def _(t=t):
                wait_bytes(unit, go_ss.at[t, p, n, 1])

        return 0

    lax.fori_loop(0, period, drain_units, 0)

    def drain_relay(p, _):
        wait_bytes(grelay.at[p], gl_ss.at[p])
        return 0

    lax.fori_loop(0, nz, drain_relay, 0)
    for way in range(2):
        ahead = nz - 1 - z if way == 0 else z
        for slot in range(4):
            @pl.when(slot < 2 * ahead)
            def _(way=way, slot=slot):
                wait_bytes(gleave.at[way, slot], ga_ss.at[way, slot])

    for l in range(SECTIONS):
        @pl.when(l != s)
        def _(l=l):
            for k in range(2):
                for n in range(2):
                    wait_bytes(w_unit(l, k, n), w_fs.at[l, k, n])

        wait_bytes(pre_recv.at[pl.ds(0, nz - 1), pl.ds(4 * l, 4)], pre_ss.at[l])
        wait_bytes(ex_recv.at[l, pl.ds(0, nz - 1)], ex_ss.at[l])
        wait_bytes(e1_recv.at[l, pl.ds(0, nz - 1)], e1_ss.at[l])
        wait_bytes(sibsend.at[l], sb_ss.at[l])
        wait_bytes(ysend.at[l], xp_ss.at[l])
        for h in range(2):
            @pl.when(not_me(l, h))
            def _(l=l, h=h):
                wait_bytes(dbuf.at[mine, c], cot_ss.at[l, h])
                wait_bytes(small.at[l], sm_ss.at[l, h])

            @pl.when(not_me(SECTIONS - 1 - l, h))
            def _(l=l, h=h):
                wait_bytes(outbuf.at[l, h], o_ss.at[l, h])
                wait_bytes(dbuf.at[items + l, h], gi_ss.at[l, h])

    def drain(i, _):
        @pl.when(i < 8)
        def _():
            wait_bytes(dpbuf.at[i, 0], dp_ss.at[i])

        @pl.when(i >= 4)
        def _():
            wait_bytes(mainbuf.at[i, j_own], mx_ss.at[i])
            wait_bytes(mainbuf.at[i, j_own], ms_ss.at[i])
            wait_bytes(mainbuf.at[i, j_x], mf_ss.at[i])

        return 0

    lax.fori_loop(0, items, drain, 0)
    for n in range(4):
        wait_bytes(in_dst, in_ss.at[n])
    for slot in range(4):
        @pl.when(slot != mine)
        def _(slot=slot):
            wait_bytes(in_dst, in_fs.at[slot])

    for n in range(3):
        wait_bytes(par.at[s], par_ss.at[n])
        for k in range(2):
            wait_bytes(wx.at[n, :, pl.ds(k * bw, bw)], w_ss.at[n, k])
    wait_bytes(flagbuf.at[c], flag_ss.at[0])


def run_kernel(sz, *args):
    nz, bw, items, groups = sz.nz, sz.bw, sz.items, sz.groups
    half, rows, part = sz.half, sz.rows, sz.part
    dma = pltpu.SemaphoreType.DMA
    vm = pltpu.VMEM
    step = (GROUP, bw)
    scratch = [
        vm((items, 4, 2, half, bw), BF16),
        vm((SECTIONS, 2, 4 * bw, bw), BF16),
        vm((4, rows, bw), BF16),
        vm((8, rows, bw), BF16),
        vm((4, groups) + step, F32),
        vm((items, groups) + step, F32),
        vm((items, groups) + step, F32),
        vm((items, 2) + step, F32),
        vm((items, 2) + step, F32),
        vm((items, 2) + step, F32),
        vm((items, 2) + step, F32),
        vm((4, groups) + step, F32),
        vm((4, groups) + step, F32),
        vm((2, 8 * sz.seqs, 128), F32),
        vm((SECTIONS,) + step, F32),
        vm((8,) + step, F32),
        vm((items,) + step, F32),
        vm((nz, items) + step, F32),
        vm((4,) + step, F32),
        vm((8, nz) + step, F32),
        vm((4,) + step, F32),
        vm((8, nz) + step, F32),
        vm((items,) + step, F32),
        vm((items,) + step, F32),
        vm((4, 2) + step, F32),
        vm((items + 4, 2, half, bw), BF16),
        vm((4, 2) + step, F32),
        vm((4, 2) + step, F32),
        vm((8, 2, rows, bw), BF16),
        vm((4, 2, rows, bw), F32),
        vm((4, 2, rows, bw), BF16),
        vm((8, 2, rows, bw), BF16),
        vm((8, rows, bw), BF16),
        vm((4 * bw, 2 * bw), F32),
        vm((SECTIONS, nz, 2, part, bw), BF16),
        vm((nz + 1, 2, part, bw), BF16),
        vm((2, 4, part, bw), BF16),
        vm((nz, part, bw), BF16),
        vm((SECTIONS,) + step, F32),
        vm((nz - 1, SECTIONS) + step, F32),
        vm((4, 2, half, bw), BF16),
        vm((2, sz.seqs, sz.frames, sz.hidden), BF16),
        vm((2, 8, half, bw), BF16),
        vm((2, bw, sz.hidden), BF16),
        vm((3, 2, 2 * bw, bw), BF16),
        vm((8, half, bw), BF16),
        vm((8, half, bw), BF16),
        vm((8,) + step, F32),
        vm(step, F32),
    ]
    sems = [
        dma((2,)), dma((2,)), dma((4,)), dma((4,)), dma((4, 2)), dma((4, 2)), dma((4, 2)),
        dma((3,)), dma((4,)), dma((1,)), dma((2,)),
        dma((3, 2)), dma((4, 4)), dma((4, 2, 2)), dma((4, 2, 2)),
        dma((4,)), dma((4,)),
        dma((items,)), dma((items,)), dma((items,)), dma((items,)), dma((items,)), dma((items,)),
        dma((4,)), dma((8,)), dma((4,)), dma((8,)),
        dma((4, 2)), dma((8,)), dma((4,)), dma((8,)),
        dma((8,)), dma((8,)), dma((4,)), dma((8,)), dma((4,)), dma((8,)),
        dma((4, 2)), dma((8,)),
        dma((2, 4)), dma((4, nz, 2)), dma((4, nz, 2, 2)), dma((nz + 1, 2)),
        dma((4, nz, 2)), dma((4, nz, 2)), dma((nz,)), dma((nz,)), dma((4, nz, 2)), dma((4, nz, 2)),
        dma, dma, dma((4, 2)), dma((8,)),
    ]
    anywhere = pl.BlockSpec(memory_space=pl.ANY)
    inside = pl.BlockSpec(memory_space=pltpu.VMEM)
    frames = jax.ShapeDtypeStruct((1, sz.seqs, sz.frames, sz.hidden), BF16)
    vector = jax.ShapeDtypeStruct((1, sz.hidden), F32)
    return pl.pallas_call(
        functools.partial(kernel, sz),
        out_shape=(frames, frames) + (vector,) * 4 + (jax.ShapeDtypeStruct((2, SECTIONS, nz, 2, part, bw), BF16),),
        in_specs=[anywhere] * 3 + [inside] * 6,
        out_specs=(inside,) * 6 + (anywhere,),
        scratch_shapes=scratch + sems,
        compiler_params=pltpu.CompilerParams(
            collective_id=0, has_side_effects=True, vmem_limit_bytes=63 * 2**20
        ),
    )(*args)


def place_weights(sz, pieces, *others):
    bw, part, hidden = sz.bw, sz.part, sz.hidden
    count = bw // part

    def body(*refs):
        src, dst = refs[0], refs[1 + len(others)]
        upper = pl.program_id(0) // 4

        @pl.when(pl.program_id(0) == 0)
        def _():
            for n in range(len(others)):
                refs[2 + len(others) + n][...] = refs[1 + n][...]

        for yy in range(2):
            @pl.when(upper == yy)
            def _(yy=yy):
                for p in range(count):
                    for e in range(8):
                        n, x, c = (0 if e // 4 == yy else 1), e % 4 // 2, e % 2
                        wide = bw if e < 7 else sz.last
                        value = src[c, x, p, n, :, :wide].astype(F32)
                        dst[p * part : (p + 1) * part, e * bw : e * bw + wide] = value

    whole = [pl.BlockSpec(v.shape, lambda q, rank=v.ndim: (0,) * rank) for v in others]
    return pl.pallas_call(
        body,
        grid=(8,),
        out_shape=[jax.ShapeDtypeStruct((hidden, hidden), F32)] + [jax.ShapeDtypeStruct(v.shape, v.dtype) for v in others],
        in_specs=[pl.BlockSpec((2, 2, count, 2, part, bw), lambda q: (0, q // 4, q % 4, 0, 0, 0))] + whole,
        out_specs=[pl.BlockSpec((bw, hidden), lambda q: (q, 0))] + whole,
        compiler_params=pltpu.CompilerParams(vmem_limit_bytes=60 * 2**20),
    )(pieces, *others)


def local(sz, inputs, resets, valid_mask, weights, recurrence, state_bias, norm_gain, norm_shift, cotangent):
    *others, pieces = run_kernel(
        sz, inputs, cotangent, weights, resets, valid_mask, recurrence, state_bias, norm_gain, norm_shift
    )
    grad_weights, outputs, grad_inputs, *vectors = place_weights(sz, pieces, *others)
    return outputs, grad_inputs, grad_weights[None], *vectors


def solution(mesh):
    def step(inputs, *rest):
        sz = Sizes(mesh.shape["rows"] // 2, inputs.shape[1], inputs.shape[2], inputs.shape[3])
        return local(sz, inputs, *rest)

    frames = P("section", None, "rows", None)
    flags = P(None, None, "rows")
    vectors = P("section", None)
    matrix = P("section", None, None)
    return jax.shard_map(
        step,
        mesh=mesh,
        in_specs=(frames, flags, flags, matrix, vectors, vectors, vectors, vectors, frames),
        out_specs=(frames, frames, matrix, vectors, vectors, vectors, vectors),
        check_vma=False,
    )
```

```python
import functools

import jax
import jax.numpy as jnp
from jax import lax
from jax.experimental import pallas as pl
from jax.experimental.pallas import tpu as pltpu
from jax.sharding import PartitionSpec as P

MESH = pl.DeviceIdType.MESH
norm_eps = 1e-05
F32, BF16 = jnp.float32, jnp.bfloat16
SECTIONS = 4
GROUP = 8


class Sizes:
    def __init__(self, nz, seqs, frames, hidden):
        self.nz, self.seqs, self.frames = nz, seqs, frames
        self.pieces = GROUP // seqs
        self.steps = frames // self.pieces
        self.half = seqs * frames
        self.rows = 2 * self.half
        self.groups = self.rows // GROUP
        self.bw = -(-hidden // 1024) * 128
        self.padded = 8 * self.bw
        self.part = 4 * self.bw // nz
        self.items = 4 * SECTIONS
        self.hidden = hidden
        self.last = hidden - 7 * self.bw


def wait_bytes(ref, sem):
    pltpu.make_async_copy(ref, ref, sem).wait()


def local_copy(src, dst, sem):
    pltpu.make_async_copy(src, dst, sem).start()


def remote(src, dst, send, recv, device):
    return pltpu.make_async_remote_copy(
        src_ref=src, dst_ref=dst, send_sem=send, recv_sem=recv, device_id=device, device_id_type=MESH
    )


def kernel(
    sz, inp_raw, cot_raw, w_raw, resets, valid_mask, recurrence, state_bias, norm_gain, norm_shift,
    out, grad_inp, grad_rec, grad_bias, grad_gain, grad_shift, gout,
    mainbuf, wbuf, ysend, yrecv, own, xbuf, states, carry_in, chunk_a, chunk_aex, chunk_s0,
    keepf, validf, flagbuf, par, parblk, pre_send, pre_recv, ex_send, ex_recv, e1_send, e1_recv,
    scal, slopes, s1ex, dbuf, cex, aexr, dpbuf, pkeep, sibsend, sibrecv, xrecv, gw, gall, gpart, gleave, grelay,
    small, small_recv, outbuf, raw, blocks, wst, wx, outg, ging, smallg, blank,
    raw_ls, wst_ls, in_ss, in_fs, in_rs, cot_ss, cot_rs, par_ss, par_rs, flag_ss, flag_rs, w_ss, w_rs, w_fs, w_ps,
    pre_ss, pre_rs, mx_ss, mx_rs, ms_ss, ms_rs, mf_ss, mf_rs, y_ss, y_rs, ex_ss, ex_rs,
    o_ss, o_rs, e1_ss, e1_rs, dp_ss, dp_rs, sb_ss, sb_rs, xp_ss, xp_rs,
    gi_ss, gi_rs, ga_ss, ga_rs, go_ss, gr_rs, gx_ss, gx_rs, gl_ss, gl_rs, gs_ss, gs_rs, st_ss, st_rs, sm_ss, sm_rs,
):
    nz, bw, items, groups, steps = sz.nz, sz.bw, sz.items, sz.groups, sz.steps
    pieces, seqs = sz.pieces, sz.seqs
    s, r = lax.axis_index("section"), lax.axis_index("rows")
    y, x, z, c = s // 2, s % 2, r // 2, r % 2
    s_x, s_y, s_d = s + 1 - 2 * x, s + 2 - 4 * y, 3 - s
    r_c = r + 1 - 2 * c
    to_x, to_y, to_d, to_c = (s_x, r), (s_y, r), (s_d, r), (s, r_c)
    j_own, j_x, j_c, j_xc = 2 * x + c, 2 * (1 - x) + c, 2 * x + 1 - c, 2 * (1 - x) + 1 - c
    me = 2 * s + c
    part, half, last = sz.part, sz.half, sz.last
    mine = SECTIONS - 1 - s
    pair_half = z % 2
    to_pair = (s, r + 2 - 4 * pair_half)
    sub = lax.broadcasted_iota(jnp.int32, (GROUP, bw), 0)
    place = sub % pieces

    def z_peer(distance):
        return (s, 2 * ((z + distance) % nz) + c)

    def z_slot(p):
        return (z - p + nz - 1) % nz

    def by_seq(rows):
        value = jnp.broadcast_to(rows[seqs - 1], (GROUP, bw))
        for q in range(seqs - 2, -1, -1):
            value = jnp.where(sub < (q + 1) * pieces, jnp.broadcast_to(rows[q], (GROUP, bw)), value)
        return value

    def last_of(value, q):
        return value[(q + 1) * pieces - 1 : (q + 1) * pieces]

    def first_of(value, q):
        return value[q * pieces : q * pieces + 1]

    def entering(a, b, reverse):
        out_a, out_b = [None, None], [None, None]
        t_a = t_b = None
        for h in (1, 0) if reverse else (0, 1):
            ia, ib = a[h], b[h]
            hop = 1
            while hop < pieces:
                if reverse:
                    ok, shift = place < pieces - hop, GROUP - hop
                else:
                    ok, shift = place >= hop, hop
                pa = jnp.where(ok, pltpu.roll(ia, shift, 0), 1.0)
                pb = jnp.where(ok, pltpu.roll(ib, shift, 0), 0.0)
                ib = ia * pb + ib
                ia = ia * pa
                hop *= 2
            if reverse:
                ok, shift, edge = place < pieces - 1, GROUP - 1, first_of
            else:
                ok, shift, edge = place >= 1, 1, last_of
            xa = jnp.where(ok, pltpu.roll(ia, shift, 0), 1.0)
            xb = jnp.where(ok, pltpu.roll(ib, shift, 0), 0.0)
            na = [edge(ia, q) for q in range(seqs)]
            nb = [edge(ib, q) for q in range(seqs)]
            if t_a is not None:
                ea, eb = by_seq(t_a), by_seq(t_b)
                xb = xa * eb + xb
                xa = xa * ea
                nb = [na[q] * t_b[q] + nb[q] for q in range(seqs)]
                na = [na[q] * t_a[q] for q in range(seqs)]
            t_a, t_b = na, nb
            out_a[h], out_b[h] = xa, xb
        return out_a, out_b, t_a, t_b

    def pack(rows):
        rows = rows + [jnp.zeros((1, bw), F32)] * (8 - len(rows))
        value = jnp.zeros((8, bw), F32)
        for q, row in enumerate(rows):
            value = jnp.where(sub == q, jnp.broadcast_to(row, (8, bw)), value)
        return value

    def total(value):
        return jnp.sum(value, axis=0, keepdims=True)

    def over_z(body, start):
        return lax.fori_loop(0, nz, body, start, unroll=nz <= 8)

    def send_z(src, dst_of, send_sem, recv_sem):
        def one(k, _):
            remote(src, dst_of(k - 1), send_sem, recv_sem, z_peer(k)).start()
            return 0

        lax.fori_loop(1, nz, one, 0, unroll=nz <= 8)

    def not_me(t, h):
        return jnp.logical_or(t != s, h != c)

    blank[...] = jnp.zeros((GROUP, bw), F32)

    def width(e):
        return bw if e < 7 else last

    barrier = pltpu.get_barrier_semaphore()
    for t in (s, s_x, s_y, s_d):
        for q in (r, r_c):
            if not (t is s and q is r):
                pl.semaphore_signal(barrier, inc=1, device_id=(t, q), device_id_type=MESH)

    def greet(k, _):
        pl.semaphore_signal(barrier, inc=1, device_id=z_peer(k), device_id_type=MESH)
        return 0

    lax.fori_loop(1, nz, greet, 0)

    local_copy(inp_raw.at[0], raw.at[0], raw_ls.at[0])
    local_copy(cot_raw.at[0], raw.at[1], raw_ls.at[1])
    w_rows = [(1 - y, 2 * pair_half), (1 - y, 2 * pair_half + 1), (y, 2 * pair_half), (y, 2 * pair_half + 1)]
    w_rows += [(y, 2 - 2 * pair_half), (y, 3 - 2 * pair_half)]

    def w_load(n, wait):
        yy, j = w_rows[n]
        k, slot = 4 * yy + j, n % 3

        def go(rows):
            copy = pltpu.make_async_copy(
                w_raw.at[0, pl.ds(pl.multiple_of(k * bw, bw), rows)], wst.at[slot, pl.ds(0, rows)], wst_ls.at[slot]
            )
            copy.wait() if wait else copy.start()

        @pl.when(k < 7)
        def _():
            go(bw)

        @pl.when(k == 7)
        def _():
            if not wait:
                wst[slot, last:] = jnp.zeros((bw - last, sz.hidden), BF16)
            go(last)

    def w_cut(n, column, toward, dst):
        slot = n % 3
        for e in range(8):
            @pl.when(column == e % 4)
            def _(e=e):
                place_of = jnp.where(toward == e // 4, 0, 1)
                if e == 7:
                    dst[place_of] = jnp.zeros((bw, bw), BF16)
                dst[place_of, :, : width(e)] = wst[slot, :, e * bw : e * bw + width(e)]

    for n in range(3):
        w_load(n, False)

    parblk[...] = jnp.zeros(parblk.shape, F32)
    for n, ref in enumerate((recurrence, state_bias, norm_gain, norm_shift)):
        for e in range(8):
            parblk[e, n : n + 1, : width(e)] = ref[0:1, e * bw : e * bw + width(e)]
    par[s] = parblk[me]
    flagbuf[c] = jnp.zeros(flagbuf.shape[1:], F32)
    for n, ref in enumerate((resets, valid_mask)):
        for m in range(4):
            row = seqs * (4 * n + m)
            flagbuf[c, row : row + seqs, : sz.frames] = ref[SECTIONS - 1 - m].astype(F32)

    def w_unit(l, j, n):
        return wbuf.at[l, n, pl.ds(pl.multiple_of(j * bw, bw), bw)]

    def w_cross():
        for k in range(2):
            j = 2 * pair_half + k
            for m, t in enumerate((s_x, s_y, s_d)):
                for n in range(2):
                    src = wx.at[m, n, pl.ds(k * bw, bw)]
                    remote(src, w_unit(s, j, n), w_ss.at[m, k, n], w_rs.at[s, j, n], (t, r)).start()

    for n in range(6):
        if n == 4:
            pl.semaphore_wait(barrier, 7 + nz - 1)

            @pl.when(s == 0)
            def _():
                w_cross()

        w_load(n, True)
        j = w_rows[n][1]
        rows = pl.ds(pl.multiple_of(j * bw, bw), bw)
        half_rows = pl.ds((n % 2) * bw, bw)
        if n < 2:
            w_cut(n, j_own, 1 - y, wx.at[1, :, half_rows])
            w_cut(n, j_x, 1 - y, wx.at[2, :, half_rows])
        elif n < 4:
            w_cut(n, j_x, y, wx.at[0, :, half_rows])
            w_cut(n, j_own, y, wbuf.at[s, :, rows])
        else:
            w_cut(n, j_own, y, wbuf.at[s, :, rows])
        if n + 3 < 6:
            w_load(n + 3, False)

    row = lax.broadcasted_iota(jnp.int32, (half, half), 0)
    col = lax.broadcasted_iota(jnp.int32, (half, half), 1)
    frame_of = (row % GROUP // pieces) * sz.frames + (row % pieces) * steps + row // GROUP
    permute = (col == frame_of).astype(BF16)
    row_of = row
    frame_at = (col % GROUP // pieces) * sz.frames + (col % pieces) * steps + col // GROUP

    def cut_frames(n):
        wait_bytes(raw.at[n], raw_ls.at[n])
        for e in range(8):
            value = raw[n, :, :, e * bw : e * bw + width(e)].reshape(half, width(e))
            if e == 7:
                blocks[n, e] = jnp.zeros((half, bw), BF16)
            blocks[n, e, :, : width(e)] = jnp.dot(permute, value, preferred_element_type=F32).astype(BF16)

    cut_frames(0)

    for n, t in enumerate((s_x, s_y, s_d)):
        remote(parblk.at[2 * t + c], par.at[s], par_ss.at[n], par_rs.at[s], (t, r)).start()
    remote(flagbuf.at[c], flagbuf.at[c], flag_ss.at[0], flag_rs.at[c], to_c).start()

    in_dst = mainbuf.at[mine, :, c]
    near, far = blocks.at[0, pl.ds(4 * y, 4)], blocks.at[0, pl.ds(4 - 4 * y, 4)]
    remote(far, in_dst, in_ss.at[2], in_rs.at[mine, c], to_d).start()
    remote(near, in_dst, in_ss.at[0], in_rs.at[mine, c], to_x).start()
    remote(far, in_dst, in_ss.at[1], in_rs.at[mine, c], to_y).start()
    remote(near, in_dst, in_ss.at[3], in_rs.at[mine, c], to_c).start()
    local_copy(near, in_dst, in_rs.at[mine, c])

    @pl.when(s != 0)
    def _():
        w_cross()

    wait_bytes(flagbuf.at[1 - c], flag_rs.at[1 - c])
    row = lax.broadcasted_iota(jnp.int32, (half, sz.frames), 0)
    col = lax.broadcasted_iota(jnp.int32, (half, sz.frames), 1)
    at_frame = col == (row % pieces) * steps + row // GROUP
    of_seq = row % GROUP // pieces
    ones = jnp.ones((sz.frames, bw), BF16)

    def masks_of(m, _):
        for h in range(2):
            lo, hi = h * steps, (h + 1) * steps
            for n in range(2):
                flags = jnp.zeros((half, sz.frames), F32)
                for q in range(seqs):
                    line = flagbuf[h, pl.ds(seqs * (4 * n + m) + q, 1), : sz.frames]
                    flags = jnp.where(jnp.logical_and(at_frame, of_seq == q), line, flags)
                value = jnp.dot(flags.astype(BF16), ones, preferred_element_type=F32).reshape(steps, GROUP, bw)
                if n == 0:
                    keepf[m, lo:hi] = 1.0 - value
                else:
                    validf[m, lo:hi] = value
        return 0

    lax.fori_loop(0, 4, masks_of, 0)
    for t in (s_x, s_y, s_d):
        wait_bytes(par.at[t], par_rs.at[t])

    def decays_of(i, _):
        l, m = i // 4, i % 4
        u = jnp.broadcast_to(par[l, 0:1], (GROUP, bw))
        a_h, v_h = [], []
        for h in range(2):
            a = jnp.ones((GROUP, bw), F32)
            v = jnp.zeros((GROUP, bw), F32)
            for t in range(steps):
                d = u * keepf[m, h * steps + t]
                a = d * a
                v = d * v + 1.0
            a_h.append(a)
            v_h.append(v)
        xa, xb, ta, tb = entering(a_h, v_h, False)
        for h in range(2):
            chunk_a[i, h] = a_h[h]
            chunk_aex[i, h] = xa[h]
            chunk_s0[i, h] = xb[h]
        valid_count = total(jnp.sum(validf[m], axis=0))
        value = pack(ta + tb + [valid_count])
        pre_send[i] = value
        pre_recv[nz - 1, i] = value
        return 0

    lax.fori_loop(0, items, decays_of, 0)

    def send_decays(l):
        some = pl.ds(4 * l, 4)
        send_z(pre_send.at[some], lambda k: pre_recv.at[k, some], pre_ss.at[l], pre_rs.at[l])

    send_decays(0)

    def inputs_on(slot):
        block = mainbuf.at[slot, :, c]

        @pl.when(slot != mine)
        def _():
            wait_bytes(block, in_rs.at[slot, c])
            remote(block, block, in_fs.at[slot], in_rs.at[slot, c], to_c).start()

        @pl.when(slot == mine)
        def _():
            wait_bytes(block, in_rs.at[slot, c])

    for slot in range(3):
        inputs_on(slot)

    def w_pass(l, k, n):
        j = 2 * pair_half + k

        @pl.when(l != s)
        def _():
            wait_bytes(w_unit(l, j, n), w_rs.at[l, j, n])
            remote(w_unit(l, j, n), w_unit(l, j, n), w_fs.at[l, k, n], w_ps.at[l, k, n], to_pair).start()

    def w_arrive(l):
        @pl.when(l != s)
        def _():
            for k in range(2):
                for n in range(2):
                    wait_bytes(w_unit(l, 2 - 2 * pair_half + k, n), w_ps.at[l, k, n])

    for n in range(2):
        w_pass(0, 0, n)

    for n in range(2):
        w_pass(0, 1, n)
    cut_frames(1)
    for t in range(SECTIONS):
        for h in range(2):
            src = blocks.at[1, 2 * t + h]

            @pl.when(not_me(t, h))
            def _(src=src, t=t, h=h):
                remote(src, dbuf.at[mine, c], cot_ss.at[t, h], cot_rs.at[mine, c], (t, 2 * z + h)).start()

            @pl.when(jnp.logical_not(not_me(t, h)))
            def _(src=src):
                local_copy(src, dbuf.at[mine, c], cot_rs.at[mine, c])

    def arrived(i):
        block = mainbuf.at[i, j_x]
        wait_bytes(block, mx_rs.at[i])
        remote(block, block, mf_ss.at[i], mf_rs.at[i], to_c).start()

    def project(i):
        l, m = i // 4, i % 4

        @pl.when(m == 0)
        def _():
            w_arrive(l)

        @pl.when(l == 0)
        def _():
            wait_bytes(mainbuf.at[i, :, 1 - c], in_rs.at[m, 1 - c])

        @pl.when(l > 0)
        def _():
            wait_bytes(mainbuf.at[i, j_c], ms_rs.at[i])
            wait_bytes(mainbuf.at[i, j_xc], mf_rs.at[i])
            wait_bytes(ysend.at[m], y_ss.at[m])

        def to_half(n):
            acc = jnp.zeros((sz.rows, bw), F32)
            for j in range(4):
                acc = acc + jnp.dot(
                    mainbuf[i, j].reshape(sz.rows, bw), wbuf[l, n, j * bw : (j + 1) * bw], preferred_element_type=F32
                )
            return acc

        ysend[m] = to_half(1).astype(BF16)
        remote(ysend.at[m], yrecv.at[i % 8], y_ss.at[m], y_rs.at[i % 8], to_y).start()
        own[m] = to_half(0).reshape(groups, GROUP, bw)

    def moments(i):
        l, m = i // 4, i % 4
        wait_bytes(yrecv.at[i % 8], y_rs.at[i % 8])
        pre = own[m] + yrecv[i % 8].astype(F32).reshape(groups, GROUP, bw)
        valid = validf[m]
        pre_sum = total(jnp.sum(pre * valid, axis=0))
        local_count = pre_send[i, 2 * seqs : 2 * seqs + 1]
        pivot = pre_sum / jnp.maximum(local_count, 1.0)
        shifted = pre - pivot
        xbuf[i] = shifted
        square = total(jnp.sum(shifted * shifted * valid, axis=0))
        u = jnp.broadcast_to(par[l, 0:1], (GROUP, bw))
        ends = []
        for h in range(2):
            v = jnp.zeros((GROUP, bw), F32)
            for t in range(steps):
                v = (u * keepf[m, h * steps + t]) * v + shifted[h * steps + t]
            ends.append(v)
        unused_a, xb, unused_t, tb = entering([chunk_a[i, 0], chunk_a[i, 1]], ends, False)
        for h in range(2):
            s1ex[m, h] = xb[h]
        value = pack([pre_sum, square] + tb)

        @pl.when(l > 0)
        def _():
            wait_bytes(ex_recv.at[i % 8, pl.ds(0, nz - 1)], ex_ss.at[m])

        ex_send[m] = value
        ex_recv[i % 8, nz - 1] = value
        send_z(ex_send.at[m], lambda k: ex_recv.at[i % 8, k], ex_ss.at[m], ex_rs.at[i % 8])

    def finish_layer(i):
        l, m = i // 4, i % 4

        @pl.when(m == 0)
        def _():
            wait_bytes(pre_recv.at[pl.ds(0, nz - 1), pl.ds(4 * l, 4)], pre_rs.at[l])

        wait_bytes(ex_recv.at[i % 8, pl.ds(0, nz - 1)], ex_rs.at[i % 8])
        u, bias = par[l, 0:1], par[l, 1:2]
        gain, shift = par[l, 2:3], par[l, 3:4]

        def add_sum(p, carry):
            slot = z_slot(p)
            return (
                carry[0] + ex_recv[i % 8, slot, 0:1],
                carry[1] + pre_recv[slot, i, 2 * seqs : 2 * seqs + 1],
            )

        zero = jnp.zeros((1, bw), F32)
        sum_all, count_all = over_z(add_sum, (zero, zero))
        mean = sum_all / count_all

        def pivot_of(slot):
            count = pre_recv[slot, i, 2 * seqs : 2 * seqs + 1]
            return ex_recv[i % 8, slot, 0:1] / jnp.maximum(count, 1.0), count

        def add_square(p, carry):
            slot = z_slot(p)
            pivot, count = pivot_of(slot)
            return carry + ex_recv[i % 8, slot, 1:2] + count * (pivot - mean) * (pivot - mean)

        var = over_z(add_square, zero) / count_all
        inv = lax.rsqrt(var + norm_eps)
        alpha = gain * inv

        def hop_in(p, carry):
            slot = z_slot(p)
            pivot, unused = pivot_of(slot)
            beta = shift + alpha * (pivot - mean)
            after = []
            for q in range(seqs):
                value = (
                    alpha * ex_recv[i % 8, slot, 2 + q : 3 + q]
                    + beta * pre_recv[slot, i, seqs + q : seqs + q + 1]
                    + pre_recv[slot, i, q : q + 1] * carry[q]
                )
                after.append(jnp.where(p < z, value, carry[q]))
            return tuple(after)

        enter = by_seq(list(over_z(hop_in, (zero,) * seqs)))
        pivot, unused = pivot_of(nz - 1)
        beta = shift + alpha * (pivot - mean)
        offset = (pivot - mean) * inv
        scal[i] = pack([alpha, 1.0 / count_all])
        wide = [jnp.broadcast_to(v, (GROUP, bw)) for v in (u, bias, alpha, beta, inv, offset)]
        u, bias, alpha, beta, inv, offset = wide
        side = mainbuf.at[jnp.maximum(i - 4, 0), j_own]
        odd = (l % 2).astype(F32)
        to_next = l < SECTIONS - 1
        target = jnp.minimum(i + 4, items - 1)
        for h in range(2):
            v = alpha * s1ex[m, h] + beta * chunk_s0[i, h] + chunk_aex[i, h] * enter
            carry_in[i, h] = v
            hidden = []
            for t in range(steps):
                g = h * steps + t
                shifted = xbuf[i, g]
                v = (u * keepf[m, g]) * v + (alpha * shifted + beta)
                states[i, g] = v
                xbuf[i, g] = shifted * inv + offset
                w = v + bias
                hidden.append(validf[m, g] * (w * jax.nn.sigmoid(w)))
            value = jnp.concatenate(hidden, axis=0) + odd * side[h].astype(F32)
            outbuf[m, h] = value.astype(BF16)

        @pl.when(to_next)
        def _():
            block = mainbuf.at[target, j_own]
            block[...] = outbuf[m]
            remote(block, block, mx_ss.at[target], mx_rs.at[target], to_x).start()
            remote(block, block, ms_ss.at[target], ms_rs.at[target], to_c).start()

        @pl.when(jnp.logical_not(to_next))
        def _():
            for h in range(2):
                @pl.when(not_me(SECTIONS - 1 - m, h))
                def _(h=h):
                    remote(outbuf.at[m, h], outg.at[me], o_ss.at[m, h], o_rs.at[me], (SECTIONS - 1 - m, 2 * z + h)).start()

                @pl.when(jnp.logical_not(not_me(SECTIONS - 1 - m, h)))
                def _(h=h):
                    local_copy(outbuf.at[m, h], outg.at[me], o_rs.at[me])

    def carry_slopes(i):
        l, m = i // 4, i % 4
        u = jnp.broadcast_to(par[l, 0:1], (GROUP, bw))
        a_h = [chunk_a[i, 0], chunk_a[i, 1]]
        xa, unused_b, unused_a, unused_t = entering(a_h, [jnp.zeros((GROUP, bw), F32)] * 2, True)
        sum_one = jnp.zeros((GROUP, bw), F32)
        sum_normed = jnp.zeros((GROUP, bw), F32)
        for h in (1, 0):
            v = xa[h]
            for t in range(steps - 1, -1, -1):
                g = h * steps + t
                sum_one = sum_one + v
                sum_normed = sum_normed + v * xbuf[i, g]
                v = (u * keepf[m, g]) * v
        rows = []
        for value in (sum_one, sum_normed):
            for q in range(seqs):
                inside = jnp.logical_and(sub >= q * pieces, sub < (q + 1) * pieces)
                rows.append(total(jnp.where(inside, value, 0.0)))
        slopes[i] = pack(rows)

    def back_index(b):
        l, m = SECTIONS - 1 - b // 4, b % 4
        return l, m, l * 4 + m

    def act_back(b):
        l, m, i = back_index(b)

        @pl.when(b < 4)
        def _():
            for h in range(2):
                wait_bytes(dbuf.at[m, h], cot_rs.at[m, h])

        u = jnp.broadcast_to(par[l, 0:1], (GROUP, bw))
        bias = jnp.broadcast_to(par[l, 1:2], (GROUP, bw))
        ends = [None, None]
        sum_act = jnp.zeros((GROUP, bw), F32)
        for h in (1, 0):
            grad = dbuf[b % 12, h].astype(F32).reshape(steps, GROUP, bw)
            v = jnp.zeros((GROUP, bw), F32)
            for t in range(steps - 1, -1, -1):
                g = h * steps + t
                w = states[i, g] + bias
                sg = jax.nn.sigmoid(w)
                da = grad[t] * validf[m, g] * (sg * (1.0 + w * (1.0 - sg)))
                own[m, g] = da
                sum_act = sum_act + da
                v = (u * keepf[m, g]) * (da + v)
            ends[h] = v
        xa, xb, unused, tb = entering([chunk_a[i, 0], chunk_a[i, 1]], ends, True)
        for h in range(2):
            aexr[m, h] = xa[h]
            cex[m, h] = xb[h]
        sum_local = jnp.zeros((GROUP, bw), F32)
        sum_normed = jnp.zeros((GROUP, bw), F32)
        for h in (1, 0):
            v = xb[h]
            for t in range(steps - 1, -1, -1):
                g = h * steps + t
                ds = own[m, g] + v
                sum_local = sum_local + ds
                sum_normed = sum_normed + ds * xbuf[i, g]
                v = (u * keepf[m, g]) * ds
        value = pack(tb + [total(sum_local), total(sum_normed)] + [slopes[i, n : n + 1] for n in range(2 * seqs)])

        @pl.when(b >= 4)
        def _():
            wait_bytes(e1_recv.at[b % 8, pl.ds(0, nz - 1)], e1_ss.at[m])

        e1_send[m] = value
        e1_recv[b % 8, nz - 1] = value
        send_z(e1_send.at[m], lambda k: e1_recv.at[b % 8, k], e1_ss.at[m], e1_rs.at[b % 8])
        add_small(l, m, 3, sum_act)

    def add_small(l, m, n, value):
        added = jnp.where(sub == n, jnp.broadcast_to(total(value), (GROUP, bw)), 0.0)
        if n == 3:
            before = jnp.where(m == 0, 0.0, 1.0)
            small[l] = jnp.where(before > 0.0, small[l], 0.0) + added
        else:
            small[l] = small[l] + added

    def state_back(b):
        l, m, i = back_index(b)
        wait_bytes(e1_recv.at[b % 8, pl.ds(0, nz - 1)], e1_rs.at[b % 8])
        zero = blank[...]

        def line(value):
            return jnp.broadcast_to(value, (GROUP, bw))

        def hop_in(n, carry):
            p = nz - 1 - n
            slot = z_slot(p)
            sum_shift, sum_gain = carry[0], carry[1]
            flow, enter = carry[2 : 2 + seqs], carry[2 + seqs :]
            sum_shift = sum_shift + line(e1_recv[b % 8, slot, seqs : seqs + 1])
            sum_gain = sum_gain + line(e1_recv[b % 8, slot, seqs + 1 : seqs + 2])
            after, inside = [], []
            for q in range(seqs):
                one = seqs + 2 + q
                normed = one + seqs
                sum_shift = sum_shift + flow[q] * line(e1_recv[b % 8, slot, one : one + 1])
                sum_gain = sum_gain + flow[q] * line(e1_recv[b % 8, slot, normed : normed + 1])
                inside.append(jnp.where(p == z, flow[q], enter[q]))
                after.append(line(e1_recv[b % 8, slot, q : q + 1]) + line(pre_recv[slot, i, q : q + 1]) * flow[q])
            return (sum_shift, sum_gain, *after, *inside)

        sum_shift, sum_gain, *rest = over_z(hop_in, (zero,) * (2 + 2 * seqs))
        enter = by_seq(rest[seqs:])
        u = jnp.broadcast_to(par[l, 0:1], (GROUP, bw))
        alpha = jnp.broadcast_to(scal[i, 0:1], (GROUP, bw))
        per_count = scal[i, 1:2]
        gain_part, shift_part = sum_gain * per_count, sum_shift * per_count
        sum_rate = jnp.zeros((GROUP, bw), F32)
        rows = [None] * groups
        for h in (1, 0):
            v = cex[m, h] + aexr[m, h] * enter
            for t in range(steps - 1, -1, -1):
                g = h * steps + t
                keep = keepf[m, g]
                ds = own[m, g] + v
                before = carry_in[i, h] if t == 0 else states[i, g - 1]
                sum_rate = sum_rate + (ds * keep) * before
                v = (u * keep) * ds
                rows[g] = alpha * (ds - validf[m, g] * (shift_part + xbuf[i, g] * gain_part))
        @pl.when(b >= 8)
        def _():
            wait_bytes(dpbuf.at[b % 8, 0], dp_ss.at[b % 8])

        dpbuf[b % 8, 0] = jnp.concatenate(rows, axis=0).astype(BF16)
        remote(dpbuf.at[b % 8, 0], dpbuf.at[b % 8, 1], dp_ss.at[b % 8], dp_rs.at[b % 8], to_y).start()
        add_small(l, m, 2, sum_rate)
        small[l] = small[l] + pack([sum_gain[0:1], sum_shift[0:1]])

    nt = (((1,), (1,)), ((), ()))
    tn = (((0,), (0,)), ((), ()))

    def input_back(b):
        l, m, i = back_index(b)
        wait_bytes(dpbuf.at[b % 8, 1], dp_rs.at[b % 8])
        dp_own, dp_other = dpbuf[b % 8, 0], dpbuf[b % 8, 1]

        def toward(j):
            rows = pl.ds(pl.multiple_of(j * bw, bw), bw)
            first = lax.dot_general(dp_own, wbuf[l, 0, rows], nt, preferred_element_type=F32)
            return first + lax.dot_general(dp_other, wbuf[l, 1, rows], nt, preferred_element_type=F32)

        @pl.when(b >= 4)
        def _():
            wait_bytes(sibsend.at[m], sb_ss.at[m])

        sibsend[m, 0] = toward(j_c).astype(BF16)
        sibsend[m, 1] = toward(j_xc).astype(BF16)
        remote(sibsend.at[m], sibrecv.at[b % 8], sb_ss.at[m], sb_rs.at[b % 8], to_c).start()
        pkeep[m, 0] = toward(j_own)
        pkeep[m, 1] = toward(j_x)

    def weight_back(b):
        l, m, i = back_index(b)
        dp = jnp.concatenate([dpbuf[b % 8, 0], dpbuf[b % 8, 1]], axis=1)
        count = nz // 4
        for j in range(4):
            rows = pl.ds(j * bw, bw)
            new = lax.dot_general(mainbuf[i, j].reshape(sz.rows, bw), dp, tn, preferred_element_type=F32)

            @pl.when(m == 0)
            def _(new=new, rows=rows):
                gw[rows] = new

            @pl.when(jnp.logical_and(m > 0, m < 3))
            def _(new=new, rows=rows):
                gw[rows] = gw[rows] + new

            @pl.when(m == 3)
            def _(new=new, rows=rows, j=j):
                all_items = (gw[rows] + new).astype(BF16)
                for n in range(2):
                    value = all_items[:, n * bw : (n + 1) * bw].reshape(count, part, bw)
                    gall[l, j * count : (j + 1) * count, n] = value

    period = 2 * nz

    def unit_of(q, v):
        return jnp.where(q < 2, SECTIONS - 1 - q, 1 - v), jnp.where(q < 2, v, q - 2)

    def round_of(l, n):
        return jnp.where(l < 2, 2 + n, SECTIONS - 1 - l), jnp.where(l < 2, 1 - l, n)

    to_end, to_start = (s, r + 2), (s, r - 2)

    def g_from(p, v, up):
        return gpart.at[p + 1 if up else p, v], gr_rs.at[p + 1 if up else p, v]

    def relayed(p):
        return jnp.abs(z - p) % 2 == 0

    def g_ready(l, p, n, cross):
        if not cross:
            return
        unit, place_out = gall.at[l, p, n], gout.at[c, s, p, n]
        by_relay = jnp.logical_and(l == s_d, relayed(p))

        @pl.when(jnp.logical_and(l != s, jnp.logical_not(by_relay)))
        def _():
            remote(unit, place_out, gx_ss.at[l, p, n], gx_rs.at[s, p, n], (l, r)).start()

        @pl.when(by_relay)
        def _():
            remote(unit, grelay.at[p, n], gx_ss.at[l, p, n], gl_rs.at[p, n], to_y).start()

        @pl.when(l == s)
        def _():
            local_copy(unit, place_out, gx_rs.at[s, p, n])
            remote(unit, place_out, gs_ss.at[s, p, n], gs_rs.at[s, p, n], to_c).start()

    def g_step(g, cross):
        for up in (True, False):
            place_z = z if up else nz - 1 - z
            ahead = nz - 1 - place_z
            t = g - 2 * place_z
            q = t // period
            k = t % period
            v = k % 2
            l, n = unit_of(q, v)
            inside = jnp.logical_and(t >= 0, q < SECTIONS)

            @pl.when(jnp.logical_and(inside, k < 2 * ahead))
            def _(up=up, place_z=place_z, q=q, k=k, l=l, n=n, v=v):
                far = nz - 1 - k // 2
                p = far if up else nz - 1 - far
                unit = gall.at[l, p, n]

                buf, sem = g_from(p, v, up)
                way, slot = 0 if up else 1, k % 4
                leaving = gleave.at[way, slot]

                @pl.when(jnp.logical_or(q > 0, k >= 4))
                def _():
                    wait_bytes(leaving, ga_ss.at[way, slot])

                @pl.when(place_z > 0)
                def _():
                    wait_bytes(buf, sem)
                    leaving[...] = (unit[...].astype(F32) + buf[...].astype(F32)).astype(BF16)

                @pl.when(place_z == 0)
                def _():
                    leaving[...] = unit[...]

                remote(leaving, buf, ga_ss.at[way, slot], sem, to_end if up else to_start).start()

            @pl.when(jnp.logical_and(inside, k >= 2 * ahead))
            def _(up=up, ahead=ahead, k=k, l=l, n=n, v=v):
                back = (k - 2 * ahead) // 2
                p = z - back if up else z + back
                unit = gall.at[l, p, n]

                @pl.when(back == 0)
                def _():
                    if up:
                        whole = unit[...].astype(F32)
                        for way, there in ((True, z > 0), (False, z < nz - 1)):
                            buf, sem = g_from(p, v, way)

                            @pl.when(there)
                            def _(buf=buf, sem=sem):
                                wait_bytes(buf, sem)

                            whole = whole + jnp.where(there, buf[...].astype(F32), 0.0)
                        unit[...] = whole.astype(BF16)
                        g_ready(l, p, n, cross)

                @pl.when(back > 0)
                def _():
                    wait_bytes(unit, ga_rs.at[l, p, n])
                    g_ready(l, p, n, cross)

                @pl.when(ahead > 0)
                def _():
                    way = 0 if up else 1
                    remote(unit, unit, go_ss.at[l, p, n, way], ga_rs.at[l, p, n], to_end if up else to_start).start()

    def cross_back(b):
        m = b % 4
        wait_bytes(sibrecv.at[b % 8], sb_rs.at[b % 8])

        @pl.when(b < 4)
        def _():
            wait_bytes(ysend.at[m], y_ss.at[m])

        @pl.when(b >= 4)
        def _():
            wait_bytes(ysend.at[m], xp_ss.at[m])

        ysend[m] = (pkeep[m, 1] + sibrecv[b % 8, 1].astype(F32)).astype(BF16)
        remote(ysend.at[m], xrecv.at[b % 8], xp_ss.at[m], xp_rs.at[b % 8], to_x).start()
        pkeep[m, 0] = pkeep[m, 0] + sibrecv[b % 8, 0].astype(F32)

    def join_back(b):
        l, m, i = back_index(b)
        wait_bytes(xrecv.at[b % 8], xp_rs.at[b % 8])
        even = (1 - l % 2).astype(F32)
        side = dbuf[jnp.maximum(b - 4, 0) % 12].astype(F32).reshape(sz.rows, bw)
        value = pkeep[m, 0] + xrecv[b % 8].astype(F32) + even * side
        dbuf[(b + 4) % 12] = value.astype(BF16).reshape(2, sz.half, bw)

        @pl.when(l == 0)
        def _():
            for h in range(2):
                src = dbuf.at[(b + 4) % 12, h]

                @pl.when(not_me(SECTIONS - 1 - m, h))
                def _(src=src, h=h):
                    remote(src, ging.at[me], gi_ss.at[m, h], gi_rs.at[me], (SECTIONS - 1 - m, 2 * z + h)).start()

                @pl.when(jnp.logical_not(not_me(SECTIONS - 1 - m, h)))
                def _(src=src):
                    local_copy(src, ging.at[me], gi_rs.at[me])

    first_step = 6

    def forward_tick(k):
        @pl.when(k < items)
        def _():
            project(k)

        @pl.when(k == 1)
        def _():
            inputs_on(3)

        @pl.when(jnp.logical_and(k >= 1, k < items + 1))
        def _():
            moments(k - 1)

        @pl.when(jnp.logical_and(k >= 2, k < items + 2))
        def _():
            finish_layer(k - 2)

        @pl.when(jnp.logical_and(k >= 2, k < items + 2))
        def _():
            carry_slopes(k - 2)

        @pl.when(jnp.logical_and(k + 1 >= 4, k + 1 < items))
        def _():
            arrived(k + 1)

        @pl.when(k < 11)
        def _():
            @pl.when(k == 0)
            def _():
                w_pass(1, 0, 0)

            unit = k + 1
            for n in range(4):
                @pl.when(unit % 4 == n)
                def _(n=n):
                    w_pass(unit // 4 + 1, n // 2, n % 2)

            @pl.when(k % 4 == 1)
            def _():
                send_decays(k // 4 + 1)

    def backward_tick(k):
        @pl.when(k >= 4)
        def _():
            join_back(k - 4)

        @pl.when(jnp.logical_and(k >= 0, k < items))
        def _():
            act_back(k)

        @pl.when(k >= first_step)
        def _():
            g_step(k - first_step, False)

        @pl.when(jnp.logical_and(k >= 1, k < items + 1))
        def _():
            state_back(k - 1)

        @pl.when(jnp.logical_and(k >= 2, k < items + 2))
        def _():
            input_back(k - 2)
            weight_back(k - 2)
            cross_back(k - 2)

    start = items - 2

    def tick(k, _):
        forward_tick(k)
        backward_tick(k - start)
        return 0

    lax.fori_loop(0, start + items + 4, tick, 0)

    send_z(small, lambda k: small_recv.at[k], st_ss, st_rs)
    steps_done = items + 4 - first_step
    steps_all = SECTIONS * period + 2 * (nz - 1)

    def whole_at(l, p, n):
        q, v = round_of(l, n)
        return q * period + 2 * (nz - 1) + 2 * jnp.abs(z - p) + v

    def crosses_at(l, p, n):
        early = whole_at(l, p, n) < steps_done
        return jnp.where(early, steps_done + 2 * p + n, whole_at(l, p, n))

    def cross_early(g):
        p, n = (g - steps_done) // 2, (g - steps_done) % 2

        @pl.when(p < nz)
        def _():
            for l in range(SECTIONS):
                @pl.when(whole_at(l, p, n) < steps_done)
                def _(l=l):
                    g_ready(l, p, n, True)

    def relay_lag(l):
        return jnp.where(l < 2, 4, 12)

    def g_relay(g):
        def one(p, _):
            for n in range(2):
                @pl.when(jnp.logical_and(relayed(p), crosses_at(s_x, p, n) + relay_lag(s_x) == g))
                def _(n=n):
                    wait_bytes(grelay.at[p, n], gl_rs.at[p, n])
                    remote(grelay.at[p, n], gout.at[c, s_y, p, n], gl_ss.at[p, n], gx_rs.at[s_y, p, n], to_x).start()

            return 0

        lax.fori_loop(0, nz, one, 0)

    def g_to_other_core(g):
        lag = jnp.where(s < 2, 6, 14)

        def one(p, _):
            for n in range(2):
                sent = crosses_at(s, p, n) + lag

                def onward(t, n=n):
                    unit = gout.at[c, t, p, n]
                    wait_bytes(unit, gx_rs.at[t, p, n])
                    remote(unit, unit, gs_ss.at[t, p, n], gs_rs.at[t, p, n], to_c).start()

                @pl.when(sent == g)
                def _(onward=onward):
                    onward(s_x)
                    onward(s_y)

                @pl.when(sent + jnp.where(relayed(p), relay_lag(s), 0) == g)
                def _(onward=onward):
                    onward(s_d)

            return 0

        lax.fori_loop(0, nz, one, 0)

    def late_step(g, _):
        g_step(g, True)
        cross_early(g)
        g_relay(g)
        g_to_other_core(g)
        return 0

    def late_steps(first, last_step):
        lax.fori_loop(first, last_step, late_step, 0)

    late_steps(steps_done, steps_done + 3)
    wait_bytes(small_recv, st_rs)
    wait_bytes(small_recv, st_ss)

    def add_rest(k, _):
        for l in range(SECTIONS):
            small[l] = small[l] + jnp.where(sub >= 2, small_recv[k, l], 0.0)
        return 0

    lax.fori_loop(0, nz - 1, add_rest, 0)
    for t in range(SECTIONS):
        for h in range(2):
            @pl.when(not_me(t, h))
            def _(t=t, h=h):
                remote(small.at[t], smallg.at[me], sm_ss.at[t, h], sm_rs.at[me], (t, 2 * z + h)).start()

            @pl.when(jnp.logical_not(not_me(t, h)))
            def _(t=t):
                local_copy(small.at[t], smallg.at[me], sm_rs.at[me])

    late_steps(steps_done + 3, steps_done + 9)

    restore = (row_of == frame_at).astype(BF16)
    for e in range(8):
        wait_bytes(outg.at[e], o_rs.at[e])
        wait_bytes(ging.at[e], gi_rs.at[e])
        wait_bytes(smallg.at[e], sm_rs.at[e])
        for src, dst in ((outg, out), (ging, grad_inp)):
            value = jnp.dot(restore, src[e], preferred_element_type=F32).astype(BF16)
            value = value.reshape(seqs, sz.frames, bw)
            dst[0, :, :, e * bw : e * bw + width(e)] = value[:, :, : width(e)]
        for n, dst in enumerate((grad_gain, grad_shift, grad_rec, grad_bias)):
            dst[0:1, e * bw : e * bw + width(e)] = smallg[e, n : n + 1, : width(e)]

    late_steps(steps_done + 9, steps_all + 10)

    def drain_units(k, _):
        p, n = k // 2, k % 2
        unit = gall.at[0, p, n]
        for t in range(SECTIONS):
            wait_bytes(unit, gs_rs.at[t, p, n])
            wait_bytes(unit, gs_ss.at[t, p, n])

            @pl.when(t != s)
            def _(t=t):
                wait_bytes(unit, gx_ss.at[t, p, n])

            @pl.when(t == s)
            def _(t=t):
                wait_bytes(unit, gx_rs.at[t, p, n])

            @pl.when(jnp.logical_and(p <= z, z < nz - 1))
            def _(t=t):
                wait_bytes(unit, go_ss.at[t, p, n, 0])

            @pl.when(jnp.logical_and(p >= z, z > 0))
            def _(t=t):
                wait_bytes(unit, go_ss.at[t, p, n, 1])

        return 0

    lax.fori_loop(0, period, drain_units, 0)

    def drain_relay(p, _):
        @pl.when(relayed(p))
        def _():
            for n in range(2):
                wait_bytes(grelay.at[p, n], gl_ss.at[p, n])

        return 0

    lax.fori_loop(0, nz, drain_relay, 0)
    for way in range(2):
        ahead = nz - 1 - z if way == 0 else z
        for slot in range(4):
            @pl.when(slot < 2 * ahead)
            def _(way=way, slot=slot):
                wait_bytes(gleave.at[way, slot], ga_ss.at[way, slot])

    for l in range(SECTIONS):
        @pl.when(l != s)
        def _(l=l):
            for k in range(2):
                for n in range(2):
                    wait_bytes(w_unit(l, k, n), w_fs.at[l, k, n])

        wait_bytes(pre_recv.at[pl.ds(0, nz - 1), pl.ds(4 * l, 4)], pre_ss.at[l])
        wait_bytes(ex_recv.at[l, pl.ds(0, nz - 1)], ex_ss.at[l])
        wait_bytes(e1_recv.at[l, pl.ds(0, nz - 1)], e1_ss.at[l])
        wait_bytes(sibsend.at[l], sb_ss.at[l])
        wait_bytes(ysend.at[l], xp_ss.at[l])
        for h in range(2):
            @pl.when(not_me(l, h))
            def _(l=l, h=h):
                wait_bytes(dbuf.at[mine, c], cot_ss.at[l, h])
                wait_bytes(small.at[l], sm_ss.at[l, h])

            @pl.when(not_me(SECTIONS - 1 - l, h))
            def _(l=l, h=h):
                wait_bytes(outbuf.at[l, h], o_ss.at[l, h])
                wait_bytes(dbuf.at[(items + l) % 12, h], gi_ss.at[l, h])

    def drain(i, _):
        @pl.when(i < 8)
        def _():
            wait_bytes(dpbuf.at[i, 0], dp_ss.at[i])

        @pl.when(i >= 4)
        def _():
            wait_bytes(mainbuf.at[i, j_own], mx_ss.at[i])
            wait_bytes(mainbuf.at[i, j_own], ms_ss.at[i])
            wait_bytes(mainbuf.at[i, j_x], mf_ss.at[i])

        return 0

    lax.fori_loop(0, items, drain, 0)
    for n in range(4):
        wait_bytes(in_dst, in_ss.at[n])
    for slot in range(4):
        @pl.when(slot != mine)
        def _(slot=slot):
            wait_bytes(in_dst, in_fs.at[slot])

    for n in range(3):
        wait_bytes(par.at[s], par_ss.at[n])
        for k in range(2):
            for m in range(2):
                wait_bytes(wx.at[n, m, pl.ds(k * bw, bw)], w_ss.at[n, k, m])

    wait_bytes(flagbuf.at[c], flag_ss.at[0])


def run_kernel(sz, *args):
    nz, bw, items, groups = sz.nz, sz.bw, sz.items, sz.groups
    half, rows, part = sz.half, sz.rows, sz.part
    dma = pltpu.SemaphoreType.DMA
    vm = pltpu.VMEM
    step = (GROUP, bw)
    scratch = [
        vm((items, 4, 2, half, bw), BF16),
        vm((SECTIONS, 2, 4 * bw, bw), BF16),
        vm((4, rows, bw), BF16),
        vm((8, rows, bw), BF16),
        vm((4, groups) + step, F32),
        vm((items, groups) + step, F32),
        vm((items, groups) + step, F32),
        vm((items, 2) + step, F32),
        vm((items, 2) + step, F32),
        vm((items, 2) + step, F32),
        vm((items, 2) + step, F32),
        vm((4, groups) + step, F32),
        vm((4, groups) + step, F32),
        vm((2, 8 * sz.seqs, 128), F32),
        vm((SECTIONS,) + step, F32),
        vm((8,) + step, F32),
        vm((items,) + step, F32),
        vm((nz, items) + step, F32),
        vm((4,) + step, F32),
        vm((8, nz) + step, F32),
        vm((4,) + step, F32),
        vm((8, nz) + step, F32),
        vm((items,) + step, F32),
        vm((items,) + step, F32),
        vm((4, 2) + step, F32),
        vm((12, 2, half, bw), BF16),
        vm((4, 2) + step, F32),
        vm((4, 2) + step, F32),
        vm((8, 2, rows, bw), BF16),
        vm((4, 2, rows, bw), F32),
        vm((4, 2, rows, bw), BF16),
        vm((8, 2, rows, bw), BF16),
        vm((8, rows, bw), BF16),
        vm((4 * bw, 2 * bw), F32),
        vm((SECTIONS, nz, 2, part, bw), BF16),
        vm((nz + 1, 2, part, bw), BF16),
        vm((2, 4, part, bw), BF16),
        vm((nz, 2, part, bw), BF16),
        vm((SECTIONS,) + step, F32),
        vm((nz - 1, SECTIONS) + step, F32),
        vm((4, 2, half, bw), BF16),
        vm((2, sz.seqs, sz.frames, sz.hidden), BF16),
        vm((2, 8, half, bw), BF16),
        vm((3, bw, sz.hidden), BF16),
        vm((3, 2, 2 * bw, bw), BF16),
        vm((8, half, bw), BF16),
        vm((8, half, bw), BF16),
        vm((8,) + step, F32),
        vm(step, F32),
    ]
    sems = [
        dma((2,)), dma((4,)), dma((4,)), dma((4,)), dma((4, 2)), dma((4, 2)), dma((4, 2)),
        dma((3,)), dma((4,)), dma((1,)), dma((2,)),
        dma((3, 2, 2)), dma((4, 4, 2)), dma((4, 2, 2)), dma((4, 2, 2)),
        dma((4,)), dma((4,)),
        dma((items,)), dma((items,)), dma((items,)), dma((items,)), dma((items,)), dma((items,)),
        dma((4,)), dma((8,)), dma((4,)), dma((8,)),
        dma((4, 2)), dma((8,)), dma((4,)), dma((8,)),
        dma((8,)), dma((8,)), dma((4,)), dma((8,)), dma((4,)), dma((8,)),
        dma((4, 2)), dma((8,)),
        dma((2, 4)), dma((4, nz, 2)), dma((4, nz, 2, 2)), dma((nz + 1, 2)),
        dma((4, nz, 2)), dma((4, nz, 2)), dma((nz, 2)), dma((nz, 2)), dma((4, nz, 2)), dma((4, nz, 2)),
        dma, dma, dma((4, 2)), dma((8,)),
    ]
    anywhere = pl.BlockSpec(memory_space=pl.ANY)
    inside = pl.BlockSpec(memory_space=pltpu.VMEM)
    frames = jax.ShapeDtypeStruct((1, sz.seqs, sz.frames, sz.hidden), BF16)
    vector = jax.ShapeDtypeStruct((1, sz.hidden), F32)
    return pl.pallas_call(
        functools.partial(kernel, sz),
        out_shape=(frames, frames) + (vector,) * 4 + (jax.ShapeDtypeStruct((2, SECTIONS, nz, 2, part, bw), BF16),),
        in_specs=[anywhere] * 3 + [inside] * 6,
        out_specs=(inside,) * 6 + (anywhere,),
        scratch_shapes=scratch + sems,
        compiler_params=pltpu.CompilerParams(
            collective_id=0, has_side_effects=True, vmem_limit_bytes=63 * 2**20
        ),
    )(*args)


def place_weights(sz, pieces, *others):
    bw, part, hidden = sz.bw, sz.part, sz.hidden
    count = bw // part

    def body(*refs):
        src, dst = refs[0], refs[1 + len(others)]
        upper = pl.program_id(0) // 4
        for n in range(len(others)):
            refs[2 + len(others) + n][...] = refs[1 + n][...]

        for yy in range(2):
            @pl.when(upper == yy)
            def _(yy=yy):
                for p in range(count):
                    for e in range(8):
                        n, x, c = (0 if e // 4 == yy else 1), e % 4 // 2, e % 2
                        wide = bw if e < 7 else sz.last
                        value = src[c, x, p, n, :, :wide].astype(F32)
                        dst[p * part : (p + 1) * part, e * bw : e * bw + wide] = value

    def spec(value):
        if value.ndim < 4:
            return pl.BlockSpec(value.shape, lambda q: (0,) * value.ndim)
        eighth = sz.seqs * sz.frames // 8
        per_seq = sz.frames // eighth
        return pl.BlockSpec((1, 1, eighth, hidden), lambda q: (0, q // per_seq, q % per_seq, 0))

    specs = [spec(v) for v in others]
    return pl.pallas_call(
        body,
        grid=(8,),
        out_shape=[jax.ShapeDtypeStruct((hidden, hidden), F32)] + [jax.ShapeDtypeStruct(v.shape, v.dtype) for v in others],
        in_specs=[pl.BlockSpec((2, 2, count, 2, part, bw), lambda q: (0, q // 4, q % 4, 0, 0, 0))] + specs,
        out_specs=[pl.BlockSpec((bw, hidden), lambda q: (q, 0))] + specs,
        compiler_params=pltpu.CompilerParams(vmem_limit_bytes=60 * 2**20),
    )(pieces, *others)


def local(sz, inputs, resets, valid_mask, weights, recurrence, state_bias, norm_gain, norm_shift, cotangent):
    *others, pieces = run_kernel(
        sz, inputs, cotangent, weights, resets, valid_mask, recurrence, state_bias, norm_gain, norm_shift
    )
    grad_weights, outputs, grad_inputs, *vectors = place_weights(sz, pieces, *others)
    return outputs, grad_inputs, grad_weights[None], *vectors


def solution(mesh):
    def step(inputs, *rest):
        sz = Sizes(mesh.shape["rows"] // 2, inputs.shape[1], inputs.shape[2], inputs.shape[3])
        return local(sz, inputs, *rest)

    frames = P("section", None, "rows", None)
    flags = P(None, None, "rows")
    vectors = P("section", None)
    matrix = P("section", None, None)
    return jax.shard_map(
        step,
        mesh=mesh,
        in_specs=(frames, flags, flags, matrix, vectors, vectors, vectors, vectors, frames),
        out_specs=(frames, frames, matrix, vectors, vectors, vectors, vectors),
        check_vma=False,
    )
```

```python
import functools

import jax
import jax.numpy as jnp
from jax import lax
from jax.experimental import pallas as pl
from jax.experimental.pallas import tpu as pltpu
from jax.sharding import PartitionSpec as P

MESH = pl.DeviceIdType.MESH
norm_eps = 1e-05
F32, BF16 = jnp.float32, jnp.bfloat16
SECTIONS = 4
GROUP = 8


class Sizes:
    def __init__(self, nz, seqs, frames, hidden):
        self.nz, self.seqs, self.frames = nz, seqs, frames
        self.pieces = GROUP // seqs
        self.steps = frames // self.pieces
        self.half = seqs * frames
        self.rows = 2 * self.half
        self.groups = self.rows // GROUP
        self.bw = -(-hidden // 1024) * 128
        self.padded = 8 * self.bw
        self.part = 4 * self.bw // nz
        self.items = 4 * SECTIONS
        self.hidden = hidden
        self.last = hidden - 7 * self.bw


def wait_bytes(ref, sem):
    pltpu.make_async_copy(ref, ref, sem).wait()


def local_copy(src, dst, sem):
    pltpu.make_async_copy(src, dst, sem).start()


def remote(src, dst, send, recv, device):
    return pltpu.make_async_remote_copy(
        src_ref=src, dst_ref=dst, send_sem=send, recv_sem=recv, device_id=device, device_id_type=MESH
    )


def kernel(
    sz, inp_raw, cot_raw, w_raw, resets, valid_mask, recurrence, state_bias, norm_gain, norm_shift,
    out, grad_inp, grad_rec, grad_bias, grad_gain, grad_shift, gout,
    mainbuf, wbuf, ysend, yrecv, own, xbuf, states, carry_in, chunk_a, chunk_aex, chunk_s0,
    keepf, validf, flagbuf, par, parblk, pre_send, pre_recv, ex_send, ex_recv, e1_send, e1_recv,
    scal, slopes, s1ex, dbuf, cex, aexr, dpbuf, pkeep, sibsend, sibrecv, xrecv, gw, gall, gpart, gleave, grelay,
    small, small_send, small_recv, outbuf, raw, blocks, wst, wx, outg, ging, smallg, blank,
    raw_ls, wst_ls, in_ss, in_fs, in_rs, cot_ss, cot_rs, par_ss, par_rs, flag_ss, flag_rs, w_ss, w_rs, w_fs, w_ps,
    pre_ss, pre_rs, mx_ss, mx_rs, ms_ss, ms_rs, mf_ss, mf_rs, y_ss, y_rs, ex_ss, ex_rs,
    o_ss, o_rs, e1_ss, e1_rs, dp_ss, dp_rs, sb_ss, sb_rs, xp_ss, xp_rs,
    gi_ss, gi_rs, ga_ss, ga_rs, go_ss, gr_rs, gx_ss, gx_rs, gl_ss, gl_rs, gs_ss, gs_rs, st_ss, st_rs, sm_ss, sm_rs,
):
    nz, bw, items, groups, steps = sz.nz, sz.bw, sz.items, sz.groups, sz.steps
    pieces, seqs = sz.pieces, sz.seqs
    s, r = lax.axis_index("section"), lax.axis_index("rows")
    y, x, z, c = s // 2, s % 2, r // 2, r % 2
    s_x, s_y, s_d = s + 1 - 2 * x, s + 2 - 4 * y, 3 - s
    r_c = r + 1 - 2 * c
    to_x, to_y, to_d, to_c = (s_x, r), (s_y, r), (s_d, r), (s, r_c)
    j_own, j_x, j_c, j_xc = 2 * x + c, 2 * (1 - x) + c, 2 * x + 1 - c, 2 * (1 - x) + 1 - c
    me = 2 * s + c
    part, half, last = sz.part, sz.half, sz.last
    mine = SECTIONS - 1 - s
    pair_half = z % 2
    to_pair = (s, r + 2 - 4 * pair_half)
    sub = lax.broadcasted_iota(jnp.int32, (GROUP, bw), 0)
    place = sub % pieces

    def z_peer(distance):
        return (s, 2 * ((z + distance) % nz) + c)

    def z_slot(p):
        return (z - p + nz - 1) % nz

    def by_seq(rows):
        value = jnp.broadcast_to(rows[seqs - 1], (GROUP, bw))
        for q in range(seqs - 2, -1, -1):
            value = jnp.where(sub < (q + 1) * pieces, jnp.broadcast_to(rows[q], (GROUP, bw)), value)
        return value

    def last_of(value, q):
        return value[(q + 1) * pieces - 1 : (q + 1) * pieces]

    def first_of(value, q):
        return value[q * pieces : q * pieces + 1]

    def entering(a, b, reverse):
        out_a, out_b = [None, None], [None, None]
        t_a = t_b = None
        for h in (1, 0) if reverse else (0, 1):
            ia, ib = a[h], b[h]
            hop = 1
            while hop < pieces:
                if reverse:
                    ok, shift = place < pieces - hop, GROUP - hop
                else:
                    ok, shift = place >= hop, hop
                pa = jnp.where(ok, pltpu.roll(ia, shift, 0), 1.0)
                pb = jnp.where(ok, pltpu.roll(ib, shift, 0), 0.0)
                ib = ia * pb + ib
                ia = ia * pa
                hop *= 2
            if reverse:
                ok, shift, edge = place < pieces - 1, GROUP - 1, first_of
            else:
                ok, shift, edge = place >= 1, 1, last_of
            xa = jnp.where(ok, pltpu.roll(ia, shift, 0), 1.0)
            xb = jnp.where(ok, pltpu.roll(ib, shift, 0), 0.0)
            na = [edge(ia, q) for q in range(seqs)]
            nb = [edge(ib, q) for q in range(seqs)]
            if t_a is not None:
                ea, eb = by_seq(t_a), by_seq(t_b)
                xb = xa * eb + xb
                xa = xa * ea
                nb = [na[q] * t_b[q] + nb[q] for q in range(seqs)]
                na = [na[q] * t_a[q] for q in range(seqs)]
            t_a, t_b = na, nb
            out_a[h], out_b[h] = xa, xb
        return out_a, out_b, t_a, t_b

    def pack(rows):
        rows = rows + [jnp.zeros((1, bw), F32)] * (8 - len(rows))
        value = jnp.zeros((8, bw), F32)
        for q, row in enumerate(rows):
            value = jnp.where(sub == q, jnp.broadcast_to(row, (8, bw)), value)
        return value

    def total(value):
        return jnp.sum(value, axis=0, keepdims=True)

    def over_z(body, start):
        return lax.fori_loop(0, nz, body, start, unroll=nz <= 8)

    def send_z(src, dst_of, send_sem, recv_sem):
        def one(k, _):
            remote(src, dst_of(k - 1), send_sem, recv_sem, z_peer(k)).start()
            return 0

        lax.fori_loop(1, nz, one, 0, unroll=nz <= 8)

    def not_me(t, h):
        return jnp.logical_or(t != s, h != c)

    blank[...] = jnp.zeros((GROUP, bw), F32)

    def width(e):
        return bw if e < 7 else last

    barrier = pltpu.get_barrier_semaphore()
    for t in (s, s_x, s_y, s_d):
        for q in (r, r_c):
            if not (t is s and q is r):
                pl.semaphore_signal(barrier, inc=1, device_id=(t, q), device_id_type=MESH)

    def greet(k, _):
        pl.semaphore_signal(barrier, inc=1, device_id=z_peer(k), device_id_type=MESH)
        return 0

    lax.fori_loop(1, nz, greet, 0)

    local_copy(inp_raw.at[0], raw.at[0], raw_ls.at[0])
    local_copy(cot_raw.at[0], raw.at[1], raw_ls.at[1])
    w_rows = [(1 - y, 2 * pair_half), (1 - y, 2 * pair_half + 1), (y, 2 * pair_half), (y, 2 * pair_half + 1)]
    w_rows += [(y, 2 - 2 * pair_half), (y, 3 - 2 * pair_half)]

    def w_load(n, wait):
        yy, j = w_rows[n]
        k, slot = 4 * yy + j, n % 3

        def go(rows):
            copy = pltpu.make_async_copy(
                w_raw.at[0, pl.ds(pl.multiple_of(k * bw, bw), rows)], wst.at[slot, pl.ds(0, rows)], wst_ls.at[slot]
            )
            copy.wait() if wait else copy.start()

        @pl.when(k < 7)
        def _():
            go(bw)

        @pl.when(k == 7)
        def _():
            if not wait:
                wst[slot, last:] = jnp.zeros((bw - last, sz.hidden), BF16)
            go(last)

    def w_cut(n, column, toward, dst):
        slot = n % 3
        for e in range(8):
            @pl.when(column == e % 4)
            def _(e=e):
                place_of = jnp.where(toward == e // 4, 0, 1)
                if e == 7:
                    dst[place_of] = jnp.zeros((bw, bw), BF16)
                dst[place_of, :, : width(e)] = wst[slot, :, e * bw : e * bw + width(e)]

    for n in range(3):
        w_load(n, False)

    parblk[...] = jnp.zeros(parblk.shape, F32)
    for n, ref in enumerate((recurrence, state_bias, norm_gain, norm_shift)):
        for e in range(8):
            parblk[e, n : n + 1, : width(e)] = ref[0:1, e * bw : e * bw + width(e)]
    par[s] = parblk[me]
    flagbuf[c] = jnp.zeros(flagbuf.shape[1:], F32)
    for n, ref in enumerate((resets, valid_mask)):
        for m in range(4):
            row = seqs * (4 * n + m)
            flagbuf[c, row : row + seqs, : sz.frames] = ref[SECTIONS - 1 - m].astype(F32)

    def w_unit(l, j, n):
        return wbuf.at[l, n, pl.ds(pl.multiple_of(j * bw, bw), bw)]

    def w_cross():
        for k in range(2):
            j = 2 * pair_half + k
            for m, t in enumerate((s_x, s_y, s_d)):
                for n in range(2):
                    src = wx.at[m, n, pl.ds(k * bw, bw)]
                    remote(src, w_unit(s, j, n), w_ss.at[m, k, n], w_rs.at[s, j, n], (t, r)).start()

    for n in range(6):
        if n == 4:
            pl.semaphore_wait(barrier, 7 + nz - 1)

            @pl.when(s == 0)
            def _():
                w_cross()

        w_load(n, True)
        j = w_rows[n][1]
        rows = pl.ds(pl.multiple_of(j * bw, bw), bw)
        half_rows = pl.ds((n % 2) * bw, bw)
        if n < 2:
            w_cut(n, j_own, 1 - y, wx.at[1, :, half_rows])
            w_cut(n, j_x, 1 - y, wx.at[2, :, half_rows])
        elif n < 4:
            w_cut(n, j_x, y, wx.at[0, :, half_rows])
            w_cut(n, j_own, y, wbuf.at[s, :, rows])
        else:
            w_cut(n, j_own, y, wbuf.at[s, :, rows])
        if n + 3 < 6:
            w_load(n + 3, False)

    row = lax.broadcasted_iota(jnp.int32, (half, half), 0)
    col = lax.broadcasted_iota(jnp.int32, (half, half), 1)
    frame_of = (row % GROUP // pieces) * sz.frames + (row % pieces) * steps + row // GROUP
    permute = (col == frame_of).astype(BF16)
    row_of = row
    frame_at = (col % GROUP // pieces) * sz.frames + (col % pieces) * steps + col // GROUP

    def cut_frames(n):
        wait_bytes(raw.at[n], raw_ls.at[n])
        for e in range(8):
            value = raw[n, :, :, e * bw : e * bw + width(e)].reshape(half, width(e))
            if e == 7:
                blocks[n, e] = jnp.zeros((half, bw), BF16)
            blocks[n, e, :, : width(e)] = jnp.dot(permute, value, preferred_element_type=F32).astype(BF16)

    cut_frames(0)

    for n, t in enumerate((s_x, s_y, s_d)):
        remote(parblk.at[2 * t + c], par.at[s], par_ss.at[n], par_rs.at[s], (t, r)).start()
    remote(flagbuf.at[c], flagbuf.at[c], flag_ss.at[0], flag_rs.at[c], to_c).start()

    in_dst = mainbuf.at[mine, :, c]
    near, far = blocks.at[0, pl.ds(4 * y, 4)], blocks.at[0, pl.ds(4 - 4 * y, 4)]
    remote(far, in_dst, in_ss.at[2], in_rs.at[mine, c], to_d).start()
    remote(near, in_dst, in_ss.at[0], in_rs.at[mine, c], to_x).start()
    remote(far, in_dst, in_ss.at[1], in_rs.at[mine, c], to_y).start()
    remote(near, in_dst, in_ss.at[3], in_rs.at[mine, c], to_c).start()
    local_copy(near, in_dst, in_rs.at[mine, c])

    @pl.when(s != 0)
    def _():
        w_cross()

    wait_bytes(flagbuf.at[1 - c], flag_rs.at[1 - c])
    row = lax.broadcasted_iota(jnp.int32, (half, sz.frames), 0)
    col = lax.broadcasted_iota(jnp.int32, (half, sz.frames), 1)
    at_frame = col == (row % pieces) * steps + row // GROUP
    of_seq = row % GROUP // pieces
    ones = jnp.ones((sz.frames, bw), BF16)

    def masks_of(m, _):
        for h in range(2):
            lo, hi = h * steps, (h + 1) * steps
            for n in range(2):
                flags = jnp.zeros((half, sz.frames), F32)
                for q in range(seqs):
                    line = flagbuf[h, pl.ds(seqs * (4 * n + m) + q, 1), : sz.frames]
                    flags = jnp.where(jnp.logical_and(at_frame, of_seq == q), line, flags)
                value = jnp.dot(flags.astype(BF16), ones, preferred_element_type=F32).reshape(steps, GROUP, bw)
                if n == 0:
                    keepf[m, lo:hi] = 1.0 - value
                else:
                    validf[m, lo:hi] = value
        return 0

    lax.fori_loop(0, 4, masks_of, 0)
    for t in (s_x, s_y, s_d):
        wait_bytes(par.at[t], par_rs.at[t])

    def decays_of(i, _):
        l, m = i // 4, i % 4
        u = jnp.broadcast_to(par[l, 0:1], (GROUP, bw))
        a_h, v_h = [], []
        for h in range(2):
            a = jnp.ones((GROUP, bw), F32)
            v = jnp.zeros((GROUP, bw), F32)
            for t in range(steps):
                d = u * keepf[m, h * steps + t]
                a = d * a
                v = d * v + 1.0
            a_h.append(a)
            v_h.append(v)
        xa, xb, ta, tb = entering(a_h, v_h, False)
        for h in range(2):
            chunk_a[i, h] = a_h[h]
            chunk_aex[i, h] = xa[h]
            chunk_s0[i, h] = xb[h]
        valid_count = total(jnp.sum(validf[m], axis=0))
        value = pack(ta + tb + [valid_count])
        pre_send[i] = value
        pre_recv[nz - 1, i] = value
        return 0

    lax.fori_loop(0, items, decays_of, 0)

    def send_decays(l):
        some = pl.ds(4 * l, 4)
        send_z(pre_send.at[some], lambda k: pre_recv.at[k, some], pre_ss.at[l], pre_rs.at[l])

    send_decays(0)

    def inputs_on(slot):
        block = mainbuf.at[slot, :, c]

        @pl.when(slot != mine)
        def _():
            wait_bytes(block, in_rs.at[slot, c])
            remote(block, block, in_fs.at[slot], in_rs.at[slot, c], to_c).start()

        @pl.when(slot == mine)
        def _():
            wait_bytes(block, in_rs.at[slot, c])

    for slot in range(3):
        inputs_on(slot)

    def w_pass(l, k, n):
        j = 2 * pair_half + k

        @pl.when(l != s)
        def _():
            wait_bytes(w_unit(l, j, n), w_rs.at[l, j, n])
            remote(w_unit(l, j, n), w_unit(l, j, n), w_fs.at[l, k, n], w_ps.at[l, k, n], to_pair).start()

    def w_arrive(l):
        @pl.when(l != s)
        def _():
            for k in range(2):
                for n in range(2):
                    wait_bytes(w_unit(l, 2 - 2 * pair_half + k, n), w_ps.at[l, k, n])

    for n in range(2):
        w_pass(0, 0, n)

    for n in range(2):
        w_pass(0, 1, n)
    cut_frames(1)
    def cotangent_out(e):
        t, h = (s, s_x, s_y, s_d)[e // 2], e % 2
        src = blocks.at[1, 2 * t + h]

        @pl.when(not_me(t, h))
        def _():
            remote(src, dbuf.at[mine, c], cot_ss.at[t, h], cot_rs.at[mine, c], (t, 2 * z + h)).start()

        @pl.when(jnp.logical_not(not_me(t, h)))
        def _():
            local_copy(src, dbuf.at[mine, c], cot_rs.at[mine, c])

    def arrived(i):
        block = mainbuf.at[i, j_x]
        wait_bytes(block, mx_rs.at[i])
        remote(block, block, mf_ss.at[i], mf_rs.at[i], to_c).start()

    def project(i):
        l, m = i // 4, i % 4

        @pl.when(m == 0)
        def _():
            w_arrive(l)

        @pl.when(l == 0)
        def _():
            wait_bytes(mainbuf.at[i, :, 1 - c], in_rs.at[m, 1 - c])

        @pl.when(l > 0)
        def _():
            wait_bytes(mainbuf.at[i, j_c], ms_rs.at[i])
            wait_bytes(mainbuf.at[i, j_xc], mf_rs.at[i])
            wait_bytes(ysend.at[m], y_ss.at[m])

        def to_half(n):
            acc = jnp.zeros((sz.rows, bw), F32)
            for j in range(4):
                acc = acc + jnp.dot(
                    mainbuf[i, j].reshape(sz.rows, bw), wbuf[l, n, j * bw : (j + 1) * bw], preferred_element_type=F32
                )
            return acc

        ysend[m] = to_half(1).astype(BF16)
        remote(ysend.at[m], yrecv.at[i % 8], y_ss.at[m], y_rs.at[i % 8], to_y).start()
        own[m] = to_half(0).reshape(groups, GROUP, bw)

    def moments(i):
        l, m = i // 4, i % 4
        wait_bytes(yrecv.at[i % 8], y_rs.at[i % 8])
        pre = own[m] + yrecv[i % 8].astype(F32).reshape(groups, GROUP, bw)
        valid = validf[m]
        pre_sum = total(jnp.sum(pre * valid, axis=0))
        local_count = pre_send[i, 2 * seqs : 2 * seqs + 1]
        pivot = pre_sum / jnp.maximum(local_count, 1.0)
        shifted = pre - pivot
        xbuf[i] = shifted
        square = total(jnp.sum(shifted * shifted * valid, axis=0))
        u = jnp.broadcast_to(par[l, 0:1], (GROUP, bw))
        ends = []
        for h in range(2):
            v = jnp.zeros((GROUP, bw), F32)
            for t in range(steps):
                v = (u * keepf[m, h * steps + t]) * v + shifted[h * steps + t]
            ends.append(v)
        unused_a, xb, unused_t, tb = entering([chunk_a[i, 0], chunk_a[i, 1]], ends, False)
        for h in range(2):
            s1ex[m, h] = xb[h]
        value = pack([pre_sum, square] + tb)

        @pl.when(l > 0)
        def _():
            wait_bytes(ex_recv.at[i % 8, pl.ds(0, nz - 1)], ex_ss.at[m])

        ex_send[m] = value
        ex_recv[i % 8, nz - 1] = value
        send_z(ex_send.at[m], lambda k: ex_recv.at[i % 8, k], ex_ss.at[m], ex_rs.at[i % 8])

    def finish_layer(i):
        l, m = i // 4, i % 4

        @pl.when(m == 0)
        def _():
            wait_bytes(pre_recv.at[pl.ds(0, nz - 1), pl.ds(4 * l, 4)], pre_rs.at[l])

        wait_bytes(ex_recv.at[i % 8, pl.ds(0, nz - 1)], ex_rs.at[i % 8])
        u, bias = par[l, 0:1], par[l, 1:2]
        gain, shift = par[l, 2:3], par[l, 3:4]

        def add_sum(p, carry):
            slot = z_slot(p)
            return (
                carry[0] + ex_recv[i % 8, slot, 0:1],
                carry[1] + pre_recv[slot, i, 2 * seqs : 2 * seqs + 1],
            )

        zero = jnp.zeros((1, bw), F32)
        sum_all, count_all = over_z(add_sum, (zero, zero))
        mean = sum_all / count_all

        def pivot_of(slot):
            count = pre_recv[slot, i, 2 * seqs : 2 * seqs + 1]
            return ex_recv[i % 8, slot, 0:1] / jnp.maximum(count, 1.0), count

        def add_square(p, carry):
            slot = z_slot(p)
            pivot, count = pivot_of(slot)
            return carry + ex_recv[i % 8, slot, 1:2] + count * (pivot - mean) * (pivot - mean)

        var = over_z(add_square, zero) / count_all
        inv = lax.rsqrt(var + norm_eps)
        alpha = gain * inv

        def hop_in(p, carry):
            slot = z_slot(p)
            pivot, unused = pivot_of(slot)
            beta = shift + alpha * (pivot - mean)
            after = []
            for q in range(seqs):
                value = (
                    alpha * ex_recv[i % 8, slot, 2 + q : 3 + q]
                    + beta * pre_recv[slot, i, seqs + q : seqs + q + 1]
                    + pre_recv[slot, i, q : q + 1] * carry[q]
                )
                after.append(jnp.where(p < z, value, carry[q]))
            return tuple(after)

        enter = by_seq(list(over_z(hop_in, (zero,) * seqs)))
        pivot, unused = pivot_of(nz - 1)
        beta = shift + alpha * (pivot - mean)
        offset = (pivot - mean) * inv
        scal[i] = pack([alpha, 1.0 / count_all])
        wide = [jnp.broadcast_to(v, (GROUP, bw)) for v in (u, bias, alpha, beta, inv, offset)]
        u, bias, alpha, beta, inv, offset = wide
        side = mainbuf.at[jnp.maximum(i - 4, 0), j_own]
        odd = (l % 2).astype(F32)
        to_next = l < SECTIONS - 1
        target = jnp.minimum(i + 4, items - 1)
        for h in range(2):
            v = alpha * s1ex[m, h] + beta * chunk_s0[i, h] + chunk_aex[i, h] * enter
            carry_in[i, h] = v
            hidden = []
            for t in range(steps):
                g = h * steps + t
                shifted = xbuf[i, g]
                v = (u * keepf[m, g]) * v + (alpha * shifted + beta)
                states[i, g] = v
                xbuf[i, g] = shifted * inv + offset
                w = v + bias
                hidden.append(validf[m, g] * (w * jax.nn.sigmoid(w)))
            value = jnp.concatenate(hidden, axis=0) + odd * side[h].astype(F32)
            outbuf[m, h] = value.astype(BF16)

        @pl.when(to_next)
        def _():
            block = mainbuf.at[target, j_own]
            block[...] = outbuf[m]
            remote(block, block, mx_ss.at[target], mx_rs.at[target], to_x).start()
            remote(block, block, ms_ss.at[target], ms_rs.at[target], to_c).start()

    def carry_slopes(i):
        l, m = i // 4, i % 4
        u = jnp.broadcast_to(par[l, 0:1], (GROUP, bw))
        a_h = [chunk_a[i, 0], chunk_a[i, 1]]
        xa, unused_b, unused_a, unused_t = entering(a_h, [jnp.zeros((GROUP, bw), F32)] * 2, True)
        sum_one = jnp.zeros((GROUP, bw), F32)
        sum_normed = jnp.zeros((GROUP, bw), F32)
        for h in (1, 0):
            v = xa[h]
            for t in range(steps - 1, -1, -1):
                g = h * steps + t
                sum_one = sum_one + v
                sum_normed = sum_normed + v * xbuf[i, g]
                v = (u * keepf[m, g]) * v
        rows = []
        for value in (sum_one, sum_normed):
            for q in range(seqs):
                inside = jnp.logical_and(sub >= q * pieces, sub < (q + 1) * pieces)
                rows.append(total(jnp.where(inside, value, 0.0)))
        slopes[i] = pack(rows)

    def back_index(b):
        l, m = SECTIONS - 1 - b // 4, b % 4
        return l, m, l * 4 + m

    def act_back(b):
        l, m, i = back_index(b)

        @pl.when(b < 4)
        def _():
            for h in range(2):
                wait_bytes(dbuf.at[m, h], cot_rs.at[m, h])

        u = jnp.broadcast_to(par[l, 0:1], (GROUP, bw))
        bias = jnp.broadcast_to(par[l, 1:2], (GROUP, bw))
        ends = [None, None]
        sum_act = jnp.zeros((GROUP, bw), F32)
        for h in (1, 0):
            grad = dbuf[b % 12, h].astype(F32).reshape(steps, GROUP, bw)
            v = jnp.zeros((GROUP, bw), F32)
            for t in range(steps - 1, -1, -1):
                g = h * steps + t
                w = states[i, g] + bias
                sg = jax.nn.sigmoid(w)
                da = grad[t] * validf[m, g] * (sg * (1.0 + w * (1.0 - sg)))
                own[m, g] = da
                sum_act = sum_act + da
                v = (u * keepf[m, g]) * (da + v)
            ends[h] = v
        xa, xb, unused, tb = entering([chunk_a[i, 0], chunk_a[i, 1]], ends, True)
        for h in range(2):
            aexr[m, h] = xa[h]
            cex[m, h] = xb[h]
        sum_local = jnp.zeros((GROUP, bw), F32)
        sum_normed = jnp.zeros((GROUP, bw), F32)
        for h in (1, 0):
            v = xb[h]
            for t in range(steps - 1, -1, -1):
                g = h * steps + t
                ds = own[m, g] + v
                sum_local = sum_local + ds
                sum_normed = sum_normed + ds * xbuf[i, g]
                v = (u * keepf[m, g]) * ds
        value = pack(tb + [total(sum_local), total(sum_normed)] + [slopes[i, n : n + 1] for n in range(2 * seqs)])

        @pl.when(b >= 4)
        def _():
            wait_bytes(e1_recv.at[b % 8, pl.ds(0, nz - 1)], e1_ss.at[m])

        e1_send[m] = value
        e1_recv[b % 8, nz - 1] = value
        send_z(e1_send.at[m], lambda k: e1_recv.at[b % 8, k], e1_ss.at[m], e1_rs.at[b % 8])
        add_small(l, m, 3, sum_act)

    def add_small(l, m, n, value):
        added = jnp.where(sub == n, jnp.broadcast_to(total(value), (GROUP, bw)), 0.0)
        if n == 3:
            before = jnp.where(m == 0, 0.0, 1.0)
            small[l] = jnp.where(before > 0.0, small[l], 0.0) + added
        else:
            small[l] = small[l] + added

    def state_back(b):
        l, m, i = back_index(b)
        wait_bytes(e1_recv.at[b % 8, pl.ds(0, nz - 1)], e1_rs.at[b % 8])
        zero = blank[...]

        def line(value):
            return jnp.broadcast_to(value, (GROUP, bw))

        def hop_in(n, carry):
            p = nz - 1 - n
            slot = z_slot(p)
            sum_shift, sum_gain = carry[0], carry[1]
            flow, enter = carry[2 : 2 + seqs], carry[2 + seqs :]
            sum_shift = sum_shift + line(e1_recv[b % 8, slot, seqs : seqs + 1])
            sum_gain = sum_gain + line(e1_recv[b % 8, slot, seqs + 1 : seqs + 2])
            after, inside = [], []
            for q in range(seqs):
                one = seqs + 2 + q
                normed = one + seqs
                sum_shift = sum_shift + flow[q] * line(e1_recv[b % 8, slot, one : one + 1])
                sum_gain = sum_gain + flow[q] * line(e1_recv[b % 8, slot, normed : normed + 1])
                inside.append(jnp.where(p == z, flow[q], enter[q]))
                after.append(line(e1_recv[b % 8, slot, q : q + 1]) + line(pre_recv[slot, i, q : q + 1]) * flow[q])
            return (sum_shift, sum_gain, *after, *inside)

        sum_shift, sum_gain, *rest = over_z(hop_in, (zero,) * (2 + 2 * seqs))
        enter = by_seq(rest[seqs:])
        u = jnp.broadcast_to(par[l, 0:1], (GROUP, bw))
        alpha = jnp.broadcast_to(scal[i, 0:1], (GROUP, bw))
        per_count = scal[i, 1:2]
        gain_part, shift_part = sum_gain * per_count, sum_shift * per_count
        sum_rate = jnp.zeros((GROUP, bw), F32)
        rows = [None] * groups
        for h in (1, 0):
            v = cex[m, h] + aexr[m, h] * enter
            for t in range(steps - 1, -1, -1):
                g = h * steps + t
                keep = keepf[m, g]
                ds = own[m, g] + v
                before = carry_in[i, h] if t == 0 else states[i, g - 1]
                sum_rate = sum_rate + (ds * keep) * before
                v = (u * keep) * ds
                rows[g] = alpha * (ds - validf[m, g] * (shift_part + xbuf[i, g] * gain_part))
        @pl.when(b >= 8)
        def _():
            wait_bytes(dpbuf.at[b % 8, 0], dp_ss.at[b % 8])

        dpbuf[b % 8, 0] = jnp.concatenate(rows, axis=0).astype(BF16)
        remote(dpbuf.at[b % 8, 0], dpbuf.at[b % 8, 1], dp_ss.at[b % 8], dp_rs.at[b % 8], to_y).start()
        add_small(l, m, 2, sum_rate)
        small[l] = small[l] + pack([sum_gain[0:1], sum_shift[0:1]])

    nt = (((1,), (1,)), ((), ()))
    tn = (((0,), (0,)), ((), ()))

    def input_back(b):
        l, m, i = back_index(b)
        wait_bytes(dpbuf.at[b % 8, 1], dp_rs.at[b % 8])
        dp_own, dp_other = dpbuf[b % 8, 0], dpbuf[b % 8, 1]

        def toward(j):
            rows = pl.ds(pl.multiple_of(j * bw, bw), bw)
            first = lax.dot_general(dp_own, wbuf[l, 0, rows], nt, preferred_element_type=F32)
            return first + lax.dot_general(dp_other, wbuf[l, 1, rows], nt, preferred_element_type=F32)

        @pl.when(b >= 4)
        def _():
            wait_bytes(sibsend.at[m], sb_ss.at[m])

        sibsend[m, 0] = toward(j_c).astype(BF16)
        sibsend[m, 1] = toward(j_xc).astype(BF16)
        remote(sibsend.at[m], sibrecv.at[b % 8], sb_ss.at[m], sb_rs.at[b % 8], to_c).start()
        pkeep[m, 0] = toward(j_own)
        pkeep[m, 1] = toward(j_x)

    def weight_back(b):
        l, m, i = back_index(b)
        dp = jnp.concatenate([dpbuf[b % 8, 0], dpbuf[b % 8, 1]], axis=1)
        count = nz // 4
        for j in range(4):
            rows = pl.ds(j * bw, bw)
            new = lax.dot_general(mainbuf[i, j].reshape(sz.rows, bw), dp, tn, preferred_element_type=F32)

            @pl.when(m == 0)
            def _(new=new, rows=rows):
                gw[rows] = new

            @pl.when(jnp.logical_and(m > 0, m < 3))
            def _(new=new, rows=rows):
                gw[rows] = gw[rows] + new

            @pl.when(m == 3)
            def _(new=new, rows=rows, j=j):
                all_items = (gw[rows] + new).astype(BF16)
                for n in range(2):
                    value = all_items[:, n * bw : (n + 1) * bw].reshape(count, part, bw)
                    gall[l, j * count : (j + 1) * count, n] = value

    period = 2 * nz

    def unit_of(q, v):
        return jnp.where(q < 2, SECTIONS - 1 - q, 1 - v), jnp.where(q < 2, v, q - 2)

    def round_of(l, n):
        return jnp.where(l < 2, 2 + n, SECTIONS - 1 - l), jnp.where(l < 2, 1 - l, n)

    to_end, to_start = (s, r + 2), (s, r - 2)

    def g_from(p, v, up):
        return gpart.at[p + 1 if up else p, v], gr_rs.at[p + 1 if up else p, v]

    def relayed(p):
        return jnp.abs(z - p) % 2 == 0

    def g_ready(l, p, n, cross):
        if not cross:
            return
        unit, place_out = gall.at[l, p, n], gout.at[c, s, p, n]
        by_relay = jnp.logical_and(l == s_d, relayed(p))

        @pl.when(jnp.logical_and(l != s, jnp.logical_not(by_relay)))
        def _():
            remote(unit, place_out, gx_ss.at[l, p, n], gx_rs.at[s, p, n], (l, r)).start()

        @pl.when(by_relay)
        def _():
            remote(unit, grelay.at[p, n], gx_ss.at[l, p, n], gl_rs.at[p, n], to_y).start()

        @pl.when(l == s)
        def _():
            local_copy(unit, place_out, gx_rs.at[s, p, n])
            remote(unit, place_out, gs_ss.at[s, p, n], gs_rs.at[s, p, n], to_c).start()

    def g_step(g, cross):
        for up in (True, False):
            place_z = z if up else nz - 1 - z
            ahead = nz - 1 - place_z
            t = g - 2 * place_z
            q = t // period
            k = t % period
            v = k % 2
            l, n = unit_of(q, v)
            inside = jnp.logical_and(t >= 0, q < SECTIONS)

            @pl.when(jnp.logical_and(inside, k < 2 * ahead))
            def _(up=up, place_z=place_z, q=q, k=k, l=l, n=n, v=v):
                far = nz - 1 - k // 2
                p = far if up else nz - 1 - far
                unit = gall.at[l, p, n]

                buf, sem = g_from(p, v, up)
                way, slot = 0 if up else 1, k % 4
                leaving = gleave.at[way, slot]

                @pl.when(jnp.logical_or(q > 0, k >= 4))
                def _():
                    wait_bytes(leaving, ga_ss.at[way, slot])

                @pl.when(place_z > 0)
                def _():
                    wait_bytes(buf, sem)
                    leaving[...] = (unit[...].astype(F32) + buf[...].astype(F32)).astype(BF16)

                @pl.when(place_z == 0)
                def _():
                    leaving[...] = unit[...]

                remote(leaving, buf, ga_ss.at[way, slot], sem, to_end if up else to_start).start()

            @pl.when(jnp.logical_and(inside, k >= 2 * ahead))
            def _(up=up, ahead=ahead, k=k, l=l, n=n, v=v):
                back = (k - 2 * ahead) // 2
                p = z - back if up else z + back
                unit = gall.at[l, p, n]

                @pl.when(back == 0)
                def _():
                    if up:
                        whole = unit[...].astype(F32)
                        for way, there in ((True, z > 0), (False, z < nz - 1)):
                            buf, sem = g_from(p, v, way)

                            @pl.when(there)
                            def _(buf=buf, sem=sem):
                                wait_bytes(buf, sem)

                            whole = whole + jnp.where(there, buf[...].astype(F32), 0.0)
                        unit[...] = whole.astype(BF16)
                        g_ready(l, p, n, cross)

                @pl.when(back > 0)
                def _():
                    wait_bytes(unit, ga_rs.at[l, p, n])
                    g_ready(l, p, n, cross)

                @pl.when(ahead > 0)
                def _():
                    way = 0 if up else 1
                    remote(unit, unit, go_ss.at[l, p, n, way], ga_rs.at[l, p, n], to_end if up else to_start).start()

    def cross_back(b):
        m = b % 4
        wait_bytes(sibrecv.at[b % 8], sb_rs.at[b % 8])

        @pl.when(b < 4)
        def _():
            wait_bytes(ysend.at[m], y_ss.at[m])

        @pl.when(b >= 4)
        def _():
            wait_bytes(ysend.at[m], xp_ss.at[m])

        ysend[m] = (pkeep[m, 1] + sibrecv[b % 8, 1].astype(F32)).astype(BF16)
        remote(ysend.at[m], xrecv.at[b % 8], xp_ss.at[m], xp_rs.at[b % 8], to_x).start()
        pkeep[m, 0] = pkeep[m, 0] + sibrecv[b % 8, 0].astype(F32)

    def join_back(b):
        l, m, i = back_index(b)
        wait_bytes(xrecv.at[b % 8], xp_rs.at[b % 8])
        even = (1 - l % 2).astype(F32)
        side = dbuf[jnp.maximum(b - 4, 0) % 12].astype(F32).reshape(sz.rows, bw)
        value = pkeep[m, 0] + xrecv[b % 8].astype(F32) + even * side
        dbuf[(b + 4) % 12] = value.astype(BF16).reshape(2, sz.half, bw)

    def frames_out(m):
        t = SECTIONS - 1 - m
        for h in range(2):
            grads = dbuf.at[(items + m) % 12, h]

            @pl.when(not_me(t, h))
            def _(h=h, grads=grads):
                remote(outbuf.at[m, h], outg.at[me], o_ss.at[m, h], o_rs.at[me], (t, 2 * z + h)).start()
                remote(grads, ging.at[me], gi_ss.at[m, h], gi_rs.at[me], (t, 2 * z + h)).start()

            @pl.when(jnp.logical_not(not_me(t, h)))
            def _(h=h, grads=grads):
                local_copy(outbuf.at[m, h], outg.at[me], o_rs.at[me])
                local_copy(grads, ging.at[me], gi_rs.at[me])

    first_step = 6


    def forward_tick(k):
        @pl.when(k < items)
        def _():
            project(k)

        @pl.when(k == 1)
        def _():
            inputs_on(3)

        @pl.when(jnp.logical_and(k >= 1, k < items + 1))
        def _():
            moments(k - 1)

        @pl.when(jnp.logical_and(k >= 2, k < items + 2))
        def _():
            finish_layer(k - 2)

        @pl.when(jnp.logical_and(k >= 2, k < items + 2))
        def _():
            carry_slopes(k - 2)

        @pl.when(jnp.logical_and(k + 1 >= 4, k + 1 < items))
        def _():
            arrived(k + 1)

        for e in range(8):
            @pl.when(k == 3 + e)
            def _(e=e):
                cotangent_out(e)

        @pl.when(k < 11)
        def _():
            @pl.when(k == 0)
            def _():
                w_pass(1, 0, 0)

            unit = k + 1
            for n in range(4):
                @pl.when(unit % 4 == n)
                def _(n=n):
                    w_pass(unit // 4 + 1, n // 2, n % 2)

            @pl.when(k % 4 == 1)
            def _():
                send_decays(k // 4 + 1)

    def backward_tick(k):
        @pl.when(k >= 4)
        def _():
            join_back(k - 4)

        @pl.when(jnp.logical_and(k >= 0, k < items))
        def _():
            act_back(k)

        @pl.when(k >= first_step)
        def _():
            g_step(k - first_step, False)

        @pl.when(jnp.logical_and(k >= 1, k < items + 1))
        def _():
            state_back(k - 1)

        @pl.when(jnp.logical_and(k >= 2, k < items + 2))
        def _():
            input_back(k - 2)
            weight_back(k - 2)
            cross_back(k - 2)

    start = items - 2

    def tick(k, _):
        forward_tick(k)
        backward_tick(k - start)
        return 0

    lax.fori_loop(0, start + items + 4, tick, 0)

    small_send[...] = pack([small[l, n : n + 1] for l in range(SECTIONS) for n in (2, 3)])
    send_z(small_send, lambda k: small_recv.at[k], st_ss, st_rs)
    steps_done = items + 4 - first_step
    steps_all = SECTIONS * period + 2 * (nz - 1)

    def whole_at(l, p, n):
        q, v = round_of(l, n)
        return q * period + 2 * (nz - 1) + 2 * jnp.abs(z - p) + v

    def crosses_at(l, p, n):
        early = whole_at(l, p, n) < steps_done
        return jnp.where(early, steps_done + 2 * p + n, whole_at(l, p, n))

    def cross_early(g):
        p, n = (g - steps_done) // 2, (g - steps_done) % 2

        @pl.when(p < nz)
        def _():
            for l in range(SECTIONS):
                @pl.when(whole_at(l, p, n) < steps_done)
                def _(l=l):
                    g_ready(l, p, n, True)

    def relay_lag(l):
        return jnp.where(l < 2, 4, 12)

    def g_relay(g):
        def one(p, _):
            for n in range(2):
                @pl.when(jnp.logical_and(relayed(p), crosses_at(s_x, p, n) + relay_lag(s_x) == g))
                def _(n=n):
                    wait_bytes(grelay.at[p, n], gl_rs.at[p, n])
                    remote(grelay.at[p, n], gout.at[c, s_y, p, n], gl_ss.at[p, n], gx_rs.at[s_y, p, n], to_x).start()

            return 0

        lax.fori_loop(0, nz, one, 0)

    def g_to_other_core(g):
        lag = jnp.where(s < 2, 6, 14)

        def one(p, _):
            for n in range(2):
                sent = crosses_at(s, p, n) + lag

                def onward(t, n=n):
                    unit = gout.at[c, t, p, n]
                    wait_bytes(unit, gx_rs.at[t, p, n])
                    remote(unit, unit, gs_ss.at[t, p, n], gs_rs.at[t, p, n], to_c).start()

                @pl.when(sent == g)
                def _(onward=onward):
                    onward(s_x)
                    onward(s_y)

                @pl.when(sent + jnp.where(relayed(p), relay_lag(s), 0) == g)
                def _(onward=onward):
                    onward(s_d)

            return 0

        lax.fori_loop(0, nz, one, 0)

    def sum_small():
        wait_bytes(small_recv, st_rs)
        wait_bytes(small_recv, st_ss)

        def add_rest(k, carry):
            return carry + small_recv[k]

        sums = lax.fori_loop(0, nz - 1, add_rest, small_send[...])
        for l in range(SECTIONS):
            rate = jnp.broadcast_to(sums[2 * l : 2 * l + 1], (GROUP, bw))
            bias = jnp.broadcast_to(sums[2 * l + 1 : 2 * l + 2], (GROUP, bw))
            small[l] = jnp.where(sub == 2, rate, jnp.where(sub == 3, bias, small[l]))
        for t in range(SECTIONS):
            for h in range(2):
                @pl.when(not_me(t, h))
                def _(t=t, h=h):
                    remote(small.at[t], smallg.at[me], sm_ss.at[t, h], sm_rs.at[me], (t, 2 * z + h)).start()

                @pl.when(jnp.logical_not(not_me(t, h)))
                def _(t=t):
                    local_copy(small.at[t], smallg.at[me], sm_rs.at[me])

    restore = (row_of == frame_at).astype(BF16)

    def place_block(e):
        wait_bytes(outg.at[e], o_rs.at[e])
        wait_bytes(ging.at[e], gi_rs.at[e])
        for src, dst in ((outg, out), (ging, grad_inp)):
            value = jnp.dot(restore, src[e], preferred_element_type=F32).astype(BF16)
            value = value.reshape(seqs, sz.frames, bw)
            dst[0, :, :, e * bw : e * bw + width(e)] = value[:, :, : width(e)]

    def drain_layers():
        for l in range(SECTIONS):
            @pl.when(l != s)
            def _(l=l):
                for k in range(2):
                    for n in range(2):
                        wait_bytes(w_unit(l, k, n), w_fs.at[l, k, n])

            wait_bytes(pre_recv.at[pl.ds(0, nz - 1), pl.ds(4 * l, 4)], pre_ss.at[l])
            wait_bytes(ex_recv.at[l, pl.ds(0, nz - 1)], ex_ss.at[l])
            wait_bytes(e1_recv.at[l, pl.ds(0, nz - 1)], e1_ss.at[l])
            wait_bytes(sibsend.at[l], sb_ss.at[l])
            wait_bytes(ysend.at[l], xp_ss.at[l])
            for h in range(2):
                @pl.when(not_me(l, h))
                def _(l=l, h=h):
                    wait_bytes(dbuf.at[mine, c], cot_ss.at[l, h])
                    wait_bytes(small.at[l], sm_ss.at[l, h])

                @pl.when(not_me(SECTIONS - 1 - l, h))
                def _(l=l, h=h):
                    wait_bytes(outbuf.at[l, h], o_ss.at[l, h])
                    wait_bytes(dbuf.at[(items + l) % 12, h], gi_ss.at[l, h])

        def drain(i, _):
            @pl.when(i < 8)
            def _():
                wait_bytes(dpbuf.at[i, 0], dp_ss.at[i])

            @pl.when(i >= 4)
            def _():
                wait_bytes(mainbuf.at[i, j_own], mx_ss.at[i])
                wait_bytes(mainbuf.at[i, j_own], ms_ss.at[i])
                wait_bytes(mainbuf.at[i, j_x], mf_ss.at[i])

            return 0

        lax.fori_loop(0, items, drain, 0)
        for n in range(4):
            wait_bytes(in_dst, in_ss.at[n])
        for slot in range(4):
            @pl.when(slot != mine)
            def _(slot=slot):
                wait_bytes(in_dst, in_fs.at[slot])

        for n in range(3):
            wait_bytes(par.at[s], par_ss.at[n])
            for k in range(2):
                for m in range(2):
                    wait_bytes(wx.at[n, m, pl.ds(k * bw, bw)], w_ss.at[n, k, m])

        wait_bytes(flagbuf.at[c], flag_ss.at[0])

    def late_step(g, _):
        g_step(g, True)
        cross_early(g)
        g_relay(g)
        g_to_other_core(g)

        @pl.when(g == steps_done)
        def _():
            for m in range(4):
                frames_out(m)

        @pl.when(g == steps_done + 5)
        def _():
            sum_small()

        for e in range(8):
            @pl.when(g == steps_done + 16 + e)
            def _(e=e):
                place_block(e)

        @pl.when(g == steps_done + 24)
        def _():
            drain_layers()

        return 0

    lax.fori_loop(steps_done, max(steps_all + 10, steps_done + period + 26), late_step, 0)

    for e in range(8):
        wait_bytes(smallg.at[e], sm_rs.at[e])
        for n, dst in enumerate((grad_gain, grad_shift, grad_rec, grad_bias)):
            dst[0:1, e * bw : e * bw + width(e)] = smallg[e, n : n + 1, : width(e)]

    def drain_units(k, _):
        p, n = k // 2, k % 2
        unit = gall.at[0, p, n]
        for t in range(SECTIONS):
            wait_bytes(unit, gs_rs.at[t, p, n])
            wait_bytes(unit, gs_ss.at[t, p, n])

            @pl.when(t != s)
            def _(t=t):
                wait_bytes(unit, gx_ss.at[t, p, n])

            @pl.when(t == s)
            def _(t=t):
                wait_bytes(unit, gx_rs.at[t, p, n])

            @pl.when(jnp.logical_and(p <= z, z < nz - 1))
            def _(t=t):
                wait_bytes(unit, go_ss.at[t, p, n, 0])

            @pl.when(jnp.logical_and(p >= z, z > 0))
            def _(t=t):
                wait_bytes(unit, go_ss.at[t, p, n, 1])

        return 0

    lax.fori_loop(0, period, drain_units, 0)

    def drain_relay(p, _):
        @pl.when(relayed(p))
        def _():
            for n in range(2):
                wait_bytes(grelay.at[p, n], gl_ss.at[p, n])

        return 0

    lax.fori_loop(0, nz, drain_relay, 0)
    for way in range(2):
        ahead = nz - 1 - z if way == 0 else z
        for slot in range(4):
            @pl.when(slot < 2 * ahead)
            def _(way=way, slot=slot):
                wait_bytes(gleave.at[way, slot], ga_ss.at[way, slot])


def run_kernel(sz, *args):
    nz, bw, items, groups = sz.nz, sz.bw, sz.items, sz.groups
    half, rows, part = sz.half, sz.rows, sz.part
    dma = pltpu.SemaphoreType.DMA
    vm = pltpu.VMEM
    step = (GROUP, bw)
    scratch = [
        vm((items, 4, 2, half, bw), BF16),
        vm((SECTIONS, 2, 4 * bw, bw), BF16),
        vm((4, rows, bw), BF16),
        vm((8, rows, bw), BF16),
        vm((4, groups) + step, F32),
        vm((items, groups) + step, F32),
        vm((items, groups) + step, F32),
        vm((items, 2) + step, F32),
        vm((items, 2) + step, F32),
        vm((items, 2) + step, F32),
        vm((items, 2) + step, F32),
        vm((4, groups) + step, F32),
        vm((4, groups) + step, F32),
        vm((2, 8 * sz.seqs, 128), F32),
        vm((SECTIONS,) + step, F32),
        vm((8,) + step, F32),
        vm((items,) + step, F32),
        vm((nz, items) + step, F32),
        vm((4,) + step, F32),
        vm((8, nz) + step, F32),
        vm((4,) + step, F32),
        vm((8, nz) + step, F32),
        vm((items,) + step, F32),
        vm((items,) + step, F32),
        vm((4, 2) + step, F32),
        vm((12, 2, half, bw), BF16),
        vm((4, 2) + step, F32),
        vm((4, 2) + step, F32),
        vm((8, 2, rows, bw), BF16),
        vm((4, 2, rows, bw), F32),
        vm((4, 2, rows, bw), BF16),
        vm((8, 2, rows, bw), BF16),
        vm((8, rows, bw), BF16),
        vm((4 * bw, 2 * bw), F32),
        vm((SECTIONS, nz, 2, part, bw), BF16),
        vm((nz + 1, 2, part, bw), BF16),
        vm((2, 4, part, bw), BF16),
        vm((nz, 2, part, bw), BF16),
        vm((SECTIONS,) + step, F32),
        vm(step, F32),
        vm((nz - 1,) + step, F32),
        vm((4, 2, half, bw), BF16),
        vm((2, sz.seqs, sz.frames, sz.hidden), BF16),
        vm((2, 8, half, bw), BF16),
        vm((3, bw, sz.hidden), BF16),
        vm((3, 2, 2 * bw, bw), BF16),
        vm((8, half, bw), BF16),
        vm((8, half, bw), BF16),
        vm((8,) + step, F32),
        vm(step, F32),
    ]
    sems = [
        dma((2,)), dma((4,)), dma((4,)), dma((4,)), dma((4, 2)), dma((4, 2)), dma((4, 2)),
        dma((3,)), dma((4,)), dma((1,)), dma((2,)),
        dma((3, 2, 2)), dma((4, 4, 2)), dma((4, 2, 2)), dma((4, 2, 2)),
        dma((4,)), dma((4,)),
        dma((items,)), dma((items,)), dma((items,)), dma((items,)), dma((items,)), dma((items,)),
        dma((4,)), dma((8,)), dma((4,)), dma((8,)),
        dma((4, 2)), dma((8,)), dma((4,)), dma((8,)),
        dma((8,)), dma((8,)), dma((4,)), dma((8,)), dma((4,)), dma((8,)),
        dma((4, 2)), dma((8,)),
        dma((2, 4)), dma((4, nz, 2)), dma((4, nz, 2, 2)), dma((nz + 1, 2)),
        dma((4, nz, 2)), dma((4, nz, 2)), dma((nz, 2)), dma((nz, 2)), dma((4, nz, 2)), dma((4, nz, 2)),
        dma, dma, dma((4, 2)), dma((8,)),
    ]
    anywhere = pl.BlockSpec(memory_space=pl.ANY)
    inside = pl.BlockSpec(memory_space=pltpu.VMEM)
    frames = jax.ShapeDtypeStruct((1, sz.seqs, sz.frames, sz.hidden), BF16)
    vector = jax.ShapeDtypeStruct((1, sz.hidden), F32)
    return pl.pallas_call(
        functools.partial(kernel, sz),
        out_shape=(frames, frames) + (vector,) * 4 + (jax.ShapeDtypeStruct((2, SECTIONS, nz, 2, part, bw), BF16),),
        in_specs=[anywhere] * 3 + [inside] * 6,
        out_specs=(inside,) * 6 + (anywhere,),
        scratch_shapes=scratch + sems,
        compiler_params=pltpu.CompilerParams(
            collective_id=0, has_side_effects=True, vmem_limit_bytes=63 * 2**20
        ),
    )(*args)


def place_weights(sz, pieces, *others):
    bw, part, hidden = sz.bw, sz.part, sz.hidden
    count, strips, ring = bw // part, 8, 3

    def body(*refs):
        src, rest = refs[0], refs[1 : 1 + len(others)]
        dst, rest_out = refs[1 + len(others)], refs[2 + len(others) : 2 + 2 * len(others)]
        arrived, leaving, in_sem, out_sem, rest_in, rest_sem = refs[2 + 2 * len(others) :][:6]
        held = refs[8 + 2 * len(others) :]

        def load(q):
            some = src.at[:, pl.ds(2 * (q // 4), 2), pl.ds(q % 4 * count, count)]
            return pltpu.make_async_copy(some, arrived.at[q], in_sem.at[q])

        def store(q):
            rows = bw if q < 7 else sz.last
            some = dst.at[pl.ds(q * bw, rows)]
            return pltpu.make_async_copy(leaving.at[q % ring, pl.ds(0, rows)], some, out_sem.at[q % ring])

        def through(n, out):
            if out:
                return pltpu.make_async_copy(held[n], rest_out[n], rest_sem.at[n])
            return pltpu.make_async_copy(rest[n], held[n], rest_in.at[n])

        for q in range(strips):
            load(q).start()
        for n in range(len(others)):
            through(n, False).start()
        for q in range(strips):
            load(q).wait()
            if q >= ring:
                store(q - ring).wait()
            for p in range(count):
                for e in range(8):
                    n, x, c = (0 if e // 4 == q // 4 else 1), e % 4 // 2, e % 2
                    wide = bw if e < 7 else sz.last
                    value = arrived[q, c, x, p, n, :, :wide].astype(F32)
                    leaving[q % ring, p * part : (p + 1) * part, e * bw : e * bw + wide] = value
            store(q).start()
            if q == 1:
                for n in range(len(others)):
                    through(n, False).wait()
                    through(n, True).start()
        for q in range(strips - ring, strips):
            store(q).wait()
        for n in range(len(others)):
            through(n, True).wait()

    anywhere = pl.BlockSpec(memory_space=pl.ANY)
    dma = pltpu.SemaphoreType.DMA
    return pl.pallas_call(
        body,
        out_shape=[jax.ShapeDtypeStruct((hidden, hidden), F32)] + [jax.ShapeDtypeStruct(v.shape, v.dtype) for v in others],
        in_specs=[anywhere] * (1 + len(others)),
        out_specs=[anywhere] * (1 + len(others)),
        scratch_shapes=[
            pltpu.VMEM((strips, 2, 2, count, 2, part, bw), BF16),
            pltpu.VMEM((ring, bw, hidden), F32),
            dma((strips,)), dma((ring,)), dma((len(others),)), dma((len(others),)),
        ] + [pltpu.VMEM(v.shape, v.dtype) for v in others],
        compiler_params=pltpu.CompilerParams(vmem_limit_bytes=60 * 2**20),
    )(pieces, *others)


def local(sz, inputs, resets, valid_mask, weights, recurrence, state_bias, norm_gain, norm_shift, cotangent):
    *others, pieces = run_kernel(
        sz, inputs, cotangent, weights, resets, valid_mask, recurrence, state_bias, norm_gain, norm_shift
    )
    grad_weights, outputs, grad_inputs, *vectors = place_weights(sz, pieces, *others)
    return outputs, grad_inputs, grad_weights[None], *vectors


def solution(mesh):
    def step(inputs, *rest):
        sz = Sizes(mesh.shape["rows"] // 2, inputs.shape[1], inputs.shape[2], inputs.shape[3])
        return local(sz, inputs, *rest)

    frames = P("section", None, "rows", None)
    flags = P(None, None, "rows")
    vectors = P("section", None)
    matrix = P("section", None, None)
    return jax.shard_map(
        step,
        mesh=mesh,
        in_specs=(frames, flags, flags, matrix, vectors, vectors, vectors, vectors, frames),
        out_specs=(frames, frames, matrix, vectors, vectors, vectors, vectors),
        check_vma=False,
    )
```

```python
import functools

import jax
import jax.numpy as jnp
from jax import lax
from jax.experimental import pallas as pl
from jax.experimental.pallas import tpu as pltpu
from jax.sharding import PartitionSpec as P

MESH = pl.DeviceIdType.MESH
norm_eps = 1e-05
F32, BF16 = jnp.float32, jnp.bfloat16
SECTIONS = 4
GROUP = 8


class Sizes:
    def __init__(self, nz, seqs, frames, hidden):
        self.nz, self.seqs, self.frames = nz, seqs, frames
        self.pieces = GROUP // seqs
        self.steps = frames // self.pieces
        self.half = seqs * frames
        self.rows = 2 * self.half
        self.groups = self.rows // GROUP
        self.bw = -(-hidden // 1024) * 128
        self.padded = 8 * self.bw
        self.part = 4 * self.bw // nz
        self.items = 4 * SECTIONS
        self.hidden = hidden
        self.last = hidden - 7 * self.bw


def wait_bytes(ref, sem):
    pltpu.make_async_copy(ref, ref, sem).wait()


def local_copy(src, dst, sem):
    pltpu.make_async_copy(src, dst, sem).start()


def remote(src, dst, send, recv, device):
    return pltpu.make_async_remote_copy(
        src_ref=src, dst_ref=dst, send_sem=send, recv_sem=recv, device_id=device, device_id_type=MESH
    )


def kernel(
    sz, inp_raw, cot_raw, w_raw, resets, valid_mask, recurrence, state_bias, norm_gain, norm_shift,
    out, grad_inp, grad_rec, grad_bias, grad_gain, grad_shift, gout,
    mainbuf, wbuf, ysend, yrecv, own, xbuf, states, carry_in, chunk_a, chunk_aex, chunk_s0,
    keepf, validf, flagbuf, par, parblk, pre_send, pre_recv, ex_send, ex_recv, e1_send, e1_recv,
    scal, slopes, s1ex, dbuf, cex, aexr, dpbuf, pkeep, sibsend, sibrecv, xrecv, gw, gall, gpart, gleave, grelay,
    small, small_send, small_recv, outbuf, raw, blocks, wst, wx, outg, ging, smallg, blank,
    raw_ls, wst_ls, in_ss, in_fs, in_rs, cot_ss, cot_rs, par_ss, par_rs, flag_ss, flag_rs, w_ss, w_rs, w_fs, w_ps,
    pre_ss, pre_rs, mx_ss, mx_rs, ms_ss, ms_rs, mf_ss, mf_rs, y_ss, y_rs, ex_ss, ex_rs,
    o_ss, o_rs, e1_ss, e1_rs, dp_ss, dp_rs, sb_ss, sb_rs, xp_ss, xp_rs,
    gi_ss, gi_rs, ga_ss, ga_rs, go_ss, gr_rs, gx_ss, gx_rs, gl_ss, gl_rs, gs_ss, gs_rs, st_ss, st_rs, sm_ss, sm_rs,
):
    nz, bw, items, groups, steps = sz.nz, sz.bw, sz.items, sz.groups, sz.steps
    pieces, seqs = sz.pieces, sz.seqs
    s, r = lax.axis_index("section"), lax.axis_index("rows")
    y, x, z, c = s // 2, s % 2, r // 2, r % 2
    s_x, s_y, s_d = s + 1 - 2 * x, s + 2 - 4 * y, 3 - s
    r_c = r + 1 - 2 * c
    to_x, to_y, to_d, to_c = (s_x, r), (s_y, r), (s_d, r), (s, r_c)
    j_own, j_x, j_c, j_xc = 2 * x + c, 2 * (1 - x) + c, 2 * x + 1 - c, 2 * (1 - x) + 1 - c
    me = 2 * s + c
    part, half, last = sz.part, sz.half, sz.last
    mine = SECTIONS - 1 - s
    pair_half = z % 2
    to_pair = (s, r + 2 - 4 * pair_half)
    sub = lax.broadcasted_iota(jnp.int32, (GROUP, bw), 0)
    place = sub % pieces

    def z_peer(distance):
        return (s, 2 * ((z + distance) % nz) + c)

    def z_slot(p):
        return (z - p + nz - 1) % nz

    def by_seq(rows):
        value = jnp.broadcast_to(rows[seqs - 1], (GROUP, bw))
        for q in range(seqs - 2, -1, -1):
            value = jnp.where(sub < (q + 1) * pieces, jnp.broadcast_to(rows[q], (GROUP, bw)), value)
        return value

    def last_of(value, q):
        return value[(q + 1) * pieces - 1 : (q + 1) * pieces]

    def first_of(value, q):
        return value[q * pieces : q * pieces + 1]

    def entering(a, b, reverse):
        out_a, out_b = [None, None], [None, None]
        t_a = t_b = None
        for h in (1, 0) if reverse else (0, 1):
            ia, ib = a[h], b[h]
            hop = 1
            while hop < pieces:
                if reverse:
                    ok, shift = place < pieces - hop, GROUP - hop
                else:
                    ok, shift = place >= hop, hop
                pa = jnp.where(ok, pltpu.roll(ia, shift, 0), 1.0)
                pb = jnp.where(ok, pltpu.roll(ib, shift, 0), 0.0)
                ib = ia * pb + ib
                ia = ia * pa
                hop *= 2
            if reverse:
                ok, shift, edge = place < pieces - 1, GROUP - 1, first_of
            else:
                ok, shift, edge = place >= 1, 1, last_of
            xa = jnp.where(ok, pltpu.roll(ia, shift, 0), 1.0)
            xb = jnp.where(ok, pltpu.roll(ib, shift, 0), 0.0)
            na = [edge(ia, q) for q in range(seqs)]
            nb = [edge(ib, q) for q in range(seqs)]
            if t_a is not None:
                ea, eb = by_seq(t_a), by_seq(t_b)
                xb = xa * eb + xb
                xa = xa * ea
                nb = [na[q] * t_b[q] + nb[q] for q in range(seqs)]
                na = [na[q] * t_a[q] for q in range(seqs)]
            t_a, t_b = na, nb
            out_a[h], out_b[h] = xa, xb
        return out_a, out_b, t_a, t_b

    def pack(rows):
        rows = rows + [jnp.zeros((1, bw), F32)] * (8 - len(rows))
        value = jnp.zeros((8, bw), F32)
        for q, row in enumerate(rows):
            value = jnp.where(sub == q, jnp.broadcast_to(row, (8, bw)), value)
        return value

    def total(value):
        return jnp.sum(value, axis=0, keepdims=True)

    def over_z(body, start):
        return lax.fori_loop(0, nz, body, start, unroll=nz <= 8)

    def send_z(src, dst_of, send_sem, recv_sem):
        def one(k, _):
            remote(src, dst_of(k - 1), send_sem, recv_sem, z_peer(k)).start()
            return 0

        lax.fori_loop(1, nz, one, 0, unroll=nz <= 8)

    def not_me(t, h):
        return jnp.logical_or(t != s, h != c)

    blank[...] = jnp.zeros((GROUP, bw), F32)

    def width(e):
        return bw if e < 7 else last

    barrier = pltpu.get_barrier_semaphore()
    for t in (s, s_x, s_y, s_d):
        for q in (r, r_c):
            if not (t is s and q is r):
                pl.semaphore_signal(barrier, inc=1, device_id=(t, q), device_id_type=MESH)

    def greet(k, _):
        pl.semaphore_signal(barrier, inc=1, device_id=z_peer(k), device_id_type=MESH)
        return 0

    lax.fori_loop(1, nz, greet, 0)

    local_copy(inp_raw.at[0], raw.at[0], raw_ls.at[0])
    local_copy(cot_raw.at[0], raw.at[1], raw_ls.at[1])
    w_rows = [(1 - y, 2 * pair_half), (1 - y, 2 * pair_half + 1), (y, 2 * pair_half), (y, 2 * pair_half + 1)]
    w_rows += [(y, 2 - 2 * pair_half), (y, 3 - 2 * pair_half)]

    def w_load(n, wait):
        yy, j = w_rows[n]
        k, slot = 4 * yy + j, n % 3

        def go(rows):
            copy = pltpu.make_async_copy(
                w_raw.at[0, pl.ds(pl.multiple_of(k * bw, bw), rows)], wst.at[slot, pl.ds(0, rows)], wst_ls.at[slot]
            )
            copy.wait() if wait else copy.start()

        @pl.when(k < 7)
        def _():
            go(bw)

        @pl.when(k == 7)
        def _():
            if not wait:
                wst[slot, last:] = jnp.zeros((bw - last, sz.hidden), BF16)
            go(last)

    def w_cut(n, column, toward, dst):
        slot = n % 3
        for e in range(8):
            @pl.when(column == e % 4)
            def _(e=e):
                place_of = jnp.where(toward == e // 4, 0, 1)
                if e == 7:
                    dst[place_of] = jnp.zeros((bw, bw), BF16)
                dst[place_of, :, : width(e)] = wst[slot, :, e * bw : e * bw + width(e)]

    for n in range(3):
        w_load(n, False)

    parblk[...] = jnp.zeros(parblk.shape, F32)
    for n, ref in enumerate((recurrence, state_bias, norm_gain, norm_shift)):
        for e in range(8):
            parblk[e, n : n + 1, : width(e)] = ref[0:1, e * bw : e * bw + width(e)]
    par[s] = parblk[me]
    flagbuf[c] = jnp.zeros(flagbuf.shape[1:], F32)
    for n, ref in enumerate((resets, valid_mask)):
        for m in range(4):
            row = seqs * (4 * n + m)
            flagbuf[c, row : row + seqs, : sz.frames] = ref[SECTIONS - 1 - m].astype(F32)

    def w_unit(l, j, n):
        return wbuf.at[l, n, pl.ds(pl.multiple_of(j * bw, bw), bw)]

    def w_cross():
        for k in range(2):
            j = 2 * pair_half + k
            for m, t in enumerate((s_x, s_y, s_d)):
                for n in range(2):
                    src = wx.at[m, n, pl.ds(k * bw, bw)]
                    remote(src, w_unit(s, j, n), w_ss.at[m, k, n], w_rs.at[s, j, n], (t, r)).start()

    for n in range(6):
        if n == 4:
            pl.semaphore_wait(barrier, 7 + nz - 1)

            @pl.when(s == 0)
            def _():
                w_cross()

        w_load(n, True)
        j = w_rows[n][1]
        rows = pl.ds(pl.multiple_of(j * bw, bw), bw)
        half_rows = pl.ds((n % 2) * bw, bw)
        if n < 2:
            w_cut(n, j_own, 1 - y, wx.at[1, :, half_rows])
            w_cut(n, j_x, 1 - y, wx.at[2, :, half_rows])
        elif n < 4:
            w_cut(n, j_x, y, wx.at[0, :, half_rows])
            w_cut(n, j_own, y, wbuf.at[s, :, rows])
        else:
            w_cut(n, j_own, y, wbuf.at[s, :, rows])
        if n + 3 < 6:
            w_load(n + 3, False)

    row = lax.broadcasted_iota(jnp.int32, (half, half), 0)
    col = lax.broadcasted_iota(jnp.int32, (half, half), 1)
    frame_of = (row % GROUP // pieces) * sz.frames + (row % pieces) * steps + row // GROUP
    permute = (col == frame_of).astype(BF16)
    row_of = row
    frame_at = (col % GROUP // pieces) * sz.frames + (col % pieces) * steps + col // GROUP

    def cut_frames(n):
        wait_bytes(raw.at[n], raw_ls.at[n])
        for e in range(8):
            value = raw[n, :, :, e * bw : e * bw + width(e)].reshape(half, width(e))
            if e == 7:
                blocks[n, e] = jnp.zeros((half, bw), BF16)
            blocks[n, e, :, : width(e)] = jnp.dot(permute, value, preferred_element_type=F32).astype(BF16)

    cut_frames(0)

    for n, t in enumerate((s_x, s_y, s_d)):
        remote(parblk.at[2 * t + c], par.at[s], par_ss.at[n], par_rs.at[s], (t, r)).start()
    remote(flagbuf.at[c], flagbuf.at[c], flag_ss.at[0], flag_rs.at[c], to_c).start()

    in_dst = mainbuf.at[mine, :, c]
    near, far = blocks.at[0, pl.ds(4 * y, 4)], blocks.at[0, pl.ds(4 - 4 * y, 4)]
    remote(far, in_dst, in_ss.at[2], in_rs.at[mine, c], to_d).start()
    remote(near, in_dst, in_ss.at[0], in_rs.at[mine, c], to_x).start()
    remote(far, in_dst, in_ss.at[1], in_rs.at[mine, c], to_y).start()
    remote(near, in_dst, in_ss.at[3], in_rs.at[mine, c], to_c).start()
    local_copy(near, in_dst, in_rs.at[mine, c])

    @pl.when(s != 0)
    def _():
        w_cross()

    wait_bytes(flagbuf.at[1 - c], flag_rs.at[1 - c])
    row = lax.broadcasted_iota(jnp.int32, (half, sz.frames), 0)
    col = lax.broadcasted_iota(jnp.int32, (half, sz.frames), 1)
    at_frame = col == (row % pieces) * steps + row // GROUP
    of_seq = row % GROUP // pieces
    ones = jnp.ones((sz.frames, bw), BF16)

    def masks_of(m, _):
        for h in range(2):
            lo, hi = h * steps, (h + 1) * steps
            for n in range(2):
                flags = jnp.zeros((half, sz.frames), F32)
                for q in range(seqs):
                    line = flagbuf[h, pl.ds(seqs * (4 * n + m) + q, 1), : sz.frames]
                    flags = jnp.where(jnp.logical_and(at_frame, of_seq == q), line, flags)
                value = jnp.dot(flags.astype(BF16), ones, preferred_element_type=F32).reshape(steps, GROUP, bw)
                if n == 0:
                    keepf[m, lo:hi] = 1.0 - value
                else:
                    validf[m, lo:hi] = value
        return 0

    lax.fori_loop(0, 4, masks_of, 0)
    for t in (s_x, s_y, s_d):
        wait_bytes(par.at[t], par_rs.at[t])

    def decays_of(i, _):
        l, m = i // 4, i % 4
        u = jnp.broadcast_to(par[l, 0:1], (GROUP, bw))
        a_h, v_h = [], []
        for h in range(2):
            a = jnp.ones((GROUP, bw), F32)
            v = jnp.zeros((GROUP, bw), F32)
            for t in range(steps):
                d = u * keepf[m, h * steps + t]
                a = d * a
                v = d * v + 1.0
            a_h.append(a)
            v_h.append(v)
        xa, xb, ta, tb = entering(a_h, v_h, False)
        for h in range(2):
            chunk_a[i, h] = a_h[h]
            chunk_aex[i, h] = xa[h]
            chunk_s0[i, h] = xb[h]
        valid_count = total(jnp.sum(validf[m], axis=0))
        value = pack(ta + tb + [valid_count])
        pre_send[i] = value
        pre_recv[nz - 1, i] = value
        return 0

    lax.fori_loop(0, items, decays_of, 0)

    def send_decays(l):
        some = pl.ds(4 * l, 4)
        send_z(pre_send.at[some], lambda k: pre_recv.at[k, some], pre_ss.at[l], pre_rs.at[l])

    send_decays(0)

    def inputs_on(slot):
        block = mainbuf.at[slot, :, c]

        @pl.when(slot != mine)
        def _():
            wait_bytes(block, in_rs.at[slot, c])
            remote(block, block, in_fs.at[slot], in_rs.at[slot, c], to_c).start()

        @pl.when(slot == mine)
        def _():
            wait_bytes(block, in_rs.at[slot, c])

    for slot in range(3):
        inputs_on(slot)

    def w_pass(l, k, n):
        j = 2 * pair_half + k

        @pl.when(l != s)
        def _():
            wait_bytes(w_unit(l, j, n), w_rs.at[l, j, n])
            remote(w_unit(l, j, n), w_unit(l, j, n), w_fs.at[l, k, n], w_ps.at[l, k, n], to_pair).start()

    def w_arrive(l):
        @pl.when(l != s)
        def _():
            for k in range(2):
                for n in range(2):
                    wait_bytes(w_unit(l, 2 - 2 * pair_half + k, n), w_ps.at[l, k, n])

    for n in range(2):
        w_pass(0, 0, n)

    for n in range(2):
        w_pass(0, 1, n)
    cut_frames(1)
    def cotangent_out(e):
        t, h = (s, s_x, s_y, s_d)[e // 2], e % 2
        src = blocks.at[1, 2 * t + h]

        @pl.when(not_me(t, h))
        def _():
            remote(src, dbuf.at[mine, c], cot_ss.at[t, h], cot_rs.at[mine, c], (t, 2 * z + h)).start()

        @pl.when(jnp.logical_not(not_me(t, h)))
        def _():
            local_copy(src, dbuf.at[mine, c], cot_rs.at[mine, c])

    def arrived(i):
        block = mainbuf.at[i, j_x]
        wait_bytes(block, mx_rs.at[i])
        remote(block, block, mf_ss.at[i], mf_rs.at[i], to_c).start()

    def project(i):
        l, m = i // 4, i % 4

        @pl.when(m == 0)
        def _():
            w_arrive(l)

        @pl.when(l == 0)
        def _():
            wait_bytes(mainbuf.at[i, :, 1 - c], in_rs.at[m, 1 - c])

        @pl.when(l > 0)
        def _():
            wait_bytes(mainbuf.at[i, j_c], ms_rs.at[i])
            wait_bytes(mainbuf.at[i, j_xc], mf_rs.at[i])
            wait_bytes(ysend.at[m], y_ss.at[m])

        def to_half(n):
            acc = jnp.zeros((sz.rows, bw), F32)
            for j in range(4):
                acc = acc + jnp.dot(
                    mainbuf[i, j].reshape(sz.rows, bw), wbuf[l, n, j * bw : (j + 1) * bw], preferred_element_type=F32
                )
            return acc

        ysend[m] = to_half(1).astype(BF16)
        remote(ysend.at[m], yrecv.at[i % 8], y_ss.at[m], y_rs.at[i % 8], to_y).start()
        own[m] = to_half(0).reshape(groups, GROUP, bw)

    def moments(i):
        l, m = i // 4, i % 4
        wait_bytes(yrecv.at[i % 8], y_rs.at[i % 8])
        pre = own[m] + yrecv[i % 8].astype(F32).reshape(groups, GROUP, bw)
        valid = validf[m]
        pre_sum = total(jnp.sum(pre * valid, axis=0))
        local_count = pre_send[i, 2 * seqs : 2 * seqs + 1]
        pivot = pre_sum / jnp.maximum(local_count, 1.0)
        shifted = pre - pivot
        xbuf[i] = shifted
        square = total(jnp.sum(shifted * shifted * valid, axis=0))
        u = jnp.broadcast_to(par[l, 0:1], (GROUP, bw))
        ends = []
        for h in range(2):
            v = jnp.zeros((GROUP, bw), F32)
            for t in range(steps):
                v = (u * keepf[m, h * steps + t]) * v + shifted[h * steps + t]
            ends.append(v)
        unused_a, xb, unused_t, tb = entering([chunk_a[i, 0], chunk_a[i, 1]], ends, False)
        for h in range(2):
            s1ex[m, h] = xb[h]
        value = pack([pre_sum, square] + tb)

        @pl.when(l > 0)
        def _():
            wait_bytes(ex_recv.at[i % 8, pl.ds(0, nz - 1)], ex_ss.at[m])

        ex_send[m] = value
        ex_recv[i % 8, nz - 1] = value
        send_z(ex_send.at[m], lambda k: ex_recv.at[i % 8, k], ex_ss.at[m], ex_rs.at[i % 8])

    def finish_layer(i):
        l, m = i // 4, i % 4

        @pl.when(m == 0)
        def _():
            wait_bytes(pre_recv.at[pl.ds(0, nz - 1), pl.ds(4 * l, 4)], pre_rs.at[l])

        wait_bytes(ex_recv.at[i % 8, pl.ds(0, nz - 1)], ex_rs.at[i % 8])
        u, bias = par[l, 0:1], par[l, 1:2]
        gain, shift = par[l, 2:3], par[l, 3:4]

        def add_sum(p, carry):
            slot = z_slot(p)
            return (
                carry[0] + ex_recv[i % 8, slot, 0:1],
                carry[1] + pre_recv[slot, i, 2 * seqs : 2 * seqs + 1],
            )

        zero = jnp.zeros((1, bw), F32)
        sum_all, count_all = over_z(add_sum, (zero, zero))
        mean = sum_all / count_all

        def pivot_of(slot):
            count = pre_recv[slot, i, 2 * seqs : 2 * seqs + 1]
            return ex_recv[i % 8, slot, 0:1] / jnp.maximum(count, 1.0), count

        def add_square(p, carry):
            slot = z_slot(p)
            pivot, count = pivot_of(slot)
            return carry + ex_recv[i % 8, slot, 1:2] + count * (pivot - mean) * (pivot - mean)

        var = over_z(add_square, zero) / count_all
        inv = lax.rsqrt(var + norm_eps)
        alpha = gain * inv

        def hop_in(p, carry):
            slot = z_slot(p)
            pivot, unused = pivot_of(slot)
            beta = shift + alpha * (pivot - mean)
            after = []
            for q in range(seqs):
                value = (
                    alpha * ex_recv[i % 8, slot, 2 + q : 3 + q]
                    + beta * pre_recv[slot, i, seqs + q : seqs + q + 1]
                    + pre_recv[slot, i, q : q + 1] * carry[q]
                )
                after.append(jnp.where(p < z, value, carry[q]))
            return tuple(after)

        enter = by_seq(list(over_z(hop_in, (zero,) * seqs)))
        pivot, unused = pivot_of(nz - 1)
        beta = shift + alpha * (pivot - mean)
        offset = (pivot - mean) * inv
        scal[i] = pack([alpha, 1.0 / count_all])
        wide = [jnp.broadcast_to(v, (GROUP, bw)) for v in (u, bias, alpha, beta, inv, offset)]
        u, bias, alpha, beta, inv, offset = wide
        side = mainbuf.at[jnp.maximum(i - 4, 0), j_own]
        odd = (l % 2).astype(F32)
        to_next = l < SECTIONS - 1
        target = jnp.minimum(i + 4, items - 1)
        for h in range(2):
            v = alpha * s1ex[m, h] + beta * chunk_s0[i, h] + chunk_aex[i, h] * enter
            carry_in[i, h] = v
            hidden = []
            for t in range(steps):
                g = h * steps + t
                shifted = xbuf[i, g]
                v = (u * keepf[m, g]) * v + (alpha * shifted + beta)
                states[i, g] = v
                xbuf[i, g] = shifted * inv + offset
                w = v + bias
                hidden.append(validf[m, g] * (w * jax.nn.sigmoid(w)))
            value = jnp.concatenate(hidden, axis=0) + odd * side[h].astype(F32)
            outbuf[m, h] = value.astype(BF16)

        @pl.when(to_next)
        def _():
            block = mainbuf.at[target, j_own]
            block[...] = outbuf[m]
            remote(block, block, mx_ss.at[target], mx_rs.at[target], to_x).start()
            remote(block, block, ms_ss.at[target], ms_rs.at[target], to_c).start()

    def carry_slopes(i):
        l, m = i // 4, i % 4
        u = jnp.broadcast_to(par[l, 0:1], (GROUP, bw))
        a_h = [chunk_a[i, 0], chunk_a[i, 1]]
        xa, unused_b, unused_a, unused_t = entering(a_h, [jnp.zeros((GROUP, bw), F32)] * 2, True)
        sum_one = jnp.zeros((GROUP, bw), F32)
        sum_normed = jnp.zeros((GROUP, bw), F32)
        for h in (1, 0):
            v = xa[h]
            for t in range(steps - 1, -1, -1):
                g = h * steps + t
                sum_one = sum_one + v
                sum_normed = sum_normed + v * xbuf[i, g]
                v = (u * keepf[m, g]) * v
        rows = []
        for value in (sum_one, sum_normed):
            for q in range(seqs):
                inside = jnp.logical_and(sub >= q * pieces, sub < (q + 1) * pieces)
                rows.append(total(jnp.where(inside, value, 0.0)))
        slopes[i] = pack(rows)

    def back_index(b):
        l, m = SECTIONS - 1 - b // 4, b % 4
        return l, m, l * 4 + m

    def act_back(b):
        l, m, i = back_index(b)

        @pl.when(b < 4)
        def _():
            for h in range(2):
                wait_bytes(dbuf.at[m, h], cot_rs.at[m, h])

        u = jnp.broadcast_to(par[l, 0:1], (GROUP, bw))
        bias = jnp.broadcast_to(par[l, 1:2], (GROUP, bw))
        ends = [None, None]
        sum_act = jnp.zeros((GROUP, bw), F32)
        for h in (1, 0):
            grad = dbuf[b % 12, h].astype(F32).reshape(steps, GROUP, bw)
            v = jnp.zeros((GROUP, bw), F32)
            for t in range(steps - 1, -1, -1):
                g = h * steps + t
                w = states[i, g] + bias
                sg = jax.nn.sigmoid(w)
                da = grad[t] * validf[m, g] * (sg * (1.0 + w * (1.0 - sg)))
                own[m, g] = da
                sum_act = sum_act + da
                v = (u * keepf[m, g]) * (da + v)
            ends[h] = v
        xa, xb, unused, tb = entering([chunk_a[i, 0], chunk_a[i, 1]], ends, True)
        for h in range(2):
            aexr[m, h] = xa[h]
            cex[m, h] = xb[h]
        sum_local = jnp.zeros((GROUP, bw), F32)
        sum_normed = jnp.zeros((GROUP, bw), F32)
        for h in (1, 0):
            v = xb[h]
            for t in range(steps - 1, -1, -1):
                g = h * steps + t
                ds = own[m, g] + v
                sum_local = sum_local + ds
                sum_normed = sum_normed + ds * xbuf[i, g]
                v = (u * keepf[m, g]) * ds
        value = pack(tb + [total(sum_local), total(sum_normed)] + [slopes[i, n : n + 1] for n in range(2 * seqs)])

        @pl.when(b >= 4)
        def _():
            wait_bytes(e1_recv.at[b % 8, pl.ds(0, nz - 1)], e1_ss.at[m])

        e1_send[m] = value
        e1_recv[b % 8, nz - 1] = value
        send_z(e1_send.at[m], lambda k: e1_recv.at[b % 8, k], e1_ss.at[m], e1_rs.at[b % 8])
        add_small(l, m, 3, sum_act)

    def add_small(l, m, n, value):
        added = jnp.where(sub == n, jnp.broadcast_to(total(value), (GROUP, bw)), 0.0)
        if n == 3:
            before = jnp.where(m == 0, 0.0, 1.0)
            small[l] = jnp.where(before > 0.0, small[l], 0.0) + added
        else:
            small[l] = small[l] + added

    def state_back(b):
        l, m, i = back_index(b)
        wait_bytes(e1_recv.at[b % 8, pl.ds(0, nz - 1)], e1_rs.at[b % 8])
        zero = blank[...]

        def line(value):
            return jnp.broadcast_to(value, (GROUP, bw))

        def hop_in(n, carry):
            p = nz - 1 - n
            slot = z_slot(p)
            sum_shift, sum_gain = carry[0], carry[1]
            flow, enter = carry[2 : 2 + seqs], carry[2 + seqs :]
            sum_shift = sum_shift + line(e1_recv[b % 8, slot, seqs : seqs + 1])
            sum_gain = sum_gain + line(e1_recv[b % 8, slot, seqs + 1 : seqs + 2])
            after, inside = [], []
            for q in range(seqs):
                one = seqs + 2 + q
                normed = one + seqs
                sum_shift = sum_shift + flow[q] * line(e1_recv[b % 8, slot, one : one + 1])
                sum_gain = sum_gain + flow[q] * line(e1_recv[b % 8, slot, normed : normed + 1])
                inside.append(jnp.where(p == z, flow[q], enter[q]))
                after.append(line(e1_recv[b % 8, slot, q : q + 1]) + line(pre_recv[slot, i, q : q + 1]) * flow[q])
            return (sum_shift, sum_gain, *after, *inside)

        sum_shift, sum_gain, *rest = over_z(hop_in, (zero,) * (2 + 2 * seqs))
        enter = by_seq(rest[seqs:])
        u = jnp.broadcast_to(par[l, 0:1], (GROUP, bw))
        alpha = jnp.broadcast_to(scal[i, 0:1], (GROUP, bw))
        per_count = scal[i, 1:2]
        gain_part, shift_part = sum_gain * per_count, sum_shift * per_count
        sum_rate = jnp.zeros((GROUP, bw), F32)
        rows = [None] * groups
        for h in (1, 0):
            v = cex[m, h] + aexr[m, h] * enter
            for t in range(steps - 1, -1, -1):
                g = h * steps + t
                keep = keepf[m, g]
                ds = own[m, g] + v
                before = carry_in[i, h] if t == 0 else states[i, g - 1]
                sum_rate = sum_rate + (ds * keep) * before
                v = (u * keep) * ds
                rows[g] = alpha * (ds - validf[m, g] * (shift_part + xbuf[i, g] * gain_part))
        @pl.when(b >= 8)
        def _():
            wait_bytes(dpbuf.at[b % 8, 0], dp_ss.at[b % 8])

        dpbuf[b % 8, 0] = jnp.concatenate(rows, axis=0).astype(BF16)
        remote(dpbuf.at[b % 8, 0], dpbuf.at[b % 8, 1], dp_ss.at[b % 8], dp_rs.at[b % 8], to_y).start()
        add_small(l, m, 2, sum_rate)
        small[l] = small[l] + pack([sum_gain[0:1], sum_shift[0:1]])

    nt = (((1,), (1,)), ((), ()))
    tn = (((0,), (0,)), ((), ()))

    def input_back(b):
        l, m, i = back_index(b)
        wait_bytes(dpbuf.at[b % 8, 1], dp_rs.at[b % 8])
        dp_own, dp_other = dpbuf[b % 8, 0], dpbuf[b % 8, 1]

        def toward(j):
            rows = pl.ds(pl.multiple_of(j * bw, bw), bw)
            first = lax.dot_general(dp_own, wbuf[l, 0, rows], nt, preferred_element_type=F32)
            return first + lax.dot_general(dp_other, wbuf[l, 1, rows], nt, preferred_element_type=F32)

        @pl.when(b >= 4)
        def _():
            wait_bytes(sibsend.at[m], sb_ss.at[m])

        sibsend[m, 0] = toward(j_c).astype(BF16)
        sibsend[m, 1] = toward(j_xc).astype(BF16)
        remote(sibsend.at[m], sibrecv.at[b % 8], sb_ss.at[m], sb_rs.at[b % 8], to_c).start()
        pkeep[m, 0] = toward(j_own)
        pkeep[m, 1] = toward(j_x)

    def weight_back(b):
        l, m, i = back_index(b)
        dp = jnp.concatenate([dpbuf[b % 8, 0], dpbuf[b % 8, 1]], axis=1)
        count = nz // 4
        for j in range(4):
            rows = pl.ds(j * bw, bw)
            new = lax.dot_general(mainbuf[i, j].reshape(sz.rows, bw), dp, tn, preferred_element_type=F32)

            @pl.when(m == 0)
            def _(new=new, rows=rows):
                gw[rows] = new

            @pl.when(jnp.logical_and(m > 0, m < 3))
            def _(new=new, rows=rows):
                gw[rows] = gw[rows] + new

            @pl.when(m == 3)
            def _(new=new, rows=rows, j=j):
                all_items = (gw[rows] + new).astype(BF16)
                for n in range(2):
                    value = all_items[:, n * bw : (n + 1) * bw].reshape(count, part, bw)
                    gall[l, j * count : (j + 1) * count, n] = value

    period = 2 * nz

    def unit_of(q, v):
        return jnp.where(q < 2, SECTIONS - 1 - q, 1 - v), jnp.where(q < 2, v, q - 2)

    def round_of(l, n):
        return jnp.where(l < 2, 2 + n, SECTIONS - 1 - l), jnp.where(l < 2, 1 - l, n)

    to_end, to_start = (s, r + 2), (s, r - 2)

    def g_from(p, v, up):
        return gpart.at[p + 1 if up else p, v], gr_rs.at[p + 1 if up else p, v]

    def relayed(p):
        return jnp.abs(z - p) % 2 == 0

    def g_ready(l, p, n, cross):
        if not cross:
            return
        unit, place_out = gall.at[l, p, n], gout.at[c, s, p, n]
        by_relay = jnp.logical_and(l == s_d, relayed(p))

        @pl.when(jnp.logical_and(l != s, jnp.logical_not(by_relay)))
        def _():
            remote(unit, place_out, gx_ss.at[l, p, n], gx_rs.at[s, p, n], (l, r)).start()

        @pl.when(by_relay)
        def _():
            remote(unit, grelay.at[p, n], gx_ss.at[l, p, n], gl_rs.at[p, n], to_y).start()

        @pl.when(l == s)
        def _():
            local_copy(unit, place_out, gx_rs.at[s, p, n])
            remote(unit, place_out, gs_ss.at[s, p, n], gs_rs.at[s, p, n], to_c).start()

    def g_step(g, cross):
        for up in (True, False):
            place_z = z if up else nz - 1 - z
            ahead = nz - 1 - place_z
            t = g - 2 * place_z
            q = t // period
            k = t % period
            v = k % 2
            l, n = unit_of(q, v)
            inside = jnp.logical_and(t >= 0, q < SECTIONS)

            @pl.when(jnp.logical_and(inside, k < 2 * ahead))
            def _(up=up, place_z=place_z, q=q, k=k, l=l, n=n, v=v):
                far = nz - 1 - k // 2
                p = far if up else nz - 1 - far
                unit = gall.at[l, p, n]

                buf, sem = g_from(p, v, up)
                way, slot = 0 if up else 1, k % 4
                leaving = gleave.at[way, slot]

                @pl.when(jnp.logical_or(q > 0, k >= 4))
                def _():
                    wait_bytes(leaving, ga_ss.at[way, slot])

                @pl.when(place_z > 0)
                def _():
                    wait_bytes(buf, sem)
                    leaving[...] = (unit[...].astype(F32) + buf[...].astype(F32)).astype(BF16)

                @pl.when(place_z == 0)
                def _():
                    leaving[...] = unit[...]

                remote(leaving, buf, ga_ss.at[way, slot], sem, to_end if up else to_start).start()

            @pl.when(jnp.logical_and(inside, k >= 2 * ahead))
            def _(up=up, ahead=ahead, k=k, l=l, n=n, v=v):
                back = (k - 2 * ahead) // 2
                p = z - back if up else z + back
                unit = gall.at[l, p, n]

                @pl.when(back == 0)
                def _():
                    if up:
                        whole = unit[...].astype(F32)
                        for way, there in ((True, z > 0), (False, z < nz - 1)):
                            buf, sem = g_from(p, v, way)

                            @pl.when(there)
                            def _(buf=buf, sem=sem):
                                wait_bytes(buf, sem)

                            whole = whole + jnp.where(there, buf[...].astype(F32), 0.0)
                        unit[...] = whole.astype(BF16)
                        g_ready(l, p, n, cross)

                @pl.when(back > 0)
                def _():
                    wait_bytes(unit, ga_rs.at[l, p, n])
                    g_ready(l, p, n, cross)

                @pl.when(ahead > 0)
                def _():
                    way = 0 if up else 1
                    remote(unit, unit, go_ss.at[l, p, n, way], ga_rs.at[l, p, n], to_end if up else to_start).start()

    def cross_back(b):
        m = b % 4
        wait_bytes(sibrecv.at[b % 8], sb_rs.at[b % 8])

        @pl.when(b < 4)
        def _():
            wait_bytes(ysend.at[m], y_ss.at[m])

        @pl.when(b >= 4)
        def _():
            wait_bytes(ysend.at[m], xp_ss.at[m])

        ysend[m] = (pkeep[m, 1] + sibrecv[b % 8, 1].astype(F32)).astype(BF16)
        remote(ysend.at[m], xrecv.at[b % 8], xp_ss.at[m], xp_rs.at[b % 8], to_x).start()
        pkeep[m, 0] = pkeep[m, 0] + sibrecv[b % 8, 0].astype(F32)

    def join_back(b):
        l, m, i = back_index(b)
        wait_bytes(xrecv.at[b % 8], xp_rs.at[b % 8])
        even = (1 - l % 2).astype(F32)
        side = dbuf[jnp.maximum(b - 4, 0) % 12].astype(F32).reshape(sz.rows, bw)
        value = pkeep[m, 0] + xrecv[b % 8].astype(F32) + even * side
        dbuf[(b + 4) % 12] = value.astype(BF16).reshape(2, sz.half, bw)

    def frames_out(m):
        t = SECTIONS - 1 - m
        for h in range(2):
            grads = dbuf.at[(items + m) % 12, h]

            @pl.when(not_me(t, h))
            def _(h=h, grads=grads):
                remote(outbuf.at[m, h], outg.at[me], o_ss.at[m, h], o_rs.at[me], (t, 2 * z + h)).start()
                remote(grads, ging.at[me], gi_ss.at[m, h], gi_rs.at[me], (t, 2 * z + h)).start()

            @pl.when(jnp.logical_not(not_me(t, h)))
            def _(h=h, grads=grads):
                local_copy(outbuf.at[m, h], outg.at[me], o_rs.at[me])
                local_copy(grads, ging.at[me], gi_rs.at[me])

    first_step = 6


    def forward_tick(k):
        @pl.when(k < items)
        def _():
            project(k)

        @pl.when(k == 1)
        def _():
            inputs_on(3)

        @pl.when(jnp.logical_and(k >= 1, k < items + 1))
        def _():
            moments(k - 1)

        @pl.when(jnp.logical_and(k >= 2, k < items + 2))
        def _():
            finish_layer(k - 2)

        @pl.when(jnp.logical_and(k >= 2, k < items + 2))
        def _():
            carry_slopes(k - 2)

        @pl.when(jnp.logical_and(k + 1 >= 4, k + 1 < items))
        def _():
            arrived(k + 1)

        for e in range(8):
            @pl.when(k == 3 + e)
            def _(e=e):
                cotangent_out(e)

        @pl.when(k < 11)
        def _():
            @pl.when(k == 0)
            def _():
                w_pass(1, 0, 0)

            unit = k + 1
            for n in range(4):
                @pl.when(unit % 4 == n)
                def _(n=n):
                    w_pass(unit // 4 + 1, n // 2, n % 2)

            @pl.when(k % 4 == 1)
            def _():
                send_decays(k // 4 + 1)

    def backward_tick(k):
        @pl.when(k >= 4)
        def _():
            join_back(k - 4)

        @pl.when(jnp.logical_and(k >= 0, k < items))
        def _():
            act_back(k)

        @pl.when(jnp.logical_and(k >= 1, k < items + 1))
        def _():
            state_back(k - 1)

        @pl.when(k >= first_step)
        def _():
            g_step(k - first_step, False)

        @pl.when(jnp.logical_and(k >= 2, k < items + 2))
        def _():
            input_back(k - 2)
            weight_back(k - 2)
            cross_back(k - 2)

    start = items - 2

    def tick(k, _):
        forward_tick(k)
        backward_tick(k - start)
        return 0

    lax.fori_loop(0, start + items + 4, tick, 0)

    small_send[...] = pack([small[l, n : n + 1] for l in range(SECTIONS) for n in (2, 3)])
    send_z(small_send, lambda k: small_recv.at[k], st_ss, st_rs)
    steps_done = items + 4 - first_step
    steps_all = SECTIONS * period + 2 * (nz - 1)

    def whole_at(l, p, n):
        q, v = round_of(l, n)
        return q * period + 2 * (nz - 1) + 2 * jnp.abs(z - p) + v

    def crosses_at(l, p, n):
        early = whole_at(l, p, n) < steps_done
        return jnp.where(early, steps_done + 2 * p + n, whole_at(l, p, n))

    def cross_early(g):
        p, n = (g - steps_done) // 2, (g - steps_done) % 2

        @pl.when(p < nz)
        def _():
            for l in range(SECTIONS):
                @pl.when(whole_at(l, p, n) < steps_done)
                def _(l=l):
                    g_ready(l, p, n, True)

    def relay_lag(l):
        return jnp.where(l < 2, 4, 12)

    def g_relay(g):
        def one(p, _):
            for n in range(2):
                @pl.when(jnp.logical_and(relayed(p), crosses_at(s_x, p, n) + relay_lag(s_x) == g))
                def _(n=n):
                    wait_bytes(grelay.at[p, n], gl_rs.at[p, n])
                    remote(grelay.at[p, n], gout.at[c, s_y, p, n], gl_ss.at[p, n], gx_rs.at[s_y, p, n], to_x).start()

            return 0

        lax.fori_loop(0, nz, one, 0)

    def g_to_other_core(g):
        lag = jnp.where(s < 2, 6, 14)

        def one(p, _):
            for n in range(2):
                sent = crosses_at(s, p, n) + lag

                def onward(t, n=n):
                    unit = gout.at[c, t, p, n]
                    wait_bytes(unit, gx_rs.at[t, p, n])
                    remote(unit, unit, gs_ss.at[t, p, n], gs_rs.at[t, p, n], to_c).start()

                @pl.when(sent == g)
                def _(onward=onward):
                    onward(s_x)
                    onward(s_y)

                @pl.when(sent + jnp.where(relayed(p), relay_lag(s), 0) == g)
                def _(onward=onward):
                    onward(s_d)

            return 0

        lax.fori_loop(0, nz, one, 0)

    def sum_small():
        wait_bytes(small_recv, st_rs)
        wait_bytes(small_recv, st_ss)

        def add_rest(k, carry):
            return carry + small_recv[k]

        sums = lax.fori_loop(0, nz - 1, add_rest, small_send[...])
        for l in range(SECTIONS):
            rate = jnp.broadcast_to(sums[2 * l : 2 * l + 1], (GROUP, bw))
            bias = jnp.broadcast_to(sums[2 * l + 1 : 2 * l + 2], (GROUP, bw))
            small[l] = jnp.where(sub == 2, rate, jnp.where(sub == 3, bias, small[l]))
        for t in range(SECTIONS):
            for h in range(2):
                @pl.when(not_me(t, h))
                def _(t=t, h=h):
                    remote(small.at[t], smallg.at[me], sm_ss.at[t, h], sm_rs.at[me], (t, 2 * z + h)).start()

                @pl.when(jnp.logical_not(not_me(t, h)))
                def _(t=t):
                    local_copy(small.at[t], smallg.at[me], sm_rs.at[me])

    restore = (row_of == frame_at).astype(BF16)

    def place_block(e):
        wait_bytes(outg.at[e], o_rs.at[e])
        wait_bytes(ging.at[e], gi_rs.at[e])
        for src, dst in ((outg, out), (ging, grad_inp)):
            value = jnp.dot(restore, src[e], preferred_element_type=F32).astype(BF16)
            value = value.reshape(seqs, sz.frames, bw)
            dst[0, :, :, e * bw : e * bw + width(e)] = value[:, :, : width(e)]

    def drain_layers():
        for l in range(SECTIONS):
            @pl.when(l != s)
            def _(l=l):
                for k in range(2):
                    for n in range(2):
                        wait_bytes(w_unit(l, k, n), w_fs.at[l, k, n])

            wait_bytes(pre_recv.at[pl.ds(0, nz - 1), pl.ds(4 * l, 4)], pre_ss.at[l])
            wait_bytes(ex_recv.at[l, pl.ds(0, nz - 1)], ex_ss.at[l])
            wait_bytes(e1_recv.at[l, pl.ds(0, nz - 1)], e1_ss.at[l])
            wait_bytes(sibsend.at[l], sb_ss.at[l])
            wait_bytes(ysend.at[l], xp_ss.at[l])
            for h in range(2):
                @pl.when(not_me(l, h))
                def _(l=l, h=h):
                    wait_bytes(dbuf.at[mine, c], cot_ss.at[l, h])
                    wait_bytes(small.at[l], sm_ss.at[l, h])

                @pl.when(not_me(SECTIONS - 1 - l, h))
                def _(l=l, h=h):
                    wait_bytes(outbuf.at[l, h], o_ss.at[l, h])
                    wait_bytes(dbuf.at[(items + l) % 12, h], gi_ss.at[l, h])

        def drain(i, _):
            @pl.when(i < 8)
            def _():
                wait_bytes(dpbuf.at[i, 0], dp_ss.at[i])

            @pl.when(i >= 4)
            def _():
                wait_bytes(mainbuf.at[i, j_own], mx_ss.at[i])
                wait_bytes(mainbuf.at[i, j_own], ms_ss.at[i])
                wait_bytes(mainbuf.at[i, j_x], mf_ss.at[i])

            return 0

        lax.fori_loop(0, items, drain, 0)
        for n in range(4):
            wait_bytes(in_dst, in_ss.at[n])
        for slot in range(4):
            @pl.when(slot != mine)
            def _(slot=slot):
                wait_bytes(in_dst, in_fs.at[slot])

        for n in range(3):
            wait_bytes(par.at[s], par_ss.at[n])
            for k in range(2):
                for m in range(2):
                    wait_bytes(wx.at[n, m, pl.ds(k * bw, bw)], w_ss.at[n, k, m])

        wait_bytes(flagbuf.at[c], flag_ss.at[0])

    def late_step(g, _):
        g_step(g, True)
        cross_early(g)
        g_relay(g)
        g_to_other_core(g)

        @pl.when(g == steps_done)
        def _():
            for m in range(4):
                frames_out(m)

        @pl.when(g == steps_done + 5)
        def _():
            sum_small()

        for e in range(8):
            @pl.when(g == steps_done + 16 + e)
            def _(e=e):
                place_block(e)

        @pl.when(g == steps_done + 24)
        def _():
            drain_layers()

        return 0

    lax.fori_loop(steps_done, max(steps_all + 10, steps_done + period + 26), late_step, 0)

    for e in range(8):
        wait_bytes(smallg.at[e], sm_rs.at[e])
        for n, dst in enumerate((grad_gain, grad_shift, grad_rec, grad_bias)):
            dst[0:1, e * bw : e * bw + width(e)] = smallg[e, n : n + 1, : width(e)]

    def drain_units(k, _):
        p, n = k // 2, k % 2
        unit = gall.at[0, p, n]
        for t in range(SECTIONS):
            wait_bytes(unit, gs_rs.at[t, p, n])
            wait_bytes(unit, gs_ss.at[t, p, n])

            @pl.when(t != s)
            def _(t=t):
                wait_bytes(unit, gx_ss.at[t, p, n])

            @pl.when(t == s)
            def _(t=t):
                wait_bytes(unit, gx_rs.at[t, p, n])

            @pl.when(jnp.logical_and(p <= z, z < nz - 1))
            def _(t=t):
                wait_bytes(unit, go_ss.at[t, p, n, 0])

            @pl.when(jnp.logical_and(p >= z, z > 0))
            def _(t=t):
                wait_bytes(unit, go_ss.at[t, p, n, 1])

        return 0

    lax.fori_loop(0, period, drain_units, 0)

    def drain_relay(p, _):
        @pl.when(relayed(p))
        def _():
            for n in range(2):
                wait_bytes(grelay.at[p, n], gl_ss.at[p, n])

        return 0

    lax.fori_loop(0, nz, drain_relay, 0)
    for way in range(2):
        ahead = nz - 1 - z if way == 0 else z
        for slot in range(4):
            @pl.when(slot < 2 * ahead)
            def _(way=way, slot=slot):
                wait_bytes(gleave.at[way, slot], ga_ss.at[way, slot])


def run_kernel(sz, *args):
    nz, bw, items, groups = sz.nz, sz.bw, sz.items, sz.groups
    half, rows, part = sz.half, sz.rows, sz.part
    dma = pltpu.SemaphoreType.DMA
    vm = pltpu.VMEM
    step = (GROUP, bw)
    scratch = [
        vm((items, 4, 2, half, bw), BF16),
        vm((SECTIONS, 2, 4 * bw, bw), BF16),
        vm((4, rows, bw), BF16),
        vm((8, rows, bw), BF16),
        vm((4, groups) + step, F32),
        vm((items, groups) + step, F32),
        vm((items, groups) + step, F32),
        vm((items, 2) + step, F32),
        vm((items, 2) + step, F32),
        vm((items, 2) + step, F32),
        vm((items, 2) + step, F32),
        vm((4, groups) + step, F32),
        vm((4, groups) + step, F32),
        vm((2, 8 * sz.seqs, 128), F32),
        vm((SECTIONS,) + step, F32),
        vm((8,) + step, F32),
        vm((items,) + step, F32),
        vm((nz, items) + step, F32),
        vm((4,) + step, F32),
        vm((8, nz) + step, F32),
        vm((4,) + step, F32),
        vm((8, nz) + step, F32),
        vm((items,) + step, F32),
        vm((items,) + step, F32),
        vm((4, 2) + step, F32),
        vm((12, 2, half, bw), BF16),
        vm((4, 2) + step, F32),
        vm((4, 2) + step, F32),
        vm((8, 2, rows, bw), BF16),
        vm((4, 2, rows, bw), F32),
        vm((4, 2, rows, bw), BF16),
        vm((8, 2, rows, bw), BF16),
        vm((8, rows, bw), BF16),
        vm((4 * bw, 2 * bw), F32),
        vm((SECTIONS, nz, 2, part, bw), BF16),
        vm((nz + 1, 2, part, bw), BF16),
        vm((2, 4, part, bw), BF16),
        vm((nz, 2, part, bw), BF16),
        vm((SECTIONS,) + step, F32),
        vm(step, F32),
        vm((nz - 1,) + step, F32),
        vm((4, 2, half, bw), BF16),
        vm((2, sz.seqs, sz.frames, sz.hidden), BF16),
        vm((2, 8, half, bw), BF16),
        vm((3, bw, sz.hidden), BF16),
        vm((3, 2, 2 * bw, bw), BF16),
        vm((8, half, bw), BF16),
        vm((8, half, bw), BF16),
        vm((8,) + step, F32),
        vm(step, F32),
    ]
    sems = [
        dma((2,)), dma((4,)), dma((4,)), dma((4,)), dma((4, 2)), dma((4, 2)), dma((4, 2)),
        dma((3,)), dma((4,)), dma((1,)), dma((2,)),
        dma((3, 2, 2)), dma((4, 4, 2)), dma((4, 2, 2)), dma((4, 2, 2)),
        dma((4,)), dma((4,)),
        dma((items,)), dma((items,)), dma((items,)), dma((items,)), dma((items,)), dma((items,)),
        dma((4,)), dma((8,)), dma((4,)), dma((8,)),
        dma((4, 2)), dma((8,)), dma((4,)), dma((8,)),
        dma((8,)), dma((8,)), dma((4,)), dma((8,)), dma((4,)), dma((8,)),
        dma((4, 2)), dma((8,)),
        dma((2, 4)), dma((4, nz, 2)), dma((4, nz, 2, 2)), dma((nz + 1, 2)),
        dma((4, nz, 2)), dma((4, nz, 2)), dma((nz, 2)), dma((nz, 2)), dma((4, nz, 2)), dma((4, nz, 2)),
        dma, dma, dma((4, 2)), dma((8,)),
    ]
    anywhere = pl.BlockSpec(memory_space=pl.ANY)
    inside = pl.BlockSpec(memory_space=pltpu.VMEM)
    frames = jax.ShapeDtypeStruct((1, sz.seqs, sz.frames, sz.hidden), BF16)
    vector = jax.ShapeDtypeStruct((1, sz.hidden), F32)
    return pl.pallas_call(
        functools.partial(kernel, sz),
        out_shape=(frames, frames) + (vector,) * 4 + (jax.ShapeDtypeStruct((2, SECTIONS, nz, 2, part, bw), BF16),),
        in_specs=[anywhere] * 3 + [inside] * 6,
        out_specs=(inside,) * 6 + (anywhere,),
        scratch_shapes=scratch + sems,
        compiler_params=pltpu.CompilerParams(
            collective_id=0, has_side_effects=True, vmem_limit_bytes=63 * 2**20
        ),
    )(*args)


def place_weights(sz, pieces, *others):
    bw, part, hidden = sz.bw, sz.part, sz.hidden
    count, strips, ring = bw // part, 8, 3

    def body(*refs):
        src, rest = refs[0], refs[1 : 1 + len(others)]
        dst, rest_out = refs[1 + len(others)], refs[2 + len(others) : 2 + 2 * len(others)]
        arrived, leaving, in_sem, out_sem, rest_in, rest_sem = refs[2 + 2 * len(others) :][:6]
        held = refs[8 + 2 * len(others) :]

        def load(q):
            some = src.at[:, pl.ds(2 * (q // 4), 2), pl.ds(q % 4 * count, count)]
            return pltpu.make_async_copy(some, arrived.at[q], in_sem.at[q])

        def store(q):
            rows = bw if q < 7 else sz.last
            some = dst.at[pl.ds(q * bw, rows)]
            return pltpu.make_async_copy(leaving.at[q % ring, pl.ds(0, rows)], some, out_sem.at[q % ring])

        def through(n, out):
            if out:
                return pltpu.make_async_copy(held[n], rest_out[n], rest_sem.at[n])
            return pltpu.make_async_copy(rest[n], held[n], rest_in.at[n])

        for q in range(strips):
            load(q).start()
        for n in range(len(others)):
            through(n, False).start()
        for q in range(strips):
            load(q).wait()
            if q >= ring:
                store(q - ring).wait()
            for p in range(count):
                for e in range(8):
                    n, x, c = (0 if e // 4 == q // 4 else 1), e % 4 // 2, e % 2
                    wide = bw if e < 7 else sz.last
                    value = arrived[q, c, x, p, n, :, :wide].astype(F32)
                    leaving[q % ring, p * part : (p + 1) * part, e * bw : e * bw + wide] = value
            store(q).start()
            if q == 1:
                for n in range(len(others)):
                    through(n, False).wait()
                    through(n, True).start()
        for q in range(strips - ring, strips):
            store(q).wait()
        for n in range(len(others)):
            through(n, True).wait()

    anywhere = pl.BlockSpec(memory_space=pl.ANY)
    dma = pltpu.SemaphoreType.DMA
    return pl.pallas_call(
        body,
        out_shape=[jax.ShapeDtypeStruct((hidden, hidden), F32)] + [jax.ShapeDtypeStruct(v.shape, v.dtype) for v in others],
        in_specs=[anywhere] * (1 + len(others)),
        out_specs=[anywhere] * (1 + len(others)),
        scratch_shapes=[
            pltpu.VMEM((strips, 2, 2, count, 2, part, bw), BF16),
            pltpu.VMEM((ring, bw, hidden), F32),
            dma((strips,)), dma((ring,)), dma((len(others),)), dma((len(others),)),
        ] + [pltpu.VMEM(v.shape, v.dtype) for v in others],
        compiler_params=pltpu.CompilerParams(vmem_limit_bytes=60 * 2**20),
    )(pieces, *others)


def local(sz, inputs, resets, valid_mask, weights, recurrence, state_bias, norm_gain, norm_shift, cotangent):
    *others, pieces = run_kernel(
        sz, inputs, cotangent, weights, resets, valid_mask, recurrence, state_bias, norm_gain, norm_shift
    )
    grad_weights, outputs, grad_inputs, *vectors = place_weights(sz, pieces, *others)
    return outputs, grad_inputs, grad_weights[None], *vectors


def solution(mesh):
    def step(inputs, *rest):
        sz = Sizes(mesh.shape["rows"] // 2, inputs.shape[1], inputs.shape[2], inputs.shape[3])
        return local(sz, inputs, *rest)

    frames = P("section", None, "rows", None)
    flags = P(None, None, "rows")
    vectors = P("section", None)
    matrix = P("section", None, None)
    return jax.shard_map(
        step,
        mesh=mesh,
        in_specs=(frames, flags, flags, matrix, vectors, vectors, vectors, vectors, frames),
        out_specs=(frames, frames, matrix, vectors, vectors, vectors, vectors),
        check_vma=False,
    )
```

```python
import functools

import jax
import jax.numpy as jnp
from jax import lax
from jax.experimental import pallas as pl
from jax.experimental.pallas import tpu as pltpu
from jax.sharding import PartitionSpec as P

MESH = pl.DeviceIdType.MESH
norm_eps = 1e-05
F32, BF16 = jnp.float32, jnp.bfloat16
SECTIONS = 4
GROUP = 8


class Sizes:
    def __init__(self, nz, seqs, frames, hidden):
        self.nz, self.seqs, self.frames = nz, seqs, frames
        self.pieces = GROUP // seqs
        self.steps = frames // self.pieces
        self.half = seqs * frames
        self.rows = 2 * self.half
        self.groups = self.rows // GROUP
        self.bw = -(-hidden // 1024) * 128
        self.padded = 8 * self.bw
        self.part = 4 * self.bw // nz
        self.items = 4 * SECTIONS
        self.hidden = hidden
        self.last = hidden - 7 * self.bw


def wait_bytes(ref, sem):
    pltpu.make_async_copy(ref, ref, sem).wait()


def local_copy(src, dst, sem):
    pltpu.make_async_copy(src, dst, sem).start()


def remote(src, dst, send, recv, device):
    return pltpu.make_async_remote_copy(
        src_ref=src, dst_ref=dst, send_sem=send, recv_sem=recv, device_id=device, device_id_type=MESH
    )


def kernel(
    sz, inp_raw, cot_raw, w_raw, resets, valid_mask, recurrence, state_bias, norm_gain, norm_shift,
    out, grad_inp, grad_rec, grad_bias, grad_gain, grad_shift, gout,
    mainbuf, wbuf, ysend, yrecv, own, xbuf, states, carry_in, chunk_a, chunk_aex, chunk_s0,
    keepf, validf, flagbuf, par, parblk, pre_send, pre_recv, ex_send, ex_recv, e1_send, e1_recv,
    scal, slopes, s1ex, dbuf, cex, aexr, dpbuf, pkeep, sibsend, sibrecv, xrecv, gw, gall, gpart, gleave, grelay,
    small, small_send, small_recv, outbuf, raw, blocks, wst, wx, outg, ging, smallg, blank,
    raw_ls, wst_ls, in_ss, in_fs, in_rs, cot_ss, cot_rs, par_ss, par_rs, flag_ss, flag_rs, w_ss, w_rs, w_fs, w_ps,
    pre_ss, pre_rs, mx_ss, mx_rs, ms_ss, ms_rs, mf_ss, mf_rs, y_ss, y_rs, ex_ss, ex_rs,
    o_ss, o_rs, e1_ss, e1_rs, dp_ss, dp_rs, sb_ss, sb_rs, xp_ss, xp_rs,
    gi_ss, gi_rs, ga_ss, ga_rs, go_ss, gr_rs, gx_ss, gx_rs, gl_ss, gl_rs, gs_ss, gs_rs, st_ss, st_rs, sm_ss, sm_rs,
):
    nz, bw, items, groups, steps = sz.nz, sz.bw, sz.items, sz.groups, sz.steps
    pieces, seqs = sz.pieces, sz.seqs
    s, r = lax.axis_index("section"), lax.axis_index("rows")
    y, x, z, c = s // 2, s % 2, r // 2, r % 2
    s_x, s_y, s_d = s + 1 - 2 * x, s + 2 - 4 * y, 3 - s
    r_c = r + 1 - 2 * c
    to_x, to_y, to_d, to_c = (s_x, r), (s_y, r), (s_d, r), (s, r_c)
    j_own, j_x, j_c, j_xc = 2 * x + c, 2 * (1 - x) + c, 2 * x + 1 - c, 2 * (1 - x) + 1 - c
    me = 2 * s + c
    part, half, last = sz.part, sz.half, sz.last
    mine = SECTIONS - 1 - s
    pair_half = z % 2
    to_pair = (s, r + 2 - 4 * pair_half)
    sub = lax.broadcasted_iota(jnp.int32, (GROUP, bw), 0)
    place = sub % pieces

    def z_peer(distance):
        return (s, 2 * ((z + distance) % nz) + c)

    def z_slot(p):
        return (z - p + nz - 1) % nz

    def by_seq(rows):
        value = jnp.broadcast_to(rows[seqs - 1], (GROUP, bw))
        for q in range(seqs - 2, -1, -1):
            value = jnp.where(sub < (q + 1) * pieces, jnp.broadcast_to(rows[q], (GROUP, bw)), value)
        return value

    def last_of(value, q):
        return value[(q + 1) * pieces - 1 : (q + 1) * pieces]

    def first_of(value, q):
        return value[q * pieces : q * pieces + 1]

    def entering(a, b, reverse):
        out_a, out_b = [None, None], [None, None]
        t_a = t_b = None
        for h in (1, 0) if reverse else (0, 1):
            ia, ib = a[h], b[h]
            hop = 1
            while hop < pieces:
                if reverse:
                    ok, shift = place < pieces - hop, GROUP - hop
                else:
                    ok, shift = place >= hop, hop
                pa = jnp.where(ok, pltpu.roll(ia, shift, 0), 1.0)
                pb = jnp.where(ok, pltpu.roll(ib, shift, 0), 0.0)
                ib = ia * pb + ib
                ia = ia * pa
                hop *= 2
            if reverse:
                ok, shift, edge = place < pieces - 1, GROUP - 1, first_of
            else:
                ok, shift, edge = place >= 1, 1, last_of
            xa = jnp.where(ok, pltpu.roll(ia, shift, 0), 1.0)
            xb = jnp.where(ok, pltpu.roll(ib, shift, 0), 0.0)
            na = [edge(ia, q) for q in range(seqs)]
            nb = [edge(ib, q) for q in range(seqs)]
            if t_a is not None:
                ea, eb = by_seq(t_a), by_seq(t_b)
                xb = xa * eb + xb
                xa = xa * ea
                nb = [na[q] * t_b[q] + nb[q] for q in range(seqs)]
                na = [na[q] * t_a[q] for q in range(seqs)]
            t_a, t_b = na, nb
            out_a[h], out_b[h] = xa, xb
        return out_a, out_b, t_a, t_b

    def pack(rows):
        rows = rows + [jnp.zeros((1, bw), F32)] * (8 - len(rows))
        value = jnp.zeros((8, bw), F32)
        for q, row in enumerate(rows):
            value = jnp.where(sub == q, jnp.broadcast_to(row, (8, bw)), value)
        return value

    def total(value):
        return jnp.sum(value, axis=0, keepdims=True)

    def over_z(body, start):
        return lax.fori_loop(0, nz, body, start, unroll=nz <= 8)

    def send_z(src, dst_of, send_sem, recv_sem):
        def one(k, _):
            remote(src, dst_of(k - 1), send_sem, recv_sem, z_peer(k)).start()
            return 0

        lax.fori_loop(1, nz, one, 0, unroll=nz <= 8)

    def not_me(t, h):
        return jnp.logical_or(t != s, h != c)

    blank[...] = jnp.zeros((GROUP, bw), F32)

    def width(e):
        return bw if e < 7 else last

    barrier = pltpu.get_barrier_semaphore()
    for t in (s, s_x, s_y, s_d):
        for q in (r, r_c):
            if not (t is s and q is r):
                pl.semaphore_signal(barrier, inc=1, device_id=(t, q), device_id_type=MESH)

    def greet(k, _):
        pl.semaphore_signal(barrier, inc=1, device_id=z_peer(k), device_id_type=MESH)
        return 0

    lax.fori_loop(1, nz, greet, 0)

    local_copy(inp_raw.at[0], raw.at[0], raw_ls.at[0])
    local_copy(cot_raw.at[0], raw.at[1], raw_ls.at[1])
    w_rows = [(1 - y, 2 * pair_half), (1 - y, 2 * pair_half + 1), (y, 2 * pair_half), (y, 2 * pair_half + 1)]
    w_rows += [(y, 2 - 2 * pair_half), (y, 3 - 2 * pair_half)]

    def w_load(n, wait):
        yy, j = w_rows[n]
        k, slot = 4 * yy + j, n % 3

        def go(rows):
            copy = pltpu.make_async_copy(
                w_raw.at[0, pl.ds(pl.multiple_of(k * bw, bw), rows)], wst.at[slot, pl.ds(0, rows)], wst_ls.at[slot]
            )
            copy.wait() if wait else copy.start()

        @pl.when(k < 7)
        def _():
            go(bw)

        @pl.when(k == 7)
        def _():
            if not wait:
                wst[slot, last:] = jnp.zeros((bw - last, sz.hidden), BF16)
            go(last)

    def w_cut(n, column, toward, dst):
        slot = n % 3
        for e in range(8):
            @pl.when(column == e % 4)
            def _(e=e):
                place_of = jnp.where(toward == e // 4, 0, 1)
                if e == 7:
                    dst[place_of] = jnp.zeros((bw, bw), BF16)
                dst[place_of, :, : width(e)] = wst[slot, :, e * bw : e * bw + width(e)]

    for n in range(3):
        w_load(n, False)

    parblk[...] = jnp.zeros(parblk.shape, F32)
    for n, ref in enumerate((recurrence, state_bias, norm_gain, norm_shift)):
        for e in range(8):
            parblk[e, n : n + 1, : width(e)] = ref[0:1, e * bw : e * bw + width(e)]
    par[s] = parblk[me]
    flagbuf[c] = jnp.zeros(flagbuf.shape[1:], F32)
    for n, ref in enumerate((resets, valid_mask)):
        for m in range(4):
            row = seqs * (4 * n + m)
            flagbuf[c, row : row + seqs, : sz.frames] = ref[SECTIONS - 1 - m].astype(F32)

    def w_unit(l, j, n):
        return wbuf.at[l, n, pl.ds(pl.multiple_of(j * bw, bw), bw)]

    def w_cross():
        for k in range(2):
            j = 2 * pair_half + k
            for m, t in enumerate((s_x, s_y, s_d)):
                for n in range(2):
                    src = wx.at[m, n, pl.ds(k * bw, bw)]
                    remote(src, w_unit(s, j, n), w_ss.at[m, k, n], w_rs.at[s, j, n], (t, r)).start()

    for n in range(6):
        if n == 4:
            pl.semaphore_wait(barrier, 7 + nz - 1)

            @pl.when(s == 0)
            def _():
                w_cross()

        w_load(n, True)
        j = w_rows[n][1]
        rows = pl.ds(pl.multiple_of(j * bw, bw), bw)
        half_rows = pl.ds((n % 2) * bw, bw)
        if n < 2:
            w_cut(n, j_own, 1 - y, wx.at[1, :, half_rows])
            w_cut(n, j_x, 1 - y, wx.at[2, :, half_rows])
        elif n < 4:
            w_cut(n, j_x, y, wx.at[0, :, half_rows])
            w_cut(n, j_own, y, wbuf.at[s, :, rows])
        else:
            w_cut(n, j_own, y, wbuf.at[s, :, rows])
        if n + 3 < 6:
            w_load(n + 3, False)

    row = lax.broadcasted_iota(jnp.int32, (half, half), 0)
    col = lax.broadcasted_iota(jnp.int32, (half, half), 1)
    frame_of = (row % GROUP // pieces) * sz.frames + (row % pieces) * steps + row // GROUP
    permute = (col == frame_of).astype(BF16)
    row_of = row
    frame_at = (col % GROUP // pieces) * sz.frames + (col % pieces) * steps + col // GROUP

    def cut_frames(n):
        wait_bytes(raw.at[n], raw_ls.at[n])
        for e in range(8):
            value = raw[n, :, :, e * bw : e * bw + width(e)].reshape(half, width(e))
            if e == 7:
                blocks[n, e] = jnp.zeros((half, bw), BF16)
            blocks[n, e, :, : width(e)] = jnp.dot(permute, value, preferred_element_type=F32).astype(BF16)

    cut_frames(0)

    for n, t in enumerate((s_x, s_y, s_d)):
        remote(parblk.at[2 * t + c], par.at[s], par_ss.at[n], par_rs.at[s], (t, r)).start()
    remote(flagbuf.at[c], flagbuf.at[c], flag_ss.at[0], flag_rs.at[c], to_c).start()

    in_dst = mainbuf.at[mine, :, c]
    near, far = blocks.at[0, pl.ds(4 * y, 4)], blocks.at[0, pl.ds(4 - 4 * y, 4)]
    remote(far, in_dst, in_ss.at[2], in_rs.at[mine, c], to_d).start()
    remote(near, in_dst, in_ss.at[0], in_rs.at[mine, c], to_x).start()
    remote(far, in_dst, in_ss.at[1], in_rs.at[mine, c], to_y).start()
    remote(near, in_dst, in_ss.at[3], in_rs.at[mine, c], to_c).start()
    local_copy(near, in_dst, in_rs.at[mine, c])

    @pl.when(s != 0)
    def _():
        w_cross()

    wait_bytes(flagbuf.at[1 - c], flag_rs.at[1 - c])
    row = lax.broadcasted_iota(jnp.int32, (half, sz.frames), 0)
    col = lax.broadcasted_iota(jnp.int32, (half, sz.frames), 1)
    at_frame = col == (row % pieces) * steps + row // GROUP
    of_seq = row % GROUP // pieces
    ones = jnp.ones((sz.frames, bw), BF16)

    def masks_of(m, _):
        for h in range(2):
            lo, hi = h * steps, (h + 1) * steps
            for n in range(2):
                flags = jnp.zeros((half, sz.frames), F32)
                for q in range(seqs):
                    line = flagbuf[h, pl.ds(seqs * (4 * n + m) + q, 1), : sz.frames]
                    flags = jnp.where(jnp.logical_and(at_frame, of_seq == q), line, flags)
                value = jnp.dot(flags.astype(BF16), ones, preferred_element_type=F32).reshape(steps, GROUP, bw)
                if n == 0:
                    keepf[m, lo:hi] = 1.0 - value
                else:
                    validf[m, lo:hi] = value
        return 0

    lax.fori_loop(0, 4, masks_of, 0)
    for t in (s_x, s_y, s_d):
        wait_bytes(par.at[t], par_rs.at[t])

    def decays_of(i, _):
        l, m = i // 4, i % 4
        u = jnp.broadcast_to(par[l, 0:1], (GROUP, bw))
        a_h, v_h = [], []
        for h in range(2):
            a = jnp.ones((GROUP, bw), F32)
            v = jnp.zeros((GROUP, bw), F32)
            for t in range(steps):
                d = u * keepf[m, h * steps + t]
                a = d * a
                v = d * v + 1.0
            a_h.append(a)
            v_h.append(v)
        xa, xb, ta, tb = entering(a_h, v_h, False)
        for h in range(2):
            chunk_a[i, h] = a_h[h]
            chunk_aex[i, h] = xa[h]
            chunk_s0[i, h] = xb[h]
        valid_count = total(jnp.sum(validf[m], axis=0))
        value = pack(ta + tb + [valid_count])
        pre_send[i] = value
        pre_recv[nz - 1, i] = value
        return 0

    lax.fori_loop(0, items, decays_of, 0)

    def send_decays(l):
        some = pl.ds(4 * l, 4)
        send_z(pre_send.at[some], lambda k: pre_recv.at[k, some], pre_ss.at[l], pre_rs.at[l])

    send_decays(0)

    def inputs_on(slot):
        block = mainbuf.at[slot, :, c]

        @pl.when(slot != mine)
        def _():
            wait_bytes(block, in_rs.at[slot, c])
            remote(block, block, in_fs.at[slot], in_rs.at[slot, c], to_c).start()

        @pl.when(slot == mine)
        def _():
            wait_bytes(block, in_rs.at[slot, c])

    for slot in range(3):
        inputs_on(slot)

    def w_pass(l, k, n):
        j = 2 * pair_half + k

        @pl.when(l != s)
        def _():
            wait_bytes(w_unit(l, j, n), w_rs.at[l, j, n])
            remote(w_unit(l, j, n), w_unit(l, j, n), w_fs.at[l, k, n], w_ps.at[l, k, n], to_pair).start()

    def w_arrive(l):
        @pl.when(l != s)
        def _():
            for k in range(2):
                for n in range(2):
                    wait_bytes(w_unit(l, 2 - 2 * pair_half + k, n), w_ps.at[l, k, n])

    for n in range(2):
        w_pass(0, 0, n)

    for n in range(2):
        w_pass(0, 1, n)
    cut_frames(1)
    def cotangent_out(e):
        t, h = (s, s_x, s_y, s_d)[e // 2], e % 2
        src = blocks.at[1, 2 * t + h]

        @pl.when(not_me(t, h))
        def _():
            remote(src, dbuf.at[mine, c], cot_ss.at[t, h], cot_rs.at[mine, c], (t, 2 * z + h)).start()

        @pl.when(jnp.logical_not(not_me(t, h)))
        def _():
            local_copy(src, dbuf.at[mine, c], cot_rs.at[mine, c])

    def arrived(i):
        block = mainbuf.at[i, j_x]
        wait_bytes(block, mx_rs.at[i])
        remote(block, block, mf_ss.at[i], mf_rs.at[i], to_c).start()

    def project(i):
        l, m = i // 4, i % 4

        @pl.when(m == 0)
        def _():
            w_arrive(l)

        @pl.when(l == 0)
        def _():
            wait_bytes(mainbuf.at[i, :, 1 - c], in_rs.at[m, 1 - c])

        @pl.when(l > 0)
        def _():
            wait_bytes(mainbuf.at[i, j_c], ms_rs.at[i])
            wait_bytes(mainbuf.at[i, j_xc], mf_rs.at[i])
            wait_bytes(ysend.at[m], y_ss.at[m])

        def to_half(n):
            acc = jnp.zeros((sz.rows, bw), F32)
            for j in range(4):
                acc = acc + jnp.dot(
                    mainbuf[i, j].reshape(sz.rows, bw), wbuf[l, n, j * bw : (j + 1) * bw], preferred_element_type=F32
                )
            return acc

        ysend[m] = to_half(1).astype(BF16)
        remote(ysend.at[m], yrecv.at[i % 8], y_ss.at[m], y_rs.at[i % 8], to_y).start()
        own[m] = to_half(0).reshape(groups, GROUP, bw)

    def moments(i):
        l, m = i // 4, i % 4
        wait_bytes(yrecv.at[i % 8], y_rs.at[i % 8])
        pre = own[m] + yrecv[i % 8].astype(F32).reshape(groups, GROUP, bw)
        valid = validf[m]
        pre_sum = total(jnp.sum(pre * valid, axis=0))
        local_count = pre_send[i, 2 * seqs : 2 * seqs + 1]
        pivot = pre_sum / jnp.maximum(local_count, 1.0)
        shifted = pre - pivot
        xbuf[i] = shifted
        square = total(jnp.sum(shifted * shifted * valid, axis=0))
        u = jnp.broadcast_to(par[l, 0:1], (GROUP, bw))
        ends = []
        for h in range(2):
            v = jnp.zeros((GROUP, bw), F32)
            for t in range(steps):
                v = (u * keepf[m, h * steps + t]) * v + shifted[h * steps + t]
            ends.append(v)
        unused_a, xb, unused_t, tb = entering([chunk_a[i, 0], chunk_a[i, 1]], ends, False)
        for h in range(2):
            s1ex[m, h] = xb[h]
        value = pack([pre_sum, square] + tb)

        @pl.when(l > 0)
        def _():
            wait_bytes(ex_recv.at[i % 8, pl.ds(0, nz - 1)], ex_ss.at[m])

        ex_send[m] = value
        ex_recv[i % 8, nz - 1] = value
        send_z(ex_send.at[m], lambda k: ex_recv.at[i % 8, k], ex_ss.at[m], ex_rs.at[i % 8])

    def finish_layer(i):
        l, m = i // 4, i % 4

        @pl.when(m == 0)
        def _():
            wait_bytes(pre_recv.at[pl.ds(0, nz - 1), pl.ds(4 * l, 4)], pre_rs.at[l])

        wait_bytes(ex_recv.at[i % 8, pl.ds(0, nz - 1)], ex_rs.at[i % 8])
        u, bias = par[l, 0:1], par[l, 1:2]
        gain, shift = par[l, 2:3], par[l, 3:4]

        def add_sum(p, carry):
            slot = z_slot(p)
            return (
                carry[0] + ex_recv[i % 8, slot, 0:1],
                carry[1] + pre_recv[slot, i, 2 * seqs : 2 * seqs + 1],
            )

        zero = jnp.zeros((1, bw), F32)
        sum_all, count_all = over_z(add_sum, (zero, zero))
        mean = sum_all / count_all

        def pivot_of(slot):
            count = pre_recv[slot, i, 2 * seqs : 2 * seqs + 1]
            return ex_recv[i % 8, slot, 0:1] / jnp.maximum(count, 1.0), count

        def add_square(p, carry):
            slot = z_slot(p)
            pivot, count = pivot_of(slot)
            return carry + ex_recv[i % 8, slot, 1:2] + count * (pivot - mean) * (pivot - mean)

        var = over_z(add_square, zero) / count_all
        inv = lax.rsqrt(var + norm_eps)
        alpha = gain * inv

        def hop_in(p, carry):
            slot = z_slot(p)
            pivot, unused = pivot_of(slot)
            beta = shift + alpha * (pivot - mean)
            after = []
            for q in range(seqs):
                value = (
                    alpha * ex_recv[i % 8, slot, 2 + q : 3 + q]
                    + beta * pre_recv[slot, i, seqs + q : seqs + q + 1]
                    + pre_recv[slot, i, q : q + 1] * carry[q]
                )
                after.append(jnp.where(p < z, value, carry[q]))
            return tuple(after)

        enter = by_seq(list(over_z(hop_in, (zero,) * seqs)))
        pivot, unused = pivot_of(nz - 1)
        beta = shift + alpha * (pivot - mean)
        offset = (pivot - mean) * inv
        scal[i] = pack([alpha, 1.0 / count_all])
        wide = [jnp.broadcast_to(v, (GROUP, bw)) for v in (u, bias, alpha, beta, inv, offset)]
        u, bias, alpha, beta, inv, offset = wide
        side = mainbuf.at[jnp.maximum(i - 4, 0), j_own]
        odd = (l % 2).astype(F32)
        to_next = l < SECTIONS - 1
        target = jnp.minimum(i + 4, items - 1)
        for h in range(2):
            v = alpha * s1ex[m, h] + beta * chunk_s0[i, h] + chunk_aex[i, h] * enter
            carry_in[i, h] = v
            hidden = []
            for t in range(steps):
                g = h * steps + t
                shifted = xbuf[i, g]
                v = (u * keepf[m, g]) * v + (alpha * shifted + beta)
                states[i, g] = v
                xbuf[i, g] = shifted * inv + offset
                w = v + bias
                hidden.append(validf[m, g] * (w * jax.nn.sigmoid(w)))
            value = jnp.concatenate(hidden, axis=0) + odd * side[h].astype(F32)
            outbuf[m, h] = value.astype(BF16)

        @pl.when(to_next)
        def _():
            block = mainbuf.at[target, j_own]
            block[...] = outbuf[m]
            remote(block, block, mx_ss.at[target], mx_rs.at[target], to_x).start()
            remote(block, block, ms_ss.at[target], ms_rs.at[target], to_c).start()

    def carry_slopes(i):
        l, m = i // 4, i % 4
        u = jnp.broadcast_to(par[l, 0:1], (GROUP, bw))
        a_h = [chunk_a[i, 0], chunk_a[i, 1]]
        xa, unused_b, unused_a, unused_t = entering(a_h, [jnp.zeros((GROUP, bw), F32)] * 2, True)
        sum_one = jnp.zeros((GROUP, bw), F32)
        sum_normed = jnp.zeros((GROUP, bw), F32)
        for h in (1, 0):
            v = xa[h]
            for t in range(steps - 1, -1, -1):
                g = h * steps + t
                sum_one = sum_one + v
                sum_normed = sum_normed + v * xbuf[i, g]
                v = (u * keepf[m, g]) * v
        rows = []
        for value in (sum_one, sum_normed):
            for q in range(seqs):
                inside = jnp.logical_and(sub >= q * pieces, sub < (q + 1) * pieces)
                rows.append(total(jnp.where(inside, value, 0.0)))
        slopes[i] = pack(rows)

    def back_index(b):
        l, m = SECTIONS - 1 - b // 4, b % 4
        return l, m, l * 4 + m

    def act_back(b):
        l, m, i = back_index(b)

        @pl.when(b < 4)
        def _():
            for h in range(2):
                wait_bytes(dbuf.at[m, h], cot_rs.at[m, h])

        u = jnp.broadcast_to(par[l, 0:1], (GROUP, bw))
        bias = jnp.broadcast_to(par[l, 1:2], (GROUP, bw))
        ends = [None, None]
        sum_act = jnp.zeros((GROUP, bw), F32)
        for h in (1, 0):
            grad = dbuf[b % 12, h].astype(F32).reshape(steps, GROUP, bw)
            v = jnp.zeros((GROUP, bw), F32)
            for t in range(steps - 1, -1, -1):
                g = h * steps + t
                w = states[i, g] + bias
                sg = jax.nn.sigmoid(w)
                da = grad[t] * validf[m, g] * (sg * (1.0 + w * (1.0 - sg)))
                own[m, g] = da
                sum_act = sum_act + da
                v = (u * keepf[m, g]) * (da + v)
            ends[h] = v
        xa, xb, unused, tb = entering([chunk_a[i, 0], chunk_a[i, 1]], ends, True)
        for h in range(2):
            aexr[m, h] = xa[h]
            cex[m, h] = xb[h]
        sum_local = jnp.zeros((GROUP, bw), F32)
        sum_normed = jnp.zeros((GROUP, bw), F32)
        for h in (1, 0):
            v = xb[h]
            for t in range(steps - 1, -1, -1):
                g = h * steps + t
                ds = own[m, g] + v
                sum_local = sum_local + ds
                sum_normed = sum_normed + ds * xbuf[i, g]
                v = (u * keepf[m, g]) * ds
        value = pack(tb + [total(sum_local), total(sum_normed)] + [slopes[i, n : n + 1] for n in range(2 * seqs)])

        @pl.when(b >= 4)
        def _():
            wait_bytes(e1_recv.at[b % 8, pl.ds(0, nz - 1)], e1_ss.at[m])

        e1_send[m] = value
        e1_recv[b % 8, nz - 1] = value
        send_z(e1_send.at[m], lambda k: e1_recv.at[b % 8, k], e1_ss.at[m], e1_rs.at[b % 8])
        add_small(l, m, 3, sum_act)

    def add_small(l, m, n, value):
        added = jnp.where(sub == n, jnp.broadcast_to(total(value), (GROUP, bw)), 0.0)
        if n == 3:
            before = jnp.where(m == 0, 0.0, 1.0)
            small[l] = jnp.where(before > 0.0, small[l], 0.0) + added
        else:
            small[l] = small[l] + added

    def state_back(b):
        l, m, i = back_index(b)
        wait_bytes(e1_recv.at[b % 8, pl.ds(0, nz - 1)], e1_rs.at[b % 8])
        zero = blank[...]

        def line(value):
            return jnp.broadcast_to(value, (GROUP, bw))

        def hop_in(n, carry):
            p = nz - 1 - n
            slot = z_slot(p)
            sum_shift, sum_gain = carry[0], carry[1]
            flow, enter = carry[2 : 2 + seqs], carry[2 + seqs :]
            sum_shift = sum_shift + line(e1_recv[b % 8, slot, seqs : seqs + 1])
            sum_gain = sum_gain + line(e1_recv[b % 8, slot, seqs + 1 : seqs + 2])
            after, inside = [], []
            for q in range(seqs):
                one = seqs + 2 + q
                normed = one + seqs
                sum_shift = sum_shift + flow[q] * line(e1_recv[b % 8, slot, one : one + 1])
                sum_gain = sum_gain + flow[q] * line(e1_recv[b % 8, slot, normed : normed + 1])
                inside.append(jnp.where(p == z, flow[q], enter[q]))
                after.append(line(e1_recv[b % 8, slot, q : q + 1]) + line(pre_recv[slot, i, q : q + 1]) * flow[q])
            return (sum_shift, sum_gain, *after, *inside)

        sum_shift, sum_gain, *rest = over_z(hop_in, (zero,) * (2 + 2 * seqs))
        enter = by_seq(rest[seqs:])
        u = jnp.broadcast_to(par[l, 0:1], (GROUP, bw))
        alpha = jnp.broadcast_to(scal[i, 0:1], (GROUP, bw))
        per_count = scal[i, 1:2]
        gain_part, shift_part = sum_gain * per_count, sum_shift * per_count
        sum_rate = jnp.zeros((GROUP, bw), F32)
        rows = [None] * groups
        for h in (1, 0):
            v = cex[m, h] + aexr[m, h] * enter
            for t in range(steps - 1, -1, -1):
                g = h * steps + t
                keep = keepf[m, g]
                ds = own[m, g] + v
                before = carry_in[i, h] if t == 0 else states[i, g - 1]
                sum_rate = sum_rate + (ds * keep) * before
                v = (u * keep) * ds
                rows[g] = alpha * (ds - validf[m, g] * (shift_part + xbuf[i, g] * gain_part))
        @pl.when(b >= 8)
        def _():
            wait_bytes(dpbuf.at[b % 8, 0], dp_ss.at[b % 8])

        dpbuf[b % 8, 0] = jnp.concatenate(rows, axis=0).astype(BF16)
        remote(dpbuf.at[b % 8, 0], dpbuf.at[b % 8, 1], dp_ss.at[b % 8], dp_rs.at[b % 8], to_y).start()
        add_small(l, m, 2, sum_rate)
        small[l] = small[l] + pack([sum_gain[0:1], sum_shift[0:1]])

    nt = (((1,), (1,)), ((), ()))
    tn = (((0,), (0,)), ((), ()))

    def input_back(b):
        l, m, i = back_index(b)
        wait_bytes(dpbuf.at[b % 8, 1], dp_rs.at[b % 8])
        dp_own, dp_other = dpbuf[b % 8, 0], dpbuf[b % 8, 1]

        def toward(j):
            rows = pl.ds(pl.multiple_of(j * bw, bw), bw)
            first = lax.dot_general(dp_own, wbuf[l, 0, rows], nt, preferred_element_type=F32)
            return first + lax.dot_general(dp_other, wbuf[l, 1, rows], nt, preferred_element_type=F32)

        @pl.when(b >= 4)
        def _():
            wait_bytes(sibsend.at[m], sb_ss.at[m])

        sibsend[m, 0] = toward(j_c).astype(BF16)
        sibsend[m, 1] = toward(j_xc).astype(BF16)
        remote(sibsend.at[m], sibrecv.at[b % 8], sb_ss.at[m], sb_rs.at[b % 8], to_c).start()
        pkeep[m, 0] = toward(j_own)
        pkeep[m, 1] = toward(j_x)

    def weight_back(b):
        l, m, i = back_index(b)
        dp = jnp.concatenate([dpbuf[b % 8, 0], dpbuf[b % 8, 1]], axis=1)
        count = nz // 4
        for j in range(4):
            rows = pl.ds(j * bw, bw)
            new = lax.dot_general(mainbuf[i, j].reshape(sz.rows, bw), dp, tn, preferred_element_type=F32)

            @pl.when(m == 0)
            def _(new=new, rows=rows):
                gw[rows] = new

            @pl.when(jnp.logical_and(m > 0, m < 3))
            def _(new=new, rows=rows):
                gw[rows] = gw[rows] + new

            @pl.when(m == 3)
            def _(new=new, rows=rows, j=j):
                all_items = (gw[rows] + new).astype(BF16)
                for n in range(2):
                    value = all_items[:, n * bw : (n + 1) * bw].reshape(count, part, bw)
                    gall[l, j * count : (j + 1) * count, n] = value

    period = 2 * nz

    def unit_of(q, v):
        return jnp.where(q < 2, SECTIONS - 1 - q, 1 - v), jnp.where(q < 2, v, q - 2)

    def round_of(l, n):
        return jnp.where(l < 2, 2 + n, SECTIONS - 1 - l), jnp.where(l < 2, 1 - l, n)

    to_end, to_start = (s, r + 2), (s, r - 2)

    def g_from(p, v, up):
        return gpart.at[p + 1 if up else p, v], gr_rs.at[p + 1 if up else p, v]

    def relayed(p):
        return jnp.abs(z - p) % 2 == 0

    def g_ready(l, p, n, cross):
        if not cross:
            return
        unit, place_out = gall.at[l, p, n], gout.at[c, s, p, n]
        by_relay = jnp.logical_and(l == s_d, relayed(p))

        @pl.when(jnp.logical_and(l != s, jnp.logical_not(by_relay)))
        def _():
            remote(unit, place_out, gx_ss.at[l, p, n], gx_rs.at[s, p, n], (l, r)).start()

        @pl.when(by_relay)
        def _():
            remote(unit, grelay.at[p, n], gx_ss.at[l, p, n], gl_rs.at[p, n], to_y).start()

        @pl.when(l == s)
        def _():
            local_copy(unit, place_out, gx_rs.at[s, p, n])
            remote(unit, place_out, gs_ss.at[s, p, n], gs_rs.at[s, p, n], to_c).start()

    def g_step(g, cross):
        for up in (True, False):
            place_z = z if up else nz - 1 - z
            ahead = nz - 1 - place_z
            t = g - 2 * place_z
            q = t // period
            k = t % period
            v = k % 2
            l, n = unit_of(q, v)
            inside = jnp.logical_and(t >= 0, q < SECTIONS)

            @pl.when(jnp.logical_and(inside, k < 2 * ahead))
            def _(up=up, place_z=place_z, q=q, k=k, l=l, n=n, v=v):
                far = nz - 1 - k // 2
                p = far if up else nz - 1 - far
                unit = gall.at[l, p, n]

                buf, sem = g_from(p, v, up)
                way, slot = 0 if up else 1, k % 4
                leaving = gleave.at[way, slot]

                @pl.when(jnp.logical_or(q > 0, k >= 4))
                def _():
                    wait_bytes(leaving, ga_ss.at[way, slot])

                @pl.when(place_z > 0)
                def _():
                    wait_bytes(buf, sem)
                    leaving[...] = (unit[...].astype(F32) + buf[...].astype(F32)).astype(BF16)

                @pl.when(place_z == 0)
                def _():
                    leaving[...] = unit[...]

                remote(leaving, buf, ga_ss.at[way, slot], sem, to_end if up else to_start).start()

            @pl.when(jnp.logical_and(inside, k >= 2 * ahead))
            def _(up=up, ahead=ahead, k=k, l=l, n=n, v=v):
                back = (k - 2 * ahead) // 2
                p = z - back if up else z + back
                unit = gall.at[l, p, n]

                @pl.when(back == 0)
                def _():
                    if up:
                        whole = unit[...].astype(F32)
                        for way, there in ((True, z > 0), (False, z < nz - 1)):
                            buf, sem = g_from(p, v, way)

                            @pl.when(there)
                            def _(buf=buf, sem=sem):
                                wait_bytes(buf, sem)

                            whole = whole + jnp.where(there, buf[...].astype(F32), 0.0)
                        unit[...] = whole.astype(BF16)
                        g_ready(l, p, n, cross)

                @pl.when(back > 0)
                def _():
                    wait_bytes(unit, ga_rs.at[l, p, n])
                    g_ready(l, p, n, cross)

                @pl.when(ahead > 0)
                def _():
                    way = 0 if up else 1
                    remote(unit, unit, go_ss.at[l, p, n, way], ga_rs.at[l, p, n], to_end if up else to_start).start()

    def cross_back(b):
        m = b % 4
        wait_bytes(sibrecv.at[b % 8], sb_rs.at[b % 8])

        @pl.when(b < 4)
        def _():
            wait_bytes(ysend.at[m], y_ss.at[m])

        @pl.when(b >= 4)
        def _():
            wait_bytes(ysend.at[m], xp_ss.at[m])

        ysend[m] = (pkeep[m, 1] + sibrecv[b % 8, 1].astype(F32)).astype(BF16)
        remote(ysend.at[m], xrecv.at[b % 8], xp_ss.at[m], xp_rs.at[b % 8], to_x).start()
        pkeep[m, 0] = pkeep[m, 0] + sibrecv[b % 8, 0].astype(F32)

    def join_back(b):
        l, m, i = back_index(b)
        wait_bytes(xrecv.at[b % 8], xp_rs.at[b % 8])
        even = (1 - l % 2).astype(F32)
        side = dbuf[jnp.maximum(b - 4, 0) % 12].astype(F32).reshape(sz.rows, bw)
        value = pkeep[m, 0] + xrecv[b % 8].astype(F32) + even * side
        dbuf[(b + 4) % 12] = value.astype(BF16).reshape(2, sz.half, bw)

    def frames_out(m):
        t = SECTIONS - 1 - m
        for h in range(2):
            grads = dbuf.at[(items + m) % 12, h]

            @pl.when(not_me(t, h))
            def _(h=h, grads=grads):
                remote(outbuf.at[m, h], outg.at[me], o_ss.at[m, h], o_rs.at[me], (t, 2 * z + h)).start()
                remote(grads, ging.at[me], gi_ss.at[m, h], gi_rs.at[me], (t, 2 * z + h)).start()

            @pl.when(jnp.logical_not(not_me(t, h)))
            def _(h=h, grads=grads):
                local_copy(outbuf.at[m, h], outg.at[me], o_rs.at[me])
                local_copy(grads, ging.at[me], gi_rs.at[me])

    first_step = 6


    def forward_tick(k):
        @pl.when(k < items)
        def _():
            project(k)

        @pl.when(k == 1)
        def _():
            inputs_on(3)

        @pl.when(jnp.logical_and(k >= 1, k < items + 1))
        def _():
            moments(k - 1)

        @pl.when(jnp.logical_and(k >= 2, k < items + 2))
        def _():
            finish_layer(k - 2)

        @pl.when(jnp.logical_and(k >= 2, k < items + 2))
        def _():
            carry_slopes(k - 2)

        @pl.when(jnp.logical_and(k + 1 >= 4, k + 1 < items))
        def _():
            arrived(k + 1)

        for e in range(8):
            @pl.when(k == 3 + e)
            def _(e=e):
                cotangent_out(e)

        @pl.when(k < 11)
        def _():
            @pl.when(k == 0)
            def _():
                w_pass(1, 0, 0)

            unit = k + 1
            for n in range(4):
                @pl.when(unit % 4 == n)
                def _(n=n):
                    w_pass(unit // 4 + 1, n // 2, n % 2)

            @pl.when(k % 4 == 1)
            def _():
                send_decays(k // 4 + 1)

    def backward_tick(k):
        @pl.when(k >= 4)
        def _():
            join_back(k - 4)

        @pl.when(jnp.logical_and(k >= 0, k < items))
        def _():
            act_back(k)

        @pl.when(jnp.logical_and(k >= 1, k < items + 1))
        def _():
            state_back(k - 1)

        @pl.when(k >= first_step)
        def _():
            g_step(k - first_step, False)

        @pl.when(jnp.logical_and(k >= 2, k < items + 2))
        def _():
            input_back(k - 2)
            weight_back(k - 2)
            cross_back(k - 2)

    start = items - 2

    def tick(k, _):
        forward_tick(k)
        backward_tick(k - start)
        return 0

    lax.fori_loop(0, start + items + 4, tick, 0)

    small_send[...] = pack([small[l, n : n + 1] for l in range(SECTIONS) for n in (2, 3)])
    send_z(small_send, lambda k: small_recv.at[k], st_ss, st_rs)
    steps_done = items + 4 - first_step
    steps_all = SECTIONS * period + 2 * (nz - 1)

    def whole_at(l, p, n):
        q, v = round_of(l, n)
        return q * period + 2 * (nz - 1) + 2 * jnp.abs(z - p) + v

    def crosses_at(l, p, n):
        early = whole_at(l, p, n) < steps_done
        return jnp.where(early, steps_done + 2 + 2 * p + n, whole_at(l, p, n))

    def cross_early(g):
        p, n = (g - steps_done - 2) // 2, (g - steps_done - 2) % 2

        @pl.when(jnp.logical_and(g >= steps_done + 2, p < nz))
        def _():
            for l in range(SECTIONS):
                @pl.when(whole_at(l, p, n) < steps_done)
                def _(l=l):
                    g_ready(l, p, n, True)

    def relay_lag(l):
        return jnp.where(l < 2, 4, 12)

    def g_relay(g):
        def one(p, _):
            for n in range(2):
                @pl.when(jnp.logical_and(relayed(p), crosses_at(s_x, p, n) + relay_lag(s_x) == g))
                def _(n=n):
                    wait_bytes(grelay.at[p, n], gl_rs.at[p, n])
                    remote(grelay.at[p, n], gout.at[c, s_y, p, n], gl_ss.at[p, n], gx_rs.at[s_y, p, n], to_x).start()

            return 0

        lax.fori_loop(0, nz, one, 0)

    def g_to_other_core(g):
        lag = jnp.where(s < 2, 6, 14)

        def one(p, _):
            for n in range(2):
                sent = crosses_at(s, p, n) + lag

                def onward(t, n=n):
                    unit = gout.at[c, t, p, n]
                    wait_bytes(unit, gx_rs.at[t, p, n])
                    remote(unit, unit, gs_ss.at[t, p, n], gs_rs.at[t, p, n], to_c).start()

                @pl.when(sent == g)
                def _(onward=onward):
                    onward(s_x)
                    onward(s_y)

                @pl.when(sent + jnp.where(relayed(p), relay_lag(s), 0) == g)
                def _(onward=onward):
                    onward(s_d)

            return 0

        lax.fori_loop(0, nz, one, 0)

    def sum_small():
        wait_bytes(small_recv, st_rs)
        wait_bytes(small_recv, st_ss)

        def add_rest(k, carry):
            return carry + small_recv[k]

        sums = lax.fori_loop(0, nz - 1, add_rest, small_send[...])
        for l in range(SECTIONS):
            rate = jnp.broadcast_to(sums[2 * l : 2 * l + 1], (GROUP, bw))
            bias = jnp.broadcast_to(sums[2 * l + 1 : 2 * l + 2], (GROUP, bw))
            small[l] = jnp.where(sub == 2, rate, jnp.where(sub == 3, bias, small[l]))
        for t in range(SECTIONS):
            for h in range(2):
                @pl.when(not_me(t, h))
                def _(t=t, h=h):
                    remote(small.at[t], smallg.at[me], sm_ss.at[t, h], sm_rs.at[me], (t, 2 * z + h)).start()

                @pl.when(jnp.logical_not(not_me(t, h)))
                def _(t=t):
                    local_copy(small.at[t], smallg.at[me], sm_rs.at[me])

    restore = (row_of == frame_at).astype(BF16)

    def place_block(e):
        wait_bytes(outg.at[e], o_rs.at[e])
        wait_bytes(ging.at[e], gi_rs.at[e])
        for src, dst in ((outg, out), (ging, grad_inp)):
            value = jnp.dot(restore, src[e], preferred_element_type=F32).astype(BF16)
            value = value.reshape(seqs, sz.frames, bw)
            dst[0, :, :, e * bw : e * bw + width(e)] = value[:, :, : width(e)]

    def drain_layers():
        for l in range(SECTIONS):
            @pl.when(l != s)
            def _(l=l):
                for k in range(2):
                    for n in range(2):
                        wait_bytes(w_unit(l, k, n), w_fs.at[l, k, n])

            wait_bytes(pre_recv.at[pl.ds(0, nz - 1), pl.ds(4 * l, 4)], pre_ss.at[l])
            wait_bytes(ex_recv.at[l, pl.ds(0, nz - 1)], ex_ss.at[l])
            wait_bytes(e1_recv.at[l, pl.ds(0, nz - 1)], e1_ss.at[l])
            wait_bytes(sibsend.at[l], sb_ss.at[l])
            wait_bytes(ysend.at[l], xp_ss.at[l])
            for h in range(2):
                @pl.when(not_me(l, h))
                def _(l=l, h=h):
                    wait_bytes(dbuf.at[mine, c], cot_ss.at[l, h])
                    wait_bytes(small.at[l], sm_ss.at[l, h])

                @pl.when(not_me(SECTIONS - 1 - l, h))
                def _(l=l, h=h):
                    wait_bytes(outbuf.at[l, h], o_ss.at[l, h])
                    wait_bytes(dbuf.at[(items + l) % 12, h], gi_ss.at[l, h])

        def drain(i, _):
            @pl.when(i < 8)
            def _():
                wait_bytes(dpbuf.at[i, 0], dp_ss.at[i])

            @pl.when(i >= 4)
            def _():
                wait_bytes(mainbuf.at[i, j_own], mx_ss.at[i])
                wait_bytes(mainbuf.at[i, j_own], ms_ss.at[i])
                wait_bytes(mainbuf.at[i, j_x], mf_ss.at[i])

            return 0

        lax.fori_loop(0, items, drain, 0)
        for n in range(4):
            wait_bytes(in_dst, in_ss.at[n])
        for slot in range(4):
            @pl.when(slot != mine)
            def _(slot=slot):
                wait_bytes(in_dst, in_fs.at[slot])

        for n in range(3):
            wait_bytes(par.at[s], par_ss.at[n])
            for k in range(2):
                for m in range(2):
                    wait_bytes(wx.at[n, m, pl.ds(k * bw, bw)], w_ss.at[n, k, m])

        wait_bytes(flagbuf.at[c], flag_ss.at[0])

    def late_step(g, _):
        g_step(g, True)
        cross_early(g)
        g_relay(g)
        g_to_other_core(g)

        @pl.when(g == steps_done)
        def _():
            for m in range(4):
                frames_out(m)

        @pl.when(g == steps_done + 5)
        def _():
            sum_small()

        for e in range(8):
            @pl.when(g == steps_done + 16 + e)
            def _(e=e):
                place_block(e)

        @pl.when(g == steps_done + 24)
        def _():
            drain_layers()

        return 0

    lax.fori_loop(steps_done, max(steps_all + 10, steps_done + period + 28), late_step, 0)

    for e in range(8):
        wait_bytes(smallg.at[e], sm_rs.at[e])
        for n, dst in enumerate((grad_gain, grad_shift, grad_rec, grad_bias)):
            dst[0:1, e * bw : e * bw + width(e)] = smallg[e, n : n + 1, : width(e)]

    def drain_units(k, _):
        p, n = k // 2, k % 2
        unit = gall.at[0, p, n]
        for t in range(SECTIONS):
            wait_bytes(unit, gs_rs.at[t, p, n])
            wait_bytes(unit, gs_ss.at[t, p, n])

            @pl.when(t != s)
            def _(t=t):
                wait_bytes(unit, gx_ss.at[t, p, n])

            @pl.when(t == s)
            def _(t=t):
                wait_bytes(unit, gx_rs.at[t, p, n])

            @pl.when(jnp.logical_and(p <= z, z < nz - 1))
            def _(t=t):
                wait_bytes(unit, go_ss.at[t, p, n, 0])

            @pl.when(jnp.logical_and(p >= z, z > 0))
            def _(t=t):
                wait_bytes(unit, go_ss.at[t, p, n, 1])

        return 0

    lax.fori_loop(0, period, drain_units, 0)

    def drain_relay(p, _):
        @pl.when(relayed(p))
        def _():
            for n in range(2):
                wait_bytes(grelay.at[p, n], gl_ss.at[p, n])

        return 0

    lax.fori_loop(0, nz, drain_relay, 0)
    for way in range(2):
        ahead = nz - 1 - z if way == 0 else z
        for slot in range(4):
            @pl.when(slot < 2 * ahead)
            def _(way=way, slot=slot):
                wait_bytes(gleave.at[way, slot], ga_ss.at[way, slot])


def run_kernel(sz, *args):
    nz, bw, items, groups = sz.nz, sz.bw, sz.items, sz.groups
    half, rows, part = sz.half, sz.rows, sz.part
    dma = pltpu.SemaphoreType.DMA
    vm = pltpu.VMEM
    step = (GROUP, bw)
    scratch = [
        vm((items, 4, 2, half, bw), BF16),
        vm((SECTIONS, 2, 4 * bw, bw), BF16),
        vm((4, rows, bw), BF16),
        vm((8, rows, bw), BF16),
        vm((4, groups) + step, F32),
        vm((items, groups) + step, F32),
        vm((items, groups) + step, F32),
        vm((items, 2) + step, F32),
        vm((items, 2) + step, F32),
        vm((items, 2) + step, F32),
        vm((items, 2) + step, F32),
        vm((4, groups) + step, F32),
        vm((4, groups) + step, F32),
        vm((2, 8 * sz.seqs, 128), F32),
        vm((SECTIONS,) + step, F32),
        vm((8,) + step, F32),
        vm((items,) + step, F32),
        vm((nz, items) + step, F32),
        vm((4,) + step, F32),
        vm((8, nz) + step, F32),
        vm((4,) + step, F32),
        vm((8, nz) + step, F32),
        vm((items,) + step, F32),
        vm((items,) + step, F32),
        vm((4, 2) + step, F32),
        vm((12, 2, half, bw), BF16),
        vm((4, 2) + step, F32),
        vm((4, 2) + step, F32),
        vm((8, 2, rows, bw), BF16),
        vm((4, 2, rows, bw), F32),
        vm((4, 2, rows, bw), BF16),
        vm((8, 2, rows, bw), BF16),
        vm((8, rows, bw), BF16),
        vm((4 * bw, 2 * bw), F32),
        vm((SECTIONS, nz, 2, part, bw), BF16),
        vm((nz + 1, 2, part, bw), BF16),
        vm((2, 4, part, bw), BF16),
        vm((nz, 2, part, bw), BF16),
        vm((SECTIONS,) + step, F32),
        vm(step, F32),
        vm((nz - 1,) + step, F32),
        vm((4, 2, half, bw), BF16),
        vm((2, sz.seqs, sz.frames, sz.hidden), BF16),
        vm((2, 8, half, bw), BF16),
        vm((3, bw, sz.hidden), BF16),
        vm((3, 2, 2 * bw, bw), BF16),
        vm((8, half, bw), BF16),
        vm((8, half, bw), BF16),
        vm((8,) + step, F32),
        vm(step, F32),
    ]
    sems = [
        dma((2,)), dma((4,)), dma((4,)), dma((4,)), dma((4, 2)), dma((4, 2)), dma((4, 2)),
        dma((3,)), dma((4,)), dma((1,)), dma((2,)),
        dma((3, 2, 2)), dma((4, 4, 2)), dma((4, 2, 2)), dma((4, 2, 2)),
        dma((4,)), dma((4,)),
        dma((items,)), dma((items,)), dma((items,)), dma((items,)), dma((items,)), dma((items,)),
        dma((4,)), dma((8,)), dma((4,)), dma((8,)),
        dma((4, 2)), dma((8,)), dma((4,)), dma((8,)),
        dma((8,)), dma((8,)), dma((4,)), dma((8,)), dma((4,)), dma((8,)),
        dma((4, 2)), dma((8,)),
        dma((2, 4)), dma((4, nz, 2)), dma((4, nz, 2, 2)), dma((nz + 1, 2)),
        dma((4, nz, 2)), dma((4, nz, 2)), dma((nz, 2)), dma((nz, 2)), dma((4, nz, 2)), dma((4, nz, 2)),
        dma, dma, dma((4, 2)), dma((8,)),
    ]
    anywhere = pl.BlockSpec(memory_space=pl.ANY)
    inside = pl.BlockSpec(memory_space=pltpu.VMEM)
    frames = jax.ShapeDtypeStruct((1, sz.seqs, sz.frames, sz.hidden), BF16)
    vector = jax.ShapeDtypeStruct((1, sz.hidden), F32)
    return pl.pallas_call(
        functools.partial(kernel, sz),
        out_shape=(frames, frames) + (vector,) * 4 + (jax.ShapeDtypeStruct((2, SECTIONS, nz, 2, part, bw), BF16),),
        in_specs=[anywhere] * 3 + [inside] * 6,
        out_specs=(inside,) * 6 + (anywhere,),
        scratch_shapes=scratch + sems,
        compiler_params=pltpu.CompilerParams(
            collective_id=0, has_side_effects=True, vmem_limit_bytes=63 * 2**20
        ),
    )(*args)


def place_weights(sz, pieces, *others):
    bw, part, hidden = sz.bw, sz.part, sz.hidden
    count, strips, ring = bw // part, 8, 3

    def body(*refs):
        src, rest = refs[0], refs[1 : 1 + len(others)]
        dst, rest_out = refs[1 + len(others)], refs[2 + len(others) : 2 + 2 * len(others)]
        arrived, leaving, in_sem, out_sem, rest_in, rest_sem = refs[2 + 2 * len(others) :][:6]
        held = refs[8 + 2 * len(others) :]

        def load(q):
            some = src.at[:, pl.ds(2 * (q // 4), 2), pl.ds(q % 4 * count, count)]
            return pltpu.make_async_copy(some, arrived.at[q], in_sem.at[q])

        def store(q):
            rows = bw if q < 7 else sz.last
            some = dst.at[pl.ds(q * bw, rows)]
            return pltpu.make_async_copy(leaving.at[q % ring, pl.ds(0, rows)], some, out_sem.at[q % ring])

        def through(n, out):
            if out:
                return pltpu.make_async_copy(held[n], rest_out[n], rest_sem.at[n])
            return pltpu.make_async_copy(rest[n], held[n], rest_in.at[n])

        for q in range(strips):
            load(q).start()
        for n in range(len(others)):
            through(n, False).start()
        for q in range(strips):
            load(q).wait()
            if q >= ring:
                store(q - ring).wait()
            for p in range(count):
                for e in range(8):
                    n, x, c = (0 if e // 4 == q // 4 else 1), e % 4 // 2, e % 2
                    wide = bw if e < 7 else sz.last
                    value = arrived[q, c, x, p, n, :, :wide].astype(F32)
                    leaving[q % ring, p * part : (p + 1) * part, e * bw : e * bw + wide] = value
            store(q).start()
            if q == 1:
                for n in range(len(others)):
                    through(n, False).wait()
                    through(n, True).start()
        for q in range(strips - ring, strips):
            store(q).wait()
        for n in range(len(others)):
            through(n, True).wait()

    anywhere = pl.BlockSpec(memory_space=pl.ANY)
    dma = pltpu.SemaphoreType.DMA
    return pl.pallas_call(
        body,
        out_shape=[jax.ShapeDtypeStruct((hidden, hidden), F32)] + [jax.ShapeDtypeStruct(v.shape, v.dtype) for v in others],
        in_specs=[anywhere] * (1 + len(others)),
        out_specs=[anywhere] * (1 + len(others)),
        scratch_shapes=[
            pltpu.VMEM((strips, 2, 2, count, 2, part, bw), BF16),
            pltpu.VMEM((ring, bw, hidden), F32),
            dma((strips,)), dma((ring,)), dma((len(others),)), dma((len(others),)),
        ] + [pltpu.VMEM(v.shape, v.dtype) for v in others],
        compiler_params=pltpu.CompilerParams(vmem_limit_bytes=60 * 2**20),
    )(pieces, *others)


def local(sz, inputs, resets, valid_mask, weights, recurrence, state_bias, norm_gain, norm_shift, cotangent):
    *others, pieces = run_kernel(
        sz, inputs, cotangent, weights, resets, valid_mask, recurrence, state_bias, norm_gain, norm_shift
    )
    grad_weights, outputs, grad_inputs, *vectors = place_weights(sz, pieces, *others)
    return outputs, grad_inputs, grad_weights[None], *vectors


def solution(mesh):
    def step(inputs, *rest):
        sz = Sizes(mesh.shape["rows"] // 2, inputs.shape[1], inputs.shape[2], inputs.shape[3])
        return local(sz, inputs, *rest)

    frames = P("section", None, "rows", None)
    flags = P(None, None, "rows")
    vectors = P("section", None)
    matrix = P("section", None, None)
    return jax.shard_map(
        step,
        mesh=mesh,
        in_specs=(frames, flags, flags, matrix, vectors, vectors, vectors, vectors, frames),
        out_specs=(frames, frames, matrix, vectors, vectors, vectors, vectors),
        check_vma=False,
    )
```
